32 devices in a mesh: dp: 4 (over y, core), expert: 8 (over z, x).
Axes of the slice: x: 2, y: 2, z: 4, core: 2. Of those that a mesh axis runs over, the one named last changes fastest.
Arguments:
- tokens: bfloat16 [16384, 768], P(('dp', 'expert')), may hold values from -6 to 6
- segments: int32 [32, 512], P(('dp', 'expert')), may hold values from 0 to 4, never falling along the last dimension, each value on 1 to 256 neighbouring positions
- routes: int32 [16384], P(('dp', 'expert')), may hold values from 0 to 15
- slots: int32 [16384], P(('dp', 'expert')), may hold values from -1 to 39, as said below
- bucket_table: int32 [1023], replicated, may hold values from 0 to 31
- gain_attn: float32 [768], replicated, may hold values from 0.1 to 1.9
- w_query: bfloat16 [768, 768], P('dp'), may hold values from -0.21875 to 0.21875
- w_key: bfloat16 [768, 768], P('dp'), may hold values from -0.21875 to 0.21875
- w_value: bfloat16 [768, 768], P('dp'), may hold values from -0.21875 to 0.21875
- w_output: bfloat16 [768, 768], P('dp'), may hold values from -0.625 to 0.625
- rel_bias: float32 [32, 12], replicated, may hold values from -4 to 4
- gain_ffn: float32 [768], replicated, may hold values from 0.1 to 1.9
- w_router: bfloat16 [768, 16], P('dp'), may hold values from -0.15625 to 0.15625
- w_in: bfloat16 [16, 768, 3072], P('expert'), may hold values from -0.21875 to 0.21875
- w_out: bfloat16 [16, 3072, 768], P('expert'), may hold values from -1.75 to 1.75
- cotangent: bfloat16 [16384, 768], P(('dp', 'expert')), may hold values from -6 to 6
Outputs:
- output: bfloat16 [16384, 768], P(('dp', 'expert'))
- grad_tokens: float32 [16384, 768], P(('dp', 'expert'))
- grad_gain_attn: float32 [768], replicated
- grad_query: float32 [768, 768], P('dp')
- grad_key: float32 [768, 768], P('dp')
- grad_value: float32 [768, 768], P('dp')
- grad_output: float32 [768, 768], P('dp')
- grad_rel_bias: float32 [32, 12], replicated
- grad_gain_ffn: float32 [768], replicated
- grad_router: float32 [768, 16], P('dp')
- grad_w_in: float32 [16, 768, 3072], P('expert', None, 'dp')
- grad_w_out: float32 [16, 3072, 768], P('expert', 'dp')
The draws below stay inside these ranges and needn't reach their ends.
Inputs may be any that keep to these rules, and one draw needn't show every extreme that they name: `slots`: a token's slot is the number of earlier tokens of its device with the same route when that number is under 40, and -1 otherwise.
All inputs are finite; a program needn't handle non-finite values.
Results may differ from the reference program's by a relative error of at most 0.02.
Values may be sent and summed in bfloat16 or wider, within the bound.
No kernel may reach another device: no remote copies, remote signals or barrier semaphores. Data moves between devices by JAX's collectives and lax.ppermute only.
A program may use at most 256 MiB of HBM per device.

```python
import math
import jax
import jax.numpy as jnp
import numpy as np
from jax import lax

D = 768
HEADS = 12
HEAD_DIM = 64
FF = 3072
BUCKETS = 32
TOK_DEV = 512
EXPERTS = 16
SEQS = 32
TOKENS = 16384
CAP = 40
N_DP = 4
N_EXPERT = 8


def route_plan(key):
    blocks = TOKENS // TOK_DEV
    groups = blocks // N_EXPERT
    base_key, hot_key, pick_key = jax.random.split(key, 3)
    chosen = jax.random.randint(base_key, (blocks, TOK_DEV), 0, EXPERTS, dtype=jnp.int32)
    hot_expert = jax.random.randint(hot_key, (groups,), 0, EXPERTS, dtype=jnp.int32)
    hot_rows = jnp.repeat(hot_expert, N_EXPERT)
    shuffled = jax.vmap(lambda sub_key: jax.random.permutation(sub_key, TOK_DEV))(jax.random.split(pick_key, blocks))
    crowded = shuffled <= CAP
    chosen = jnp.where(crowded, hot_rows[:, None], chosen)
    onehot = (chosen[:, :, None] == jnp.arange(EXPERTS, dtype=jnp.int32)[None, None, :]).astype(jnp.int32)
    before = jnp.cumsum(onehot, axis=1) - onehot
    ranking = jnp.sum(before * onehot, axis=2)
    slot_ids = jnp.where(ranking < CAP, ranking, -1)
    return (chosen.reshape(TOKENS).astype(jnp.int32), slot_ids.reshape(TOKENS).astype(jnp.int32))


def draw_routes(key, part):
    return route_plan(key)[0]


def draw_slots(key, part):
    return route_plan(key)[1]


def set_ends(values, key, low, largest):
    place = [jax.random.randint(jax.random.fold_in(key, axis), (), 0, length) for axis, length in enumerate(values.shape)]
    main_axis = values.shape.index(max(values.shape))
    neighbour = place[:main_axis] + [(place[main_axis] + 1) % values.shape[main_axis]] + place[main_axis + 1:]
    return values.at[tuple(place)].set(low).at[tuple(neighbour)].set(largest)


def block_levels(rng, dims, pieces, low, largest):
    level, own = 1.0, jax.random.fold_in(rng, 6)
    for position, shards_of in pieces:
        heights = jnp.exp(jax.random.uniform(jax.random.fold_in(own, position), (shards_of,), jnp.float32, low / len(pieces), largest / len(pieces)))
        level = level * jnp.repeat(heights, dims[position] // shards_of).reshape([-1 if axis == position else 1 for axis in range(len(dims))])
    return level


def split_up(count, total, limit, skew):
    loads = [(1 << 20) // math.isqrt(standing ** skew) + 1 for standing in range(2, count + 1)]
    spare, given = total - limit - (count - 1), [1] * (count - 1)
    while spare > 0:
        candidates = [i for i in range(count - 1) if given[i] < limit]
        whole, remaining = sum([loads[i] for i in candidates]), spare
        for i in candidates:
            extra = min(limit - given[i], max(1, remaining * loads[i] // whole), spare)
            given[i] = given[i] + extra
            spare = spare - extra
    return np.array([limit] + given)


def uneven(own_key, count, total, limit, skew):
    if count == 2:
        one = jax.random.randint(own_key, (), max(1, total - limit), min(limit, total - 1) + 1)
        return jnp.stack([one, total - one])
    lengths = jnp.asarray(split_up(count, total, limit, skew), jnp.int32)
    couples = (count - 1) // 2
    donor, sink = lengths[1:1 + 2 * couples:2], lengths[2:2 + 2 * couples:2]
    slack = jnp.minimum(donor - 1, limit - sink)
    shifted = jax.random.randint(jax.random.fold_in(own_key, 1), (couples,), 0, 1 << 20) % (slack + 1)
    lengths = lengths.at[1:1 + 2 * couples:2].set(donor - shifted).at[2:2 + 2 * couples:2].set(sink + shifted)
    return lengths[jax.random.permutation(jax.random.fold_in(own_key, 2), count)]


def normal_values(rng, extent, deviation, limit, cuts=(), kind=jnp.bfloat16):
    factor_of = block_levels(rng, extent, cuts, -0.22, 0.18) if cuts else 1.0
    entries = jax.random.normal(rng, extent, jnp.float32) * deviation * factor_of
    return jnp.minimum(jnp.maximum(entries, -limit), limit).astype(kind)


def setup_inputs(seed: int = 0) -> dict:
    splits = jax.random.split(jax.random.key(seed), 17)
    tokens = normal_values(splits[0], (TOKENS, D), 1.0, 6.0, ((0, 32),))
    segments = jax.vmap(lambda own: jnp.searchsorted(jnp.cumsum(uneven(own, max(4, TOK_DEV // 100), TOK_DEV, min(800, TOK_DEV // 2), 0)), jnp.arange(TOK_DEV), side="right"))(jax.random.split(splits[1], SEQS)).reshape((SEQS, TOK_DEV)).astype(jnp.int32)
    routes = draw_routes(jax.random.fold_in(splits[16], 71), 0)
    slots = draw_slots(jax.random.fold_in(splits[16], 71), 0)
    bucket_table = set_ends(jax.random.randint(splits[4], (2 * TOK_DEV - 1,), 0, BUCKETS), jax.random.fold_in(splits[4], 1), 0, BUCKETS - 1).astype(jnp.int32)
    gain_attn = jnp.clip(1.0 + 0.18 * jax.random.normal(splits[5], (D,), jnp.float32), 0.1, 1.9)
    w_query = normal_values(splits[6], (D, D), D ** -0.5, 0.21875, ((0, 4),))
    w_key = normal_values(splits[7], (D, D), D ** -0.5, 0.21875, ((0, 4),))
    w_value = normal_values(splits[8], (D, D), D ** -0.5, 0.21875, ((0, 4),))
    w_output = normal_values(splits[9], (D, D), (D // 8) ** -0.5, 0.625, ((0, 4),))
    rel_bias = normal_values(splits[10], (BUCKETS, HEADS), 1.0, 4.0, (), jnp.float32)
    gain_ffn = jnp.clip(1.0 + 0.18 * jax.random.normal(splits[11], (D,), jnp.float32), 0.1, 1.9)
    w_router = normal_values(splits[12], (D, EXPERTS), (2 * D) ** -0.5, 0.15625, ((0, 4),))
    w_in = normal_values(splits[13], (EXPERTS, D, FF), D ** -0.5, 0.21875, ((0, 8),))
    w_out = normal_values(splits[14], (EXPERTS, FF, D), (max(1, FF // (EXPERTS * EXPERTS))) ** -0.5, 1.75, ((0, 8),))
    cotangent = normal_values(splits[15], (TOKENS, D), 1.0, 6.0, ((0, 32),))
    return {"tokens": tokens, "segments": segments, "routes": routes, "slots": slots, "bucket_table": bucket_table, "gain_attn": gain_attn, "w_query": w_query, "w_key": w_key, "w_value": w_value, "w_output": w_output, "rel_bias": rel_bias, "gain_ffn": gain_ffn, "w_router": w_router, "w_in": w_in, "w_out": w_out, "cotangent": cotangent}


@jax.custom_vjp
def low(v):
    return lax.optimization_barrier(v.astype(jnp.bfloat16)).astype(jnp.float32)

@jax.custom_vjp
def low_back(v):
    return v

def low_keep(v):
    return (low(v), None)

def low_pass(kept, grad):
    return (grad,)

def back_keep(v):
    return (v, None)

def back_low(kept, grad):
    return (low(grad),)
low.defvjp(low_keep, low_pass)
low_back.defvjp(back_keep, back_low)
EPS = 1e-06
HIGH = lax.Precision.HIGHEST

def rounded(value):
    return low(low_back(value))

def rms_norm(stream, gain):
    return stream * lax.rsqrt(lax.optimization_barrier(jnp.mean(stream * stream, axis=-1, keepdims=True)) + EPS) * gain

def attend_sequence(stream, doc_ids, query_w, key_w, value_w, output_w, relative, gain_a):
    normed = low(rms_norm(stream, gain_a))
    queries = rounded(jnp.dot(normed, query_w, precision=HIGH)).reshape(TOK_DEV, HEADS, HEAD_DIM)
    key_rows = rounded(jnp.dot(normed, key_w, precision=HIGH)).reshape(TOK_DEV, HEADS, HEAD_DIM)
    value_rows = rounded(jnp.dot(normed, value_w, precision=HIGH)).reshape(TOK_DEV, HEADS, HEAD_DIM)
    positions = jnp.arange(TOK_DEV, dtype=jnp.int32)
    offsets = positions[None, :] - positions[:, None] + (TOK_DEV - 1)
    pos_bias = jnp.transpose(relative[offsets], (2, 0, 1))
    scores = jnp.einsum('ihd,jhd->hij', queries, key_rows, precision=HIGH) * (1.0 / math.sqrt(HEAD_DIM)) + pos_bias
    same_doc = doc_ids[:, None] == doc_ids[None, :]
    scores = low_back(jnp.where(same_doc[None], scores, -1000000000.0))
    weights = low(jax.nn.softmax(scores, axis=-1))
    context = jnp.einsum('hij,jhd->ihd', weights, value_rows, precision=HIGH).reshape(TOK_DEV, HEADS * HEAD_DIM)
    context = rounded(context)
    return stream + low_back(jnp.dot(context, output_w, precision=HIGH))

def expert_rows(triple):
    slot_rows, w_first, second = triple
    pre_act = low_back(jnp.dot(slot_rows, w_first, precision=HIGH))
    hidden = low(jax.nn.gelu(pre_act))
    return rounded(jnp.dot(hidden, second, precision=HIGH))

def reference(tokens, segments, routes, slots, bucket_table, gain_attn, w_query, w_key, w_value, w_output, rel_bias, gain_ffn, w_router, w_in, w_out, cotangent):
    table_hot = (bucket_table[:, None] == jnp.arange(BUCKETS, dtype=jnp.int32)[None, :]).astype(jnp.float32)
    device = jnp.arange(TOKENS, dtype=jnp.int32) // TOK_DEV
    group_ids = device // N_EXPERT
    member = device % N_EXPERT
    total_rows = EXPERTS * N_DP * N_EXPERT * CAP
    target = ((routes * N_DP + group_ids) * N_EXPERT + member) * CAP + slots
    target = jnp.where(slots >= 0, target, total_rows).astype(jnp.int32)
    route_hot = (routes[:, None] == jnp.arange(EXPERTS, dtype=jnp.int32)[None, :]).astype(jnp.float32)

    def forward(stream, gain_a, query_w, key_w, value_w, output_w, bias_table, gain_f, router_w, in_w, out_w):
        relative = jnp.dot(table_hot, bias_table, precision=HIGH)
        attend = jax.checkpoint(lambda seq_pair: attend_sequence(seq_pair[0], seq_pair[1], query_w, key_w, value_w, output_w, relative, gain_a))
        middle = lax.map(attend, (stream.reshape(SEQS, TOK_DEV, D), segments)).reshape(TOKENS, D)
        normed = low(rms_norm(middle, gain_f))
        logits = low_back(jnp.dot(normed, router_w, precision=HIGH))
        gate_prob = lax.optimization_barrier(jnp.sum(jax.nn.softmax(logits, axis=-1) * route_hot, axis=-1))
        dispatched = jnp.zeros((total_rows, D), jnp.float32).at[target].set(normed, mode='drop')
        dispatched = low_back(dispatched).reshape(EXPERTS, total_rows // EXPERTS, D)
        produced = lax.map(jax.checkpoint(expert_rows), (dispatched, in_w, out_w)).reshape(total_rows, D)
        returned = jnp.take(produced, target, axis=0, mode='fill', fill_value=0.0)
        return middle + gate_prob[:, None] * returned
    output, pullback = jax.vjp(forward, tokens.astype(jnp.float32), gain_attn.astype(jnp.float32), w_query.astype(jnp.float32), w_key.astype(jnp.float32), w_value.astype(jnp.float32), w_output.astype(jnp.float32), rel_bias.astype(jnp.float32), gain_ffn.astype(jnp.float32), w_router.astype(jnp.float32), w_in.astype(jnp.float32), w_out.astype(jnp.float32))
    gradients = pullback(cotangent.astype(jnp.float32))
    return (output.astype(jnp.bfloat16), gradients[0], gradients[1], gradients[2], gradients[3], gradients[4], gradients[5], gradients[6], gradients[7], gradients[8], gradients[9], gradients[10])
```

```python
import math

import jax
import jax.numpy as jnp
from jax import lax
from jax.experimental import pallas as pl
from jax.experimental.pallas import tpu as pltpu
from jax.sharding import PartitionSpec as P

EPS = 1e-06
HIGH = lax.Precision.HIGHEST
F32 = jnp.float32
BF16 = jnp.bfloat16
VMEM_LIMIT = 56 * 1024 * 1024
TILE = 128
STRIP = 256
GELU_A = math.sqrt(2.0 / math.pi)
GELU_B = 0.044715


def dot(a, b):
    return jnp.dot(a, b, preferred_element_type=F32)


def dot_nt(a, b):
    return lax.dot_general(a, b, (((1,), (1,)), ((), ())), preferred_element_type=F32)


def params(**kw):
    return pltpu.CompilerParams(vmem_limit_bytes=VMEM_LIMIT, **kw)


def cost(flops, nbytes, trans=0):
    return pl.CostEstimate(flops=int(flops), bytes_accessed=int(nbytes), transcendentals=int(trans))


def rms_scale(stream):
    return lax.rsqrt(jnp.mean(stream * stream, axis=-1, keepdims=True) + EPS)


def norm_back(stream, gain, grad_out):
    scale = rms_scale(stream)
    grad_gain = jnp.sum(grad_out * (stream * scale), axis=0, keepdims=True)
    scaled = grad_out * gain
    inner = jnp.mean(scaled * stream, axis=-1, keepdims=True)
    grad_in = scale * scaled - stream * (scale * scale * scale * inner)
    return grad_in, grad_gain


def gelu_pair(v):
    sq = v * v
    inner = GELU_A * (v + GELU_B * (sq * v))
    th = jnp.tanh(inner)
    half = 0.5 * (1.0 + th)
    slope = half + (0.5 * v) * (1.0 - th * th) * (GELU_A + (3.0 * GELU_A * GELU_B) * sq)
    return v * half, slope


def place_kernel(target_ref, rows_ref, out_ref):
    slots, seq = out_ref.shape[0], rows_ref.shape[0]
    ids = lax.broadcasted_iota(jnp.int32, (slots, seq), 0)
    hot = (ids == target_ref[...]).astype(F32).astype(BF16)
    out_ref[...] = dot(hot, rows_ref[...]).astype(BF16)


def place(target_row, rows, slots):
    seq, width = rows.shape
    return pl.pallas_call(
        place_kernel,
        out_shape=jax.ShapeDtypeStruct((slots, width), BF16),
        compiler_params=params(),
        cost_estimate=cost(2 * slots * seq * width, 2 * (slots + seq) * width),
        name="place_cotangent",
    )(target_row, rows)


def bias_kernel(rel_ref, out_ref):
    heads, width = rel_ref.shape
    wide = out_ref.shape[2]
    for h in range(heads):
        base = jnp.broadcast_to(rel_ref[h : h + 1, :], (TILE, width))
        turned = pltpu.roll(base, width - (TILE - 1), 1, stride=1, stride_axis=0)
        out_ref[h] = turned[:, :wide]


def bias_tiles(rel_rev, seq):
    heads, width = rel_rev.shape
    wide = 2 * seq - TILE
    return pl.pallas_call(
        bias_kernel,
        out_shape=jax.ShapeDtypeStruct((heads, TILE, wide), F32),
        compiler_params=params(),
        cost_estimate=cost(heads * TILE * width, 4 * heads * TILE * wide),
        name="bias_tiles",
    )(rel_rev)


def attend_kernel(
    tok_ref, gain_ref, wq_ref, wk_ref, wv_ref, bias_ref, kseg_ref, qseg_ref,
    q_ref, k_ref, v_ref, kt_ref, e_ref, rinv_ref, ctxt_ref, normt_ref, normed_ref,
):
    seq = tok_ref.shape[0]
    heads = e_ref.shape[0]
    hd = q_ref.shape[1] // heads
    per_tile = TILE // hd

    @pl.when(pl.program_id(0) == 0)
    def _():
        stream = tok_ref[...].astype(F32)
        normed = stream * rms_scale(stream) * gain_ref[...]
        normed_ref[...] = normed.astype(BF16)
        normt_ref[...] = normed.T.astype(BF16)

    normed = normed_ref[...]
    q = (dot(normed, wq_ref[...]).astype(BF16).astype(F32) * (1.0 / math.sqrt(hd))).astype(BF16)
    k32 = dot(normed, wk_ref[...])
    v32 = dot(normed, wv_ref[...])
    q_ref[...] = q
    k_ref[...] = k32.astype(BF16)
    v_ref[...] = v32.astype(BF16)
    kt_ref[...] = k32.T.astype(BF16)
    vt = v32.T.astype(BF16)
    lane = lax.broadcasted_iota(jnp.int32, (seq, TILE), 1) // hd
    kseg = kseg_ref[...]
    qseg = qseg_ref[...]
    for h in range(heads):
        tile = h // per_tile
        k_pair = k_ref[:, tile * TILE : (tile + 1) * TILE]
        q_pair = q_ref[:, tile * TILE : (tile + 1) * TILE]
        q_own = jnp.where(lane == h % per_tile, q_pair, jnp.zeros_like(q_pair))
        k_all = jnp.concatenate([k_pair, kseg], axis=1)
        q_all = jnp.concatenate([q_own, qseg], axis=1)
        for start in range(0, seq, STRIP):
            scores = dot_nt(k_all, q_all[start : start + STRIP])
            parts = []
            for b in range(0, seq, TILE):
                off = seq - TILE - b + start
                parts.append(scores[b : b + TILE] + bias_ref[h, :, off : off + STRIP])
            scores = jnp.concatenate(parts, axis=0)
            e = jnp.exp(scores - jnp.max(scores, axis=0, keepdims=True))
            rinv = 1.0 / jnp.sum(e, axis=0, keepdims=True)
            eb = e.astype(BF16)
            e_ref[h, :, start : start + STRIP] = eb
            rinv_ref[h, :, start : start + STRIP] = rinv
            ctxt = dot(vt[h * hd : (h + 1) * hd], eb) * rinv
            ctxt_ref[h * hd : (h + 1) * hd, start : start + STRIP] = ctxt.astype(BF16)


def attend(tokens, gain, w_qkv, bias, kseg, qseg, heads, group):
    seq, width = tokens.shape
    cols = width // heads * group
    steps = heads // group
    wide = bias.shape[2]
    whole = lambda a: pl.BlockSpec(a.shape, lambda g: (0,) * a.ndim)
    col = lambda base: pl.BlockSpec((width, cols), lambda g: (0, base * steps + g))
    nat = pl.BlockSpec((seq, cols), lambda g: (0, g))
    tr = pl.BlockSpec((cols, seq), lambda g: (g, 0))
    sds = jax.ShapeDtypeStruct
    return pl.pallas_call(
        attend_kernel,
        grid=(steps,),
        in_specs=[
            whole(tokens), whole(gain), col(0), col(1), col(2),
            pl.BlockSpec((group, TILE, wide), lambda g: (g, 0, 0)), whole(kseg), whole(qseg),
        ],
        out_specs=[
            nat, nat, nat, tr,
            pl.BlockSpec((group, seq, seq), lambda g: (g, 0, 0)),
            pl.BlockSpec((group, 1, seq), lambda g: (g, 0, 0)),
            tr,
            pl.BlockSpec((width, seq), lambda g: (0, 0)),
        ],
        out_shape=[
            sds((seq, width), BF16), sds((seq, width), BF16), sds((seq, width), BF16),
            sds((width, seq), BF16), sds((heads, seq, seq), BF16), sds((heads, 1, seq), F32),
            sds((width, seq), BF16), sds((width, seq), BF16),
        ],
        scratch_shapes=[pltpu.VMEM((seq, width), BF16)],
        compiler_params=params(dimension_semantics=("arbitrary",)),
        cost_estimate=cost(
            6 * seq * width * width + 4 * seq * seq * width,
            2 * (3 * width * width + 9 * seq * width + heads * seq * seq) + 4 * bias.size,
            heads * seq * seq,
        ),
        name="attention_forward",
    )(tokens, gain, w_qkv, w_qkv, w_qkv, bias, kseg, qseg)


def middle_kernel(tok_ref, ctxt_ref, wo_ref, gain_ref, target_ref, middle_ref, placed_ref):
    seq = tok_ref.shape[0]
    context = ctxt_ref[...].astype(F32).T.astype(BF16)
    middle = tok_ref[...].astype(F32) + dot(context, wo_ref[...])
    middle_ref[...] = middle
    normed = (middle * rms_scale(middle) * gain_ref[...]).astype(BF16)
    slots = placed_ref.shape[0]
    ids = lax.broadcasted_iota(jnp.int32, (slots, seq), 0)
    hot = (ids == target_ref[...]).astype(F32).astype(BF16)
    placed_ref[...] = dot(hot, normed).astype(BF16)


def middle_step(tokens, ctxt, w_out, gain, target_row, slots):
    seq, width = tokens.shape
    return pl.pallas_call(
        middle_kernel,
        out_shape=[
            jax.ShapeDtypeStruct((seq, width), F32),
            jax.ShapeDtypeStruct((slots, width), BF16),
        ],
        compiler_params=params(),
        cost_estimate=cost(
            2 * seq * width * width + 2 * slots * seq * width,
            2 * width * width + 8 * seq * width + 2 * slots * width,
        ),
        name="output_projection_dispatch",
    )(tokens, ctxt, w_out, gain, target_row)


def gate_of(logits, expert):
    top = jnp.max(logits, axis=-1, keepdims=True)
    ex = jnp.exp(logits - top)
    prob = ex / jnp.sum(ex, axis=-1, keepdims=True)
    hot = lax.broadcasted_iota(jnp.int32, logits.shape, 1) == expert
    gate = jnp.sum(jnp.where(hot, prob, 0.0), axis=-1, keepdims=True)
    return prob, hot, gate


def expert_kernel(
    num_ref, x_ref, c_ref, wr_ref, win_ref, wout_ref,
    scaled_ref, grad_ref, router_ref, gp_ref, acc_p, acc_g,
):
    step = pl.program_id(0)

    @pl.when(step == 0)
    def _():
        _, _, gate = gate_of(dot(x_ref[...], wr_ref[...]), num_ref[0])
        gp_ref[...] = (gate * c_ref[...].astype(F32)).astype(BF16)
        acc_p[...] = jnp.zeros_like(acc_p)
        acc_g[...] = jnp.zeros_like(acc_g)

    pre = dot(x_ref[...], win_ref[0])
    hidden, slope = gelu_pair(pre)
    acc_p[...] += dot(hidden.astype(BF16), wout_ref[0])
    grad_hidden = dot_nt(gp_ref[...], wout_ref[0])
    acc_g[...] += dot_nt((grad_hidden * slope).astype(BF16), win_ref[0])

    @pl.when(step == pl.num_programs(0) - 1)
    def _():
        x = x_ref[...]
        prob, hot, gate = gate_of(dot(x, wr_ref[...]), num_ref[0])
        produced = acc_p[...]
        scaled_ref[...] = (gate * produced).astype(BF16)
        grad_gate = jnp.sum(
            c_ref[...].astype(F32) * produced.astype(BF16).astype(F32), axis=-1, keepdims=True
        )
        grad_logits = prob * (jnp.where(hot, grad_gate, 0.0) - gate * grad_gate)
        logits_b = grad_logits.astype(BF16)
        grad_ref[...] = (acc_g[...] + dot_nt(logits_b, wr_ref[...])).astype(BF16)
        router_ref[...] = dot(grad_logits.T.astype(BF16), x)


def expert_step(number, x, c, w_router, w_in, w_out, local, block):
    rows, width = x.shape
    ff = w_in.shape[2]
    experts = w_router.shape[1]
    whole = lambda a: pl.BlockSpec(a.shape, lambda f: (0,) * a.ndim)
    row_spec = pl.BlockSpec((rows, width), lambda f: (0, 0))
    return pl.pallas_call(
        expert_kernel,
        grid=(ff // block,),
        in_specs=[
            pl.BlockSpec(memory_space=pltpu.SMEM),
            whole(x),
            pl.BlockSpec((rows, width), lambda f: (local, 0)),
            whole(w_router),
            pl.BlockSpec((1, width, block), lambda f: (local, 0, f)),
            pl.BlockSpec((1, block, width), lambda f: (local, f, 0)),
        ],
        out_specs=[row_spec, row_spec, pl.BlockSpec((experts, width), lambda f: (0, 0))],
        out_shape=[
            jax.ShapeDtypeStruct((rows, width), BF16),
            jax.ShapeDtypeStruct((rows, width), BF16),
            jax.ShapeDtypeStruct((experts, width), F32),
        ],
        scratch_shapes=[
            pltpu.VMEM((rows, width), BF16),
            pltpu.VMEM((rows, width), F32),
            pltpu.VMEM((rows, width), F32),
        ],
        compiler_params=params(dimension_semantics=("arbitrary",)),
        cost_estimate=cost(
            8 * rows * width * ff, 4 * width * ff + 8 * rows * width, rows * ff
        ),
        name="expert_rows",
    )(number, x, c, w_router, w_in, w_out)


def expert_grad_kernel(
    num_ref, x_ref, c_ref, wr_ref, win_ref, wout_ref, gin_ref, gout_ref, gp_ref, xt_ref
):
    parts, rows, width = x_ref.shape
    x = x_ref[...].reshape(parts * rows, width)

    @pl.when(pl.program_id(0) == 0)
    def _():
        _, _, gate = gate_of(dot(x, wr_ref[...]), num_ref[1])
        c = c_ref[...].reshape(parts * rows, width)
        gp_ref[...] = (gate * c.astype(F32)).astype(BF16)
        xt_ref[...] = x.astype(F32).T.astype(BF16)

    gp = gp_ref[...]
    pre_t = dot_nt(win_ref[0].astype(F32).T.astype(BF16), x)
    hidden_t, slope_t = gelu_pair(pre_t)
    grad_hidden_t = dot_nt(wout_ref[0], gp)
    gout_ref[0] = dot(hidden_t.astype(BF16), gp)
    gin_ref[0] = dot_nt(xt_ref[...], (grad_hidden_t * slope_t).astype(BF16))


def expert_grads(numbers, x_all, c_all, w_router, w_in, w_out, local, n_dp):
    parts, rows, width = x_all.shape
    ff = w_in.shape[2]
    part = ff // n_dp
    block = 256 if part % 256 == 0 else 128
    steps = part // block
    whole = lambda a: pl.BlockSpec(a.shape, lambda f, n: (0,) * a.ndim)
    return pl.pallas_call(
        expert_grad_kernel,
        grid_spec=pltpu.PrefetchScalarGridSpec(
            num_scalar_prefetch=1,
            grid=(steps,),
            in_specs=[
                whole(x_all),
                pl.BlockSpec((parts, rows, width), lambda f, n: (0, local, 0)),
                whole(w_router),
                pl.BlockSpec((1, width, block), lambda f, n: (local, 0, n[0] * steps + f)),
                pl.BlockSpec((1, block, width), lambda f, n: (local, n[0] * steps + f, 0)),
            ],
            out_specs=[
                pl.BlockSpec((1, width, block), lambda f, n: (0, 0, f)),
                pl.BlockSpec((1, block, width), lambda f, n: (0, f, 0)),
            ],
            scratch_shapes=[
                pltpu.VMEM((parts * rows, width), BF16),
                pltpu.VMEM((width, parts * rows), BF16),
            ],
        ),
        out_shape=[
            jax.ShapeDtypeStruct((1, width, part), F32),
            jax.ShapeDtypeStruct((1, part, width), F32),
        ],
        compiler_params=params(dimension_semantics=("arbitrary",)),
        cost_estimate=cost(
            8 * parts * rows * width * part,
            4 * parts * rows * width + 12 * width * part,
            parts * rows * part,
        ),
        name="expert_weight_grads",
    )(numbers, x_all, c_all, w_router, w_in, w_out)


def middle_back_kernel(
    *refs,
):
    (cot_ref, middle_ref, gain_ref, target_ref, ctxt_ref, wo_ref), refs = refs[:6], refs[6:]
    back_refs, (gmid_ref, gctx_ref, gwo_ref, ggain_ref) = refs[:-4], refs[-4:]
    seq, width = cot_ref.shape
    target = target_ref[...]
    grad = jnp.zeros((seq, width), F32)
    for l, back in enumerate(back_refs):
        rows = back.shape[0]
        ids = lax.broadcasted_iota(jnp.int32, (seq, rows), 1) + l * rows
        hot = (ids == target).astype(F32).astype(BF16)
        grad = grad + dot(hot, back[...])
    grad_in, grad_gain = norm_back(middle_ref[...], gain_ref[...], grad)
    ggain_ref[...] = grad_gain
    grad_middle = cot_ref[...].astype(F32) + grad_in
    gmid_ref[...] = grad_middle
    grad_attn = grad_middle.astype(BF16)
    gctx_ref[...] = dot_nt(grad_attn, wo_ref[...]).astype(BF16)
    gwo_ref[...] = dot(ctxt_ref[...], grad_attn).astype(BF16)


def middle_back(cot, middle, gain, target_col, ctxt, w_out, backs):
    seq, width = cot.shape
    sds = jax.ShapeDtypeStruct
    slots = sum(b.shape[0] for b in backs)
    return pl.pallas_call(
        middle_back_kernel,
        out_shape=[
            sds((seq, width), F32), sds((seq, width), BF16), sds((width, width), BF16),
            sds((1, width), F32),
        ],
        compiler_params=params(),
        cost_estimate=cost(
            4 * seq * width * width + 2 * slots * seq * width,
            4 * width * width + 14 * seq * width + 2 * slots * width,
        ),
        name="second_norm_backward",
    )(cot, middle, gain, target_col, ctxt, w_out, *backs)


def attend_back_kernel(
    tok_ref, gain_ref, gmid_ref, normt_ref, q_ref, k_ref, v_ref, kt_ref, e_ref, rinv_ref, do_ref,
    wq_ref, wk_ref, wv_ref,
    gq_ref, gk_ref, gv_ref, diag_ref, gtok_ref, ggain_ref, sum_ref, acc_ref,
):
    seq = tok_ref.shape[0]
    heads = e_ref.shape[0]
    cols = q_ref.shape[1]
    hd = cols // heads
    per_tile = TILE // hd
    step = pl.program_id(0)
    lane = lax.broadcasted_iota(jnp.int32, (seq, TILE), 1) // hd
    row_bit = lax.broadcasted_iota(jnp.int32, (8, 2 * seq), 0)
    dk_tiles, dv_tiles, dqt_rows = [], [], []
    for h in range(heads):
        tile = h // per_tile
        sl = slice(tile * TILE, (tile + 1) * TILE)
        zero = jnp.zeros((seq, TILE), BF16)
        q_own = jnp.where(lane == h % per_tile, q_ref[:, sl], zero)
        do_own = jnp.where(lane == h % per_tile, do_ref[:, sl], zero)
        v_pair = v_ref[:, sl]
        acc_ref[...] = jnp.zeros_like(acc_ref)
        dk = jnp.zeros((seq, TILE), F32)
        dv = jnp.zeros((seq, TILE), F32)
        dqt_parts = []
        for start in range(0, seq, STRIP):
            st = slice(start, start + STRIP)
            p = e_ref[h, :, st].astype(F32) * rinv_ref[h, :, st]
            t = dot_nt(v_pair, do_own[st]) * p
            ds = t - p * jnp.sum(t, axis=0, keepdims=True)
            dsb = ds.astype(BF16)
            dv = dv + dot(p.astype(BF16), do_own[st])
            dk = dk + dot(dsb, q_own[st])
            dqt_parts.append(dot(kt_ref[h * hd : (h + 1) * hd, :], dsb))
            for b in range(0, seq, TILE):
                off = seq - TILE - b + start
                acc_ref[:, off : off + STRIP] += ds[b : b + TILE]
        if h % per_tile == 0:
            dk_tiles.append(dk)
            dv_tiles.append(dv)
        else:
            dk_tiles[-1] = dk_tiles[-1] + dk
            dv_tiles[-1] = dv_tiles[-1] + dv
        dqt_rows.append(jnp.concatenate(dqt_parts, axis=1))
        folded = acc_ref[...]
        half = TILE // 2
        while half >= 8:
            folded = folded[:half] + pltpu.roll(folded[half:], 2 * seq - half, 1)
            half //= 2
        for bit in (4, 2, 1):
            turned = pltpu.roll(folded, 2 * seq - bit, 1)
            folded = jnp.where((row_bit & bit) != 0, turned, folded)
        diag_ref[h] = jnp.sum(folded, axis=0, keepdims=True)
    dqt = (jnp.concatenate(dqt_rows, axis=0) * (1.0 / math.sqrt(hd))).astype(BF16)
    dq = dqt.astype(F32).T.astype(BF16)
    dk = jnp.concatenate(dk_tiles, axis=1).astype(BF16)
    dv = jnp.concatenate(dv_tiles, axis=1).astype(BF16)
    normt = normt_ref[...]
    gq_ref[...] = dot(normt, dq).astype(BF16)
    gk_ref[...] = dot(normt, dk).astype(BF16)
    gv_ref[...] = dot(normt, dv).astype(BF16)
    grad = dot_nt(dq, wq_ref[...]) + dot_nt(dk, wk_ref[...]) + dot_nt(dv, wv_ref[...])

    @pl.when(step == 0)
    def _():
        sum_ref[...] = grad

    @pl.when(step > 0)
    def _():
        sum_ref[...] += grad

    @pl.when(step == pl.num_programs(0) - 1)
    def _():
        stream = tok_ref[...].astype(F32)
        grad_in, grad_gain = norm_back(stream, gain_ref[...], sum_ref[...])
        gtok_ref[...] = gmid_ref[...] + grad_in
        ggain_ref[...] = grad_gain


def attend_back(tokens, gain, grad_middle, normt, q, k, v, kt, e, rinv, grad_ctx, w_qkv, group):
    seq, width = tokens.shape
    heads = e.shape[0]
    cols = width // heads * group
    steps = heads // group
    whole = lambda a: pl.BlockSpec(a.shape, lambda g: (0,) * a.ndim)
    col = lambda base: pl.BlockSpec((width, cols), lambda g: (0, base * steps + g))
    nat = pl.BlockSpec((seq, cols), lambda g: (0, g))
    tr = pl.BlockSpec((cols, seq), lambda g: (g, 0))
    gcol = pl.BlockSpec((width, cols), lambda g: (0, g))
    sds = jax.ShapeDtypeStruct
    return pl.pallas_call(
        attend_back_kernel,
        grid=(steps,),
        in_specs=[
            whole(tokens), whole(gain), whole(grad_middle), whole(normt), nat, nat, nat, tr,
            pl.BlockSpec((group, seq, seq), lambda g: (g, 0, 0)),
            pl.BlockSpec((group, 1, seq), lambda g: (g, 0, 0)),
            nat, col(0), col(1), col(2),
        ],
        out_specs=[
            gcol, gcol, gcol,
            pl.BlockSpec((group, 1, 2 * seq), lambda g: (g, 0, 0)),
            pl.BlockSpec((seq, width), lambda g: (0, 0)),
            pl.BlockSpec((1, width), lambda g: (0, 0)),
        ],
        out_shape=[
            sds((width, width), BF16), sds((width, width), BF16), sds((width, width), BF16),
            sds((heads, 1, 2 * seq), F32), sds((seq, width), F32), sds((1, width), F32),
        ],
        scratch_shapes=[pltpu.VMEM((seq, width), F32), pltpu.VMEM((TILE, 2 * seq), F32)],
        compiler_params=params(dimension_semantics=("arbitrary",)),
        cost_estimate=cost(
            12 * seq * width * width + 8 * seq * seq * width,
            2 * (6 * width * width + 8 * seq * width + heads * seq * seq) + 8 * seq * width,
        ),
        name="attention_backward",
    )(tokens, gain, grad_middle, normt, q, k, v, kt, e, rinv, grad_ctx, w_qkv, w_qkv, w_qkv)


def output_kernel(middle_ref, target_ref, *refs):
    out_ref = refs[-1]
    seq = middle_ref.shape[0]
    total = middle_ref[...]
    for l, back in enumerate(refs[:-1]):
        rows = back.shape[0]
        ids = lax.broadcasted_iota(jnp.int32, (seq, rows), 1) + l * rows
        hot = (ids == target_ref[...]).astype(F32).astype(BF16)
        total = total + dot(hot, back[...])
    out_ref[...] = total.astype(BF16)


def output_step(middle, target_col, backs):
    seq, width = middle.shape
    slots = sum(b.shape[0] for b in backs)
    return pl.pallas_call(
        output_kernel,
        out_shape=jax.ShapeDtypeStruct((seq, width), BF16),
        compiler_params=params(),
        cost_estimate=cost(2 * slots * seq * width, 6 * seq * width + 2 * slots * width),
        name="layer_output",
    )(middle, target_col, *backs)


def butterfly_sum(value, axes):
    for axis in axes:
        size = lax.axis_size(axis)
        if size & (size - 1):
            value = lax.psum(value, axis)
            continue
        bit = 1
        while bit < size:
            value = value + lax.ppermute(value, axis, [(i, i ^ bit) for i in range(size)])
            bit *= 2
    return value


def body(
    tokens, segments, routes, slots, bucket_table, gain_attn, w_query, w_key, w_value, w_output,
    rel_bias, gain_ffn, w_router, w_in, w_out, cotangent,
):
    seq, width = tokens.shape
    buckets, heads = rel_bias.shape
    experts = w_router.shape[1]
    n_dp = lax.axis_size("dp")
    peers = lax.axis_size("expert")
    local = w_in.shape[0]
    capacity = max(2, (5 * seq + 4 * experts - 1) // (4 * experts))
    rows = peers * capacity
    dp_index = lax.axis_index("dp")
    expert_index = lax.axis_index("expert")

    w_qkv = lax.all_gather(
        jnp.concatenate([w_query, w_key, w_value], axis=1), "dp", axis=0, tiled=True
    )
    full_o = lax.all_gather(w_output, "dp", axis=0, tiled=True)
    full_r = lax.all_gather(w_router, "dp", axis=0, tiled=True)

    order = (routes % local) * rows + (routes // local) * capacity + slots
    target = jnp.where(slots >= 0, order, -1)
    target_row = target[None, :]
    target_col = target[:, None]
    gain_one = gain_attn[None, :]
    gain_two = gain_ffn[None, :]

    def exchange(values):
        parts = values.reshape(peers, capacity, width)
        return lax.all_to_all(parts, "expert", split_axis=0, concat_axis=0, tiled=True).reshape(
            rows, width
        )

    c_placed = place(target_row, cotangent, local * rows)
    c_here = jnp.concatenate(
        [exchange(c_placed[l * rows : (l + 1) * rows]) for l in range(local)], axis=0
    )
    c_all = lax.all_gather(c_here, "dp", axis=0, tiled=False)

    span = 2 * seq
    reversed_table = jnp.concatenate([bucket_table[::-1], jnp.full((1,), -1, jnp.int32)])
    bucket_ids = jnp.arange(buckets, dtype=jnp.int32)
    hot_rev = (bucket_ids[:, None] == reversed_table[None, :]).astype(F32)
    rel_rev = jnp.dot(rel_bias.T, hot_rev, precision=HIGH)
    shifted = jnp.roll(reversed_table, 1 - TILE)
    hot_shifted = (shifted[:, None] == bucket_ids[None, :]).astype(F32)
    bias = bias_tiles(rel_rev, seq)
    marks = jnp.arange(TILE, dtype=jnp.int32)[None, :]
    same = segments[0][:, None] == marks
    kseg = same.astype(BF16)
    qseg = jnp.where(same, 0.0, -1e9).astype(BF16)

    q, k, v, kt, e, rinv, ctxt, normt = attend(
        tokens, gain_one, w_qkv, bias, kseg, qseg, heads, 4
    )
    middle, placed = middle_step(tokens, ctxt, full_o, gain_two, target_row, local * rows)

    backs, returns, router_terms, gin, gout = [], [], [], [], []
    for l in range(local):
        x = exchange(placed[l * rows : (l + 1) * rows])
        number = jnp.reshape(expert_index * local + l, (1,)).astype(jnp.int32)
        scaled, grad_x, router_term = expert_step(
            number, x, c_here, full_r, w_in, w_out, l, 512
        )
        backs.append(exchange(grad_x))
        returns.append(exchange(scaled))
        router_terms.append(router_term)
        numbers = jnp.stack([dp_index, expert_index * local + l]).astype(jnp.int32)
        x_all = lax.all_gather(x, "dp", axis=0, tiled=False)
        gi, go = expert_grads(numbers, x_all, c_all, full_r, w_in, w_out, l, n_dp)
        gin.append(gi)
        gout.append(go)
    grad_w_in = jnp.concatenate(gin, axis=0)
    grad_w_out = jnp.concatenate(gout, axis=0)

    grad_middle, grad_ctx, gw_o, ggain_two = middle_back(
        cotangent, middle, gain_two, target_col, ctxt, full_o, backs
    )
    gw_q, gw_k, gw_v, diag, grad_tokens, ggain_one = attend_back(
        tokens, gain_one, grad_middle, normt, q, k, v, kt, e, rinv, grad_ctx, w_qkv, 4
    )
    output = output_step(middle, target_col, returns)

    def reduce_dense(term):
        part = lax.psum_scatter(term, "dp", scatter_dimension=0, tiled=True)
        return lax.psum(part, "expert").astype(F32)

    shard_o = reduce_dense(gw_o)
    shard_qkv = reduce_dense(jnp.concatenate([gw_q, gw_k, gw_v], axis=1))

    grad_rel = jnp.dot(diag.reshape(heads, span), hot_shifted, precision=HIGH)
    early = butterfly_sum(
        jnp.concatenate([sum(router_terms), ggain_two], axis=0), ("dp", "expert")
    )
    rel_row = jnp.pad(grad_rel.reshape(1, heads * buckets), ((0, 0), (0, width - heads * buckets)))
    late = butterfly_sum(jnp.concatenate([ggain_one, rel_row], axis=0), ("dp", "expert"))
    shard_rows = width // n_dp
    grad_router = lax.dynamic_slice_in_dim(early[:experts], dp_index * shard_rows, shard_rows, 1).T
    total_rel = late[1, : heads * buckets].reshape(heads, buckets).T
    return (
        output,
        grad_tokens,
        late[0],
        shard_qkv[:, :width],
        shard_qkv[:, width : 2 * width],
        shard_qkv[:, 2 * width :],
        shard_o,
        total_rel,
        early[experts],
        grad_router,
        grad_w_in,
        grad_w_out,
    )


def solution(mesh):
    in_specs = (
        P(("dp", "expert"), None),
        P(("dp", "expert"), None),
        P(("dp", "expert")),
        P(("dp", "expert")),
        P(),
        P(),
        P("dp", None),
        P("dp", None),
        P("dp", None),
        P("dp", None),
        P(),
        P(),
        P("dp", None),
        P("expert", None, None),
        P("expert", None, None),
        P(("dp", "expert"), None),
    )
    out_specs = (
        P(("dp", "expert"), None),
        P(("dp", "expert"), None),
        P(),
        P("dp", None),
        P("dp", None),
        P("dp", None),
        P("dp", None),
        P(),
        P(),
        P("dp", None),
        P("expert", None, "dp"),
        P("expert", "dp", None),
    )
    return jax.shard_map(body, mesh=mesh, in_specs=in_specs, out_specs=out_specs, check_vma=False)
```

```python
import math

import jax
import jax.numpy as jnp
from jax import lax
from jax.experimental import pallas as pl
from jax.experimental.pallas import tpu as pltpu
from jax.sharding import PartitionSpec as P

EPS = 1e-06
HIGH = lax.Precision.HIGHEST
F32 = jnp.float32
BF16 = jnp.bfloat16
VMEM_LIMIT = 56 * 1024 * 1024
TILE = 128
STRIP = 256
GELU_A = math.sqrt(2.0 / math.pi)
GELU_B = 0.044715


def dot(a, b):
    return jnp.dot(a, b, preferred_element_type=F32)


def dot_nt(a, b):
    return lax.dot_general(a, b, (((1,), (1,)), ((), ())), preferred_element_type=F32)


def params(**kw):
    return pltpu.CompilerParams(vmem_limit_bytes=VMEM_LIMIT, **kw)


def cost(flops, nbytes, trans=0):
    return pl.CostEstimate(flops=int(flops), bytes_accessed=int(nbytes), transcendentals=int(trans))


def rms_scale(stream):
    return lax.rsqrt(jnp.mean(stream * stream, axis=-1, keepdims=True) + EPS)


def norm_back(stream, gain, grad_out):
    scale = rms_scale(stream)
    grad_gain = jnp.sum(grad_out * (stream * scale), axis=0, keepdims=True)
    scaled = grad_out * gain
    inner = jnp.mean(scaled * stream, axis=-1, keepdims=True)
    grad_in = scale * scaled - stream * (scale * scale * scale * inner)
    return grad_in, grad_gain


def gelu_pair(v):
    sq = v * v
    inner = GELU_A * (v + GELU_B * (sq * v))
    th = jnp.tanh(inner)
    half = 0.5 * (1.0 + th)
    slope = half + (0.5 * v) * (1.0 - th * th) * (GELU_A + (3.0 * GELU_A * GELU_B) * sq)
    return v * half, slope


def slot_hot(target_row, start, rows):
    seq = target_row.shape[1]
    ids = lax.broadcasted_iota(jnp.int32, (rows, seq), 0) + start
    return (ids == target_row).astype(F32).astype(BF16)


def token_hot(target_col, start, rows):
    seq = target_col.shape[0]
    ids = lax.broadcasted_iota(jnp.int32, (seq, rows), 1) + start
    return (ids == target_col).astype(F32).astype(BF16)


def place_kernel(target_ref, rows_ref, *out_refs):
    for l, out_ref in enumerate(out_refs):
        rows = out_ref.shape[0]
        out_ref[...] = dot(slot_hot(target_ref[...], l * rows, rows), rows_ref[...]).astype(BF16)


def place(target_row, values, local, rows):
    seq, width = values.shape
    return pl.pallas_call(
        place_kernel,
        out_shape=[jax.ShapeDtypeStruct((rows, width), BF16)] * local,
        compiler_params=params(),
        cost_estimate=cost(2 * local * rows * seq * width, 2 * (local * rows + seq) * width),
        name="place_cotangent",
    )(target_row, values)


def prepare_kernel(rel_ref, tok_ref, gain_ref, out_ref, normed_ref, normt_ref):
    heads, width = rel_ref.shape
    wide = out_ref.shape[2]
    for h in range(heads):
        base = jnp.broadcast_to(rel_ref[h : h + 1, :], (TILE, width))
        turned = pltpu.roll(base, width - (TILE - 1), 1, stride=1, stride_axis=0)
        out_ref[h] = turned[:, :wide]
    stream = tok_ref[...].astype(F32)
    normed = stream * rms_scale(stream) * gain_ref[...]
    normed_ref[...] = normed.astype(BF16)
    normt_ref[...] = normed.T.astype(BF16)


def prepare(rel_rev, tokens, gain):
    heads, span = rel_rev.shape
    seq, width = tokens.shape
    wide = 2 * seq - TILE
    return pl.pallas_call(
        prepare_kernel,
        out_shape=[
            jax.ShapeDtypeStruct((heads, TILE, wide), F32),
            jax.ShapeDtypeStruct((seq, width), BF16),
            jax.ShapeDtypeStruct((width, seq), BF16),
        ],
        compiler_params=params(),
        cost_estimate=cost(heads * TILE * span, 4 * heads * TILE * wide + 6 * seq * width),
        name="bias_and_first_norm",
    )(rel_rev, tokens, gain)


def attend_kernel(num_ref, normed_ref, bias_ref, kseg_ref, qseg_ref, *refs):
    pieces, refs = refs[:-8], refs[-8:]
    q_ref, k_ref, v_ref, kt_ref, e_ref, rinv_ref, ctxt_ref, w_ref = refs
    seq = normed_ref.shape[0]
    pair = e_ref.shape[0]
    cols = q_ref.shape[1]
    hd = TILE // pair
    step = pl.program_id(0)

    @pl.when(step == 0)
    def _():
        part = pieces[0].shape[0]
        for mask, piece in enumerate(pieces):
            row = pl.multiple_of((num_ref[0] ^ mask) * part, 16)
            w_ref[pl.ds(row, part), :] = piece[...]
        normed = normed_ref[...]
        q = dot(normed, w_ref[:, :cols]).astype(BF16).astype(F32) * (1.0 / math.sqrt(hd))
        k = dot(normed, w_ref[:, cols : 2 * cols])
        q_ref[...] = q.astype(BF16)
        k_ref[...] = k.astype(BF16)
        kt_ref[...] = k.T.astype(BF16)
        v_ref[...] = dot(normed, w_ref[:, 2 * cols :]).astype(BF16)

    lane = lax.broadcasted_iota(jnp.int32, (seq, TILE), 1) // hd
    sl = pl.ds(pl.multiple_of(step * TILE, TILE), TILE)
    q_pair = q_ref[:, sl]
    k_all = jnp.concatenate([k_ref[:, sl], kseg_ref[...]], axis=1)
    vt = v_ref[:, sl].astype(F32).T.astype(BF16)
    qseg = qseg_ref[...]
    for h in range(pair):
        q_own = jnp.where(lane == h, q_pair, jnp.zeros_like(q_pair))
        q_all = jnp.concatenate([q_own, qseg], axis=1)
        for start in range(0, seq, STRIP):
            scores = dot_nt(k_all, q_all[start : start + STRIP])
            parts = []
            for b in range(0, seq, TILE):
                off = seq - TILE - b + start
                parts.append(scores[b : b + TILE] + bias_ref[h, :, off : off + STRIP])
            scores = jnp.concatenate(parts, axis=0)
            e = jnp.exp(scores - jnp.max(scores, axis=0, keepdims=True))
            rinv = 1.0 / jnp.sum(e, axis=0, keepdims=True)
            eb = e.astype(BF16)
            e_ref[h, :, start : start + STRIP] = eb
            rinv_ref[h, :, start : start + STRIP] = rinv
            ctxt = dot(vt[h * hd : (h + 1) * hd], eb) * rinv
            ctxt_ref[h * hd : (h + 1) * hd, start : start + STRIP] = ctxt.astype(BF16)


def attend(number, normed, bias, kseg, qseg, pieces, group, heads_in):
    seq, width = normed.shape
    wide = bias.shape[2]
    cols = pieces[0].shape[1] // 3
    pair = heads_in * TILE // cols
    steps = cols // TILE
    whole = lambda a: pl.BlockSpec(a.shape, lambda g: (0,) * a.ndim)
    full = lambda shape: pl.BlockSpec(shape, lambda g: (0,) * len(shape))
    sds = jax.ShapeDtypeStruct
    return pl.pallas_call(
        attend_kernel,
        grid=(steps,),
        in_specs=[
            pl.BlockSpec(memory_space=pltpu.SMEM), whole(normed),
            pl.BlockSpec((pair, TILE, wide), lambda g: (group * steps + g, 0, 0)),
            whole(kseg), whole(qseg),
        ]
        + [whole(p) for p in pieces],
        out_specs=[
            full((seq, cols)), full((seq, cols)), full((seq, cols)), full((cols, seq)),
            pl.BlockSpec((pair, seq, seq), lambda g: (g, 0, 0)),
            pl.BlockSpec((pair, 1, seq), lambda g: (g, 0, 0)),
            pl.BlockSpec((TILE, seq), lambda g: (g, 0)),
            full((width, 3 * cols)),
        ],
        out_shape=[
            sds((seq, cols), BF16), sds((seq, cols), BF16), sds((seq, cols), BF16),
            sds((cols, seq), BF16), sds((heads_in, seq, seq), BF16), sds((heads_in, 1, seq), F32),
            sds((cols, seq), BF16), sds((width, 3 * cols), BF16),
        ],
        compiler_params=params(dimension_semantics=("arbitrary",)),
        cost_estimate=cost(
            6 * seq * width * cols + 4 * seq * seq * cols,
            2 * (6 * width * cols + 6 * seq * cols + heads_in * seq * seq) + 4 * pair * steps * TILE * wide,
            heads_in * seq * seq,
        ),
        name="attention_forward",
    )(number, normed, bias, kseg, qseg, *pieces)


def middle_kernel(tok_ref, wo_ref, gain_ref, target_ref, *refs):
    groups = 3
    ctx_refs, (middle_ref, *placed_refs) = refs[:groups], refs[groups:]
    middle = tok_ref[...].astype(F32)
    row = 0
    for ctx_ref in ctx_refs:
        cols = ctx_ref.shape[0]
        context = ctx_ref[...].astype(F32).T.astype(BF16)
        middle = middle + dot(context, wo_ref[row : row + cols, :])
        row += cols
    middle_ref[...] = middle
    normed = (middle * rms_scale(middle) * gain_ref[...]).astype(BF16)
    for l, placed_ref in enumerate(placed_refs):
        rows = placed_ref.shape[0]
        placed_ref[...] = dot(slot_hot(target_ref[...], l * rows, rows), normed).astype(BF16)


def middle_step(tokens, w_out, gain, target_row, ctxts, local, rows):
    seq, width = tokens.shape
    return pl.pallas_call(
        middle_kernel,
        out_shape=[jax.ShapeDtypeStruct((seq, width), F32)]
        + [jax.ShapeDtypeStruct((rows, width), BF16)] * local,
        compiler_params=params(),
        cost_estimate=cost(
            2 * seq * width * width + 2 * local * rows * seq * width,
            2 * width * width + 8 * seq * width + 2 * local * rows * width,
        ),
        name="output_projection_dispatch",
    )(tokens, w_out, gain, target_row, *ctxts)


def gate_of(logits, expert):
    top = jnp.max(logits, axis=-1, keepdims=True)
    ex = jnp.exp(logits - top)
    prob = ex / jnp.sum(ex, axis=-1, keepdims=True)
    hot = lax.broadcasted_iota(jnp.int32, logits.shape, 1) == expert
    gate = jnp.sum(jnp.where(hot, prob, 0.0), axis=-1, keepdims=True)
    return prob, hot, gate


def expert_kernel(
    num_ref, x_ref, c_ref, wr_ref, win_ref, wout_ref,
    scaled_ref, grad_ref, router_ref, gp_ref, acc_p, acc_g,
):
    step = pl.program_id(0)

    @pl.when(step == 0)
    def _():
        _, _, gate = gate_of(dot(x_ref[...], wr_ref[...]), num_ref[1])
        gp_ref[...] = (gate * c_ref[...].astype(F32)).astype(BF16)
        acc_p[...] = jnp.zeros_like(acc_p)
        acc_g[...] = jnp.zeros_like(acc_g)

    pre = dot(x_ref[...], win_ref[0])
    hidden, slope = gelu_pair(pre)
    acc_p[...] += dot(hidden.astype(BF16), wout_ref[0])
    grad_hidden = dot_nt(gp_ref[...], wout_ref[0])
    acc_g[...] += dot_nt((grad_hidden * slope).astype(BF16), win_ref[0])

    @pl.when(step == pl.num_programs(0) - 1)
    def _():
        x = x_ref[...]
        prob, hot, gate = gate_of(dot(x, wr_ref[...]), num_ref[1])
        produced = acc_p[...]
        scaled_ref[...] = (gate * produced).astype(BF16)
        grad_gate = jnp.sum(
            c_ref[...].astype(F32) * produced.astype(BF16).astype(F32), axis=-1, keepdims=True
        )
        grad_logits = prob * (jnp.where(hot, grad_gate, 0.0) - gate * grad_gate)
        logits_b = grad_logits.astype(BF16)
        grad_ref[...] = (acc_g[...] + dot_nt(logits_b, wr_ref[...])).astype(BF16)
        router_ref[...] = dot(grad_logits.T.astype(BF16), x)


def expert_step(number, x, c, w_router, w_in, w_out, local, block):
    rows, width = x.shape
    ff = w_in.shape[2]
    experts = w_router.shape[1]
    whole = lambda a: pl.BlockSpec(a.shape, lambda f: (0,) * a.ndim)
    row_spec = pl.BlockSpec((rows, width), lambda f: (0, 0))
    return pl.pallas_call(
        expert_kernel,
        grid=(ff // block,),
        in_specs=[
            pl.BlockSpec(memory_space=pltpu.SMEM),
            whole(x),
            whole(c),
            whole(w_router),
            pl.BlockSpec((1, width, block), lambda f: (local, 0, f)),
            pl.BlockSpec((1, block, width), lambda f: (local, f, 0)),
        ],
        out_specs=[row_spec, row_spec, pl.BlockSpec((experts, width), lambda f: (0, 0))],
        out_shape=[
            jax.ShapeDtypeStruct((rows, width), BF16),
            jax.ShapeDtypeStruct((rows, width), BF16),
            jax.ShapeDtypeStruct((experts, width), F32),
        ],
        scratch_shapes=[
            pltpu.VMEM((rows, width), BF16),
            pltpu.VMEM((rows, width), F32),
            pltpu.VMEM((rows, width), F32),
        ],
        compiler_params=params(dimension_semantics=("arbitrary",)),
        cost_estimate=cost(
            8 * rows * width * ff, 4 * width * ff + 8 * rows * width, rows * ff
        ),
        name="expert_rows",
    )(number, x, c, w_router, w_in, w_out)


def expert_grad_kernel(num_ref, x_ref, c_ref, wr_ref, win_ref, wout_ref, *refs):
    gin_ref, gout_ref, gp_ref, xt_ref = refs[-4:]
    parts, rows, width = x_ref.shape
    x = x_ref[...].reshape(parts * rows, width)

    @pl.when(pl.program_id(0) == 0)
    def _():
        _, _, gate = gate_of(dot(x, wr_ref[...]), num_ref[1])
        c = c_ref[...].reshape(parts * rows, width)
        gp_ref[...] = (gate * c.astype(F32)).astype(BF16)
        xt_ref[...] = x.astype(F32).T.astype(BF16)

    gp = gp_ref[...]
    pre_t = dot_nt(win_ref[0].astype(F32).T.astype(BF16), x)
    hidden_t, slope_t = gelu_pair(pre_t)
    grad_hidden_t = dot_nt(wout_ref[0], gp)
    gout_ref[0] = dot(hidden_t.astype(BF16), gp)
    gin_ref[0] = dot_nt(xt_ref[...], (grad_hidden_t * slope_t).astype(BF16))


def expert_grads(numbers, x_all, c_all, w_router, w_in, w_out, local, n_dp, prior=()):
    parts, rows, width = x_all.shape
    ff = w_in.shape[2]
    part = ff // n_dp
    block = 256 if part % 256 == 0 else 128
    steps = part // block
    whole = lambda a: pl.BlockSpec(a.shape, lambda f, n: (0,) * a.ndim)
    return pl.pallas_call(
        expert_grad_kernel,
        grid_spec=pltpu.PrefetchScalarGridSpec(
            num_scalar_prefetch=1,
            grid=(steps,),
            in_specs=[
                whole(x_all),
                whole(c_all),
                whole(w_router),
                pl.BlockSpec((1, width, block), lambda f, n: (local, 0, n[0] * steps + f)),
                pl.BlockSpec((1, block, width), lambda f, n: (local, n[0] * steps + f, 0)),
            ]
            + [pl.BlockSpec(memory_space=pl.ANY)] * len(prior),
            out_specs=[
                pl.BlockSpec((1, width, block), lambda f, n: (local, 0, f)),
                pl.BlockSpec((1, block, width), lambda f, n: (local, f, 0)),
            ],
            scratch_shapes=[
                pltpu.VMEM((parts * rows, width), BF16),
                pltpu.VMEM((width, parts * rows), BF16),
            ],
        ),
        out_shape=[
            jax.ShapeDtypeStruct((w_in.shape[0], width, part), F32),
            jax.ShapeDtypeStruct((w_in.shape[0], part, width), F32),
        ],
        compiler_params=params(dimension_semantics=("arbitrary",)),
        cost_estimate=cost(
            8 * parts * rows * width * part,
            4 * parts * rows * width + 12 * width * part,
            parts * rows * part,
        ),
        input_output_aliases={6 + i: i for i in range(len(prior))},
        name="expert_weight_grads",
    )(numbers, x_all, c_all, w_router, w_in, w_out, *prior)


def split_rows(num_ref, full_ref, keep_ref, send_ref):
    part = keep_ref.shape[1]
    core = num_ref[0] & 1
    for y in range(keep_ref.shape[0]):
        own = pl.multiple_of((2 * y + core) * part, 16)
        other = pl.multiple_of((2 * y + 1 - core) * part, 16)
        keep_ref[y] = full_ref[pl.ds(own, part), :]
        send_ref[y] = full_ref[pl.ds(other, part), :]


def middle_back_kernel(num_ref, cot_ref, middle_ref, gain_ref, target_ref, wo_ref, *refs):
    groups = 3
    ctx_refs, refs = refs[:groups], refs[groups:]
    back_refs, (gmid_ref, gctx_ref, keep_ref, send_ref, ggain_ref, gwo_ref) = refs[:-6], refs[-6:]
    seq, width = cot_ref.shape
    target = target_ref[...]
    grad = jnp.zeros((seq, width), F32)
    for l, back in enumerate(back_refs):
        rows = back.shape[0]
        grad = grad + dot(token_hot(target, l * rows, rows), back[...])
    grad_in, grad_gain = norm_back(middle_ref[...], gain_ref[...], grad)
    ggain_ref[...] = grad_gain
    grad_middle = cot_ref[...].astype(F32) + grad_in
    gmid_ref[...] = grad_middle
    grad_attn = grad_middle.astype(BF16)
    gctx_ref[...] = dot_nt(grad_attn, wo_ref[...]).astype(BF16)
    row = 0
    for ctx_ref in ctx_refs:
        cols = ctx_ref.shape[0]
        gwo_ref[row : row + cols, :] = dot(ctx_ref[...], grad_attn).astype(BF16)
        row += cols
    split_rows(num_ref, gwo_ref, keep_ref, send_ref)


def middle_back(number, cot, middle, gain, target_col, w_out, ctxts, backs, n_dp):
    seq, width = cot.shape
    sds = jax.ShapeDtypeStruct
    slots = sum(b.shape[0] for b in backs)
    half = sds((n_dp // 2, width // n_dp, width), BF16)
    vmem = pl.BlockSpec(memory_space=pltpu.VMEM)
    return pl.pallas_call(
        middle_back_kernel,
        in_specs=[pl.BlockSpec(memory_space=pltpu.SMEM)] + [vmem] * (5 + len(ctxts) + len(backs)),
        out_shape=[sds((seq, width), F32), sds((seq, width), BF16), half, half, sds((1, width), F32)],
        scratch_shapes=[pltpu.VMEM((width, width), BF16)],
        compiler_params=params(),
        cost_estimate=cost(
            4 * seq * width * width + 2 * slots * seq * width,
            4 * width * width + 14 * seq * width + 2 * slots * width,
        ),
        name="second_norm_backward",
    )(number, cot, middle, gain, target_col, w_out, *ctxts, *backs)


def attend_back_kernel(
    num_ref, normt_ref, q_ref, k_ref, v_ref, kt_ref, e_ref, rinv_ref, do_ref,
    keep_ref, send_ref, grads_ref, diag_ref, acc_ref, dqt_ref, gw_ref,
):
    seq = q_ref.shape[0]
    pair = e_ref.shape[0]
    hd = TILE // pair
    cols = grads_ref.shape[1] // 3
    step = pl.program_id(0)
    lane = lax.broadcasted_iota(jnp.int32, (seq, TILE), 1) // hd
    row_bit = lax.broadcasted_iota(jnp.int32, (8, 2 * seq), 0)
    zero = jnp.zeros((seq, TILE), BF16)
    dk = jnp.zeros((seq, TILE), F32)
    dv = jnp.zeros((seq, TILE), F32)
    v_pair = v_ref[...]
    for h in range(pair):
        q_own = jnp.where(lane == h, q_ref[...], zero)
        do_own = jnp.where(lane == h, do_ref[...], zero)
        acc_ref[...] = jnp.zeros_like(acc_ref)
        for start in range(0, seq, STRIP):
            st = slice(start, start + STRIP)
            p = e_ref[h, :, st].astype(F32) * rinv_ref[h, :, st]
            t = dot_nt(v_pair, do_own[st]) * p
            ds = t - p * jnp.sum(t, axis=0, keepdims=True)
            dsb = ds.astype(BF16)
            dv = dv + dot(p.astype(BF16), do_own[st])
            dk = dk + dot(dsb, q_own[st])
            dqt_ref[h * hd : (h + 1) * hd, st] = dot(kt_ref[h * hd : (h + 1) * hd, :], dsb) * (
                1.0 / math.sqrt(hd)
            )
            for b in range(0, seq, TILE):
                off = seq - TILE - b + start
                acc_ref[:, off : off + STRIP] += ds[b : b + TILE]
        folded = acc_ref[...]
        half = TILE // 2
        while half >= 8:
            folded = folded[:half] + pltpu.roll(folded[half:], 2 * seq - half, 1)
            half //= 2
        for bit in (4, 2, 1):
            turned = pltpu.roll(folded, 2 * seq - bit, 1)
            folded = jnp.where((row_bit & bit) != 0, turned, folded)
        diag_ref[h] = jnp.sum(folded, axis=0, keepdims=True)
    at = lambda base: pl.ds(pl.multiple_of(base * cols + step * TILE, TILE), TILE)
    grads_ref[:, at(0)] = dqt_ref[...].T.astype(BF16)
    grads_ref[:, at(1)] = dk.astype(BF16)
    grads_ref[:, at(2)] = dv.astype(BF16)

    @pl.when(step == pl.num_programs(0) - 1)
    def _():
        gw_ref[...] = dot(normt_ref[...], grads_ref[...]).astype(BF16)
        split_rows(num_ref, gw_ref, keep_ref, send_ref)


def attend_back(number, normt, q, k, v, kt, e, rinv, grad_ctx, group, n_dp):
    seq, cols = q.shape
    width = normt.shape[0]
    heads_in = e.shape[0]
    pair = heads_in * TILE // cols
    steps = cols // TILE
    whole = lambda a: pl.BlockSpec(a.shape, lambda g: (0,) * a.ndim)
    full = lambda shape: pl.BlockSpec(shape, lambda g: (0,) * len(shape))
    nat = pl.BlockSpec((seq, TILE), lambda g: (0, g))
    sds = jax.ShapeDtypeStruct
    half = (n_dp // 2, width // n_dp, 3 * cols)
    return pl.pallas_call(
        attend_back_kernel,
        grid=(steps,),
        in_specs=[
            pl.BlockSpec(memory_space=pltpu.SMEM), whole(normt), nat, nat, nat,
            pl.BlockSpec((TILE, seq), lambda g: (g, 0)),
            pl.BlockSpec((pair, seq, seq), lambda g: (g, 0, 0)),
            pl.BlockSpec((pair, 1, seq), lambda g: (g, 0, 0)),
            pl.BlockSpec((seq, TILE), lambda g: (0, group * steps + g)),
        ],
        out_specs=[
            full(half), full(half), full((seq, 3 * cols)),
            pl.BlockSpec((pair, 1, 2 * seq), lambda g: (g, 0, 0)),
        ],
        out_shape=[
            sds(half, BF16), sds(half, BF16), sds((seq, 3 * cols), BF16),
            sds((heads_in, 1, 2 * seq), F32),
        ],
        scratch_shapes=[
            pltpu.VMEM((TILE, 2 * seq), F32), pltpu.VMEM((TILE, seq), F32),
            pltpu.VMEM((width, 3 * cols), BF16),
        ],
        compiler_params=params(dimension_semantics=("arbitrary",)),
        cost_estimate=cost(
            6 * seq * width * cols + 8 * seq * seq * cols,
            2 * (6 * width * cols + 8 * seq * cols + heads_in * seq * seq),
        ),
        name="attention_backward",
    )(number, normt, q, k, v, kt, e, rinv, grad_ctx)


def first_back_kernel(tok_ref, gain_ref, gmid_ref, *refs):
    gtok_ref, ggain_ref = refs[-2:]
    groups = (len(refs) - 2) // 2
    grad = jnp.zeros(tok_ref.shape, F32)
    for g in range(groups):
        grad = grad + dot_nt(refs[g][...], refs[groups + g][...])
    grad_in, grad_gain = norm_back(tok_ref[...].astype(F32), gain_ref[...], grad)
    gtok_ref[...] = gmid_ref[...] + grad_in
    ggain_ref[...] = grad_gain


def first_back(tokens, gain, grad_middle, grads, weights):
    seq, width = tokens.shape
    return pl.pallas_call(
        first_back_kernel,
        out_shape=[
            jax.ShapeDtypeStruct((seq, width), F32), jax.ShapeDtypeStruct((1, width), F32)
        ],
        compiler_params=params(),
        cost_estimate=cost(6 * seq * width * width, 6 * width * width + 16 * seq * width),
        name="first_norm_backward",
    )(tokens, gain, grad_middle, *grads, *weights)


def output_kernel(middle_ref, target_ref, *refs):
    out_ref = refs[-1]
    total = middle_ref[...]
    for l, back in enumerate(refs[:-1]):
        rows = back.shape[0]
        total = total + dot(token_hot(target_ref[...], l * rows, rows), back[...])
    out_ref[...] = total.astype(BF16)


def output_step(middle, target_col, backs):
    seq, width = middle.shape
    slots = sum(b.shape[0] for b in backs)
    return pl.pallas_call(
        output_kernel,
        out_shape=jax.ShapeDtypeStruct((seq, width), BF16),
        compiler_params=params(),
        cost_estimate=cost(2 * slots * seq * width, 6 * seq * width + 2 * slots * width),
        name="layer_output",
    )(middle, target_col, *backs)


def flip(value, axis, bit):
    size = lax.axis_size(axis)
    return lax.ppermute(value, axis, [(i, i ^ bit) for i in range(size)])


def butterfly_sum(value, axes):
    for axis in axes:
        bit = 1
        while bit < lax.axis_size(axis):
            value = value + flip(value, axis, bit)
            bit *= 2
    return value


def gather_pieces(piece):
    pieces = {0: piece}
    bits = []
    bit = 2
    while bit < lax.axis_size("dp"):
        bits.append(bit)
        bit *= 2
    for bit in bits + [1]:
        pieces.update({m | bit: flip(p, "dp", bit) for m, p in pieces.items()})
    return [pieces[m] for m in sorted(pieces)]


def reduce_rows(keep, send, dp_index):
    peers = lax.axis_size("expert")
    total = keep.astype(F32) + flip(send, "dp", 1).astype(F32)
    bit = lax.axis_size("dp") // 2
    while bit > 1:
        halves = total.reshape(2, total.shape[0] // 2, *total.shape[1:])
        mine = jnp.where((dp_index & bit) != 0, 1, 0)
        sent = lax.dynamic_index_in_dim(halves, 1 - mine, 0, keepdims=False).astype(BF16)
        kept = lax.dynamic_index_in_dim(halves, mine, 0, keepdims=False)
        total = kept + flip(sent, "dp", bit).astype(F32)
        bit //= 2
    rows, cols = total.shape[1:]
    parts = total.astype(BF16).reshape(peers, rows // peers, cols)
    arrived = lax.all_to_all(parts, "expert", split_axis=0, concat_axis=0, tiled=True)
    summed = jnp.sum(arrived.astype(F32), axis=0, keepdims=True).astype(BF16)
    spread = jnp.broadcast_to(summed, parts.shape)
    shared = lax.all_to_all(spread, "expert", split_axis=0, concat_axis=0, tiled=True)
    return shared.reshape(rows, cols).astype(F32)


def body(
    tokens, segments, routes, slots, bucket_table, gain_attn, w_query, w_key, w_value, w_output,
    rel_bias, gain_ffn, w_router, w_in, w_out, cotangent,
):
    seq, width = tokens.shape
    buckets, heads = rel_bias.shape
    experts = w_router.shape[1]
    n_dp = lax.axis_size("dp")
    peers = lax.axis_size("expert")
    local = w_in.shape[0]
    capacity = max(2, (5 * seq + 4 * experts - 1) // (4 * experts))
    rows = peers * capacity
    dp_index = lax.axis_index("dp")
    expert_index = lax.axis_index("expert")
    number = jnp.reshape(dp_index, (1,)).astype(jnp.int32)
    groups = 3
    heads_in = heads // groups
    cols = width // groups

    group_pieces = []
    for g in range(groups):
        mine = jnp.concatenate(
            [w[:, g * cols : (g + 1) * cols] for w in (w_query, w_key, w_value)], axis=1
        )
        group_pieces.append(gather_pieces(mine))
    router_pad = jnp.pad(w_router, ((0, 0), (0, -experts % TILE)))
    full_or = lax.all_gather(
        jnp.concatenate([w_output, router_pad], axis=1), "dp", axis=0, tiled=True
    )
    full_o = full_or[:, :width]
    full_r = full_or[:, width : width + experts]

    order = (routes % local) * rows + (routes // local) * capacity + slots
    target = jnp.where(slots >= 0, order, -1)
    target_row = target[None, :]
    target_col = target[:, None]
    gain_one = gain_attn[None, :]
    gain_two = gain_ffn[None, :]

    def exchange(values):
        parts = values.reshape(peers, capacity, width)
        return lax.all_to_all(parts, "expert", split_axis=0, concat_axis=0, tiled=True).reshape(
            rows, width
        )

    c_here = [exchange(part) for part in place(target_row, cotangent, local, rows)]
    c_all = [lax.all_gather(part, "dp", axis=0, tiled=False) for part in c_here]

    reversed_table = jnp.concatenate([bucket_table[::-1], jnp.full((1,), -1, jnp.int32)])
    bucket_ids = jnp.arange(buckets, dtype=jnp.int32)
    hot_rev = (bucket_ids[:, None] == reversed_table[None, :]).astype(F32)
    rel_rev = jnp.dot(rel_bias.T, hot_rev, precision=HIGH)
    shifted = jnp.roll(reversed_table, 1 - TILE)
    hot_shifted = (shifted[:, None] == bucket_ids[None, :]).astype(F32)
    bias, normed, normt = prepare(rel_rev, tokens, gain_one)
    marks = jnp.arange(TILE, dtype=jnp.int32)[None, :]
    same = segments[0][:, None] == marks
    kseg = same.astype(BF16)
    qseg = jnp.where(same, 0.0, -1e9).astype(BF16)

    saved, ctxts, weights = [], [], []
    for g in range(groups):
        *kept, ctxt, weight = attend(
            number, normed, bias, kseg, qseg, group_pieces[g], g, heads_in
        )
        saved.append(kept)
        ctxts.append(ctxt)
        weights.append(weight)
    middle, *placed = middle_step(tokens, full_o, gain_two, target_row, ctxts, local, rows)

    arrived = [exchange(part) for part in placed]
    arrived[-1], c_all = lax.optimization_barrier((arrived[-1], c_all))
    x_all = [lax.all_gather(part, "dp", axis=0, tiled=False) for part in arrived]
    backs, scaled, router_terms, numbers = [], [], [], []
    for l in range(local):
        numbers.append(jnp.stack([dp_index, expert_index * local + l]).astype(jnp.int32))
        out, grad_x, router_term = expert_step(
            numbers[l], arrived[l], c_here[l], full_r, w_in, w_out, l, 512
        )
        backs.append(exchange(grad_x))
        scaled.append(out)
        router_terms.append(router_term)

    expert_terms = expert_grads(numbers[0], x_all[0], c_all[0], full_r, w_in, w_out, 0, n_dp)
    backs[-1], expert_terms = lax.optimization_barrier((backs[-1], expert_terms))
    scaled, _ = lax.optimization_barrier((scaled, backs[-1]))
    returns = [exchange(part) for part in scaled]

    grad_middle, grad_ctx, keep, send, ggain_two = middle_back(
        number, cotangent, middle, gain_two, target_col, full_o, ctxts, backs, n_dp
    )
    shard_o = reduce_rows(keep, send, dp_index)
    shards, grads, diags = [], [], []
    for g in range(groups):
        if g == groups - 1:
            grad_ctx, returns = lax.optimization_barrier((grad_ctx, returns))
        keep, send, grad, diag = attend_back(
            number, normt, *saved[g], grad_ctx, g, n_dp
        )
        shards.append(reduce_rows(keep, send, dp_index))
        grads.append(grad)
        diags.append(diag)
    grad_tokens, ggain_one = first_back(tokens, gain_one, grad_middle, grads, weights)
    output = output_step(middle, target_col, returns)
    for l in range(1, local):
        expert_terms = expert_grads(
            numbers[l], x_all[l], c_all[l], full_r, w_in, w_out, l, n_dp, expert_terms
        )

    diag = jnp.concatenate(diags, axis=0).reshape(heads, 2 * seq)
    grad_rel = jnp.dot(diag, hot_shifted, precision=HIGH)
    rel_row = jnp.pad(grad_rel.reshape(1, heads * buckets), ((0, 0), (0, width - heads * buckets)))
    small = butterfly_sum(
        jnp.concatenate([sum(router_terms), ggain_two, ggain_one, rel_row], axis=0),
        ("dp", "expert"),
    )
    shard_rows = width // n_dp
    grad_router = lax.dynamic_slice_in_dim(small[:experts], dp_index * shard_rows, shard_rows, 1).T
    total_rel = small[experts + 2, : heads * buckets].reshape(heads, buckets).T
    shard_q, shard_k, shard_v = [
        jnp.concatenate([s[:, i * cols : (i + 1) * cols] for s in shards], axis=1)
        for i in range(3)
    ]
    return (
        output,
        grad_tokens,
        small[experts + 1],
        shard_q,
        shard_k,
        shard_v,
        shard_o,
        total_rel,
        small[experts],
        grad_router,
        expert_terms[0],
        expert_terms[1],
    )


def solution(mesh):
    in_specs = (
        P(("dp", "expert"), None),
        P(("dp", "expert"), None),
        P(("dp", "expert")),
        P(("dp", "expert")),
        P(),
        P(),
        P("dp", None),
        P("dp", None),
        P("dp", None),
        P("dp", None),
        P(),
        P(),
        P("dp", None),
        P("expert", None, None),
        P("expert", None, None),
        P(("dp", "expert"), None),
    )
    out_specs = (
        P(("dp", "expert"), None),
        P(("dp", "expert"), None),
        P(),
        P("dp", None),
        P("dp", None),
        P("dp", None),
        P("dp", None),
        P(),
        P(),
        P("dp", None),
        P("expert", None, "dp"),
        P("expert", "dp", None),
    )
    return jax.shard_map(body, mesh=mesh, in_specs=in_specs, out_specs=out_specs, check_vma=False)
```

```python
import functools
import math

import jax
import jax.numpy as jnp
from jax import lax
from jax.experimental import pallas as pl
from jax.experimental.pallas import tpu as pltpu
from jax.sharding import PartitionSpec as P

EPS = 1e-06
HIGH = lax.Precision.HIGHEST
F32 = jnp.float32
BF16 = jnp.bfloat16
VMEM_LIMIT = 56 * 1024 * 1024
TILE = 128
STRIP = 256
GELU_A = math.sqrt(2.0 / math.pi)
GELU_B = 0.044715


def dot(a, b):
    return jnp.dot(a, b, preferred_element_type=F32)


def dot_nt(a, b):
    return lax.dot_general(a, b, (((1,), (1,)), ((), ())), preferred_element_type=F32)


def params(**kw):
    return pltpu.CompilerParams(vmem_limit_bytes=VMEM_LIMIT, **kw)


def cost(flops, nbytes, trans=0):
    return pl.CostEstimate(flops=int(flops), bytes_accessed=int(nbytes), transcendentals=int(trans))


def rms_scale(stream):
    return lax.rsqrt(jnp.mean(stream * stream, axis=-1, keepdims=True) + EPS)


def norm_back(stream, gain, grad_out):
    scale = rms_scale(stream)
    grad_gain = jnp.sum(grad_out * (stream * scale), axis=0, keepdims=True)
    scaled = grad_out * gain
    inner = jnp.mean(scaled * stream, axis=-1, keepdims=True)
    grad_in = scale * scaled - stream * (scale * scale * scale * inner)
    return grad_in, grad_gain


def gelu_pair(v):
    sq = v * v
    inner = GELU_A * (v + GELU_B * (sq * v))
    th = jnp.tanh(inner)
    half = 0.5 * (1.0 + th)
    slope = half + (0.5 * v) * (1.0 - th * th) * (GELU_A + (3.0 * GELU_A * GELU_B) * sq)
    return v * half, slope


def slot_hot(target_row, start, rows):
    seq = target_row.shape[1]
    ids = lax.broadcasted_iota(jnp.int32, (rows, seq), 0) + start
    return (ids == target_row).astype(F32).astype(BF16)


def token_hot(target_col, start, rows):
    seq = target_col.shape[0]
    ids = lax.broadcasted_iota(jnp.int32, (seq, rows), 1) + start
    return (ids == target_col).astype(F32).astype(BF16)


def place_kernel(target_ref, rows_ref, out_ref):
    out_ref[...] = dot(slot_hot(target_ref[...], 0, out_ref.shape[0]), rows_ref[...]).astype(BF16)


def place(target_row, values, rows):
    seq, width = values.shape
    return pl.pallas_call(
        place_kernel,
        out_shape=jax.ShapeDtypeStruct((rows, width), BF16),
        compiler_params=params(),
        cost_estimate=cost(2 * rows * seq * width, 2 * (rows + seq) * width),
        name="place_cotangent",
    )(target_row, values)


def prepare_kernel(rel_ref, tok_ref, gain_ref, out_ref, normed_ref, normt_ref):
    heads, width = rel_ref.shape
    wide = out_ref.shape[2]
    for h in range(heads):
        base = jnp.broadcast_to(rel_ref[h : h + 1, :], (TILE, width))
        turned = pltpu.roll(base, width - (TILE - 1), 1, stride=1, stride_axis=0)
        out_ref[h] = turned[:, :wide]
    stream = tok_ref[...].astype(F32)
    normed = stream * rms_scale(stream) * gain_ref[...]
    normed_ref[...] = normed.astype(BF16)
    normt_ref[...] = normed.T.astype(BF16)


def prepare(rel_rev, tokens, gain):
    heads, span = rel_rev.shape
    seq, width = tokens.shape
    wide = 2 * seq - TILE
    return pl.pallas_call(
        prepare_kernel,
        out_shape=[
            jax.ShapeDtypeStruct((heads, TILE, wide), F32),
            jax.ShapeDtypeStruct((seq, width), BF16),
            jax.ShapeDtypeStruct((width, seq), BF16),
        ],
        compiler_params=params(),
        cost_estimate=cost(heads * TILE * span, 4 * heads * TILE * wide + 6 * seq * width),
        name="bias_and_first_norm",
    )(rel_rev, tokens, gain)


def attend_kernel(num_ref, normed_ref, bias_ref, kseg_ref, qseg_ref, *refs):
    pieces, refs = refs[:-8], refs[-8:]
    q_ref, k_ref, v_ref, kt_ref, e_ref, rinv_ref, ctxt_ref, w_ref = refs
    seq = normed_ref.shape[0]
    pair = e_ref.shape[0]
    cols = q_ref.shape[1]
    hd = TILE // pair
    step = pl.program_id(0)

    @pl.when(step == 0)
    def _():
        part = pieces[0].shape[0]
        for mask, piece in enumerate(pieces):
            row = pl.multiple_of((num_ref[0] ^ mask) * part, 16)
            w_ref[pl.ds(row, part), :] = piece[...]
        normed = normed_ref[...]
        q = dot(normed, w_ref[:, :cols]).astype(BF16).astype(F32) * (1.0 / math.sqrt(hd))
        k = dot(normed, w_ref[:, cols : 2 * cols])
        q_ref[...] = q.astype(BF16)
        k_ref[...] = k.astype(BF16)
        kt_ref[...] = k.T.astype(BF16)
        v_ref[...] = dot(normed, w_ref[:, 2 * cols :]).astype(BF16)

    lane = lax.broadcasted_iota(jnp.int32, (seq, TILE), 1) // hd
    sl = pl.ds(pl.multiple_of(step * TILE, TILE), TILE)
    q_pair = q_ref[:, sl]
    k_all = jnp.concatenate([k_ref[:, sl], kseg_ref[...]], axis=1)
    vt = v_ref[:, sl].astype(F32).T.astype(BF16)
    qseg = qseg_ref[...]
    for h in range(pair):
        q_own = jnp.where(lane == h, q_pair, jnp.zeros_like(q_pair))
        q_all = jnp.concatenate([q_own, qseg], axis=1)
        for start in range(0, seq, STRIP):
            scores = dot_nt(k_all, q_all[start : start + STRIP])
            parts = []
            for b in range(0, seq, TILE):
                off = seq - TILE - b + start
                parts.append(scores[b : b + TILE] + bias_ref[h, :, off : off + STRIP])
            scores = jnp.concatenate(parts, axis=0)
            e = jnp.exp(scores - jnp.max(scores, axis=0, keepdims=True))
            rinv = 1.0 / jnp.sum(e, axis=0, keepdims=True)
            eb = e.astype(BF16)
            e_ref[h, :, start : start + STRIP] = eb
            rinv_ref[h, :, start : start + STRIP] = rinv
            ctxt = dot(vt[h * hd : (h + 1) * hd], eb) * rinv
            ctxt_ref[h * hd : (h + 1) * hd, start : start + STRIP] = ctxt.astype(BF16)


def attend(number, normed, bias, kseg, qseg, pieces, group, heads_in):
    seq, width = normed.shape
    wide = bias.shape[2]
    cols = pieces[0].shape[1] // 3
    pair = heads_in * TILE // cols
    steps = cols // TILE
    whole = lambda a: pl.BlockSpec(a.shape, lambda g: (0,) * a.ndim)
    full = lambda shape: pl.BlockSpec(shape, lambda g: (0,) * len(shape))
    sds = jax.ShapeDtypeStruct
    return pl.pallas_call(
        attend_kernel,
        grid=(steps,),
        in_specs=[
            pl.BlockSpec(memory_space=pltpu.SMEM), whole(normed),
            pl.BlockSpec((pair, TILE, wide), lambda g: (group * steps + g, 0, 0)),
            whole(kseg), whole(qseg),
        ]
        + [whole(p) for p in pieces],
        out_specs=[
            full((seq, cols)), full((seq, cols)), full((seq, cols)), full((cols, seq)),
            pl.BlockSpec((pair, seq, seq), lambda g: (g, 0, 0)),
            pl.BlockSpec((pair, 1, seq), lambda g: (g, 0, 0)),
            pl.BlockSpec((TILE, seq), lambda g: (g, 0)),
            full((width, 3 * cols)),
        ],
        out_shape=[
            sds((seq, cols), BF16), sds((seq, cols), BF16), sds((seq, cols), BF16),
            sds((cols, seq), BF16), sds((heads_in, seq, seq), BF16), sds((heads_in, 1, seq), F32),
            sds((cols, seq), BF16), sds((width, 3 * cols), BF16),
        ],
        compiler_params=params(dimension_semantics=("arbitrary",)),
        cost_estimate=cost(
            6 * seq * width * cols + 4 * seq * seq * cols,
            2 * (6 * width * cols + 6 * seq * cols + heads_in * seq * seq) + 4 * pair * steps * TILE * wide,
            heads_in * seq * seq,
        ),
        name="attention_forward",
    )(number, normed, bias, kseg, qseg, *pieces)


def middle_kernel(groups, tok_ref, wo_ref, gain_ref, target_ref, *refs):
    width = tok_ref.shape[1]
    ctx_refs, (middle_ref, *placed_refs) = refs[:groups], refs[groups:]
    middle = tok_ref[...].astype(F32)
    row = 0
    for ctx_ref in ctx_refs:
        cols = ctx_ref.shape[0]
        context = ctx_ref[...].astype(F32).T.astype(BF16)
        middle = middle + dot(context, wo_ref[row : row + cols, :width])
        row += cols
    middle_ref[...] = middle
    normed = (middle * rms_scale(middle) * gain_ref[...]).astype(BF16)
    for l, placed_ref in enumerate(placed_refs):
        rows = placed_ref.shape[0]
        placed_ref[...] = dot(slot_hot(target_ref[...], l * rows, rows), normed).astype(BF16)


def middle_step(tokens, w_out, gain, target_row, ctxts, local, rows):
    seq, width = tokens.shape
    return pl.pallas_call(
        functools.partial(middle_kernel, len(ctxts)),
        out_shape=[jax.ShapeDtypeStruct((seq, width), F32)]
        + [jax.ShapeDtypeStruct((rows, width), BF16)] * local,
        compiler_params=params(),
        cost_estimate=cost(
            2 * seq * width * width + 2 * local * rows * seq * width,
            2 * width * width + 8 * seq * width + 2 * local * rows * width,
        ),
        name="output_projection_dispatch",
    )(tokens, w_out, gain, target_row, *ctxts)


def gate_of(logits, expert):
    top = jnp.max(logits, axis=-1, keepdims=True)
    ex = jnp.exp(logits - top)
    prob = ex / jnp.sum(ex, axis=-1, keepdims=True)
    hot = lax.broadcasted_iota(jnp.int32, logits.shape, 1) == expert
    gate = jnp.sum(jnp.where(hot, prob, 0.0), axis=-1, keepdims=True)
    return prob, hot, gate


def hidden_cot_kernel(*refs):
    c_refs, (wout_ref, out_ref) = refs[:-2], refs[-2:]
    for l, c_ref in enumerate(c_refs):

        @pl.when(pl.program_id(0) == l)
        def _():
            out_ref[0] = dot_nt(c_ref[...], wout_ref[0])


def hidden_cot(cs, w_out, block):
    rows, width = cs[0].shape
    local, ff = w_out.shape[:2]
    return pl.pallas_call(
        hidden_cot_kernel,
        grid=(local, ff // block),
        in_specs=[pl.BlockSpec((rows, width), lambda l, f: (0, 0)) for _ in cs]
        + [pl.BlockSpec((1, block, width), lambda l, f: (l, f, 0))],
        out_specs=pl.BlockSpec((1, rows, block), lambda l, f: (l, 0, f)),
        out_shape=jax.ShapeDtypeStruct((local, rows, ff), F32),
        compiler_params=params(dimension_semantics=("arbitrary", "arbitrary")),
        cost_estimate=cost(
            2 * local * rows * width * ff, local * ff * (2 * width + 4 * rows)
        ),
        name="cotangent_hidden",
    )(*cs, w_out)


def expert_kernel(
    num_ref, x_ref, c_ref, ch_ref, wr_ref, win_ref, wout_ref,
    scaled_ref, grad_ref, router_ref, gate_ref, acc_p, acc_g,
):
    step = pl.program_id(0)
    experts = router_ref.shape[0]

    @pl.when(step == 0)
    def _():
        _, _, gate = gate_of(dot(x_ref[...], wr_ref[...])[:, :experts], num_ref[1])
        gate_ref[...] = gate
        acc_p[...] = jnp.zeros_like(acc_p)
        acc_g[...] = jnp.zeros_like(acc_g)

    pre = dot(x_ref[...], win_ref[0])
    hidden, slope = gelu_pair(pre)
    acc_p[...] += dot(hidden.astype(BF16), wout_ref[0])
    grad_pre = (ch_ref[0] * gate_ref[...] * slope).astype(BF16)
    acc_g[...] += dot_nt(grad_pre, win_ref[0])

    @pl.when(step == pl.num_programs(0) - 1)
    def _():
        x = x_ref[...]
        prob, hot, gate = gate_of(dot(x, wr_ref[...])[:, :experts], num_ref[1])
        produced = acc_p[...]
        scaled_ref[...] = (gate * produced).astype(BF16)
        grad_gate = jnp.sum(
            c_ref[...].astype(F32) * produced.astype(BF16).astype(F32), axis=-1, keepdims=True
        )
        grad_logits = prob * (jnp.where(hot, grad_gate, 0.0) - gate * grad_gate)
        logits_b = grad_logits.astype(BF16)
        grad_ref[...] = (acc_g[...] + dot_nt(logits_b, wr_ref[:, :experts])).astype(BF16)
        router_ref[...] = dot(grad_logits.T.astype(BF16), x)


def expert_step(number, x, c, ch, w_or, w_in, w_out, local, block, experts):
    rows, width = x.shape
    ff = w_in.shape[2]
    router_cols = w_or.shape[1] - width
    whole = lambda a: pl.BlockSpec(a.shape, lambda f: (0,) * a.ndim)
    row_spec = pl.BlockSpec((rows, width), lambda f: (0, 0))
    return pl.pallas_call(
        expert_kernel,
        grid=(ff // block,),
        in_specs=[
            pl.BlockSpec(memory_space=pltpu.SMEM),
            whole(x),
            whole(c),
            pl.BlockSpec((1, rows, block), lambda f: (local, 0, f)),
            pl.BlockSpec((width, router_cols), lambda f: (0, width // router_cols)),
            pl.BlockSpec((1, width, block), lambda f: (local, 0, f)),
            pl.BlockSpec((1, block, width), lambda f: (local, f, 0)),
        ],
        out_specs=[row_spec, row_spec, pl.BlockSpec((experts, width), lambda f: (0, 0))],
        out_shape=[
            jax.ShapeDtypeStruct((rows, width), BF16),
            jax.ShapeDtypeStruct((rows, width), BF16),
            jax.ShapeDtypeStruct((experts, width), F32),
        ],
        scratch_shapes=[
            pltpu.VMEM((rows, 1), F32),
            pltpu.VMEM((rows, width), F32),
            pltpu.VMEM((rows, width), F32),
        ],
        compiler_params=params(dimension_semantics=("arbitrary",)),
        cost_estimate=cost(
            6 * rows * width * ff, 4 * width * ff + 4 * rows * ff + 8 * rows * width, rows * ff
        ),
        name="expert_rows",
    )(number, x, c, ch, w_or, w_in, w_out)


def expert_grad_kernel(experts, num_ref, x_ref, c_ref, wr_ref, win_ref, wout_ref, *refs):
    gin_ref, gout_ref, gp_ref, xt_ref = refs[-4:]
    parts, rows, width = x_ref.shape
    x = x_ref[...].reshape(parts * rows, width)

    @pl.when(pl.program_id(0) == 0)
    def _():
        _, _, gate = gate_of(dot(x, wr_ref[...])[:, :experts], num_ref[1])
        c = c_ref[...].reshape(parts * rows, width)
        gp_ref[...] = (gate * c.astype(F32)).astype(BF16)
        xt_ref[...] = x.astype(F32).T.astype(BF16)

    gp = gp_ref[...]
    pre_t = dot_nt(win_ref[0].astype(F32).T.astype(BF16), x)
    hidden_t, slope_t = gelu_pair(pre_t)
    grad_hidden_t = dot_nt(wout_ref[0], gp)
    gout_ref[0] = dot(hidden_t.astype(BF16), gp)
    gin_ref[0] = dot_nt(xt_ref[...], (grad_hidden_t * slope_t).astype(BF16))


def expert_grads(numbers, x_all, c_all, w_or, w_in, w_out, local, n_dp, experts, prior=()):
    parts, rows, width = x_all.shape
    ff = w_in.shape[2]
    router_cols = w_or.shape[1] - width
    part = ff // n_dp
    block = 256 if part % 256 == 0 else 128
    steps = part // block
    whole = lambda a: pl.BlockSpec(a.shape, lambda f, n: (0,) * a.ndim)
    return pl.pallas_call(
        functools.partial(expert_grad_kernel, experts),
        grid_spec=pltpu.PrefetchScalarGridSpec(
            num_scalar_prefetch=1,
            grid=(steps,),
            in_specs=[
                whole(x_all),
                whole(c_all),
                pl.BlockSpec((width, router_cols), lambda f, n: (0, width // router_cols)),
                pl.BlockSpec((1, width, block), lambda f, n: (local, 0, n[0] * steps + f)),
                pl.BlockSpec((1, block, width), lambda f, n: (local, n[0] * steps + f, 0)),
            ]
            + [pl.BlockSpec(memory_space=pl.ANY)] * len(prior),
            out_specs=[
                pl.BlockSpec((1, width, block), lambda f, n: (local, 0, f)),
                pl.BlockSpec((1, block, width), lambda f, n: (local, f, 0)),
            ],
            scratch_shapes=[
                pltpu.VMEM((parts * rows, width), BF16),
                pltpu.VMEM((width, parts * rows), BF16),
            ],
        ),
        out_shape=[
            jax.ShapeDtypeStruct((w_in.shape[0], width, part), F32),
            jax.ShapeDtypeStruct((w_in.shape[0], part, width), F32),
        ],
        compiler_params=params(dimension_semantics=("arbitrary",)),
        cost_estimate=cost(
            8 * parts * rows * width * part,
            4 * parts * rows * width + 12 * width * part,
            parts * rows * part,
        ),
        input_output_aliases={6 + i: i for i in range(len(prior))},
        name="expert_weight_grads",
    )(numbers, x_all, c_all, w_or, w_in, w_out, *prior)


def split_rows(num_ref, full_ref, keep_ref, send_ref):
    part = keep_ref.shape[1]
    core = num_ref[0] & 1
    for y in range(keep_ref.shape[0]):
        own = pl.multiple_of((2 * y + core) * part, 16)
        other = pl.multiple_of((2 * y + 1 - core) * part, 16)
        keep_ref[y] = full_ref[pl.ds(own, part), :]
        send_ref[y] = full_ref[pl.ds(other, part), :]


def middle_back_kernel(groups, cot_ref, middle_ref, gain_ref, target_ref, wo_ref, *refs):
    ctx_refs, refs = refs[:groups], refs[groups:]
    back_refs, (gmid_ref, gctx_ref, gwo_ref, ggain_ref) = refs[:-4], refs[-4:]
    seq, width = cot_ref.shape
    target = target_ref[...]
    grad = jnp.zeros((seq, width), F32)
    for l, back in enumerate(back_refs):
        rows = back.shape[0]
        grad = grad + dot(token_hot(target, l * rows, rows), back[...])
    grad_in, grad_gain = norm_back(middle_ref[...], gain_ref[...], grad)
    ggain_ref[...] = grad_gain
    grad_middle = cot_ref[...].astype(F32) + grad_in
    gmid_ref[...] = grad_middle
    grad_attn = grad_middle.astype(BF16)
    gctx_ref[...] = dot_nt(grad_attn, wo_ref[:, :width]).astype(BF16)
    row = 0
    for ctx_ref in ctx_refs:
        cols = ctx_ref.shape[0]
        gwo_ref[row : row + cols, :] = dot(ctx_ref[...], grad_attn).astype(BF16)
        row += cols


def middle_back(cot, middle, gain, target_col, w_out, ctxts, backs):
    seq, width = cot.shape
    sds = jax.ShapeDtypeStruct
    slots = sum(b.shape[0] for b in backs)
    return pl.pallas_call(
        functools.partial(middle_back_kernel, len(ctxts)),
        out_shape=[
            sds((seq, width), F32), sds((seq, width), BF16), sds((width, width), BF16),
            sds((1, width), F32),
        ],
        compiler_params=params(),
        cost_estimate=cost(
            4 * seq * width * width + 2 * slots * seq * width,
            4 * width * width + 14 * seq * width + 2 * slots * width,
        ),
        name="second_norm_backward",
    )(cot, middle, gain, target_col, w_out, *ctxts, *backs)


def attend_back_kernel(
    num_ref, normt_ref, q_ref, k_ref, v_ref, kt_ref, e_ref, rinv_ref, do_ref,
    keep_ref, send_ref, grads_ref, diag_ref, acc_ref, dqt_ref, gw_ref,
):
    seq = q_ref.shape[0]
    pair = e_ref.shape[0]
    hd = TILE // pair
    cols = grads_ref.shape[1] // 3
    step = pl.program_id(0)
    lane = lax.broadcasted_iota(jnp.int32, (seq, TILE), 1) // hd
    row_bit = lax.broadcasted_iota(jnp.int32, (8, 2 * seq), 0)
    zero = jnp.zeros((seq, TILE), BF16)
    dk = jnp.zeros((seq, TILE), F32)
    dv = jnp.zeros((seq, TILE), F32)
    v_pair = v_ref[...]
    for h in range(pair):
        q_own = jnp.where(lane == h, q_ref[...], zero)
        do_own = jnp.where(lane == h, do_ref[...], zero)
        acc_ref[...] = jnp.zeros_like(acc_ref)
        for start in range(0, seq, STRIP):
            st = slice(start, start + STRIP)
            p = e_ref[h, :, st].astype(F32) * rinv_ref[h, :, st]
            t = dot_nt(v_pair, do_own[st]) * p
            ds = t - p * jnp.sum(t, axis=0, keepdims=True)
            dsb = ds.astype(BF16)
            dv = dv + dot(p.astype(BF16), do_own[st])
            dk = dk + dot(dsb, q_own[st])
            dqt_ref[h * hd : (h + 1) * hd, st] = dot(kt_ref[h * hd : (h + 1) * hd, :], dsb) * (
                1.0 / math.sqrt(hd)
            )
            for b in range(0, seq, TILE):
                off = seq - TILE - b + start
                acc_ref[:, off : off + STRIP] += ds[b : b + TILE]
        folded = acc_ref[...]
        half = TILE // 2
        while half >= 8:
            folded = folded[:half] + pltpu.roll(folded[half:], 2 * seq - half, 1)
            half //= 2
        for bit in (4, 2, 1):
            turned = pltpu.roll(folded, 2 * seq - bit, 1)
            folded = jnp.where((row_bit & bit) != 0, turned, folded)
        diag_ref[h] = jnp.sum(folded, axis=0, keepdims=True)
    at = lambda base: pl.ds(pl.multiple_of(base * cols + step * TILE, TILE), TILE)
    grads_ref[:, at(0)] = dqt_ref[...].T.astype(BF16)
    grads_ref[:, at(1)] = dk.astype(BF16)
    grads_ref[:, at(2)] = dv.astype(BF16)

    @pl.when(step == pl.num_programs(0) - 1)
    def _():
        gw_ref[...] = dot(normt_ref[...], grads_ref[...]).astype(BF16)
        split_rows(num_ref, gw_ref, keep_ref, send_ref)


def attend_back(number, normt, q, k, v, kt, e, rinv, grad_ctx, group, n_dp):
    seq, cols = q.shape
    width = normt.shape[0]
    heads_in = e.shape[0]
    pair = heads_in * TILE // cols
    steps = cols // TILE
    whole = lambda a: pl.BlockSpec(a.shape, lambda g: (0,) * a.ndim)
    full = lambda shape: pl.BlockSpec(shape, lambda g: (0,) * len(shape))
    nat = pl.BlockSpec((seq, TILE), lambda g: (0, g))
    sds = jax.ShapeDtypeStruct
    half = (n_dp // 2, width // n_dp, 3 * cols)
    return pl.pallas_call(
        attend_back_kernel,
        grid=(steps,),
        in_specs=[
            pl.BlockSpec(memory_space=pltpu.SMEM), whole(normt), nat, nat, nat,
            pl.BlockSpec((TILE, seq), lambda g: (g, 0)),
            pl.BlockSpec((pair, seq, seq), lambda g: (g, 0, 0)),
            pl.BlockSpec((pair, 1, seq), lambda g: (g, 0, 0)),
            pl.BlockSpec((seq, TILE), lambda g: (0, group * steps + g)),
        ],
        out_specs=[
            full(half), full(half), full((seq, 3 * cols)),
            pl.BlockSpec((pair, 1, 2 * seq), lambda g: (g, 0, 0)),
        ],
        out_shape=[
            sds(half, BF16), sds(half, BF16), sds((seq, 3 * cols), BF16),
            sds((heads_in, 1, 2 * seq), F32),
        ],
        scratch_shapes=[
            pltpu.VMEM((TILE, 2 * seq), F32), pltpu.VMEM((TILE, seq), F32),
            pltpu.VMEM((width, 3 * cols), BF16),
        ],
        compiler_params=params(dimension_semantics=("arbitrary",)),
        cost_estimate=cost(
            6 * seq * width * cols + 8 * seq * seq * cols,
            2 * (6 * width * cols + 8 * seq * cols + heads_in * seq * seq),
        ),
        name="attention_backward",
    )(number, normt, q, k, v, kt, e, rinv, grad_ctx)


def first_back_kernel(tok_ref, gain_ref, gmid_ref, *refs):
    gtok_ref, ggain_ref = refs[-2:]
    groups = (len(refs) - 2) // 2
    grad = jnp.zeros(tok_ref.shape, F32)
    for g in range(groups):
        grad = grad + dot_nt(refs[g][...], refs[groups + g][...])
    grad_in, grad_gain = norm_back(tok_ref[...].astype(F32), gain_ref[...], grad)
    gtok_ref[...] = gmid_ref[...] + grad_in
    ggain_ref[...] = grad_gain


def first_back(tokens, gain, grad_middle, grads, weights):
    seq, width = tokens.shape
    return pl.pallas_call(
        first_back_kernel,
        out_shape=[
            jax.ShapeDtypeStruct((seq, width), F32), jax.ShapeDtypeStruct((1, width), F32)
        ],
        compiler_params=params(),
        cost_estimate=cost(6 * seq * width * width, 6 * width * width + 16 * seq * width),
        name="first_norm_backward",
    )(tokens, gain, grad_middle, *grads, *weights)


def output_kernel(middle_ref, target_ref, *refs):
    out_ref = refs[-1]
    total = middle_ref[...]
    for l, back in enumerate(refs[:-1]):
        rows = back.shape[0]
        total = total + dot(token_hot(target_ref[...], l * rows, rows), back[...])
    out_ref[...] = total.astype(BF16)


def output_step(middle, target_col, backs):
    seq, width = middle.shape
    slots = sum(b.shape[0] for b in backs)
    return pl.pallas_call(
        output_kernel,
        out_shape=jax.ShapeDtypeStruct((seq, width), BF16),
        compiler_params=params(),
        cost_estimate=cost(2 * slots * seq * width, 6 * seq * width + 2 * slots * width),
        name="layer_output",
    )(middle, target_col, *backs)


def flip(value, axis, bit):
    size = lax.axis_size(axis)
    return lax.ppermute(value, axis, [(i, i ^ bit) for i in range(size)])


def butterfly_sum(value, axes):
    for axis in axes:
        bit = 1
        while bit < lax.axis_size(axis):
            value = value + flip(value, axis, bit)
            bit *= 2
    return value


def after(value, *others):
    return lax.optimization_barrier((value, *others))[0]


def gather_rows(piece):
    pieces = {0: piece}
    bit = 2
    while bit < lax.axis_size("dp"):
        pieces.update({m | bit: flip(p, "dp", bit) for m, p in pieces.items()})
        bit *= 2
    return pieces


def gather_cores(pieces):
    pieces = {**pieces, **{m | 1: flip(p, "dp", 1) for m, p in pieces.items()}}
    return [pieces[m] for m in sorted(pieces)]


def reduce_y(total, dp_index):
    bit = lax.axis_size("dp") // 2
    while bit > 1:
        halves = total.reshape(2, total.shape[0] // 2, *total.shape[1:])
        mine = jnp.where((dp_index & bit) != 0, 1, 0)
        sent = lax.dynamic_index_in_dim(halves, 1 - mine, 0, keepdims=False).astype(BF16)
        kept = lax.dynamic_index_in_dim(halves, mine, 0, keepdims=False)
        total = kept + flip(sent, "dp", bit).astype(F32)
        bit //= 2
    return total[0]


def reduce_expert(total):
    peers = lax.axis_size("expert")
    rows, cols = total.shape
    parts = total.astype(BF16).reshape(peers, rows // peers, cols)
    arrived = lax.all_to_all(parts, "expert", split_axis=0, concat_axis=0, tiled=True)
    summed = jnp.sum(arrived.astype(F32), axis=0, keepdims=True).astype(BF16)
    return lax.all_gather(summed[0], "expert", axis=0, tiled=True).astype(F32)


def body(
    tokens, segments, routes, slots, bucket_table, gain_attn, w_query, w_key, w_value, w_output,
    rel_bias, gain_ffn, w_router, w_in, w_out, cotangent,
):
    seq, width = tokens.shape
    buckets, heads = rel_bias.shape
    experts = w_router.shape[1]
    n_dp = lax.axis_size("dp")
    peers = lax.axis_size("expert")
    local = w_in.shape[0]
    capacity = max(2, (5 * seq + 4 * experts - 1) // (4 * experts))
    rows = peers * capacity
    dp_index = lax.axis_index("dp")
    expert_index = lax.axis_index("expert")
    number = jnp.reshape(dp_index, (1,)).astype(jnp.int32)
    groups = 2
    heads_in = heads // groups
    cols = width // groups

    own = [
        jnp.concatenate(
            [w[:, g * cols : (g + 1) * cols] for w in (w_query, w_key, w_value)], axis=1
        )
        for g in range(groups)
    ]
    pieces, last = [], own[0]
    for g in range(groups):
        along_y = gather_rows(own[g] if g == 0 else after(own[g], last))
        last = along_y[max(along_y)]
        if g == 0:
            w_output = after(w_output, last)
        pieces.append(gather_cores(along_y))
    router_pad = jnp.pad(w_router, ((0, 0), (0, -experts % TILE)))
    w_or = lax.all_gather(
        jnp.concatenate([w_output, router_pad], axis=1), "dp", axis=0, tiled=True
    )

    order = (routes % local) * rows + (routes // local) * capacity + slots
    target = jnp.where(slots >= 0, order, -1)
    target_row = target[None, :]
    target_col = target[:, None]
    by_peer = jnp.where(slots >= 0, routes * capacity + slots, -1)
    gain_one = gain_attn[None, :]
    gain_two = gain_ffn[None, :]

    def exchange(values):
        return lax.all_to_all(values, "expert", split_axis=0, concat_axis=0, tiled=True)

    def exchange_rows(values):
        return exchange(values.reshape(peers, capacity, width)).reshape(rows, width)

    reversed_table = jnp.concatenate([bucket_table[::-1], jnp.full((1,), -1, jnp.int32)])
    bucket_ids = jnp.arange(buckets, dtype=jnp.int32)
    hot_rev = (bucket_ids[:, None] == reversed_table[None, :]).astype(F32)
    rel_rev = jnp.dot(rel_bias.T, hot_rev, precision=HIGH)
    shifted = jnp.roll(reversed_table, 1 - TILE)
    hot_shifted = (shifted[:, None] == bucket_ids[None, :]).astype(F32)
    bias, normed, normt = prepare(rel_rev, tokens, gain_one)
    marks = jnp.arange(TILE, dtype=jnp.int32)[None, :]
    same = segments[0][:, None] == marks
    kseg = same.astype(BF16)
    qseg = jnp.where(same, 0.0, -1e9).astype(BF16)

    saved, ctxts, weights = [], [], []
    for g in range(groups):
        *kept, ctxt, weight = attend(
            number, normed, bias, kseg, qseg, pieces[g], g, heads_in
        )
        saved.append(kept)
        ctxts.append(ctxt)
        weights.append(weight)

    c_placed = place(by_peer[None, :], after(cotangent, ctxts[0]), local * rows)
    c_split = exchange(c_placed.reshape(peers, local * capacity, width)).reshape(
        peers, local, capacity, width
    )
    c_here = [c_split[:, l].reshape(rows, width) for l in range(local)]
    c_all = [lax.all_gather(part, "dp", axis=0, tiled=False) for part in c_here]

    middle, *placed = middle_step(tokens, w_or, gain_two, target_row, ctxts, local, rows)

    arrived = [exchange_rows(part) for part in placed]
    c_late, _ = lax.optimization_barrier((c_here, placed[0]))
    ch = hidden_cot(c_late, w_out, 1024)
    arrived[0], ch = lax.optimization_barrier((arrived[0], ch))
    x_all, backs, scaled, router_terms, numbers = [], [], [], [], []
    for l in range(local):
        numbers.append(jnp.stack([dp_index, expert_index * local + l]).astype(jnp.int32))
        if l:
            arrived[l] = after(arrived[l], scaled[-1])
        x_all.append(lax.all_gather(arrived[l], "dp", axis=0, tiled=False))
        out, grad_x, router_term = expert_step(
            numbers[l], arrived[l], c_here[l], ch, w_or, w_in, w_out, l, 512, experts
        )
        backs.append(exchange_rows(grad_x))
        scaled.append(out)
        router_terms.append(router_term)

    expert_terms = expert_grads(
        numbers[0], x_all[0], c_all[0], w_or, w_in, w_out, 0, n_dp, experts
    )
    backs[-1], expert_terms = lax.optimization_barrier((backs[-1], expert_terms))
    scaled, _ = lax.optimization_barrier((scaled, backs[-1]))
    stacked = jnp.stack([part.reshape(peers, capacity, width) for part in scaled], axis=1)
    returned = exchange(stacked.reshape(peers, local * capacity, width)).reshape(-1, width)

    grad_middle, grad_ctx, gw_o, ggain_two = middle_back(
        cotangent, middle, gain_two, target_col, w_or, ctxts, backs
    )
    part_o = lax.psum_scatter(gw_o, "dp", scatter_dimension=0, tiled=True)
    shard_o = lax.psum(part_o, "expert").astype(F32)
    keeps, sends, grads, diags = [], [], [], []
    for g in range(groups):
        keep, send, grad, diag = attend_back(number, normt, *saved[g], grad_ctx, g, n_dp)
        keeps.append(keep)
        sends.append(send)
        grads.append(grad)
        diags.append(diag)
    crossed = []
    for g in range(groups):
        crossed.append(flip(sends[g], "dp", 1))
        if g + 1 < groups:
            crossed[g], sends[g + 1] = lax.optimization_barrier((crossed[g], sends[g + 1]))
    parts = [
        reduce_y(keeps[g].astype(F32) + crossed[g].astype(F32), dp_index) for g in range(groups)
    ]
    shards = [reduce_expert(part) for part in parts]
    grad_middle = after(grad_middle, returned, part_o)
    grad_tokens, ggain_one = first_back(tokens, gain_one, grad_middle, grads, weights)
    output = output_step(middle, by_peer[:, None], [returned])
    x_all[1:] = after(x_all[1:], crossed[-1], parts[0])
    for l in range(1, local):
        expert_terms = expert_grads(
            numbers[l], x_all[l], c_all[l], w_or, w_in, w_out, l, n_dp, experts, expert_terms
        )

    diag = jnp.concatenate(diags, axis=0).reshape(heads, 2 * seq)
    grad_rel = jnp.dot(diag, hot_shifted, precision=HIGH)
    rel_row = jnp.pad(grad_rel.reshape(1, heads * buckets), ((0, 0), (0, width - heads * buckets)))
    small = butterfly_sum(
        jnp.concatenate([sum(router_terms), ggain_two, ggain_one, rel_row], axis=0),
        ("dp", "expert"),
    )
    shard_rows = width // n_dp
    grad_router = lax.dynamic_slice_in_dim(small[:experts], dp_index * shard_rows, shard_rows, 1).T
    total_rel = small[experts + 2, : heads * buckets].reshape(heads, buckets).T
    shard_q, shard_k, shard_v = [
        jnp.concatenate([s[:, i * cols : (i + 1) * cols] for s in shards], axis=1)
        for i in range(3)
    ]
    return (
        output,
        grad_tokens,
        small[experts + 1],
        shard_q,
        shard_k,
        shard_v,
        shard_o,
        total_rel,
        small[experts],
        grad_router,
        expert_terms[0],
        expert_terms[1],
    )


def solution(mesh):
    in_specs = (
        P(("dp", "expert"), None),
        P(("dp", "expert"), None),
        P(("dp", "expert")),
        P(("dp", "expert")),
        P(),
        P(),
        P("dp", None),
        P("dp", None),
        P("dp", None),
        P("dp", None),
        P(),
        P(),
        P("dp", None),
        P("expert", None, None),
        P("expert", None, None),
        P(("dp", "expert"), None),
    )
    out_specs = (
        P(("dp", "expert"), None),
        P(("dp", "expert"), None),
        P(),
        P("dp", None),
        P("dp", None),
        P("dp", None),
        P("dp", None),
        P(),
        P(),
        P("dp", None),
        P("expert", None, "dp"),
        P("expert", "dp", None),
    )
    return jax.shard_map(body, mesh=mesh, in_specs=in_specs, out_specs=out_specs, check_vma=False)
```

```python
import functools
import math

import jax
import jax.numpy as jnp
from jax import lax
from jax.experimental import pallas as pl
from jax.experimental.pallas import tpu as pltpu
from jax.sharding import PartitionSpec as P

EPS = 1e-06
HIGH = lax.Precision.HIGHEST
F32 = jnp.float32
BF16 = jnp.bfloat16
VMEM_LIMIT = 56 * 1024 * 1024
TILE = 128
STRIP = 256
SUB = 256
GELU_A = math.sqrt(2.0 / math.pi)
GELU_B = 0.044715


def dot(a, b):
    return jnp.dot(a, b, preferred_element_type=F32)


def dot_nt(a, b):
    return lax.dot_general(a, b, (((1,), (1,)), ((), ())), preferred_element_type=F32)


def params(**kw):
    return pltpu.CompilerParams(vmem_limit_bytes=VMEM_LIMIT, **kw)


def cost(flops, nbytes, trans=0):
    return pl.CostEstimate(flops=int(flops), bytes_accessed=int(nbytes), transcendentals=int(trans))


def rms_scale(stream):
    return lax.rsqrt(jnp.mean(stream * stream, axis=-1, keepdims=True) + EPS)


def norm_back(stream, gain, grad_out):
    scale = rms_scale(stream)
    grad_gain = jnp.sum(grad_out * (stream * scale), axis=0, keepdims=True)
    scaled = grad_out * gain
    inner = jnp.mean(scaled * stream, axis=-1, keepdims=True)
    grad_in = scale * scaled - stream * (scale * scale * scale * inner)
    return grad_in, grad_gain


def gelu_pair(v):
    sq = v * v
    inner = GELU_A * (v + GELU_B * (sq * v))
    th = jnp.tanh(inner)
    half = 0.5 * (1.0 + th)
    slope = half + (0.5 * v) * (1.0 - th * th) * (GELU_A + (3.0 * GELU_A * GELU_B) * sq)
    return v * half, slope


def slot_hot(target_row, start, rows):
    seq = target_row.shape[1]
    ids = lax.broadcasted_iota(jnp.int32, (rows, seq), 0) + start
    return (ids == target_row).astype(F32).astype(BF16)


def token_hot(target_col, start, rows):
    seq = target_col.shape[0]
    ids = lax.broadcasted_iota(jnp.int32, (seq, rows), 1) + start
    return (ids == target_col).astype(F32).astype(BF16)


def place_kernel(target_ref, rows_ref, out_ref):
    out_ref[...] = dot(slot_hot(target_ref[...], 0, out_ref.shape[0]), rows_ref[...]).astype(BF16)


def place(target_row, values, rows):
    seq, width = values.shape
    return pl.pallas_call(
        place_kernel,
        out_shape=jax.ShapeDtypeStruct((rows, width), BF16),
        compiler_params=params(),
        cost_estimate=cost(2 * rows * seq * width, 2 * (rows + seq) * width),
        name="place_cotangent",
    )(target_row, values)


def prepare_kernel(rel_ref, tok_ref, gain_ref, out_ref, normed_ref, normt_ref):
    heads, width = rel_ref.shape
    wide = out_ref.shape[2]
    for h in range(heads):
        base = jnp.broadcast_to(rel_ref[h : h + 1, :], (TILE, width))
        turned = pltpu.roll(base, width - (TILE - 1), 1, stride=1, stride_axis=0)
        out_ref[h] = turned[:, :wide]
    stream = tok_ref[...].astype(F32)
    normed = stream * rms_scale(stream) * gain_ref[...]
    normed_ref[...] = normed.astype(BF16)
    normt_ref[...] = normed.T.astype(BF16)


def prepare(rel_rev, tokens, gain):
    heads, span = rel_rev.shape
    seq, width = tokens.shape
    wide = 2 * seq - TILE
    return pl.pallas_call(
        prepare_kernel,
        out_shape=[
            jax.ShapeDtypeStruct((heads, TILE, wide), F32),
            jax.ShapeDtypeStruct((seq, width), BF16),
            jax.ShapeDtypeStruct((width, seq), BF16),
        ],
        compiler_params=params(),
        cost_estimate=cost(heads * TILE * span, 4 * heads * TILE * wide + 6 * seq * width),
        name="bias_and_first_norm",
    )(rel_rev, tokens, gain)


def join_rows(num_ref, pieces, w_ref):
    part = pieces[0].shape[0]
    for mask, piece in enumerate(pieces):
        row = pl.multiple_of((num_ref[0] ^ mask) * part, 16)
        w_ref[pl.ds(row, part), :] = piece[...]


def attend_kernel(num_ref, normed_ref, bias_ref, kseg_ref, qseg_ref, *refs):
    pieces, refs = refs[:-8], refs[-8:]
    q_ref, k_ref, v_ref, kt_ref, e_ref, rinv_ref, ctxt_ref, w_ref = refs
    seq, width = normed_ref.shape
    heads = e_ref.shape[0]
    cols = q_ref.shape[1]
    hd = cols // heads
    per_tile = TILE // hd
    step = pl.program_id(0)

    @pl.when(step == 0)
    def _():
        join_rows(num_ref, pieces, w_ref)

    normed = normed_ref[...]
    at = lambda base: pl.ds(pl.multiple_of(base * width + step * cols, TILE), cols)
    q = dot(normed, w_ref[:, at(0)]).astype(BF16).astype(F32) * (1.0 / math.sqrt(hd))
    k32 = dot(normed, w_ref[:, at(1)])
    v32 = dot(normed, w_ref[:, at(2)])
    q_ref[...] = q.astype(BF16)
    k_ref[...] = k32.astype(BF16)
    v_ref[...] = v32.astype(BF16)
    kt_ref[...] = k32.T.astype(BF16)
    vt = v32.T.astype(BF16)
    lane = lax.broadcasted_iota(jnp.int32, (seq, TILE), 1) // hd
    kseg = kseg_ref[...]
    qseg = qseg_ref[...]
    for h in range(heads):
        tile = h // per_tile
        k_pair = k_ref[:, tile * TILE : (tile + 1) * TILE]
        q_pair = q_ref[:, tile * TILE : (tile + 1) * TILE]
        q_own = jnp.where(lane == h % per_tile, q_pair, jnp.zeros_like(q_pair))
        k_all = jnp.concatenate([k_pair, kseg], axis=1)
        q_all = jnp.concatenate([q_own, qseg], axis=1)
        for start in range(0, seq, STRIP):
            scores = dot_nt(k_all, q_all[start : start + STRIP])
            parts = []
            for b in range(0, seq, TILE):
                off = seq - TILE - b + start
                parts.append(scores[b : b + TILE] + bias_ref[h, :, off : off + STRIP])
            scores = jnp.concatenate(parts, axis=0)
            e = jnp.exp(scores - jnp.max(scores, axis=0, keepdims=True))
            rinv = 1.0 / jnp.sum(e, axis=0, keepdims=True)
            eb = e.astype(BF16)
            e_ref[h, :, start : start + STRIP] = eb
            rinv_ref[h, :, start : start + STRIP] = rinv
            ctxt = dot(vt[h * hd : (h + 1) * hd], eb) * rinv
            ctxt_ref[h * hd : (h + 1) * hd, start : start + STRIP] = ctxt.astype(BF16)


def attend(number, normed, bias, kseg, qseg, pieces, heads, group):
    seq, width = normed.shape
    cols = width // heads * group
    steps = heads // group
    wide = bias.shape[2]
    whole = lambda a: pl.BlockSpec(a.shape, lambda g: (0,) * a.ndim)
    nat = pl.BlockSpec((seq, cols), lambda g: (0, g))
    tr = pl.BlockSpec((cols, seq), lambda g: (g, 0))
    sds = jax.ShapeDtypeStruct
    return pl.pallas_call(
        attend_kernel,
        grid=(steps,),
        in_specs=[
            pl.BlockSpec(memory_space=pltpu.SMEM), whole(normed),
            pl.BlockSpec((group, TILE, wide), lambda g: (g, 0, 0)), whole(kseg), whole(qseg),
        ]
        + [whole(p) for p in pieces],
        out_specs=[
            nat, nat, nat, tr,
            pl.BlockSpec((group, seq, seq), lambda g: (g, 0, 0)),
            pl.BlockSpec((group, 1, seq), lambda g: (g, 0, 0)),
            tr,
        ],
        out_shape=[
            sds((seq, width), BF16), sds((seq, width), BF16), sds((seq, width), BF16),
            sds((width, seq), BF16), sds((heads, seq, seq), BF16), sds((heads, 1, seq), F32),
            sds((width, seq), BF16),
        ],
        scratch_shapes=[pltpu.VMEM((width, 3 * width), BF16)],
        compiler_params=params(dimension_semantics=("arbitrary",)),
        cost_estimate=cost(
            6 * seq * width * width + 4 * seq * seq * width,
            2 * (3 * width * width + 9 * seq * width + heads * seq * seq) + 4 * bias.size,
            heads * seq * seq,
        ),
        name="attention_forward",
    )(number, normed, bias, kseg, qseg, *pieces)


def middle_kernel(tok_ref, wo_ref, gain_ref, target_ref, ctx_ref, middle_ref, *placed_refs):
    width = tok_ref.shape[1]
    context = ctx_ref[...].astype(F32).T.astype(BF16)
    middle = tok_ref[...].astype(F32) + dot(context, wo_ref[:, :width])
    middle_ref[...] = middle
    normed = (middle * rms_scale(middle) * gain_ref[...]).astype(BF16)
    for l, placed_ref in enumerate(placed_refs):
        rows = placed_ref.shape[0]
        placed_ref[...] = dot(slot_hot(target_ref[...], l * rows, rows), normed).astype(BF16)


def middle_step(tokens, w_out, gain, target_row, ctxt, local, rows):
    seq, width = tokens.shape
    return pl.pallas_call(
        middle_kernel,
        out_shape=[jax.ShapeDtypeStruct((seq, width), F32)]
        + [jax.ShapeDtypeStruct((rows, width), BF16)] * local,
        compiler_params=params(),
        cost_estimate=cost(
            2 * seq * width * width + 2 * local * rows * seq * width,
            2 * width * width + 8 * seq * width + 2 * local * rows * width,
        ),
        name="output_projection_dispatch",
    )(tokens, w_out, gain, target_row, ctxt)


def gate_of(logits, expert):
    top = jnp.max(logits, axis=-1, keepdims=True)
    ex = jnp.exp(logits - top)
    prob = ex / jnp.sum(ex, axis=-1, keepdims=True)
    hot = lax.broadcasted_iota(jnp.int32, logits.shape, 1) == expert
    gate = jnp.sum(jnp.where(hot, prob, 0.0), axis=-1, keepdims=True)
    return prob, hot, gate


def expert_kernel(
    num_ref, x_ref, c_ref, wr_ref, win_ref, wout_ref,
    scaled_ref, grad_ref, router_ref, gp_ref, acc_p, acc_g,
):
    step = pl.program_id(0)
    experts = router_ref.shape[0]

    @pl.when(step == 0)
    def _():
        _, _, gate = gate_of(dot(x_ref[...], wr_ref[...])[:, :experts], num_ref[1])
        gp_ref[...] = (gate * c_ref[...].astype(F32)).astype(BF16)
        acc_p[...] = jnp.zeros_like(acc_p)
        acc_g[...] = jnp.zeros_like(acc_g)

    hiddens, grads = [], []
    for sub in range(0, win_ref.shape[2], SUB):
        pre = dot(x_ref[...], win_ref[0, :, sub : sub + SUB])
        grad_hidden = dot_nt(gp_ref[...], wout_ref[0, sub : sub + SUB, :])
        hidden, slope = gelu_pair(pre)
        hiddens.append(hidden.astype(BF16))
        grads.append((grad_hidden * slope).astype(BF16))
    acc_p[...] += dot(jnp.concatenate(hiddens, axis=1), wout_ref[0])
    acc_g[...] += dot_nt(jnp.concatenate(grads, axis=1), win_ref[0])

    @pl.when(step == pl.num_programs(0) - 1)
    def _():
        x = x_ref[...]
        prob, hot, gate = gate_of(dot(x, wr_ref[...])[:, :experts], num_ref[1])
        produced = acc_p[...]
        scaled_ref[...] = (gate * produced).astype(BF16)
        grad_gate = jnp.sum(
            c_ref[...].astype(F32) * produced.astype(BF16).astype(F32), axis=-1, keepdims=True
        )
        grad_logits = prob * (jnp.where(hot, grad_gate, 0.0) - gate * grad_gate)
        logits_b = grad_logits.astype(BF16)
        grad_ref[...] = (acc_g[...] + dot_nt(logits_b, wr_ref[:, :experts])).astype(BF16)
        router_ref[...] = dot(grad_logits.T.astype(BF16), x)


def expert_step(number, x, c, w_or, w_in, w_out, local, block, experts):
    rows, width = x.shape
    ff = w_in.shape[2]
    router_cols = w_or.shape[1] - width
    whole = lambda a: pl.BlockSpec(a.shape, lambda f: (0,) * a.ndim)
    row_spec = pl.BlockSpec((rows, width), lambda f: (0, 0))
    return pl.pallas_call(
        expert_kernel,
        grid=(ff // block,),
        in_specs=[
            pl.BlockSpec(memory_space=pltpu.SMEM),
            whole(x),
            whole(c),
            pl.BlockSpec((width, router_cols), lambda f: (0, width // router_cols)),
            pl.BlockSpec((1, width, block), lambda f: (local, 0, f)),
            pl.BlockSpec((1, block, width), lambda f: (local, f, 0)),
        ],
        out_specs=[row_spec, row_spec, pl.BlockSpec((experts, width), lambda f: (0, 0))],
        out_shape=[
            jax.ShapeDtypeStruct((rows, width), BF16),
            jax.ShapeDtypeStruct((rows, width), BF16),
            jax.ShapeDtypeStruct((experts, width), F32),
        ],
        scratch_shapes=[
            pltpu.VMEM((rows, width), BF16),
            pltpu.VMEM((rows, width), F32),
            pltpu.VMEM((rows, width), F32),
        ],
        compiler_params=params(dimension_semantics=("arbitrary",)),
        cost_estimate=cost(
            8 * rows * width * ff, 4 * width * ff + 8 * rows * width, rows * ff
        ),
        name="expert_rows",
    )(number, x, c, w_or, w_in, w_out)


def expert_grad_kernel(experts, num_ref, x_ref, c_ref, wr_ref, win_ref, wout_ref, *refs):
    gin_ref, gout_ref, gp_ref, xt_ref = refs[-4:]
    parts, rows, width = x_ref.shape
    x = x_ref[...].reshape(parts * rows, width)

    @pl.when(pl.program_id(0) == 0)
    def _():
        _, _, gate = gate_of(dot(x, wr_ref[...])[:, :experts], num_ref[1])
        c = c_ref[...].reshape(parts * rows, width)
        gp_ref[...] = (gate * c.astype(F32)).astype(BF16)
        xt_ref[...] = x.astype(F32).T.astype(BF16)

    gp = gp_ref[...]
    pre_t = dot_nt(win_ref[0].astype(F32).T.astype(BF16), x)
    hidden_t, slope_t = gelu_pair(pre_t)
    grad_hidden_t = dot_nt(wout_ref[0], gp)
    gout_ref[0] = dot(hidden_t.astype(BF16), gp)
    gin_ref[0] = dot_nt(xt_ref[...], (grad_hidden_t * slope_t).astype(BF16))


def expert_grads(numbers, x_all, c_all, w_or, w_in, w_out, local, n_dp, experts, prior=()):
    parts, rows, width = x_all.shape
    ff = w_in.shape[2]
    router_cols = w_or.shape[1] - width
    part = ff // n_dp
    block = 256 if part % 256 == 0 else 128
    steps = part // block
    whole = lambda a: pl.BlockSpec(a.shape, lambda f, n: (0,) * a.ndim)
    return pl.pallas_call(
        functools.partial(expert_grad_kernel, experts),
        grid_spec=pltpu.PrefetchScalarGridSpec(
            num_scalar_prefetch=1,
            grid=(steps,),
            in_specs=[
                whole(x_all),
                whole(c_all),
                pl.BlockSpec((width, router_cols), lambda f, n: (0, width // router_cols)),
                pl.BlockSpec((1, width, block), lambda f, n: (local, 0, n[0] * steps + f)),
                pl.BlockSpec((1, block, width), lambda f, n: (local, n[0] * steps + f, 0)),
            ]
            + [pl.BlockSpec(memory_space=pl.ANY)] * len(prior),
            out_specs=[
                pl.BlockSpec((1, width, block), lambda f, n: (local, 0, f)),
                pl.BlockSpec((1, block, width), lambda f, n: (local, f, 0)),
            ],
            scratch_shapes=[
                pltpu.VMEM((parts * rows, width), BF16),
                pltpu.VMEM((width, parts * rows), BF16),
            ],
        ),
        out_shape=[
            jax.ShapeDtypeStruct((w_in.shape[0], width, part), F32),
            jax.ShapeDtypeStruct((w_in.shape[0], part, width), F32),
        ],
        compiler_params=params(dimension_semantics=("arbitrary",)),
        cost_estimate=cost(
            8 * parts * rows * width * part,
            4 * parts * rows * width + 12 * width * part,
            parts * rows * part,
        ),
        input_output_aliases={6 + i: i for i in range(len(prior))},
        name="expert_weight_grads",
    )(numbers, x_all, c_all, w_or, w_in, w_out, *prior)


def split_rows(num_ref, full_ref, keep_ref, send_ref):
    part = keep_ref.shape[1]
    core = num_ref[0] & 1
    for y in range(keep_ref.shape[0]):
        own = pl.multiple_of((2 * y + core) * part, 16)
        other = pl.multiple_of((2 * y + 1 - core) * part, 16)
        keep_ref[y] = full_ref[pl.ds(own, part), :]
        send_ref[y] = full_ref[pl.ds(other, part), :]


def middle_back_kernel(num_ref, cot_ref, middle_ref, gain_ref, target_ref, wo_ref, ctx_ref, *refs):
    back_refs, (gmid_ref, gctx_ref, keep_ref, send_ref, ggain_ref, gwo_ref) = refs[:-6], refs[-6:]
    seq, width = cot_ref.shape
    target = target_ref[...]
    grad = jnp.zeros((seq, width), F32)
    for l, back in enumerate(back_refs):
        rows = back.shape[0]
        grad = grad + dot(token_hot(target, l * rows, rows), back[...])
    grad_in, grad_gain = norm_back(middle_ref[...], gain_ref[...], grad)
    ggain_ref[...] = grad_gain
    grad_middle = cot_ref[...].astype(F32) + grad_in
    gmid_ref[...] = grad_middle
    grad_attn = grad_middle.astype(BF16)
    gctx_ref[...] = dot_nt(grad_attn, wo_ref[:, :width]).astype(BF16)
    gwo_ref[...] = dot(ctx_ref[...], grad_attn).astype(BF16)
    split_rows(num_ref, gwo_ref, keep_ref, send_ref)


def middle_back(number, cot, middle, gain, target_col, w_out, ctxt, backs, n_dp):
    seq, width = cot.shape
    sds = jax.ShapeDtypeStruct
    slots = sum(b.shape[0] for b in backs)
    half = sds((n_dp // 2, width // n_dp, width), BF16)
    vmem = pl.BlockSpec(memory_space=pltpu.VMEM)
    return pl.pallas_call(
        middle_back_kernel,
        in_specs=[pl.BlockSpec(memory_space=pltpu.SMEM)] + [vmem] * (6 + len(backs)),
        out_shape=[sds((seq, width), F32), sds((seq, width), BF16), half, half, sds((1, width), F32)],
        scratch_shapes=[pltpu.VMEM((width, width), BF16)],
        compiler_params=params(),
        cost_estimate=cost(
            4 * seq * width * width + 2 * slots * seq * width,
            4 * width * width + 14 * seq * width + 2 * slots * width,
        ),
        name="second_norm_backward",
    )(number, cot, middle, gain, target_col, w_out, ctxt, *backs)


def attend_back_kernel(
    num_ref, normt_ref, q_ref, k_ref, v_ref, kt_ref, e_ref, rinv_ref, do_ref,
    keep_ref, send_ref, grads_ref, diag_ref, acc_ref, gw_ref,
):
    seq, cols = q_ref.shape
    heads = e_ref.shape[0]
    hd = cols // heads
    per_tile = TILE // hd
    lane = lax.broadcasted_iota(jnp.int32, (seq, TILE), 1) // hd
    row_bit = lax.broadcasted_iota(jnp.int32, (8, 2 * seq), 0)
    zero = jnp.zeros((seq, TILE), BF16)
    dk_tiles, dv_tiles, dqt_rows = [], [], []
    for h in range(heads):
        tile = h // per_tile
        sl = slice(tile * TILE, (tile + 1) * TILE)
        q_own = jnp.where(lane == h % per_tile, q_ref[:, sl], zero)
        do_own = jnp.where(lane == h % per_tile, do_ref[:, sl], zero)
        v_pair = v_ref[:, sl]
        acc_ref[...] = jnp.zeros_like(acc_ref)
        dk = jnp.zeros((seq, TILE), F32)
        dv = jnp.zeros((seq, TILE), F32)
        dqt_parts = []
        for start in range(0, seq, STRIP):
            st = slice(start, start + STRIP)
            p = e_ref[h, :, st].astype(F32) * rinv_ref[h, :, st]
            t = dot_nt(v_pair, do_own[st]) * p
            ds = t - p * jnp.sum(t, axis=0, keepdims=True)
            dsb = ds.astype(BF16)
            dv = dv + dot(p.astype(BF16), do_own[st])
            dk = dk + dot(dsb, q_own[st])
            dqt_parts.append(dot(kt_ref[h * hd : (h + 1) * hd, :], dsb))
            for b in range(0, seq, TILE):
                off = seq - TILE - b + start
                acc_ref[:, off : off + STRIP] += ds[b : b + TILE]
        if h % per_tile == 0:
            dk_tiles.append(dk)
            dv_tiles.append(dv)
        else:
            dk_tiles[-1] = dk_tiles[-1] + dk
            dv_tiles[-1] = dv_tiles[-1] + dv
        dqt_rows.append(jnp.concatenate(dqt_parts, axis=1))
        folded = acc_ref[...]
        half = TILE // 2
        while half >= 8:
            folded = folded[:half] + pltpu.roll(folded[half:], 2 * seq - half, 1)
            half //= 2
        for bit in (4, 2, 1):
            turned = pltpu.roll(folded, 2 * seq - bit, 1)
            folded = jnp.where((row_bit & bit) != 0, turned, folded)
        diag_ref[h] = jnp.sum(folded, axis=0, keepdims=True)
    dqt = jnp.concatenate(dqt_rows, axis=0) * (1.0 / math.sqrt(hd))
    grads_ref[:, :cols] = dqt.T.astype(BF16)
    for base, tiles in ((1, dk_tiles), (2, dv_tiles)):
        grads_ref[:, base * cols : (base + 1) * cols] = jnp.concatenate(tiles, axis=1).astype(BF16)
    gw_ref[...] = dot(normt_ref[...], grads_ref[...]).astype(BF16)
    split_rows(num_ref, gw_ref, keep_ref, send_ref)


def attend_back(number, normt, q, k, v, kt, e, rinv, grad_ctx, group, n_dp):
    seq, width = q.shape
    heads = e.shape[0]
    cols = width // heads * group
    steps = heads // group
    whole = lambda a: pl.BlockSpec(a.shape, lambda g: (0,) * a.ndim)
    nat = pl.BlockSpec((seq, cols), lambda g: (0, g))
    sds = jax.ShapeDtypeStruct
    half = (n_dp // 2, width // n_dp, 3 * width)
    half_spec = pl.BlockSpec((n_dp // 2, width // n_dp, 3 * cols), lambda g: (0, 0, g))
    return pl.pallas_call(
        attend_back_kernel,
        grid=(steps,),
        in_specs=[
            pl.BlockSpec(memory_space=pltpu.SMEM), whole(normt), nat, nat, nat,
            pl.BlockSpec((cols, seq), lambda g: (g, 0)),
            pl.BlockSpec((group, seq, seq), lambda g: (g, 0, 0)),
            pl.BlockSpec((group, 1, seq), lambda g: (g, 0, 0)),
            nat,
        ],
        out_specs=[
            half_spec, half_spec, pl.BlockSpec((seq, 3 * cols), lambda g: (0, g)),
            pl.BlockSpec((group, 1, 2 * seq), lambda g: (g, 0, 0)),
        ],
        out_shape=[
            sds(half, BF16), sds(half, BF16), sds((seq, 3 * width), BF16),
            sds((heads, 1, 2 * seq), F32),
        ],
        scratch_shapes=[pltpu.VMEM((TILE, 2 * seq), F32), pltpu.VMEM((width, 3 * cols), BF16)],
        compiler_params=params(dimension_semantics=("arbitrary",)),
        cost_estimate=cost(
            6 * seq * width * width + 8 * seq * seq * width,
            2 * (6 * width * width + 8 * seq * width + heads * seq * seq),
        ),
        name="attention_backward",
    )(number, normt, q, k, v, kt, e, rinv, grad_ctx)


def first_back_kernel(cols, num_ref, tok_ref, gain_ref, gmid_ref, grads_ref, *refs):
    pieces, (gtok_ref, ggain_ref, w_ref) = refs[:-3], refs[-3:]
    width = tok_ref.shape[1]
    join_rows(num_ref, pieces, w_ref)
    grad = jnp.zeros(tok_ref.shape, F32)
    for i, start in enumerate(range(0, 3 * width, cols)):
        col = i % 3 * width + i // 3 * cols
        grad = grad + dot_nt(grads_ref[:, start : start + cols], w_ref[:, col : col + cols])
    grad_in, grad_gain = norm_back(tok_ref[...].astype(F32), gain_ref[...], grad)
    gtok_ref[...] = gmid_ref[...] + grad_in
    ggain_ref[...] = grad_gain


def first_back(number, tokens, gain, grad_middle, grads, pieces, cols):
    seq, width = tokens.shape
    vmem = pl.BlockSpec(memory_space=pltpu.VMEM)
    return pl.pallas_call(
        functools.partial(first_back_kernel, cols),
        in_specs=[pl.BlockSpec(memory_space=pltpu.SMEM)] + [vmem] * (4 + len(pieces)),
        out_shape=[
            jax.ShapeDtypeStruct((seq, width), F32), jax.ShapeDtypeStruct((1, width), F32)
        ],
        scratch_shapes=[pltpu.VMEM((width, 3 * width), BF16)],
        compiler_params=params(),
        cost_estimate=cost(6 * seq * width * width, 6 * width * width + 16 * seq * width),
        name="first_norm_backward",
    )(number, tokens, gain, grad_middle, grads, *pieces)


def output_kernel(middle_ref, target_ref, *refs):
    out_ref = refs[-1]
    total = middle_ref[...]
    for l, back in enumerate(refs[:-1]):
        rows = back.shape[0]
        total = total + dot(token_hot(target_ref[...], l * rows, rows), back[...])
    out_ref[...] = total.astype(BF16)


def output_step(middle, target_col, backs):
    seq, width = middle.shape
    slots = sum(b.shape[0] for b in backs)
    return pl.pallas_call(
        output_kernel,
        out_shape=jax.ShapeDtypeStruct((seq, width), BF16),
        compiler_params=params(),
        cost_estimate=cost(2 * slots * seq * width, 6 * seq * width + 2 * slots * width),
        name="layer_output",
    )(middle, target_col, *backs)


def flip(value, axis, bit):
    size = lax.axis_size(axis)
    return lax.ppermute(value, axis, [(i, i ^ bit) for i in range(size)])


def butterfly_sum(value, axes):
    for axis in axes:
        bit = 1
        while bit < lax.axis_size(axis):
            value = value + flip(value, axis, bit)
            bit *= 2
    return value


def after(value, *others):
    return lax.optimization_barrier((value, *others))[0]


def gather_rows(piece):
    pieces = {0: piece}
    bit = 2
    while bit < lax.axis_size("dp"):
        pieces.update({m | bit: flip(p, "dp", bit) for m, p in pieces.items()})
        bit *= 2
    return pieces


def gather_cores(pieces):
    pieces = {**pieces, **{m | 1: flip(p, "dp", 1) for m, p in pieces.items()}}
    return [pieces[m] for m in sorted(pieces)]


def reduce_y(total, dp_index):
    bit = lax.axis_size("dp") // 2
    while bit > 1:
        halves = total.reshape(2, total.shape[0] // 2, *total.shape[1:])
        mine = jnp.where((dp_index & bit) != 0, 1, 0)
        sent = lax.dynamic_index_in_dim(halves, 1 - mine, 0, keepdims=False).astype(BF16)
        kept = lax.dynamic_index_in_dim(halves, mine, 0, keepdims=False)
        total = kept + flip(sent, "dp", bit).astype(F32)
        bit //= 2
    return total[0]


def reduce_expert(total):
    peers = lax.axis_size("expert")
    rows, cols = total.shape
    parts = total.astype(BF16).reshape(peers, rows // peers, cols)
    arrived = lax.all_to_all(parts, "expert", split_axis=0, concat_axis=0, tiled=True)
    summed = jnp.sum(arrived.astype(F32), axis=0, keepdims=True).astype(BF16)
    spread = jnp.broadcast_to(summed, parts.shape)
    shared = lax.all_to_all(spread, "expert", split_axis=0, concat_axis=0, tiled=True)
    return shared.reshape(rows, cols).astype(F32)


def body(
    tokens, segments, routes, slots, bucket_table, gain_attn, w_query, w_key, w_value, w_output,
    rel_bias, gain_ffn, w_router, w_in, w_out, cotangent,
):
    seq, width = tokens.shape
    buckets, heads = rel_bias.shape
    experts = w_router.shape[1]
    n_dp = lax.axis_size("dp")
    peers = lax.axis_size("expert")
    local = w_in.shape[0]
    capacity = max(2, (5 * seq + 4 * experts - 1) // (4 * experts))
    rows = peers * capacity
    dp_index = lax.axis_index("dp")
    expert_index = lax.axis_index("expert")
    number = jnp.reshape(dp_index, (1,)).astype(jnp.int32)
    group = 4
    cols = width // heads * group

    along_y = gather_rows(jnp.concatenate([w_query, w_key, w_value], axis=1))
    pieces = gather_cores(along_y)
    w_output = after(w_output, along_y[max(along_y)])
    router_pad = jnp.pad(w_router, ((0, 0), (0, -experts % TILE)))
    w_or = lax.all_gather(
        jnp.concatenate([w_output, router_pad], axis=1), "dp", axis=0, tiled=True
    )

    order = (routes % local) * rows + (routes // local) * capacity + slots
    target = jnp.where(slots >= 0, order, -1)
    target_row = target[None, :]
    target_col = target[:, None]
    by_peer = jnp.where(slots >= 0, routes * capacity + slots, -1)
    gain_one = gain_attn[None, :]
    gain_two = gain_ffn[None, :]

    def exchange(values):
        return lax.all_to_all(values, "expert", split_axis=0, concat_axis=0, tiled=True)

    def exchange_rows(values):
        return exchange(values.reshape(peers, capacity, width)).reshape(rows, width)

    reversed_table = jnp.concatenate([bucket_table[::-1], jnp.full((1,), -1, jnp.int32)])
    bucket_ids = jnp.arange(buckets, dtype=jnp.int32)
    hot_rev = (bucket_ids[:, None] == reversed_table[None, :]).astype(F32)
    rel_rev = jnp.dot(rel_bias.T, hot_rev, precision=HIGH)
    shifted = jnp.roll(reversed_table, 1 - TILE)
    hot_shifted = (shifted[:, None] == bucket_ids[None, :]).astype(F32)
    bias, normed, normt = prepare(rel_rev, tokens, gain_one)
    marks = jnp.arange(TILE, dtype=jnp.int32)[None, :]
    same = segments[0][:, None] == marks
    kseg = same.astype(BF16)
    qseg = jnp.where(same, 0.0, -1e9).astype(BF16)

    c_placed = after(place(by_peer[None, :], cotangent, local * rows), pieces[1])
    c_got = exchange(c_placed.reshape(peers, local * capacity, width))
    normed = after(normed, c_got)
    *saved, ctxt = attend(number, normed, bias, kseg, qseg, pieces, heads, group)

    c_split = c_got.reshape(peers, local, capacity, width)
    c_here = [c_split[:, l].reshape(rows, width) for l in range(local)]
    c_all = [lax.all_gather(part, "dp", axis=0, tiled=False) for part in c_here]

    middle, *placed = middle_step(tokens, w_or, gain_two, target_row, ctxt, local, rows)

    arrived = [exchange_rows(part) for part in placed]
    x_all, backs, scaled, router_terms, numbers = [], [], [], [], []
    for l in range(local):
        numbers.append(jnp.stack([dp_index, expert_index * local + l]).astype(jnp.int32))
        x_all.append(lax.all_gather(arrived[l], "dp", axis=0, tiled=False))
        out, grad_x, router_term = expert_step(
            numbers[l], arrived[l], c_here[l], w_or, w_in, w_out, l, 512, experts
        )
        backs.append(exchange_rows(grad_x))
        scaled.append(out)
        router_terms.append(router_term)

    expert_terms = expert_grads(
        numbers[0], x_all[0], c_all[0], w_or, w_in, w_out, 0, n_dp, experts
    )
    backs[-1], expert_terms = lax.optimization_barrier((backs[-1], expert_terms))
    scaled, _ = lax.optimization_barrier((scaled, backs[-1]))
    stacked = jnp.stack([part.reshape(peers, capacity, width) for part in scaled], axis=1)
    returned = exchange(stacked.reshape(peers, local * capacity, width)).reshape(-1, width)

    grad_middle, grad_ctx, keep_o, send_o, ggain_two = middle_back(
        number, cotangent, middle, gain_two, target_col, w_or, ctxt, backs, n_dp
    )
    keep, send, grads, diag = attend_back(number, normt, *saved, grad_ctx, group, n_dp)
    crossed_o = flip(send_o, "dp", 1)
    crossed_o, send = lax.optimization_barrier((crossed_o, send))
    crossed = flip(send, "dp", 1)
    shard_o, shards = [
        reduce_expert(reduce_y(kept.astype(F32) + got.astype(F32), dp_index))
        for kept, got in ((keep_o, crossed_o), (keep, crossed))
    ]
    grad_middle = after(grad_middle, returned)
    grad_tokens, ggain_one = first_back(
        number, tokens, gain_one, grad_middle, grads, pieces, cols
    )
    output = output_step(middle, by_peer[:, None], [returned])
    for l in range(1, local):
        expert_terms = expert_grads(
            numbers[l], x_all[l], c_all[l], w_or, w_in, w_out, l, n_dp, experts, expert_terms
        )

    grad_rel = jnp.dot(diag.reshape(heads, 2 * seq), hot_shifted, precision=HIGH)
    rel_row = jnp.pad(grad_rel.reshape(1, heads * buckets), ((0, 0), (0, width - heads * buckets)))
    small = butterfly_sum(
        jnp.concatenate([sum(router_terms), ggain_two, ggain_one, rel_row], axis=0),
        ("dp", "expert"),
    )
    shard_rows = width // n_dp
    grad_router = lax.dynamic_slice_in_dim(small[:experts], dp_index * shard_rows, shard_rows, 1).T
    total_rel = small[experts + 2, : heads * buckets].reshape(heads, buckets).T
    shard_q, shard_k, shard_v = [
        jnp.concatenate(
            [shards[:, g + i * cols : g + (i + 1) * cols] for g in range(0, 3 * width, 3 * cols)],
            axis=1,
        )
        for i in range(3)
    ]
    return (
        output,
        grad_tokens,
        small[experts + 1],
        shard_q,
        shard_k,
        shard_v,
        shard_o,
        total_rel,
        small[experts],
        grad_router,
        expert_terms[0],
        expert_terms[1],
    )


def solution(mesh):
    in_specs = (
        P(("dp", "expert"), None),
        P(("dp", "expert"), None),
        P(("dp", "expert")),
        P(("dp", "expert")),
        P(),
        P(),
        P("dp", None),
        P("dp", None),
        P("dp", None),
        P("dp", None),
        P(),
        P(),
        P("dp", None),
        P("expert", None, None),
        P("expert", None, None),
        P(("dp", "expert"), None),
    )
    out_specs = (
        P(("dp", "expert"), None),
        P(("dp", "expert"), None),
        P(),
        P("dp", None),
        P("dp", None),
        P("dp", None),
        P("dp", None),
        P(),
        P(),
        P("dp", None),
        P("expert", None, "dp"),
        P("expert", "dp", None),
    )
    return jax.shard_map(body, mesh=mesh, in_specs=in_specs, out_specs=out_specs, check_vma=False)
```

```python
import functools
import math

import jax
import jax.numpy as jnp
from jax import lax
from jax.experimental import pallas as pl
from jax.experimental.pallas import tpu as pltpu
from jax.sharding import PartitionSpec as P

EPS = 1e-06
HIGH = lax.Precision.HIGHEST
F32 = jnp.float32
BF16 = jnp.bfloat16
VMEM_LIMIT = 56 * 1024 * 1024
TILE = 128
STRIP = 256
SUB = 256
GELU_A = math.sqrt(2.0 / math.pi)
GELU_B = 0.044715


def dot(a, b):
    return jnp.dot(a, b, preferred_element_type=F32)


def dot_nt(a, b):
    return lax.dot_general(a, b, (((1,), (1,)), ((), ())), preferred_element_type=F32)


def params(**kw):
    return pltpu.CompilerParams(vmem_limit_bytes=VMEM_LIMIT, **kw)


def cost(flops, nbytes, trans=0):
    return pl.CostEstimate(flops=int(flops), bytes_accessed=int(nbytes), transcendentals=int(trans))


def rms_scale(stream):
    return lax.rsqrt(jnp.mean(stream * stream, axis=-1, keepdims=True) + EPS)


def norm_back(stream, gain, grad_out):
    scale = rms_scale(stream)
    grad_gain = jnp.sum(grad_out * (stream * scale), axis=0, keepdims=True)
    scaled = grad_out * gain
    inner = jnp.mean(scaled * stream, axis=-1, keepdims=True)
    grad_in = scale * scaled - stream * (scale * scale * scale * inner)
    return grad_in, grad_gain


def gelu_pair(v):
    sq = v * v
    power = jnp.minimum(v * (-2.0 * GELU_A - (2.0 * GELU_A * GELU_B) * sq), 80.0)
    total = 1.0 + jnp.exp(power)
    guess = pl.reciprocal(total, approx=True)
    half = guess * (2.0 - total * guess)
    value = v * half
    slope = half + value * (1.0 - half) * (2.0 * GELU_A + (6.0 * GELU_A * GELU_B) * sq)
    return value, slope


def slot_hot(target_row, start, rows):
    seq = target_row.shape[1]
    ids = lax.broadcasted_iota(jnp.int32, (rows, seq), 0) + start
    return (ids == target_row).astype(F32).astype(BF16)


def token_hot(target_col, start, rows):
    seq = target_col.shape[0]
    ids = lax.broadcasted_iota(jnp.int32, (seq, rows), 1) + start
    return (ids == target_col).astype(F32).astype(BF16)


def place_kernel(target_ref, rows_ref, out_ref):
    out_ref[...] = dot(slot_hot(target_ref[...], 0, out_ref.shape[0]), rows_ref[...]).astype(BF16)


def place(target_row, values, rows):
    seq, width = values.shape
    return pl.pallas_call(
        place_kernel,
        out_shape=jax.ShapeDtypeStruct((rows, width), BF16),
        compiler_params=params(),
        cost_estimate=cost(2 * rows * seq * width, 2 * (rows + seq) * width),
        name="place_cotangent",
    )(target_row, values)


def prepare_kernel(rel_ref, tok_ref, gain_ref, out_ref, normed_ref, normt_ref):
    heads, width = rel_ref.shape
    wide = out_ref.shape[2]
    for h in range(heads):
        base = jnp.broadcast_to(rel_ref[h : h + 1, :], (TILE, width))
        turned = pltpu.roll(base, width - (TILE - 1), 1, stride=1, stride_axis=0)
        out_ref[h] = turned[:, :wide]
    stream = tok_ref[...].astype(F32)
    normed = stream * rms_scale(stream) * gain_ref[...]
    normed_ref[...] = normed.astype(BF16)
    normt_ref[...] = normed.T.astype(BF16)


def prepare(rel_rev, tokens, gain):
    heads, span = rel_rev.shape
    seq, width = tokens.shape
    wide = 2 * seq - TILE
    return pl.pallas_call(
        prepare_kernel,
        out_shape=[
            jax.ShapeDtypeStruct((heads, TILE, wide), F32),
            jax.ShapeDtypeStruct((seq, width), BF16),
            jax.ShapeDtypeStruct((width, seq), BF16),
        ],
        compiler_params=params(),
        cost_estimate=cost(heads * TILE * span, 4 * heads * TILE * wide + 6 * seq * width),
        name="bias_and_first_norm",
    )(rel_rev, tokens, gain)


def join_rows(num_ref, pieces, w_ref):
    part, width = pieces[0].shape
    n_dp = w_ref.shape[0] // part
    for i, piece in enumerate(pieces):
        row = pl.multiple_of((num_ref[0] ^ (i % n_dp)) * part, 16)
        col = i // n_dp * width
        w_ref[pl.ds(row, part), col : col + width] = piece[...]


def attend_kernel(num_ref, normed_ref, bias_ref, kseg_ref, qseg_ref, *refs):
    pieces, refs = refs[:-8], refs[-8:]
    q_ref, k_ref, v_ref, kt_ref, e_ref, rinv_ref, ctxt_ref, w_ref = refs
    seq, width = normed_ref.shape
    heads = e_ref.shape[0]
    cols = q_ref.shape[1]
    hd = cols // heads
    per_tile = TILE // hd
    step = pl.program_id(0)

    @pl.when(step == 0)
    def _():
        join_rows(num_ref, pieces, w_ref)

    normed = normed_ref[...]
    at = lambda base: pl.ds(pl.multiple_of(base * width + step * cols, TILE), cols)
    q = dot(normed, w_ref[:, at(0)]).astype(BF16).astype(F32) * (1.0 / math.sqrt(hd))
    k32 = dot(normed, w_ref[:, at(1)])
    v32 = dot(normed, w_ref[:, at(2)])
    q_ref[...] = q.astype(BF16)
    k_ref[...] = k32.astype(BF16)
    v_ref[...] = v32.astype(BF16)
    kt_ref[...] = k32.T.astype(BF16)
    vt = v32.T.astype(BF16)
    lane = lax.broadcasted_iota(jnp.int32, (seq, TILE), 1) // hd
    kseg = kseg_ref[...]
    qseg = qseg_ref[...]
    for h in range(heads):
        tile = h // per_tile
        k_pair = k_ref[:, tile * TILE : (tile + 1) * TILE]
        q_pair = q_ref[:, tile * TILE : (tile + 1) * TILE]
        q_own = jnp.where(lane == h % per_tile, q_pair, jnp.zeros_like(q_pair))
        k_all = jnp.concatenate([k_pair, kseg], axis=1)
        q_all = jnp.concatenate([q_own, qseg], axis=1)
        for start in range(0, seq, STRIP):
            scores = dot_nt(k_all, q_all[start : start + STRIP])
            parts = []
            for b in range(0, seq, TILE):
                off = seq - TILE - b + start
                parts.append(scores[b : b + TILE] + bias_ref[h, :, off : off + STRIP])
            scores = jnp.concatenate(parts, axis=0)
            e = jnp.exp(scores - jnp.max(scores, axis=0, keepdims=True))
            rinv = 1.0 / jnp.sum(e, axis=0, keepdims=True)
            eb = e.astype(BF16)
            e_ref[h, :, start : start + STRIP] = eb
            rinv_ref[h, :, start : start + STRIP] = rinv
            ctxt = dot(vt[h * hd : (h + 1) * hd], eb) * rinv
            ctxt_ref[h * hd : (h + 1) * hd, start : start + STRIP] = ctxt.astype(BF16)


def attend(number, normed, bias, kseg, qseg, pieces, heads, group):
    seq, width = normed.shape
    cols = width // heads * group
    steps = heads // group
    wide = bias.shape[2]
    whole = lambda a: pl.BlockSpec(a.shape, lambda g: (0,) * a.ndim)
    nat = pl.BlockSpec((seq, cols), lambda g: (0, g))
    tr = pl.BlockSpec((cols, seq), lambda g: (g, 0))
    sds = jax.ShapeDtypeStruct
    return pl.pallas_call(
        attend_kernel,
        grid=(steps,),
        in_specs=[
            pl.BlockSpec(memory_space=pltpu.SMEM), whole(normed),
            pl.BlockSpec((group, TILE, wide), lambda g: (g, 0, 0)), whole(kseg), whole(qseg),
        ]
        + [whole(p) for p in pieces],
        out_specs=[
            nat, nat, nat, tr,
            pl.BlockSpec((group, seq, seq), lambda g: (g, 0, 0)),
            pl.BlockSpec((group, 1, seq), lambda g: (g, 0, 0)),
            tr,
        ],
        out_shape=[
            sds((seq, width), BF16), sds((seq, width), BF16), sds((seq, width), BF16),
            sds((width, seq), BF16), sds((heads, seq, seq), BF16), sds((heads, 1, seq), F32),
            sds((width, seq), BF16),
        ],
        scratch_shapes=[pltpu.VMEM((width, 3 * width), BF16)],
        compiler_params=params(dimension_semantics=("arbitrary",)),
        cost_estimate=cost(
            6 * seq * width * width + 4 * seq * seq * width,
            2 * (3 * width * width + 9 * seq * width + heads * seq * seq) + 4 * bias.size,
            heads * seq * seq,
        ),
        name="attention_forward",
    )(number, normed, bias, kseg, qseg, *pieces)


def middle_kernel(tok_ref, wo_ref, gain_ref, target_ref, ctx_ref, middle_ref, *placed_refs):
    width = tok_ref.shape[1]
    context = ctx_ref[...].astype(F32).T.astype(BF16)
    middle = tok_ref[...].astype(F32) + dot(context, wo_ref[:, :width])
    middle_ref[...] = middle
    normed = (middle * rms_scale(middle) * gain_ref[...]).astype(BF16)
    for l, placed_ref in enumerate(placed_refs):
        rows = placed_ref.shape[0]
        placed_ref[...] = dot(slot_hot(target_ref[...], l * rows, rows), normed).astype(BF16)


def middle_step(tokens, w_out, gain, target_row, ctxt, local, rows):
    seq, width = tokens.shape
    return pl.pallas_call(
        middle_kernel,
        out_shape=[jax.ShapeDtypeStruct((seq, width), F32)]
        + [jax.ShapeDtypeStruct((rows, width), BF16)] * local,
        compiler_params=params(),
        cost_estimate=cost(
            2 * seq * width * width + 2 * local * rows * seq * width,
            2 * width * width + 8 * seq * width + 2 * local * rows * width,
        ),
        name="output_projection_dispatch",
    )(tokens, w_out, gain, target_row, ctxt)


def gate_of(logits, expert):
    top = jnp.max(logits, axis=-1, keepdims=True)
    ex = jnp.exp(logits - top)
    prob = ex / jnp.sum(ex, axis=-1, keepdims=True)
    hot = lax.broadcasted_iota(jnp.int32, logits.shape, 1) == expert
    gate = jnp.sum(jnp.where(hot, prob, 0.0), axis=-1, keepdims=True)
    return prob, hot, gate


def expert_kernel(
    num_ref, x_ref, c_ref, wr_ref, win_ref, wout_ref,
    scaled_ref, grad_ref, router_ref, gp_ref, acc_p, acc_g,
):
    step = pl.program_id(0)
    experts = router_ref.shape[0]

    @pl.when(step == 0)
    def _():
        _, _, gate = gate_of(dot(x_ref[...], wr_ref[...])[:, :experts], num_ref[1])
        gp_ref[...] = (gate * c_ref[...].astype(F32)).astype(BF16)
        acc_p[...] = jnp.zeros_like(acc_p)
        acc_g[...] = jnp.zeros_like(acc_g)

    hiddens, grads = [], []
    for sub in range(0, win_ref.shape[2], SUB):
        pre = dot(x_ref[...], win_ref[0, :, sub : sub + SUB])
        grad_hidden = dot_nt(gp_ref[...], wout_ref[0, sub : sub + SUB, :])
        hidden, slope = gelu_pair(pre)
        hiddens.append(hidden.astype(BF16))
        grads.append((grad_hidden * slope).astype(BF16))
    acc_p[...] += dot(jnp.concatenate(hiddens, axis=1), wout_ref[0])
    acc_g[...] += dot_nt(jnp.concatenate(grads, axis=1), win_ref[0])

    @pl.when(step == pl.num_programs(0) - 1)
    def _():
        x = x_ref[...]
        prob, hot, gate = gate_of(dot(x, wr_ref[...])[:, :experts], num_ref[1])
        produced = acc_p[...]
        scaled_ref[...] = (gate * produced).astype(BF16)
        grad_gate = jnp.sum(
            c_ref[...].astype(F32) * produced.astype(BF16).astype(F32), axis=-1, keepdims=True
        )
        grad_logits = prob * (jnp.where(hot, grad_gate, 0.0) - gate * grad_gate)
        logits_b = grad_logits.astype(BF16)
        grad_ref[...] = (acc_g[...] + dot_nt(logits_b, wr_ref[:, :experts])).astype(BF16)
        router_ref[...] = dot(grad_logits.T.astype(BF16), x)


def expert_step(number, x, c, w_or, w_in, w_out, local, block, experts):
    rows, width = x.shape
    ff = w_in.shape[2]
    router_cols = w_or.shape[1] - width
    whole = lambda a: pl.BlockSpec(a.shape, lambda f: (0,) * a.ndim)
    row_spec = pl.BlockSpec((rows, width), lambda f: (0, 0))
    return pl.pallas_call(
        expert_kernel,
        grid=(ff // block,),
        in_specs=[
            pl.BlockSpec(memory_space=pltpu.SMEM),
            whole(x),
            whole(c),
            pl.BlockSpec((width, router_cols), lambda f: (0, width // router_cols)),
            pl.BlockSpec((1, width, block), lambda f: (local, 0, f)),
            pl.BlockSpec((1, block, width), lambda f: (local, f, 0)),
        ],
        out_specs=[row_spec, row_spec, pl.BlockSpec((experts, width), lambda f: (0, 0))],
        out_shape=[
            jax.ShapeDtypeStruct((rows, width), BF16),
            jax.ShapeDtypeStruct((rows, width), BF16),
            jax.ShapeDtypeStruct((experts, width), F32),
        ],
        scratch_shapes=[
            pltpu.VMEM((rows, width), BF16),
            pltpu.VMEM((rows, width), F32),
            pltpu.VMEM((rows, width), F32),
        ],
        compiler_params=params(dimension_semantics=("arbitrary",)),
        cost_estimate=cost(
            8 * rows * width * ff, 4 * width * ff + 8 * rows * width, rows * ff
        ),
        name="expert_rows",
    )(number, x, c, w_or, w_in, w_out)


def expert_grad_kernel(experts, num_ref, x_ref, c_ref, wr_ref, win_ref, wout_ref, *refs):
    gin_ref, gout_ref, gp_ref, xt_ref = refs[-4:]
    parts, rows, width = x_ref.shape
    x = x_ref[...].reshape(parts * rows, width)

    @pl.when(pl.program_id(0) == 0)
    def _():
        _, _, gate = gate_of(dot(x, wr_ref[...])[:, :experts], num_ref[1])
        c = c_ref[...].reshape(parts * rows, width)
        gp_ref[...] = (gate * c.astype(F32)).astype(BF16)
        xt_ref[...] = x.astype(F32).T.astype(BF16)

    gp = gp_ref[...]
    pre_t = dot_nt(win_ref[0].astype(F32).T.astype(BF16), x)
    hidden_t, slope_t = gelu_pair(pre_t)
    grad_hidden_t = dot_nt(wout_ref[0], gp)
    gout_ref[0] = dot(hidden_t.astype(BF16), gp)
    gin_ref[0] = dot_nt(xt_ref[...], (grad_hidden_t * slope_t).astype(BF16))


def expert_grads(numbers, x_all, c_all, w_or, w_in, w_out, local, n_dp, experts, prior=()):
    parts, rows, width = x_all.shape
    ff = w_in.shape[2]
    router_cols = w_or.shape[1] - width
    part = ff // n_dp
    block = 256 if part % 256 == 0 else 128
    steps = part // block
    whole = lambda a: pl.BlockSpec(a.shape, lambda f, n: (0,) * a.ndim)
    return pl.pallas_call(
        functools.partial(expert_grad_kernel, experts),
        grid_spec=pltpu.PrefetchScalarGridSpec(
            num_scalar_prefetch=1,
            grid=(steps,),
            in_specs=[
                whole(x_all),
                whole(c_all),
                pl.BlockSpec((width, router_cols), lambda f, n: (0, width // router_cols)),
                pl.BlockSpec((1, width, block), lambda f, n: (local, 0, n[0] * steps + f)),
                pl.BlockSpec((1, block, width), lambda f, n: (local, n[0] * steps + f, 0)),
            ]
            + [pl.BlockSpec(memory_space=pl.ANY)] * len(prior),
            out_specs=[
                pl.BlockSpec((1, width, block), lambda f, n: (local, 0, f)),
                pl.BlockSpec((1, block, width), lambda f, n: (local, f, 0)),
            ],
            scratch_shapes=[
                pltpu.VMEM((parts * rows, width), BF16),
                pltpu.VMEM((width, parts * rows), BF16),
            ],
        ),
        out_shape=[
            jax.ShapeDtypeStruct((w_in.shape[0], width, part), F32),
            jax.ShapeDtypeStruct((w_in.shape[0], part, width), F32),
        ],
        compiler_params=params(dimension_semantics=("arbitrary",)),
        cost_estimate=cost(
            8 * parts * rows * width * part,
            4 * parts * rows * width + 12 * width * part,
            parts * rows * part,
        ),
        input_output_aliases={6 + i: i for i in range(len(prior))},
        name="expert_weight_grads",
    )(numbers, x_all, c_all, w_or, w_in, w_out, *prior)


def split_rows(num_ref, full_ref, keep_ref, send_ref):
    part = keep_ref.shape[1]
    core = num_ref[0] & 1
    for y in range(keep_ref.shape[0]):
        own = pl.multiple_of((2 * y + core) * part, 16)
        other = pl.multiple_of((2 * y + 1 - core) * part, 16)
        keep_ref[y] = full_ref[pl.ds(own, part), :]
        send_ref[y] = full_ref[pl.ds(other, part), :]


def middle_back_kernel(num_ref, cot_ref, middle_ref, gain_ref, target_ref, wo_ref, ctx_ref, *refs):
    back_refs, (gmid_ref, gctx_ref, keep_ref, send_ref, ggain_ref, gwo_ref) = refs[:-6], refs[-6:]
    seq, width = cot_ref.shape
    target = target_ref[...]
    grad = jnp.zeros((seq, width), F32)
    for l, back in enumerate(back_refs):
        rows = back.shape[0]
        grad = grad + dot(token_hot(target, l * rows, rows), back[...])
    grad_in, grad_gain = norm_back(middle_ref[...], gain_ref[...], grad)
    ggain_ref[...] = grad_gain
    grad_middle = cot_ref[...].astype(F32) + grad_in
    gmid_ref[...] = grad_middle
    grad_attn = grad_middle.astype(BF16)
    gctx_ref[...] = dot_nt(grad_attn, wo_ref[:, :width]).astype(BF16)
    gwo_ref[...] = dot(ctx_ref[...], grad_attn).astype(BF16)
    split_rows(num_ref, gwo_ref, keep_ref, send_ref)


def middle_back(number, cot, middle, gain, target_col, w_out, ctxt, backs, n_dp):
    seq, width = cot.shape
    sds = jax.ShapeDtypeStruct
    slots = sum(b.shape[0] for b in backs)
    half = sds((n_dp // 2, width // n_dp, width), BF16)
    vmem = pl.BlockSpec(memory_space=pltpu.VMEM)
    return pl.pallas_call(
        middle_back_kernel,
        in_specs=[pl.BlockSpec(memory_space=pltpu.SMEM)] + [vmem] * (6 + len(backs)),
        out_shape=[sds((seq, width), F32), sds((seq, width), BF16), half, half, sds((1, width), F32)],
        scratch_shapes=[pltpu.VMEM((width, width), BF16)],
        compiler_params=params(),
        cost_estimate=cost(
            4 * seq * width * width + 2 * slots * seq * width,
            4 * width * width + 14 * seq * width + 2 * slots * width,
        ),
        name="second_norm_backward",
    )(number, cot, middle, gain, target_col, w_out, ctxt, *backs)


def attend_back_kernel(
    num_ref, normt_ref, q_ref, k_ref, v_ref, kt_ref, e_ref, rinv_ref, do_ref,
    keep_ref, send_ref, grads_ref, diag_ref, acc_ref, gw_ref,
):
    seq, cols = q_ref.shape
    heads = e_ref.shape[0]
    hd = cols // heads
    per_tile = TILE // hd
    lane = lax.broadcasted_iota(jnp.int32, (seq, TILE), 1) // hd
    row_bit = lax.broadcasted_iota(jnp.int32, (8, 2 * seq), 0)
    zero = jnp.zeros((seq, TILE), BF16)
    dk_tiles, dv_tiles, dqt_rows = [], [], []
    for h in range(heads):
        tile = h // per_tile
        sl = slice(tile * TILE, (tile + 1) * TILE)
        q_own = jnp.where(lane == h % per_tile, q_ref[:, sl], zero)
        do_own = jnp.where(lane == h % per_tile, do_ref[:, sl], zero)
        v_pair = v_ref[:, sl]
        acc_ref[...] = jnp.zeros_like(acc_ref)
        dk = jnp.zeros((seq, TILE), F32)
        dv = jnp.zeros((seq, TILE), F32)
        dqt_parts = []
        for start in range(0, seq, STRIP):
            st = slice(start, start + STRIP)
            p = e_ref[h, :, st].astype(F32) * rinv_ref[h, :, st]
            t = dot_nt(v_pair, do_own[st]) * p
            ds = t - p * jnp.sum(t, axis=0, keepdims=True)
            dsb = ds.astype(BF16)
            dv = dv + dot(p.astype(BF16), do_own[st])
            dk = dk + dot(dsb, q_own[st])
            dqt_parts.append(dot(kt_ref[h * hd : (h + 1) * hd, :], dsb))
            for b in range(0, seq, TILE):
                off = seq - TILE - b + start
                acc_ref[:, off : off + STRIP] += ds[b : b + TILE]
        if h % per_tile == 0:
            dk_tiles.append(dk)
            dv_tiles.append(dv)
        else:
            dk_tiles[-1] = dk_tiles[-1] + dk
            dv_tiles[-1] = dv_tiles[-1] + dv
        dqt_rows.append(jnp.concatenate(dqt_parts, axis=1))
        folded = acc_ref[...]
        half = TILE // 2
        while half >= 8:
            folded = folded[:half] + pltpu.roll(folded[half:], 2 * seq - half, 1)
            half //= 2
        for bit in (4, 2, 1):
            turned = pltpu.roll(folded, 2 * seq - bit, 1)
            folded = jnp.where((row_bit & bit) != 0, turned, folded)
        diag_ref[h] = jnp.sum(folded, axis=0, keepdims=True)
    dqt = jnp.concatenate(dqt_rows, axis=0) * (1.0 / math.sqrt(hd))
    grads_ref[:, :cols] = dqt.T.astype(BF16)
    for base, tiles in ((1, dk_tiles), (2, dv_tiles)):
        grads_ref[:, base * cols : (base + 1) * cols] = jnp.concatenate(tiles, axis=1).astype(BF16)
    gw_ref[...] = dot(normt_ref[...], grads_ref[...]).astype(BF16)
    split_rows(num_ref, gw_ref, keep_ref, send_ref)


def attend_back(number, normt, q, k, v, kt, e, rinv, grad_ctx, group, n_dp):
    seq, width = q.shape
    heads = e.shape[0]
    cols = width // heads * group
    steps = heads // group
    whole = lambda a: pl.BlockSpec(a.shape, lambda g: (0,) * a.ndim)
    nat = pl.BlockSpec((seq, cols), lambda g: (0, g))
    sds = jax.ShapeDtypeStruct
    half = (n_dp // 2, width // n_dp, 3 * width)
    half_spec = pl.BlockSpec((n_dp // 2, width // n_dp, 3 * cols), lambda g: (0, 0, g))
    return pl.pallas_call(
        attend_back_kernel,
        grid=(steps,),
        in_specs=[
            pl.BlockSpec(memory_space=pltpu.SMEM), whole(normt), nat, nat, nat,
            pl.BlockSpec((cols, seq), lambda g: (g, 0)),
            pl.BlockSpec((group, seq, seq), lambda g: (g, 0, 0)),
            pl.BlockSpec((group, 1, seq), lambda g: (g, 0, 0)),
            nat,
        ],
        out_specs=[
            half_spec, half_spec, pl.BlockSpec((seq, 3 * cols), lambda g: (0, g)),
            pl.BlockSpec((group, 1, 2 * seq), lambda g: (g, 0, 0)),
        ],
        out_shape=[
            sds(half, BF16), sds(half, BF16), sds((seq, 3 * width), BF16),
            sds((heads, 1, 2 * seq), F32),
        ],
        scratch_shapes=[pltpu.VMEM((TILE, 2 * seq), F32), pltpu.VMEM((width, 3 * cols), BF16)],
        compiler_params=params(dimension_semantics=("arbitrary",)),
        cost_estimate=cost(
            6 * seq * width * width + 8 * seq * seq * width,
            2 * (6 * width * width + 8 * seq * width + heads * seq * seq),
        ),
        name="attention_backward",
    )(number, normt, q, k, v, kt, e, rinv, grad_ctx)


def first_back_kernel(cols, num_ref, tok_ref, gain_ref, gmid_ref, grads_ref, *refs):
    pieces, (gtok_ref, ggain_ref, w_ref) = refs[:-3], refs[-3:]
    width = tok_ref.shape[1]
    join_rows(num_ref, pieces, w_ref)
    grad = jnp.zeros(tok_ref.shape, F32)
    for i, start in enumerate(range(0, 3 * width, cols)):
        col = i % 3 * width + i // 3 * cols
        grad = grad + dot_nt(grads_ref[:, start : start + cols], w_ref[:, col : col + cols])
    grad_in, grad_gain = norm_back(tok_ref[...].astype(F32), gain_ref[...], grad)
    gtok_ref[...] = gmid_ref[...] + grad_in
    ggain_ref[...] = grad_gain


def first_back(number, tokens, gain, grad_middle, grads, pieces, cols):
    seq, width = tokens.shape
    vmem = pl.BlockSpec(memory_space=pltpu.VMEM)
    return pl.pallas_call(
        functools.partial(first_back_kernel, cols),
        in_specs=[pl.BlockSpec(memory_space=pltpu.SMEM)] + [vmem] * (4 + len(pieces)),
        out_shape=[
            jax.ShapeDtypeStruct((seq, width), F32), jax.ShapeDtypeStruct((1, width), F32)
        ],
        scratch_shapes=[pltpu.VMEM((width, 3 * width), BF16)],
        compiler_params=params(),
        cost_estimate=cost(6 * seq * width * width, 6 * width * width + 16 * seq * width),
        name="first_norm_backward",
    )(number, tokens, gain, grad_middle, grads, *pieces)


def output_kernel(middle_ref, target_ref, *refs):
    out_ref = refs[-1]
    total = middle_ref[...]
    for l, back in enumerate(refs[:-1]):
        rows = back.shape[0]
        total = total + dot(token_hot(target_ref[...], l * rows, rows), back[...])
    out_ref[...] = total.astype(BF16)


def output_step(middle, target_col, backs):
    seq, width = middle.shape
    slots = sum(b.shape[0] for b in backs)
    return pl.pallas_call(
        output_kernel,
        out_shape=jax.ShapeDtypeStruct((seq, width), BF16),
        compiler_params=params(),
        cost_estimate=cost(2 * slots * seq * width, 6 * seq * width + 2 * slots * width),
        name="layer_output",
    )(middle, target_col, *backs)


def flip(value, axis, bit):
    size = lax.axis_size(axis)
    return lax.ppermute(value, axis, [(i, i ^ bit) for i in range(size)])


def butterfly_sum(value, axes):
    for axis in axes:
        bit = 1
        while bit < lax.axis_size(axis):
            value = value + flip(value, axis, bit)
            bit *= 2
    return value


def after(value, *others):
    return lax.optimization_barrier((value, *others))[0]


def gather_rows(piece):
    pieces = {0: piece}
    bit = 2
    while bit < lax.axis_size("dp"):
        pieces.update({m | bit: flip(p, "dp", bit) for m, p in pieces.items()})
        bit *= 2
    return pieces


def gather_cores(pieces):
    pieces = {**pieces, **{m | 1: flip(p, "dp", 1) for m, p in pieces.items()}}
    return [pieces[m] for m in sorted(pieces)]


def reduce_y(total, dp_index):
    bit = lax.axis_size("dp") // 2
    while bit > 1:
        halves = total.reshape(2, total.shape[0] // 2, *total.shape[1:])
        mine = jnp.where((dp_index & bit) != 0, 1, 0)
        sent = lax.dynamic_index_in_dim(halves, 1 - mine, 0, keepdims=False).astype(BF16)
        kept = lax.dynamic_index_in_dim(halves, mine, 0, keepdims=False)
        total = kept + flip(sent, "dp", bit).astype(F32)
        bit //= 2
    return total[0]


def sum_expert(total):
    peers = lax.axis_size("expert")
    rows, cols = total.shape
    parts = total.astype(BF16).reshape(peers, rows // peers, cols)
    arrived = lax.all_to_all(parts, "expert", split_axis=0, concat_axis=0, tiled=True)
    return jnp.sum(arrived.astype(F32), axis=0).astype(BF16)


def spread_expert(share, peers):
    rows, cols = share.shape
    spread = jnp.broadcast_to(share[None], (peers, rows, cols))
    shared = lax.all_to_all(spread, "expert", split_axis=0, concat_axis=0, tiled=True)
    return shared.reshape(peers * rows, cols).astype(F32)


def body(
    tokens, segments, routes, slots, bucket_table, gain_attn, w_query, w_key, w_value, w_output,
    rel_bias, gain_ffn, w_router, w_in, w_out, cotangent,
):
    seq, width = tokens.shape
    buckets, heads = rel_bias.shape
    experts = w_router.shape[1]
    n_dp = lax.axis_size("dp")
    peers = lax.axis_size("expert")
    local = w_in.shape[0]
    capacity = max(2, (5 * seq + 4 * experts - 1) // (4 * experts))
    rows = peers * capacity
    dp_index = lax.axis_index("dp")
    expert_index = lax.axis_index("expert")
    number = jnp.reshape(dp_index, (1,)).astype(jnp.int32)
    group = 4
    cols = width // heads * group

    along_y = [gather_rows(w) for w in (w_query, w_key, w_value)]
    order = (routes % local) * rows + (routes // local) * capacity + slots
    target = jnp.where(slots >= 0, order, -1)
    target_row = target[None, :]
    target_col = target[:, None]
    by_peer = jnp.where(slots >= 0, routes * capacity + slots, -1)
    gain_one = gain_attn[None, :]
    gain_two = gain_ffn[None, :]

    def exchange(values):
        return lax.all_to_all(values, "expert", split_axis=0, concat_axis=0, tiled=True)

    def exchange_rows(values):
        return exchange(values.reshape(peers, capacity, width)).reshape(rows, width)

    reversed_table = jnp.concatenate([bucket_table[::-1], jnp.full((1,), -1, jnp.int32)])
    bucket_ids = jnp.arange(buckets, dtype=jnp.int32)
    hot_rev = (bucket_ids[:, None] == reversed_table[None, :]).astype(F32)
    rel_rev = jnp.dot(rel_bias.T, hot_rev, precision=HIGH)
    shifted = jnp.roll(reversed_table, 1 - TILE)
    hot_shifted = (shifted[:, None] == bucket_ids[None, :]).astype(F32)
    bias, normed, normt = prepare(rel_rev, tokens, gain_one)
    marks = jnp.arange(TILE, dtype=jnp.int32)[None, :]
    same = segments[0][:, None] == marks
    kseg = same.astype(BF16)
    qseg = jnp.where(same, 0.0, -1e9).astype(BF16)

    c_placed = place(by_peer[None, :], cotangent, local * rows)
    along_y, bias, normed, normt, kseg, qseg, w_output = lax.optimization_barrier(
        (along_y, bias, normed, normt, kseg, qseg, w_output)
    )
    pieces = [piece for rows_of in along_y for piece in gather_cores(rows_of)]
    router_pad = jnp.pad(w_router, ((0, 0), (0, -experts % TILE)))
    w_or = lax.all_gather(
        jnp.concatenate([w_output, router_pad], axis=1), "dp", axis=0, tiled=True
    )

    c_got = exchange(c_placed.reshape(peers, local * capacity, width))
    normed, pieces, c_got = lax.optimization_barrier((normed, pieces, c_got))
    *saved, ctxt = attend(number, normed, bias, kseg, qseg, pieces, heads, group)

    c_split = c_got.reshape(peers, local, capacity, width)
    c_here = [c_split[:, l].reshape(rows, width) for l in range(local)]
    c_all = [lax.all_gather(part, "dp", axis=0, tiled=False) for part in c_here]

    middle, *placed = middle_step(tokens, w_or, gain_two, target_row, ctxt, local, rows)

    arrived = [exchange_rows(part) for part in placed]
    x_all, backs, scaled, router_terms, numbers = [], [], [], [], []
    for l in range(local):
        numbers.append(jnp.stack([dp_index, expert_index * local + l]).astype(jnp.int32))
        early = after(arrived[l], scaled[-1]) if l else arrived[l]
        x_all.append(lax.all_gather(early, "dp", axis=0, tiled=False))
        out, grad_x, router_term = expert_step(
            numbers[l], arrived[l], c_here[l], w_or, w_in, w_out, l, 1024, experts
        )
        backs.append(exchange_rows(grad_x))
        scaled.append(out)
        router_terms.append(router_term)

    expert_terms = expert_grads(
        numbers[0], x_all[0], c_all[0], w_or, w_in, w_out, 0, n_dp, experts
    )
    backs[-1], expert_terms = lax.optimization_barrier((backs[-1], expert_terms))
    scaled, _ = lax.optimization_barrier((scaled, backs[-1]))
    stacked = jnp.stack([part.reshape(peers, capacity, width) for part in scaled], axis=1)
    returned = exchange(stacked.reshape(peers, local * capacity, width)).reshape(-1, width)

    grad_middle, grad_ctx, keep_o, send_o, ggain_two = middle_back(
        number, cotangent, middle, gain_two, target_col, w_or, ctxt, backs, n_dp
    )
    keep, send, grads, diag = attend_back(number, normt, *saved, grad_ctx, group, n_dp)
    crossed_o = flip(send_o, "dp", 1)
    crossed_o, send, returned = lax.optimization_barrier((crossed_o, send, returned))
    crossed = flip(send, "dp", 1)
    part_o = reduce_y(keep_o.astype(F32) + crossed_o.astype(F32), dp_index)
    part = reduce_y(keep.astype(F32) + crossed.astype(F32), dp_index)
    shard_o = spread_expert(sum_expert(part_o), peers)
    grad_tokens, ggain_one = first_back(
        number, tokens, gain_one, grad_middle, grads, pieces, cols
    )
    for l in range(1, local):
        expert_terms = expert_grads(
            numbers[l], x_all[l], c_all[l], w_or, w_in, w_out, l, n_dp, experts, expert_terms
        )
    part, grad_tokens, ggain_one, expert_terms = lax.optimization_barrier(
        (part, grad_tokens, ggain_one, expert_terms)
    )
    summed = sum_expert(part)
    output = output_step(middle, by_peer[:, None], [returned])
    summed, output, shard_o = lax.optimization_barrier((summed, output, shard_o))
    shards = spread_expert(summed, peers)

    grad_rel = jnp.dot(diag.reshape(heads, 2 * seq), hot_shifted, precision=HIGH)
    rel_row = jnp.pad(grad_rel.reshape(1, heads * buckets), ((0, 0), (0, width - heads * buckets)))
    small = butterfly_sum(
        jnp.concatenate([sum(router_terms), ggain_two, ggain_one, rel_row], axis=0),
        ("dp", "expert"),
    )
    shard_rows = width // n_dp
    grad_router = lax.dynamic_slice_in_dim(small[:experts], dp_index * shard_rows, shard_rows, 1).T
    total_rel = small[experts + 2, : heads * buckets].reshape(heads, buckets).T
    shard_q, shard_k, shard_v = [
        jnp.concatenate(
            [shards[:, g + i * cols : g + (i + 1) * cols] for g in range(0, 3 * width, 3 * cols)],
            axis=1,
        )
        for i in range(3)
    ]
    return (
        output,
        grad_tokens,
        small[experts + 1],
        shard_q,
        shard_k,
        shard_v,
        shard_o,
        total_rel,
        small[experts],
        grad_router,
        expert_terms[0],
        expert_terms[1],
    )


def solution(mesh):
    in_specs = (
        P(("dp", "expert"), None),
        P(("dp", "expert"), None),
        P(("dp", "expert")),
        P(("dp", "expert")),
        P(),
        P(),
        P("dp", None),
        P("dp", None),
        P("dp", None),
        P("dp", None),
        P(),
        P(),
        P("dp", None),
        P("expert", None, None),
        P("expert", None, None),
        P(("dp", "expert"), None),
    )
    out_specs = (
        P(("dp", "expert"), None),
        P(("dp", "expert"), None),
        P(),
        P("dp", None),
        P("dp", None),
        P("dp", None),
        P("dp", None),
        P(),
        P(),
        P("dp", None),
        P("expert", None, "dp"),
        P("expert", "dp", None),
    )
    return jax.shard_map(body, mesh=mesh, in_specs=in_specs, out_specs=out_specs, check_vma=False)
```

```python
import functools
import math

import jax
import jax.numpy as jnp
from jax import lax
from jax.experimental import pallas as pl
from jax.experimental.pallas import tpu as pltpu
from jax.sharding import PartitionSpec as P

EPS = 1e-06
HIGH = lax.Precision.HIGHEST
F32 = jnp.float32
BF16 = jnp.bfloat16
VMEM_LIMIT = 56 * 1024 * 1024
TILE = 128
STRIP = 256
SUB = 256
GELU_A = math.sqrt(2.0 / math.pi)
GELU_B = 0.044715


def dot(a, b):
    return jnp.dot(a, b, preferred_element_type=F32)


def dot_nt(a, b):
    return lax.dot_general(a, b, (((1,), (1,)), ((), ())), preferred_element_type=F32)


def params(**kw):
    return pltpu.CompilerParams(vmem_limit_bytes=VMEM_LIMIT, **kw)


def cost(flops, nbytes, trans=0):
    return pl.CostEstimate(flops=int(flops), bytes_accessed=int(nbytes), transcendentals=int(trans))


def rms_scale(stream):
    return lax.rsqrt(jnp.mean(stream * stream, axis=-1, keepdims=True) + EPS)


def norm_back(stream, gain, grad_out):
    scale = rms_scale(stream)
    grad_gain = jnp.sum(grad_out * (stream * scale), axis=0, keepdims=True)
    scaled = grad_out * gain
    inner = jnp.mean(scaled * stream, axis=-1, keepdims=True)
    grad_in = scale * scaled - stream * (scale * scale * scale * inner)
    return grad_in, grad_gain


def gelu_pair(v):
    sq = v * v
    power = jnp.minimum(v * (-2.0 * GELU_A - (2.0 * GELU_A * GELU_B) * sq), 80.0)
    total = 1.0 + jnp.exp(power)
    guess = pl.reciprocal(total, approx=True)
    half = guess * (2.0 - total * guess)
    value = v * half
    slope = half + value * (1.0 - half) * (2.0 * GELU_A + (6.0 * GELU_A * GELU_B) * sq)
    return value, slope


def slot_hot(target_row, start, rows):
    seq = target_row.shape[1]
    ids = lax.broadcasted_iota(jnp.int32, (rows, seq), 0) + start
    return (ids == target_row).astype(F32).astype(BF16)


def token_hot(target_col, start, rows):
    seq = target_col.shape[0]
    ids = lax.broadcasted_iota(jnp.int32, (seq, rows), 1) + start
    return (ids == target_col).astype(F32).astype(BF16)


def place_kernel(target_ref, rows_ref, *out_refs):
    for l, out_ref in enumerate(out_refs):
        rows = out_ref.shape[0]
        out_ref[...] = dot(slot_hot(target_ref[...], l * rows, rows), rows_ref[...]).astype(BF16)


def place(target_row, values, local, rows):
    seq, width = values.shape
    return pl.pallas_call(
        place_kernel,
        out_shape=[jax.ShapeDtypeStruct((rows, width), BF16)] * local,
        compiler_params=params(),
        cost_estimate=cost(2 * local * rows * seq * width, 2 * (local * rows + seq) * width),
        name="place_cotangent",
    )(target_row, values)


def prepare_kernel(rel_ref, tok_ref, gain_ref, out_ref, normed_ref, normt_ref):
    heads, width = rel_ref.shape
    wide = out_ref.shape[2]
    for h in range(heads):
        base = jnp.broadcast_to(rel_ref[h : h + 1, :], (TILE, width))
        turned = pltpu.roll(base, width - (TILE - 1), 1, stride=1, stride_axis=0)
        out_ref[h] = turned[:, :wide]
    stream = tok_ref[...].astype(F32)
    normed = stream * rms_scale(stream) * gain_ref[...]
    normed_ref[...] = normed.astype(BF16)
    normt_ref[...] = normed.T.astype(BF16)


def prepare(rel_rev, tokens, gain):
    heads, span = rel_rev.shape
    seq, width = tokens.shape
    wide = 2 * seq - TILE
    return pl.pallas_call(
        prepare_kernel,
        out_shape=[
            jax.ShapeDtypeStruct((heads, TILE, wide), F32),
            jax.ShapeDtypeStruct((seq, width), BF16),
            jax.ShapeDtypeStruct((width, seq), BF16),
        ],
        compiler_params=params(),
        cost_estimate=cost(heads * TILE * span, 4 * heads * TILE * wide + 6 * seq * width),
        name="bias_and_first_norm",
    )(rel_rev, tokens, gain)


def join_rows(num_ref, pieces, w_ref):
    part, width = pieces[0].shape
    n_dp = w_ref.shape[0] // part
    for i, piece in enumerate(pieces):
        row = pl.multiple_of((num_ref[0] ^ (i % n_dp)) * part, 16)
        col = i // n_dp * width
        w_ref[pl.ds(row, part), col : col + width] = piece[...]


def attend_kernel(num_ref, normed_ref, bias_ref, kseg_ref, qseg_ref, *refs):
    pieces, refs = refs[:-8], refs[-8:]
    q_ref, k_ref, v_ref, kt_ref, e_ref, rinv_ref, ctxt_ref, w_ref = refs
    seq, width = normed_ref.shape
    heads = e_ref.shape[0]
    cols = q_ref.shape[1]
    hd = cols // heads
    per_tile = TILE // hd
    step = pl.program_id(0)

    @pl.when(step == 0)
    def _():
        join_rows(num_ref, pieces, w_ref)

    normed = normed_ref[...]
    at = lambda base: pl.ds(pl.multiple_of(base * width + step * cols, TILE), cols)
    q = dot(normed, w_ref[:, at(0)]).astype(BF16).astype(F32) * (1.0 / math.sqrt(hd))
    k32 = dot(normed, w_ref[:, at(1)])
    v32 = dot(normed, w_ref[:, at(2)])
    q_ref[...] = q.astype(BF16)
    k_ref[...] = k32.astype(BF16)
    v_ref[...] = v32.astype(BF16)
    kt_ref[...] = k32.T.astype(BF16)
    vt = v32.T.astype(BF16)
    lane = lax.broadcasted_iota(jnp.int32, (seq, TILE), 1) // hd
    kseg = kseg_ref[...]
    qseg = qseg_ref[...]
    for h in range(heads):
        tile = h // per_tile
        k_pair = k_ref[:, tile * TILE : (tile + 1) * TILE]
        q_pair = q_ref[:, tile * TILE : (tile + 1) * TILE]
        q_own = jnp.where(lane == h % per_tile, q_pair, jnp.zeros_like(q_pair))
        k_all = jnp.concatenate([k_pair, kseg], axis=1)
        q_all = jnp.concatenate([q_own, qseg], axis=1)
        for start in range(0, seq, STRIP):
            scores = dot_nt(k_all, q_all[start : start + STRIP])
            parts = []
            for b in range(0, seq, TILE):
                off = seq - TILE - b + start
                parts.append(scores[b : b + TILE] + bias_ref[h, :, off : off + STRIP])
            scores = jnp.concatenate(parts, axis=0)
            e = jnp.exp(scores - jnp.max(scores, axis=0, keepdims=True))
            rinv = 1.0 / jnp.sum(e, axis=0, keepdims=True)
            eb = e.astype(BF16)
            e_ref[h, :, start : start + STRIP] = eb
            rinv_ref[h, :, start : start + STRIP] = rinv
            ctxt = dot(vt[h * hd : (h + 1) * hd], eb) * rinv
            ctxt_ref[h * hd : (h + 1) * hd, start : start + STRIP] = ctxt.astype(BF16)


def attend(number, normed, bias, kseg, qseg, pieces, heads, group):
    seq, width = normed.shape
    cols = width // heads * group
    steps = heads // group
    wide = bias.shape[2]
    whole = lambda a: pl.BlockSpec(a.shape, lambda g: (0,) * a.ndim)
    nat = pl.BlockSpec((seq, cols), lambda g: (0, g))
    tr = pl.BlockSpec((cols, seq), lambda g: (g, 0))
    sds = jax.ShapeDtypeStruct
    return pl.pallas_call(
        attend_kernel,
        grid=(steps,),
        in_specs=[
            pl.BlockSpec(memory_space=pltpu.SMEM), whole(normed),
            pl.BlockSpec((group, TILE, wide), lambda g: (g, 0, 0)), whole(kseg), whole(qseg),
        ]
        + [whole(p) for p in pieces],
        out_specs=[
            nat, nat, nat, tr,
            pl.BlockSpec((group, seq, seq), lambda g: (g, 0, 0)),
            pl.BlockSpec((group, 1, seq), lambda g: (g, 0, 0)),
            tr,
        ],
        out_shape=[
            sds((seq, width), BF16), sds((seq, width), BF16), sds((seq, width), BF16),
            sds((width, seq), BF16), sds((heads, seq, seq), BF16), sds((heads, 1, seq), F32),
            sds((width, seq), BF16),
        ],
        scratch_shapes=[pltpu.VMEM((width, 3 * width), BF16)],
        compiler_params=params(dimension_semantics=("arbitrary",)),
        cost_estimate=cost(
            6 * seq * width * width + 4 * seq * seq * width,
            2 * (3 * width * width + 9 * seq * width + heads * seq * seq) + 4 * bias.size,
            heads * seq * seq,
        ),
        name="attention_forward",
    )(number, normed, bias, kseg, qseg, *pieces)


def middle_kernel(tok_ref, wo_ref, gain_ref, target_ref, ctx_ref, middle_ref, *placed_refs):
    width = tok_ref.shape[1]
    context = ctx_ref[...].astype(F32).T.astype(BF16)
    middle = tok_ref[...].astype(F32) + dot(context, wo_ref[:, :width])
    middle_ref[...] = middle
    normed = (middle * rms_scale(middle) * gain_ref[...]).astype(BF16)
    for l, placed_ref in enumerate(placed_refs):
        rows = placed_ref.shape[0]
        placed_ref[...] = dot(slot_hot(target_ref[...], l * rows, rows), normed).astype(BF16)


def middle_step(tokens, w_out, gain, target_row, ctxt, local, rows):
    seq, width = tokens.shape
    return pl.pallas_call(
        middle_kernel,
        out_shape=[jax.ShapeDtypeStruct((seq, width), F32)]
        + [jax.ShapeDtypeStruct((rows, width), BF16)] * local,
        compiler_params=params(),
        cost_estimate=cost(
            2 * seq * width * width + 2 * local * rows * seq * width,
            2 * width * width + 8 * seq * width + 2 * local * rows * width,
        ),
        name="output_projection_dispatch",
    )(tokens, w_out, gain, target_row, ctxt)


def gate_of(logits, expert):
    top = jnp.max(logits, axis=-1, keepdims=True)
    ex = jnp.exp(logits - top)
    prob = ex / jnp.sum(ex, axis=-1, keepdims=True)
    hot = lax.broadcasted_iota(jnp.int32, logits.shape, 1) == expert
    gate = jnp.sum(jnp.where(hot, prob, 0.0), axis=-1, keepdims=True)
    return prob, hot, gate


def expert_kernel(
    num_ref, x_ref, c_ref, wr_ref, win_ref, wout_ref,
    scaled_ref, grad_ref, router_ref, gp_ref, acc_p, acc_g,
):
    step = pl.program_id(0)
    experts = router_ref.shape[0]

    @pl.when(step == 0)
    def _():
        _, _, gate = gate_of(dot(x_ref[...], wr_ref[...])[:, :experts], num_ref[1])
        gp_ref[...] = (gate * c_ref[...].astype(F32)).astype(BF16)
        acc_p[...] = jnp.zeros_like(acc_p)
        acc_g[...] = jnp.zeros_like(acc_g)

    hiddens, grads = [], []
    for sub in range(0, win_ref.shape[2], SUB):
        pre = dot(x_ref[...], win_ref[0, :, sub : sub + SUB])
        grad_hidden = dot_nt(gp_ref[...], wout_ref[0, sub : sub + SUB, :])
        hidden, slope = gelu_pair(pre)
        hiddens.append(hidden.astype(BF16))
        grads.append((grad_hidden * slope).astype(BF16))
    acc_p[...] += dot(jnp.concatenate(hiddens, axis=1), wout_ref[0])
    acc_g[...] += dot_nt(jnp.concatenate(grads, axis=1), win_ref[0])

    @pl.when(step == pl.num_programs(0) - 1)
    def _():
        x = x_ref[...]
        prob, hot, gate = gate_of(dot(x, wr_ref[...])[:, :experts], num_ref[1])
        produced = acc_p[...]
        scaled_ref[...] = (gate * produced).astype(BF16)
        grad_gate = jnp.sum(
            c_ref[...].astype(F32) * produced.astype(BF16).astype(F32), axis=-1, keepdims=True
        )
        grad_logits = prob * (jnp.where(hot, grad_gate, 0.0) - gate * grad_gate)
        logits_b = grad_logits.astype(BF16)
        grad_ref[...] = (acc_g[...] + dot_nt(logits_b, wr_ref[:, :experts])).astype(BF16)
        router_ref[...] = dot(grad_logits.T.astype(BF16), x)


def expert_step(number, x, c, w_or, w_in, w_out, local, block, experts):
    rows, width = x.shape
    ff = w_in.shape[2]
    router_cols = w_or.shape[1] - width
    whole = lambda a: pl.BlockSpec(a.shape, lambda f: (0,) * a.ndim)
    row_spec = pl.BlockSpec((rows, width), lambda f: (0, 0))
    return pl.pallas_call(
        expert_kernel,
        grid=(ff // block,),
        in_specs=[
            pl.BlockSpec(memory_space=pltpu.SMEM),
            whole(x),
            whole(c),
            pl.BlockSpec((width, router_cols), lambda f: (0, width // router_cols)),
            pl.BlockSpec((1, width, block), lambda f: (local, 0, f)),
            pl.BlockSpec((1, block, width), lambda f: (local, f, 0)),
        ],
        out_specs=[row_spec, row_spec, pl.BlockSpec((experts, width), lambda f: (0, 0))],
        out_shape=[
            jax.ShapeDtypeStruct((rows, width), BF16),
            jax.ShapeDtypeStruct((rows, width), BF16),
            jax.ShapeDtypeStruct((experts, width), F32),
        ],
        scratch_shapes=[
            pltpu.VMEM((rows, width), BF16),
            pltpu.VMEM((rows, width), F32),
            pltpu.VMEM((rows, width), F32),
        ],
        compiler_params=params(dimension_semantics=("arbitrary",)),
        cost_estimate=cost(
            8 * rows * width * ff, 4 * width * ff + 8 * rows * width, rows * ff
        ),
        name="expert_rows",
    )(number, x, c, w_or, w_in, w_out)


def expert_grad_kernel(experts, num_ref, x_ref, c_ref, wr_ref, win_ref, wout_ref, *refs):
    gin_ref, gout_ref, gp_ref, xt_ref = refs[-4:]
    parts, rows, width = x_ref.shape
    x = x_ref[...].reshape(parts * rows, width)

    @pl.when(pl.program_id(0) == 0)
    def _():
        _, _, gate = gate_of(dot(x, wr_ref[...])[:, :experts], num_ref[1])
        c = c_ref[...].reshape(parts * rows, width)
        gp_ref[...] = (gate * c.astype(F32)).astype(BF16)
        xt_ref[...] = x.astype(F32).T.astype(BF16)

    gp = gp_ref[...]
    pre_t = dot_nt(win_ref[0].astype(F32).T.astype(BF16), x)
    hidden_t, slope_t = gelu_pair(pre_t)
    grad_hidden_t = dot_nt(wout_ref[0], gp)
    gout_ref[0] = dot(hidden_t.astype(BF16), gp)
    gin_ref[0] = dot_nt(xt_ref[...], (grad_hidden_t * slope_t).astype(BF16))


def expert_grads(numbers, x_all, c_all, w_or, w_in, w_out, local, n_dp, experts, prior=()):
    parts, rows, width = x_all.shape
    ff = w_in.shape[2]
    router_cols = w_or.shape[1] - width
    part = ff // n_dp
    block = 256 if part % 256 == 0 else 128
    steps = part // block
    whole = lambda a: pl.BlockSpec(a.shape, lambda f, n: (0,) * a.ndim)
    return pl.pallas_call(
        functools.partial(expert_grad_kernel, experts),
        grid_spec=pltpu.PrefetchScalarGridSpec(
            num_scalar_prefetch=1,
            grid=(steps,),
            in_specs=[
                whole(x_all),
                whole(c_all),
                pl.BlockSpec((width, router_cols), lambda f, n: (0, width // router_cols)),
                pl.BlockSpec((1, width, block), lambda f, n: (local, 0, n[0] * steps + f)),
                pl.BlockSpec((1, block, width), lambda f, n: (local, n[0] * steps + f, 0)),
            ]
            + [pl.BlockSpec(memory_space=pl.ANY)] * len(prior),
            out_specs=[
                pl.BlockSpec((1, width, block), lambda f, n: (local, 0, f)),
                pl.BlockSpec((1, block, width), lambda f, n: (local, f, 0)),
            ],
            scratch_shapes=[
                pltpu.VMEM((parts * rows, width), BF16),
                pltpu.VMEM((width, parts * rows), BF16),
            ],
        ),
        out_shape=[
            jax.ShapeDtypeStruct((w_in.shape[0], width, part), F32),
            jax.ShapeDtypeStruct((w_in.shape[0], part, width), F32),
        ],
        compiler_params=params(dimension_semantics=("arbitrary",)),
        cost_estimate=cost(
            8 * parts * rows * width * part,
            4 * parts * rows * width + 12 * width * part,
            parts * rows * part,
        ),
        input_output_aliases={6 + i: i for i in range(len(prior))},
        name="expert_weight_grads",
    )(numbers, x_all, c_all, w_or, w_in, w_out, *prior)


def split_rows(num_ref, full_ref, keep_ref, send_ref):
    part = keep_ref.shape[1]
    core = num_ref[0] & 1
    for y in range(keep_ref.shape[0]):
        own = pl.multiple_of((2 * y + core) * part, 16)
        other = pl.multiple_of((2 * y + 1 - core) * part, 16)
        keep_ref[y] = full_ref[pl.ds(own, part), :]
        send_ref[y] = full_ref[pl.ds(other, part), :]


def middle_back_kernel(num_ref, cot_ref, middle_ref, gain_ref, target_ref, wo_ref, ctx_ref, *refs):
    back_refs, (gmid_ref, gctx_ref, keep_ref, send_ref, ggain_ref, gwo_ref) = refs[:-6], refs[-6:]
    seq, width = cot_ref.shape
    target = target_ref[...]
    grad = jnp.zeros((seq, width), F32)
    for l, back in enumerate(back_refs):
        rows = back.shape[0]
        grad = grad + dot(token_hot(target, l * rows, rows), back[...])
    grad_in, grad_gain = norm_back(middle_ref[...], gain_ref[...], grad)
    ggain_ref[...] = grad_gain
    grad_middle = cot_ref[...].astype(F32) + grad_in
    gmid_ref[...] = grad_middle
    grad_attn = grad_middle.astype(BF16)
    gctx_ref[...] = dot_nt(grad_attn, wo_ref[:, :width]).astype(BF16)
    gwo_ref[...] = dot(ctx_ref[...], grad_attn).astype(BF16)
    split_rows(num_ref, gwo_ref, keep_ref, send_ref)


def middle_back(number, cot, middle, gain, target_col, w_out, ctxt, backs, n_dp):
    seq, width = cot.shape
    sds = jax.ShapeDtypeStruct
    slots = sum(b.shape[0] for b in backs)
    half = sds((n_dp // 2, width // n_dp, width), BF16)
    vmem = pl.BlockSpec(memory_space=pltpu.VMEM)
    return pl.pallas_call(
        middle_back_kernel,
        in_specs=[pl.BlockSpec(memory_space=pltpu.SMEM)] + [vmem] * (6 + len(backs)),
        out_shape=[sds((seq, width), F32), sds((seq, width), BF16), half, half, sds((1, width), F32)],
        scratch_shapes=[pltpu.VMEM((width, width), BF16)],
        compiler_params=params(),
        cost_estimate=cost(
            4 * seq * width * width + 2 * slots * seq * width,
            4 * width * width + 14 * seq * width + 2 * slots * width,
        ),
        name="second_norm_backward",
    )(number, cot, middle, gain, target_col, w_out, ctxt, *backs)


def attend_back_kernel(
    num_ref, normt_ref, q_ref, k_ref, v_ref, kt_ref, e_ref, rinv_ref, do_ref,
    keep_ref, send_ref, grads_ref, diag_ref, acc_ref, gw_ref,
):
    seq, cols = q_ref.shape
    heads = e_ref.shape[0]
    hd = cols // heads
    per_tile = TILE // hd
    lane = lax.broadcasted_iota(jnp.int32, (seq, TILE), 1) // hd
    row_bit = lax.broadcasted_iota(jnp.int32, (8, 2 * seq), 0)
    zero = jnp.zeros((seq, TILE), BF16)
    dk_tiles, dv_tiles, dqt_rows = [], [], []
    for h in range(heads):
        tile = h // per_tile
        sl = slice(tile * TILE, (tile + 1) * TILE)
        q_own = jnp.where(lane == h % per_tile, q_ref[:, sl], zero)
        do_own = jnp.where(lane == h % per_tile, do_ref[:, sl], zero)
        v_pair = v_ref[:, sl]
        acc_ref[...] = jnp.zeros_like(acc_ref)
        dk = jnp.zeros((seq, TILE), F32)
        dv = jnp.zeros((seq, TILE), F32)
        dqt_parts = []
        for start in range(0, seq, STRIP):
            st = slice(start, start + STRIP)
            p = e_ref[h, :, st].astype(F32) * rinv_ref[h, :, st]
            t = dot_nt(v_pair, do_own[st]) * p
            ds = t - p * jnp.sum(t, axis=0, keepdims=True)
            dsb = ds.astype(BF16)
            dv = dv + dot(p.astype(BF16), do_own[st])
            dk = dk + dot(dsb, q_own[st])
            dqt_parts.append(dot(kt_ref[h * hd : (h + 1) * hd, :], dsb))
            for b in range(0, seq, TILE):
                off = seq - TILE - b + start
                acc_ref[:, off : off + STRIP] += ds[b : b + TILE]
        if h % per_tile == 0:
            dk_tiles.append(dk)
            dv_tiles.append(dv)
        else:
            dk_tiles[-1] = dk_tiles[-1] + dk
            dv_tiles[-1] = dv_tiles[-1] + dv
        dqt_rows.append(jnp.concatenate(dqt_parts, axis=1))
        folded = acc_ref[...]
        half = TILE // 2
        while half >= 8:
            folded = folded[:half] + pltpu.roll(folded[half:], 2 * seq - half, 1)
            half //= 2
        for bit in (4, 2, 1):
            turned = pltpu.roll(folded, 2 * seq - bit, 1)
            folded = jnp.where((row_bit & bit) != 0, turned, folded)
        diag_ref[h] = jnp.sum(folded, axis=0, keepdims=True)
    dqt = jnp.concatenate(dqt_rows, axis=0) * (1.0 / math.sqrt(hd))
    grads_ref[:, :cols] = dqt.T.astype(BF16)
    for base, tiles in ((1, dk_tiles), (2, dv_tiles)):
        grads_ref[:, base * cols : (base + 1) * cols] = jnp.concatenate(tiles, axis=1).astype(BF16)
    gw_ref[...] = dot(normt_ref[...], grads_ref[...]).astype(BF16)
    split_rows(num_ref, gw_ref, keep_ref, send_ref)


def attend_back(number, normt, q, k, v, kt, e, rinv, grad_ctx, group, n_dp):
    seq, width = q.shape
    heads = e.shape[0]
    cols = width // heads * group
    steps = heads // group
    whole = lambda a: pl.BlockSpec(a.shape, lambda g: (0,) * a.ndim)
    nat = pl.BlockSpec((seq, cols), lambda g: (0, g))
    sds = jax.ShapeDtypeStruct
    half = (n_dp // 2, width // n_dp, 3 * width)
    half_spec = pl.BlockSpec((n_dp // 2, width // n_dp, 3 * cols), lambda g: (0, 0, g))
    return pl.pallas_call(
        attend_back_kernel,
        grid=(steps,),
        in_specs=[
            pl.BlockSpec(memory_space=pltpu.SMEM), whole(normt), nat, nat, nat,
            pl.BlockSpec((cols, seq), lambda g: (g, 0)),
            pl.BlockSpec((group, seq, seq), lambda g: (g, 0, 0)),
            pl.BlockSpec((group, 1, seq), lambda g: (g, 0, 0)),
            nat,
        ],
        out_specs=[
            half_spec, half_spec, pl.BlockSpec((seq, 3 * cols), lambda g: (0, g)),
            pl.BlockSpec((group, 1, 2 * seq), lambda g: (g, 0, 0)),
        ],
        out_shape=[
            sds(half, BF16), sds(half, BF16), sds((seq, 3 * width), BF16),
            sds((heads, 1, 2 * seq), F32),
        ],
        scratch_shapes=[pltpu.VMEM((TILE, 2 * seq), F32), pltpu.VMEM((width, 3 * cols), BF16)],
        compiler_params=params(dimension_semantics=("arbitrary",)),
        cost_estimate=cost(
            6 * seq * width * width + 8 * seq * seq * width,
            2 * (6 * width * width + 8 * seq * width + heads * seq * seq),
        ),
        name="attention_backward",
    )(number, normt, q, k, v, kt, e, rinv, grad_ctx)


def first_back_kernel(cols, num_ref, tok_ref, gain_ref, gmid_ref, grads_ref, *refs):
    pieces, (gtok_ref, ggain_ref, w_ref) = refs[:-3], refs[-3:]
    width = tok_ref.shape[1]
    join_rows(num_ref, pieces, w_ref)
    grad = jnp.zeros(tok_ref.shape, F32)
    for i, start in enumerate(range(0, 3 * width, cols)):
        col = i % 3 * width + i // 3 * cols
        grad = grad + dot_nt(grads_ref[:, start : start + cols], w_ref[:, col : col + cols])
    grad_in, grad_gain = norm_back(tok_ref[...].astype(F32), gain_ref[...], grad)
    gtok_ref[...] = gmid_ref[...] + grad_in
    ggain_ref[...] = grad_gain


def first_back(number, tokens, gain, grad_middle, grads, pieces, cols):
    seq, width = tokens.shape
    vmem = pl.BlockSpec(memory_space=pltpu.VMEM)
    return pl.pallas_call(
        functools.partial(first_back_kernel, cols),
        in_specs=[pl.BlockSpec(memory_space=pltpu.SMEM)] + [vmem] * (4 + len(pieces)),
        out_shape=[
            jax.ShapeDtypeStruct((seq, width), F32), jax.ShapeDtypeStruct((1, width), F32)
        ],
        scratch_shapes=[pltpu.VMEM((width, 3 * width), BF16)],
        compiler_params=params(),
        cost_estimate=cost(6 * seq * width * width, 6 * width * width + 16 * seq * width),
        name="first_norm_backward",
    )(number, tokens, gain, grad_middle, grads, *pieces)


def output_kernel(middle_ref, target_ref, *refs):
    out_ref = refs[-1]
    total = middle_ref[...]
    for l, back in enumerate(refs[:-1]):
        rows = back.shape[0]
        total = total + dot(token_hot(target_ref[...], l * rows, rows), back[...])
    out_ref[...] = total.astype(BF16)


def output_step(middle, target_col, backs):
    seq, width = middle.shape
    slots = sum(b.shape[0] for b in backs)
    return pl.pallas_call(
        output_kernel,
        out_shape=jax.ShapeDtypeStruct((seq, width), BF16),
        compiler_params=params(),
        cost_estimate=cost(2 * slots * seq * width, 6 * seq * width + 2 * slots * width),
        name="layer_output",
    )(middle, target_col, *backs)


def flip(value, axis, bit):
    size = lax.axis_size(axis)
    return lax.ppermute(value, axis, [(i, i ^ bit) for i in range(size)])


def butterfly_sum(value, axes):
    for axis in axes:
        bit = 1
        while bit < lax.axis_size(axis):
            value = value + flip(value, axis, bit)
            bit *= 2
    return value


def after(value, *others):
    return lax.optimization_barrier((value, *others))[0]


def gather_rows(piece):
    pieces = {0: piece}
    bit = 2
    while bit < lax.axis_size("dp"):
        pieces.update({m | bit: flip(p, "dp", bit) for m, p in pieces.items()})
        bit *= 2
    return pieces


def gather_cores(pieces):
    pieces = {**pieces, **{m | 1: flip(p, "dp", 1) for m, p in pieces.items()}}
    return [pieces[m] for m in sorted(pieces)]


def reduce_y(total, dp_index):
    bit = lax.axis_size("dp") // 2
    while bit > 1:
        halves = total.reshape(2, total.shape[0] // 2, *total.shape[1:])
        mine = jnp.where((dp_index & bit) != 0, 1, 0)
        sent = lax.dynamic_index_in_dim(halves, 1 - mine, 0, keepdims=False).astype(BF16)
        kept = lax.dynamic_index_in_dim(halves, mine, 0, keepdims=False)
        total = kept + flip(sent, "dp", bit).astype(F32)
        bit //= 2
    return total[0]


def sum_expert(total):
    peers = lax.axis_size("expert")
    rows, cols = total.shape
    parts = total.astype(BF16).reshape(peers, rows // peers, cols)
    arrived = lax.all_to_all(parts, "expert", split_axis=0, concat_axis=0, tiled=True)
    return jnp.sum(arrived.astype(F32), axis=0).astype(BF16)


def spread_expert(share, peers):
    rows, cols = share.shape
    spread = jnp.broadcast_to(share[None], (peers, rows, cols))
    shared = lax.all_to_all(spread, "expert", split_axis=0, concat_axis=0, tiled=True)
    return shared.reshape(peers * rows, cols).astype(F32)


def body(
    tokens, segments, routes, slots, bucket_table, gain_attn, w_query, w_key, w_value, w_output,
    rel_bias, gain_ffn, w_router, w_in, w_out, cotangent,
):
    seq, width = tokens.shape
    buckets, heads = rel_bias.shape
    experts = w_router.shape[1]
    n_dp = lax.axis_size("dp")
    peers = lax.axis_size("expert")
    local = w_in.shape[0]
    capacity = max(2, (5 * seq + 4 * experts - 1) // (4 * experts))
    rows = peers * capacity
    dp_index = lax.axis_index("dp")
    expert_index = lax.axis_index("expert")
    number = jnp.reshape(dp_index, (1,)).astype(jnp.int32)
    group = 4
    cols = width // heads * group

    along_y = [gather_rows(w) for w in (w_query, w_key, w_value)]
    order = (routes % local) * rows + (routes // local) * capacity + slots
    target = jnp.where(slots >= 0, order, -1)
    target_row = target[None, :]
    target_col = target[:, None]
    by_peer = jnp.where(slots >= 0, routes * capacity + slots, -1)
    gain_one = gain_attn[None, :]
    gain_two = gain_ffn[None, :]

    def exchange(values):
        return lax.all_to_all(values, "expert", split_axis=0, concat_axis=0, tiled=True)

    def exchange_rows(values):
        return exchange(values.reshape(peers, capacity, width)).reshape(rows, width)

    reversed_table = jnp.concatenate([bucket_table[::-1], jnp.full((1,), -1, jnp.int32)])
    bucket_ids = jnp.arange(buckets, dtype=jnp.int32)
    hot_rev = (bucket_ids[:, None] == reversed_table[None, :]).astype(F32)
    rel_rev = jnp.dot(rel_bias.T, hot_rev, precision=HIGH)
    shifted = jnp.roll(reversed_table, 1 - TILE)
    hot_shifted = (shifted[:, None] == bucket_ids[None, :]).astype(F32)
    bias, normed, normt = prepare(rel_rev, tokens, gain_one)
    marks = jnp.arange(TILE, dtype=jnp.int32)[None, :]
    same = segments[0][:, None] == marks
    kseg = same.astype(BF16)
    qseg = jnp.where(same, 0.0, -1e9).astype(BF16)

    c_placed = place(target_row, cotangent, local, rows)
    c_here = [exchange_rows(c_placed[0])]
    along_y, bias, normed, normt, kseg, qseg, w_output, c_here[0] = lax.optimization_barrier(
        (along_y, bias, normed, normt, kseg, qseg, w_output, c_here[0])
    )
    pieces = [piece for rows_of in along_y for piece in gather_cores(rows_of)]
    router_pad = jnp.pad(w_router, ((0, 0), (0, -experts % TILE)))
    w_or = lax.all_gather(
        jnp.concatenate([w_output, router_pad], axis=1), "dp", axis=0, tiled=True
    )

    *saved, ctxt = attend(number, normed, bias, kseg, qseg, pieces, heads, group)
    for part in c_placed[1:]:
        c_here.append(exchange_rows(after(part, *pieces)))
    middle, *placed = middle_step(tokens, w_or, gain_two, target_row, ctxt, local, rows)
    placed, c_here = lax.optimization_barrier((placed, c_here))
    arrived = [None] * local
    for l in reversed(range(local)):
        ready = after(placed[l], arrived[l + 1]) if l + 1 < local else placed[l]
        arrived[l] = exchange_rows(ready)
    x_all, c_all, backs, scaled, router_terms, numbers = ([None] * local for _ in range(6))
    for l in reversed(range(local)):
        numbers[l] = jnp.stack([dp_index, expert_index * local + l]).astype(jnp.int32)
        sources = (arrived[l], c_here[l])
        if l + 1 < local:
            *sources, _ = lax.optimization_barrier((*sources, scaled[l + 1]))
        x_all[l], c_all[l] = [lax.all_gather(a, "dp", axis=0, tiled=False) for a in sources]
        scaled[l], grad_x, router_terms[l] = expert_step(
            numbers[l], arrived[l], c_here[l], w_or, w_in, w_out, l, 1024, experts
        )
        backs[l] = exchange_rows(grad_x)

    def weight_terms(l, prior):
        return expert_grads(
            numbers[l], x_all[l], c_all[l], w_or, w_in, w_out, l, n_dp, experts, prior
        )

    expert_terms = weight_terms(local - 1, ())
    backs, expert_terms = lax.optimization_barrier((backs, expert_terms))
    scaled, _ = lax.optimization_barrier((scaled, backs))
    stacked = jnp.stack([part.reshape(peers, capacity, width) for part in scaled], axis=1)
    returned = exchange(stacked.reshape(peers, local * capacity, width)).reshape(-1, width)

    grad_middle, grad_ctx, keep_o, send_o, ggain_two = middle_back(
        number, cotangent, middle, gain_two, target_col, w_or, ctxt, backs, n_dp
    )
    keep, send, grads, diag = attend_back(number, normt, *saved, grad_ctx, group, n_dp)
    crossed_o = flip(send_o, "dp", 1)
    crossed_o, send, returned = lax.optimization_barrier((crossed_o, send, returned))
    crossed = flip(send, "dp", 1)
    part_o = reduce_y(keep_o.astype(F32) + crossed_o.astype(F32), dp_index)
    part = reduce_y(keep.astype(F32) + crossed.astype(F32), dp_index)
    shard_o = spread_expert(sum_expert(part_o), peers)
    grad_tokens, ggain_one = first_back(
        number, tokens, gain_one, grad_middle, grads, pieces, cols
    )
    part, grad_tokens, ggain_one, shard_o = lax.optimization_barrier(
        (part, grad_tokens, ggain_one, shard_o)
    )
    grad_rel = jnp.dot(diag.reshape(heads, 2 * seq), hot_shifted, precision=HIGH)
    rel_row = jnp.pad(grad_rel.reshape(1, heads * buckets), ((0, 0), (0, width - heads * buckets)))
    small = butterfly_sum(
        jnp.concatenate([sum(router_terms), ggain_two, ggain_one, rel_row], axis=0), ("dp",)
    )
    small_rows = small.shape[0]
    shard_rows = width // n_dp
    extra = -(-small.size // (shard_rows * TILE)) * TILE
    flat = jnp.pad(small.reshape(-1), (0, shard_rows * extra - small.size))
    summed = sum_expert(jnp.concatenate([part, flat.reshape(shard_rows, extra)], axis=1))
    for l in reversed(range(local - 1)):
        expert_terms = weight_terms(l, expert_terms)
    summed, expert_terms = lax.optimization_barrier((summed, expert_terms))
    shards = spread_expert(summed, peers)
    output = output_step(middle, by_peer[:, None], [returned])
    small = shards[:, 3 * width :].reshape(-1)[: small_rows * width].reshape(small_rows, width)
    grad_router = lax.dynamic_slice_in_dim(small[:experts], dp_index * shard_rows, shard_rows, 1).T
    total_rel = small[experts + 2, : heads * buckets].reshape(heads, buckets).T
    shard_q, shard_k, shard_v = [
        jnp.concatenate(
            [shards[:, g + i * cols : g + (i + 1) * cols] for g in range(0, 3 * width, 3 * cols)],
            axis=1,
        )
        for i in range(3)
    ]
    return (
        output,
        grad_tokens,
        small[experts + 1],
        shard_q,
        shard_k,
        shard_v,
        shard_o,
        total_rel,
        small[experts],
        grad_router,
        expert_terms[0],
        expert_terms[1],
    )


def solution(mesh):
    in_specs = (
        P(("dp", "expert"), None),
        P(("dp", "expert"), None),
        P(("dp", "expert")),
        P(("dp", "expert")),
        P(),
        P(),
        P("dp", None),
        P("dp", None),
        P("dp", None),
        P("dp", None),
        P(),
        P(),
        P("dp", None),
        P("expert", None, None),
        P("expert", None, None),
        P(("dp", "expert"), None),
    )
    out_specs = (
        P(("dp", "expert"), None),
        P(("dp", "expert"), None),
        P(),
        P("dp", None),
        P("dp", None),
        P("dp", None),
        P("dp", None),
        P(),
        P(),
        P("dp", None),
        P("expert", None, "dp"),
        P("expert", "dp", None),
    )
    return jax.shard_map(body, mesh=mesh, in_specs=in_specs, out_specs=out_specs, check_vma=False)
```

```python
import functools
import math

import jax
import jax.numpy as jnp
from jax import lax
from jax.experimental import pallas as pl
from jax.experimental.pallas import tpu as pltpu
from jax.sharding import PartitionSpec as P

EPS = 1e-06
HIGH = lax.Precision.HIGHEST
F32 = jnp.float32
BF16 = jnp.bfloat16
VMEM_LIMIT = 56 * 1024 * 1024
TILE = 128
STRIP = 256
SUB = 256
GELU_A = math.sqrt(2.0 / math.pi)
GELU_B = 0.044715


def dot(a, b):
    return jnp.dot(a, b, preferred_element_type=F32)


def dot_nt(a, b):
    return lax.dot_general(a, b, (((1,), (1,)), ((), ())), preferred_element_type=F32)


def params(**kw):
    return pltpu.CompilerParams(vmem_limit_bytes=VMEM_LIMIT, **kw)


def cost(flops, nbytes, trans=0):
    return pl.CostEstimate(flops=int(flops), bytes_accessed=int(nbytes), transcendentals=int(trans))


def rms_scale(stream):
    return lax.rsqrt(jnp.mean(stream * stream, axis=-1, keepdims=True) + EPS)


def norm_back(stream, gain, grad_out):
    scale = rms_scale(stream)
    grad_gain = jnp.sum(grad_out * (stream * scale), axis=0, keepdims=True)
    scaled = grad_out * gain
    inner = jnp.mean(scaled * stream, axis=-1, keepdims=True)
    grad_in = scale * scaled - stream * (scale * scale * scale * inner)
    return grad_in, grad_gain


def gelu_pair(v):
    sq = v * v
    power = jnp.minimum(v * (-2.0 * GELU_A - (2.0 * GELU_A * GELU_B) * sq), 80.0)
    total = 1.0 + jnp.exp(power)
    guess = pl.reciprocal(total, approx=True)
    half = guess * (2.0 - total * guess)
    value = v * half
    slope = half + value * (1.0 - half) * (2.0 * GELU_A + (6.0 * GELU_A * GELU_B) * sq)
    return value, slope


def slot_hot(target_row, start, rows):
    seq = target_row.shape[1]
    ids = lax.broadcasted_iota(jnp.int32, (rows, seq), 0) + start
    return (ids == target_row).astype(F32).astype(BF16)


def token_hot(target_col, start, rows):
    seq = target_col.shape[0]
    ids = lax.broadcasted_iota(jnp.int32, (seq, rows), 1) + start
    return (ids == target_col).astype(F32).astype(BF16)


def place_kernel(target_ref, rows_ref, *out_refs):
    for l, out_ref in enumerate(out_refs):
        rows = out_ref.shape[0]
        out_ref[...] = dot(slot_hot(target_ref[...], l * rows, rows), rows_ref[...]).astype(BF16)


def place(target_row, values, local, rows):
    seq, width = values.shape
    return pl.pallas_call(
        place_kernel,
        out_shape=[jax.ShapeDtypeStruct((rows, width), BF16)] * local,
        compiler_params=params(),
        cost_estimate=cost(2 * local * rows * seq * width, 2 * (local * rows + seq) * width),
        name="place_cotangent",
    )(target_row, values)


def prepare_kernel(rel_ref, tok_ref, gain_ref, out_ref, normed_ref, normt_ref):
    heads, width = rel_ref.shape
    wide = out_ref.shape[2]
    for h in range(heads):
        base = jnp.broadcast_to(rel_ref[h : h + 1, :], (TILE, width))
        turned = pltpu.roll(base, width - (TILE - 1), 1, stride=1, stride_axis=0)
        out_ref[h] = turned[:, :wide]
    stream = tok_ref[...].astype(F32)
    normed = stream * rms_scale(stream) * gain_ref[...]
    normed_ref[...] = normed.astype(BF16)
    normt_ref[...] = normed.T.astype(BF16)


def prepare(rel_rev, tokens, gain):
    heads, span = rel_rev.shape
    seq, width = tokens.shape
    wide = 2 * seq - TILE
    return pl.pallas_call(
        prepare_kernel,
        out_shape=[
            jax.ShapeDtypeStruct((heads, TILE, wide), F32),
            jax.ShapeDtypeStruct((seq, width), BF16),
            jax.ShapeDtypeStruct((width, seq), BF16),
        ],
        compiler_params=params(),
        cost_estimate=cost(heads * TILE * span, 4 * heads * TILE * wide + 6 * seq * width),
        name="bias_and_first_norm",
    )(rel_rev, tokens, gain)


def attend_kernel(
    normed_ref, wq_ref, wk_ref, wv_ref, bias_ref, kseg_ref, qseg_ref,
    q_ref, k_ref, v_ref, kt_ref, e_ref, rinv_ref, ctxt_ref,
):
    seq, cols = q_ref.shape
    heads = e_ref.shape[0]
    hd = cols // heads
    per_tile = TILE // hd
    normed = normed_ref[...]
    q32 = dot(normed, wq_ref[...]).astype(BF16).astype(F32) * (1.0 / math.sqrt(hd))
    k32 = dot(normed, wk_ref[...])
    v32 = dot(normed, wv_ref[...])
    q_ref[...] = q32.astype(BF16)
    k_ref[...] = k32.astype(BF16)
    v_ref[...] = v32.astype(BF16)
    kt_ref[...] = k32.T.astype(BF16)
    vt = v32.T.astype(BF16)
    lane = lax.broadcasted_iota(jnp.int32, (STRIP, TILE), 1) // hd
    kseg = kseg_ref[...]

    def scores_of(h, start):
        sl = slice(h // per_tile * TILE, (h // per_tile + 1) * TILE)
        st = slice(start, start + STRIP)
        q_pair = q_ref[st, sl]
        q_own = jnp.where(lane == h % per_tile, q_pair, jnp.zeros_like(q_pair))
        k_all = jnp.concatenate([k_ref[:, sl], kseg], axis=1)
        return dot_nt(k_all, jnp.concatenate([q_own, qseg_ref[st]], axis=1))

    items = [(h, start) for h in range(heads) for start in range(0, seq, STRIP)]
    upcoming = scores_of(*items[0])
    for i, (h, start) in enumerate(items):
        scores = upcoming
        if i + 1 < len(items):
            upcoming = scores_of(*items[i + 1])
        parts = []
        for b in range(0, seq, TILE):
            off = seq - TILE - b + start
            parts.append(scores[b : b + TILE] + bias_ref[h, :, off : off + STRIP])
        scores = jnp.concatenate(parts, axis=0)
        e = jnp.exp(scores - jnp.max(scores, axis=0, keepdims=True))
        rinv = 1.0 / jnp.sum(e, axis=0, keepdims=True)
        eb = e.astype(BF16)
        e_ref[h, :, start : start + STRIP] = eb
        rinv_ref[h, :, start : start + STRIP] = rinv
        ctxt = dot(vt[h * hd : (h + 1) * hd], eb) * rinv
        ctxt_ref[h * hd : (h + 1) * hd, start : start + STRIP] = ctxt.astype(BF16)


def attend(normed, w_qkv, bias, kseg, qseg, heads, group):
    seq, width = normed.shape
    cols = width // heads * group
    steps = heads // group
    wide = bias.shape[2]
    whole = lambda a: pl.BlockSpec(a.shape, lambda g: (0,) * a.ndim)
    col = lambda base: pl.BlockSpec((width, cols), lambda g: (0, base * steps + g))
    nat = pl.BlockSpec((seq, cols), lambda g: (0, g))
    tr = pl.BlockSpec((cols, seq), lambda g: (g, 0))
    sds = jax.ShapeDtypeStruct
    return pl.pallas_call(
        attend_kernel,
        grid=(steps,),
        in_specs=[
            whole(normed), col(0), col(1), col(2),
            pl.BlockSpec((group, TILE, wide), lambda g: (g, 0, 0)), whole(kseg), whole(qseg),
        ],
        out_specs=[
            nat, nat, nat, tr,
            pl.BlockSpec((group, seq, seq), lambda g: (g, 0, 0)),
            pl.BlockSpec((group, 1, seq), lambda g: (g, 0, 0)),
            tr,
        ],
        out_shape=[
            sds((seq, width), BF16), sds((seq, width), BF16), sds((seq, width), BF16),
            sds((width, seq), BF16), sds((heads, seq, seq), BF16), sds((heads, 1, seq), F32),
            sds((width, seq), BF16),
        ],
        compiler_params=params(dimension_semantics=("arbitrary",)),
        cost_estimate=cost(
            6 * seq * width * width + 4 * seq * seq * width,
            2 * (3 * width * width + 9 * seq * width + heads * seq * seq) + 4 * bias.size,
            heads * seq * seq,
        ),
        name="attention_forward",
    )(normed, w_qkv, w_qkv, w_qkv, bias, kseg, qseg)


def middle_kernel(tok_ref, wo_ref, gain_ref, target_ref, ctx_ref, middle_ref, *placed_refs):
    width = tok_ref.shape[1]
    context = ctx_ref[...].astype(F32).T.astype(BF16)
    middle = tok_ref[...].astype(F32) + dot(context, wo_ref[:, :width])
    middle_ref[...] = middle
    normed = (middle * rms_scale(middle) * gain_ref[...]).astype(BF16)
    for l, placed_ref in enumerate(placed_refs):
        rows = placed_ref.shape[0]
        placed_ref[...] = dot(slot_hot(target_ref[...], l * rows, rows), normed).astype(BF16)


def middle_step(tokens, w_out, gain, target_row, ctxt, local, rows):
    seq, width = tokens.shape
    return pl.pallas_call(
        middle_kernel,
        out_shape=[jax.ShapeDtypeStruct((seq, width), F32)]
        + [jax.ShapeDtypeStruct((rows, width), BF16)] * local,
        compiler_params=params(),
        cost_estimate=cost(
            2 * seq * width * width + 2 * local * rows * seq * width,
            2 * width * width + 8 * seq * width + 2 * local * rows * width,
        ),
        name="output_projection_dispatch",
    )(tokens, w_out, gain, target_row, ctxt)


def gate_of(logits, expert):
    top = jnp.max(logits, axis=-1, keepdims=True)
    ex = jnp.exp(logits - top)
    prob = ex / jnp.sum(ex, axis=-1, keepdims=True)
    hot = lax.broadcasted_iota(jnp.int32, logits.shape, 1) == expert
    gate = jnp.sum(jnp.where(hot, prob, 0.0), axis=-1, keepdims=True)
    return prob, hot, gate


def expert_kernel(
    num_ref, x_ref, c_ref, wr_ref, win_ref, wout_ref,
    scaled_ref, grad_ref, router_ref, gp_ref, acc_p, acc_g,
):
    step = pl.program_id(0)
    experts = router_ref.shape[0]

    @pl.when(step == 0)
    def _():
        _, _, gate = gate_of(dot(x_ref[...], wr_ref[...])[:, :experts], num_ref[1])
        gp_ref[...] = (gate * c_ref[...].astype(F32)).astype(BF16)
        acc_p[...] = jnp.zeros_like(acc_p)
        acc_g[...] = jnp.zeros_like(acc_g)

    def products(sub):
        pre = dot(x_ref[...], win_ref[0, :, sub : sub + SUB])
        return pre, dot_nt(gp_ref[...], wout_ref[0, sub : sub + SUB, :])

    hiddens, grads = [], []
    upcoming = products(0)
    for sub in range(SUB, win_ref.shape[2] + SUB, SUB):
        pre, grad_hidden = upcoming
        if sub < win_ref.shape[2]:
            upcoming = products(sub)
        hidden, slope = gelu_pair(pre)
        hiddens.append(hidden.astype(BF16))
        grads.append((grad_hidden * slope).astype(BF16))
    acc_p[...] += dot(jnp.concatenate(hiddens, axis=1), wout_ref[0])
    acc_g[...] += dot_nt(jnp.concatenate(grads, axis=1), win_ref[0])

    @pl.when(step == pl.num_programs(0) - 1)
    def _():
        x = x_ref[...]
        prob, hot, gate = gate_of(dot(x, wr_ref[...])[:, :experts], num_ref[1])
        produced = acc_p[...]
        scaled_ref[...] = (gate * produced).astype(BF16)
        grad_gate = jnp.sum(
            c_ref[...].astype(F32) * produced.astype(BF16).astype(F32), axis=-1, keepdims=True
        )
        grad_logits = prob * (jnp.where(hot, grad_gate, 0.0) - gate * grad_gate)
        logits_b = grad_logits.astype(BF16)
        grad_ref[...] = (acc_g[...] + dot_nt(logits_b, wr_ref[:, :experts])).astype(BF16)
        router_ref[...] = dot(grad_logits.T.astype(BF16), x)


def expert_step(number, x, c, w_or, w_in, w_out, local, block, experts):
    rows, width = x.shape
    ff = w_in.shape[2]
    router_cols = w_or.shape[1] - width
    whole = lambda a: pl.BlockSpec(a.shape, lambda f: (0,) * a.ndim)
    row_spec = pl.BlockSpec((rows, width), lambda f: (0, 0))
    return pl.pallas_call(
        expert_kernel,
        grid=(ff // block,),
        in_specs=[
            pl.BlockSpec(memory_space=pltpu.SMEM),
            whole(x),
            whole(c),
            pl.BlockSpec((width, router_cols), lambda f: (0, width // router_cols)),
            pl.BlockSpec((1, width, block), lambda f: (local, 0, f)),
            pl.BlockSpec((1, block, width), lambda f: (local, f, 0)),
        ],
        out_specs=[row_spec, row_spec, pl.BlockSpec((experts, width), lambda f: (0, 0))],
        out_shape=[
            jax.ShapeDtypeStruct((rows, width), BF16),
            jax.ShapeDtypeStruct((rows, width), BF16),
            jax.ShapeDtypeStruct((experts, width), F32),
        ],
        scratch_shapes=[
            pltpu.VMEM((rows, width), BF16),
            pltpu.VMEM((rows, width), F32),
            pltpu.VMEM((rows, width), F32),
        ],
        compiler_params=params(dimension_semantics=("arbitrary",)),
        cost_estimate=cost(
            8 * rows * width * ff, 4 * width * ff + 8 * rows * width, rows * ff
        ),
        name="expert_rows",
    )(number, x, c, w_or, w_in, w_out)


def expert_grad_kernel(experts, num_ref, x_ref, c_ref, wr_ref, win_ref, wout_ref, *refs):
    gin_ref, gout_ref, gp_ref, xt_ref = refs[-4:]
    parts, rows, width = x_ref.shape
    x = x_ref[...].reshape(parts * rows, width)

    @pl.when(pl.program_id(0) == 0)
    def _():
        _, _, gate = gate_of(dot(x, wr_ref[...])[:, :experts], num_ref[1])
        c = c_ref[...].reshape(parts * rows, width)
        gp_ref[...] = (gate * c.astype(F32)).astype(BF16)
        xt_ref[...] = x.astype(F32).T.astype(BF16)

    gp = gp_ref[...]
    pre_t = dot_nt(win_ref[0].astype(F32).T.astype(BF16), x)
    hidden_t, slope_t = gelu_pair(pre_t)
    grad_hidden_t = dot_nt(wout_ref[0], gp)
    gout_ref[0] = dot(hidden_t.astype(BF16), gp)
    gin_ref[0] = dot_nt(xt_ref[...], (grad_hidden_t * slope_t).astype(BF16))


def expert_grads(numbers, x_all, c_all, w_or, w_in, w_out, local, n_dp, experts, prior=()):
    parts, rows, width = x_all.shape
    ff = w_in.shape[2]
    router_cols = w_or.shape[1] - width
    part = ff // n_dp
    block = 256 if part % 256 == 0 else 128
    steps = part // block
    whole = lambda a: pl.BlockSpec(a.shape, lambda f, n: (0,) * a.ndim)
    return pl.pallas_call(
        functools.partial(expert_grad_kernel, experts),
        grid_spec=pltpu.PrefetchScalarGridSpec(
            num_scalar_prefetch=1,
            grid=(steps,),
            in_specs=[
                whole(x_all),
                whole(c_all),
                pl.BlockSpec((width, router_cols), lambda f, n: (0, width // router_cols)),
                pl.BlockSpec((1, width, block), lambda f, n: (local, 0, n[0] * steps + f)),
                pl.BlockSpec((1, block, width), lambda f, n: (local, n[0] * steps + f, 0)),
            ]
            + [pl.BlockSpec(memory_space=pl.ANY)] * len(prior),
            out_specs=[
                pl.BlockSpec((1, width, block), lambda f, n: (local, 0, f)),
                pl.BlockSpec((1, block, width), lambda f, n: (local, f, 0)),
            ],
            scratch_shapes=[
                pltpu.VMEM((parts * rows, width), BF16),
                pltpu.VMEM((width, parts * rows), BF16),
            ],
        ),
        out_shape=[
            jax.ShapeDtypeStruct((w_in.shape[0], width, part), F32),
            jax.ShapeDtypeStruct((w_in.shape[0], part, width), F32),
        ],
        compiler_params=params(dimension_semantics=("arbitrary",)),
        cost_estimate=cost(
            8 * parts * rows * width * part,
            4 * parts * rows * width + 12 * width * part,
            parts * rows * part,
        ),
        input_output_aliases={6 + i: i for i in range(len(prior))},
        name="expert_weight_grads",
    )(numbers, x_all, c_all, w_or, w_in, w_out, *prior)


def split_rows(num_ref, full_ref, keep_ref, send_ref):
    part = keep_ref.shape[1]
    core = num_ref[0] & 1
    for y in range(keep_ref.shape[0]):
        own = pl.multiple_of((2 * y + core) * part, 16)
        other = pl.multiple_of((2 * y + 1 - core) * part, 16)
        keep_ref[y] = full_ref[pl.ds(own, part), :]
        send_ref[y] = full_ref[pl.ds(other, part), :]


def middle_back_kernel(num_ref, cot_ref, middle_ref, gain_ref, target_ref, wo_ref, ctx_ref, *refs):
    back_refs, (gmid_ref, gctx_ref, keep_ref, send_ref, ggain_ref, gwo_ref) = refs[:-6], refs[-6:]
    seq, width = cot_ref.shape
    target = target_ref[...]
    grad = jnp.zeros((seq, width), F32)
    for l, back in enumerate(back_refs):
        rows = back.shape[0]
        grad = grad + dot(token_hot(target, l * rows, rows), back[...])
    grad_in, grad_gain = norm_back(middle_ref[...], gain_ref[...], grad)
    ggain_ref[...] = grad_gain
    grad_middle = cot_ref[...].astype(F32) + grad_in
    gmid_ref[...] = grad_middle
    grad_attn = grad_middle.astype(BF16)
    gctx_ref[...] = dot_nt(grad_attn, wo_ref[:, :width]).astype(BF16)
    gwo_ref[...] = dot(ctx_ref[...], grad_attn).astype(BF16)
    split_rows(num_ref, gwo_ref, keep_ref, send_ref)


def middle_back(number, cot, middle, gain, target_col, w_out, ctxt, backs, n_dp):
    seq, width = cot.shape
    sds = jax.ShapeDtypeStruct
    slots = sum(b.shape[0] for b in backs)
    half = sds((n_dp // 2, width // n_dp, width), BF16)
    vmem = pl.BlockSpec(memory_space=pltpu.VMEM)
    return pl.pallas_call(
        middle_back_kernel,
        in_specs=[pl.BlockSpec(memory_space=pltpu.SMEM)] + [vmem] * (6 + len(backs)),
        out_shape=[sds((seq, width), F32), sds((seq, width), BF16), half, half, sds((1, width), F32)],
        scratch_shapes=[pltpu.VMEM((width, width), BF16)],
        compiler_params=params(),
        cost_estimate=cost(
            4 * seq * width * width + 2 * slots * seq * width,
            4 * width * width + 14 * seq * width + 2 * slots * width,
        ),
        name="second_norm_backward",
    )(number, cot, middle, gain, target_col, w_out, ctxt, *backs)


def attend_back_kernel(
    num_ref, normt_ref, q_ref, k_ref, v_ref, kt_ref, e_ref, rinv_ref, do_ref,
    keep_ref, send_ref, grads_ref, diag_ref, acc_ref, gw_ref,
):
    seq, cols = q_ref.shape
    heads = e_ref.shape[0]
    hd = cols // heads
    per_tile = TILE // hd
    lane = lax.broadcasted_iota(jnp.int32, (STRIP, TILE), 1) // hd
    row_bit = lax.broadcasted_iota(jnp.int32, (8, 2 * seq), 0)
    zero = jnp.zeros((STRIP, TILE), BF16)

    def own(ref, h, start):
        sl = slice(h // per_tile * TILE, (h // per_tile + 1) * TILE)
        return jnp.where(lane == h % per_tile, ref[start : start + STRIP, sl], zero)

    def products(h, start):
        sl = slice(h // per_tile * TILE, (h // per_tile + 1) * TILE)
        do_own = own(do_ref, h, start)
        return do_own, dot_nt(v_ref[:, sl], do_own)

    dk_tiles, dv_tiles, dqt_rows = [], [], []
    items = [(h, start) for h in range(heads) for start in range(0, seq, STRIP)]
    upcoming = products(*items[0])
    for h in range(heads):
        acc_ref[...] = jnp.zeros_like(acc_ref)
        dk = jnp.zeros((seq, TILE), F32)
        dv = jnp.zeros((seq, TILE), F32)
        dqt_parts = []
        for start in range(0, seq, STRIP):
            st = slice(start, start + STRIP)
            do_own, grad_w = upcoming
            at = items.index((h, start)) + 1
            if at < len(items):
                upcoming = products(*items[at])
            p = e_ref[h, :, st].astype(F32) * rinv_ref[h, :, st]
            t = grad_w * p
            ds = t - p * jnp.sum(t, axis=0, keepdims=True)
            dsb = ds.astype(BF16)
            dv = dv + dot(p.astype(BF16), do_own)
            dk = dk + dot(dsb, own(q_ref, h, start))
            dqt_parts.append(dot(kt_ref[h * hd : (h + 1) * hd, :], dsb))
            for b in range(0, seq, TILE):
                off = seq - TILE - b + start
                acc_ref[:, off : off + STRIP] += ds[b : b + TILE]
        if h % per_tile == 0:
            dk_tiles.append(dk)
            dv_tiles.append(dv)
        else:
            dk_tiles[-1] = dk_tiles[-1] + dk
            dv_tiles[-1] = dv_tiles[-1] + dv
        dqt_rows.append(jnp.concatenate(dqt_parts, axis=1))
        folded = acc_ref[...]
        half = TILE // 2
        while half >= 8:
            folded = folded[:half] + pltpu.roll(folded[half:], 2 * seq - half, 1)
            half //= 2
        for bit in (4, 2, 1):
            turned = pltpu.roll(folded, 2 * seq - bit, 1)
            folded = jnp.where((row_bit & bit) != 0, turned, folded)
        diag_ref[h] = jnp.sum(folded, axis=0, keepdims=True)
    dqt = jnp.concatenate(dqt_rows, axis=0) * (1.0 / math.sqrt(hd))
    grads_ref[:, :cols] = dqt.T.astype(BF16)
    for base, tiles in ((1, dk_tiles), (2, dv_tiles)):
        grads_ref[:, base * cols : (base + 1) * cols] = jnp.concatenate(tiles, axis=1).astype(BF16)
    gw_ref[...] = dot(normt_ref[...], grads_ref[...]).astype(BF16)
    split_rows(num_ref, gw_ref, keep_ref, send_ref)


def attend_back(number, normt, q, k, v, kt, e, rinv, grad_ctx, group, n_dp):
    seq, width = q.shape
    heads = e.shape[0]
    cols = width // heads * group
    steps = heads // group
    whole = lambda a: pl.BlockSpec(a.shape, lambda g: (0,) * a.ndim)
    nat = pl.BlockSpec((seq, cols), lambda g: (0, g))
    sds = jax.ShapeDtypeStruct
    half = (n_dp // 2, width // n_dp, 3 * width)
    half_spec = pl.BlockSpec((n_dp // 2, width // n_dp, 3 * cols), lambda g: (0, 0, g))
    return pl.pallas_call(
        attend_back_kernel,
        grid=(steps,),
        in_specs=[
            pl.BlockSpec(memory_space=pltpu.SMEM), whole(normt), nat, nat, nat,
            pl.BlockSpec((cols, seq), lambda g: (g, 0)),
            pl.BlockSpec((group, seq, seq), lambda g: (g, 0, 0)),
            pl.BlockSpec((group, 1, seq), lambda g: (g, 0, 0)),
            nat,
        ],
        out_specs=[
            half_spec, half_spec, pl.BlockSpec((seq, 3 * cols), lambda g: (0, g)),
            pl.BlockSpec((group, 1, 2 * seq), lambda g: (g, 0, 0)),
        ],
        out_shape=[
            sds(half, BF16), sds(half, BF16), sds((seq, 3 * width), BF16),
            sds((heads, 1, 2 * seq), F32),
        ],
        scratch_shapes=[pltpu.VMEM((TILE, 2 * seq), F32), pltpu.VMEM((width, 3 * cols), BF16)],
        compiler_params=params(dimension_semantics=("arbitrary",)),
        cost_estimate=cost(
            6 * seq * width * width + 8 * seq * seq * width,
            2 * (6 * width * width + 8 * seq * width + heads * seq * seq),
        ),
        name="attention_backward",
    )(number, normt, q, k, v, kt, e, rinv, grad_ctx)


def first_back_kernel(cols, tok_ref, gain_ref, gmid_ref, grads_ref, w_ref, gtok_ref, ggain_ref):
    width = tok_ref.shape[1]
    grad = jnp.zeros(tok_ref.shape, F32)
    for i, start in enumerate(range(0, 3 * width, cols)):
        col = i % 3 * width + i // 3 * cols
        grad = grad + dot_nt(grads_ref[:, start : start + cols], w_ref[:, col : col + cols])
    grad_in, grad_gain = norm_back(tok_ref[...].astype(F32), gain_ref[...], grad)
    gtok_ref[...] = gmid_ref[...] + grad_in
    ggain_ref[...] = grad_gain


def first_back(tokens, gain, grad_middle, grads, w_qkv, cols):
    seq, width = tokens.shape
    return pl.pallas_call(
        functools.partial(first_back_kernel, cols),
        out_shape=[
            jax.ShapeDtypeStruct((seq, width), F32), jax.ShapeDtypeStruct((1, width), F32)
        ],
        compiler_params=params(),
        cost_estimate=cost(6 * seq * width * width, 6 * width * width + 16 * seq * width),
        name="first_norm_backward",
    )(tokens, gain, grad_middle, grads, w_qkv)


def output_kernel(middle_ref, target_ref, *refs):
    out_ref = refs[-1]
    total = middle_ref[...]
    for l, back in enumerate(refs[:-1]):
        rows = back.shape[0]
        total = total + dot(token_hot(target_ref[...], l * rows, rows), back[...])
    out_ref[...] = total.astype(BF16)


def output_step(middle, target_col, backs):
    seq, width = middle.shape
    slots = sum(b.shape[0] for b in backs)
    return pl.pallas_call(
        output_kernel,
        out_shape=jax.ShapeDtypeStruct((seq, width), BF16),
        compiler_params=params(),
        cost_estimate=cost(2 * slots * seq * width, 6 * seq * width + 2 * slots * width),
        name="layer_output",
    )(middle, target_col, *backs)


def flip(value, axis, bit):
    size = lax.axis_size(axis)
    return lax.ppermute(value, axis, [(i, i ^ bit) for i in range(size)])


def butterfly_sum(value, axes):
    for axis in axes:
        bit = 1
        while bit < lax.axis_size(axis):
            value = value + flip(value, axis, bit)
            bit *= 2
    return value


def after(value, *others):
    return lax.optimization_barrier((value, *others))[0]


def reduce_y(terms, dp_index):
    first = None
    bit = lax.axis_size("dp") // 2
    while bit > 1:
        mine = jnp.where((dp_index & bit) != 0, 1, 0)
        halves = [t.reshape(2, t.shape[0] // 2, *t.shape[1:]) for t in terms]
        pick = lambda i: [
            lax.dynamic_index_in_dim(t, i, 0, keepdims=False).astype(F32) for t in halves
        ]
        sent = sum(pick(1 - mine)).astype(BF16)
        first = sent if first is None else first
        terms = [sum(pick(mine)), flip(sent, "dp", bit)]
        bit //= 2
    return sum(t.astype(F32) for t in terms)[0], first


def sum_expert(total):
    peers = lax.axis_size("expert")
    rows, cols = total.shape
    parts = total.astype(BF16).reshape(peers, rows // peers, cols)
    arrived = lax.all_to_all(parts, "expert", split_axis=0, concat_axis=0, tiled=True)
    return jnp.sum(arrived.astype(F32), axis=0).astype(BF16)


def spread_expert(share, peers):
    rows, cols = share.shape
    spread = jnp.broadcast_to(share[None], (peers, rows, cols))
    shared = lax.all_to_all(spread, "expert", split_axis=0, concat_axis=0, tiled=True)
    return shared.reshape(peers * rows, cols).astype(F32)


def body(
    tokens, segments, routes, slots, bucket_table, gain_attn, w_query, w_key, w_value, w_output,
    rel_bias, gain_ffn, w_router, w_in, w_out, cotangent,
):
    seq, width = tokens.shape
    buckets, heads = rel_bias.shape
    experts = w_router.shape[1]
    n_dp = lax.axis_size("dp")
    peers = lax.axis_size("expert")
    local = w_in.shape[0]
    capacity = max(2, (5 * seq + 4 * experts - 1) // (4 * experts))
    rows = peers * capacity
    dp_index = lax.axis_index("dp")
    expert_index = lax.axis_index("expert")
    number = jnp.reshape(dp_index, (1,)).astype(jnp.int32)
    group = 4
    cols = width // heads * group

    w_qkv = lax.all_gather(
        jnp.concatenate([w_query, w_key, w_value], axis=1), "dp", axis=0, tiled=True
    )
    router_pad = jnp.pad(w_router, ((0, 0), (0, -experts % TILE)))
    w_or = lax.all_gather(
        jnp.concatenate([w_output, router_pad], axis=1), "dp", axis=0, tiled=True
    )

    order = (routes % local) * rows + (routes // local) * capacity + slots
    target = jnp.where(slots >= 0, order, -1)
    target_row = target[None, :]
    target_col = target[:, None]
    by_peer = jnp.where(slots >= 0, routes * capacity + slots, -1)
    gain_one = gain_attn[None, :]
    gain_two = gain_ffn[None, :]

    def exchange(values):
        return lax.all_to_all(values, "expert", split_axis=0, concat_axis=0, tiled=True)

    def exchange_rows(values):
        return exchange(values.reshape(peers, capacity, width)).reshape(rows, width)

    reversed_table = jnp.concatenate([bucket_table[::-1], jnp.full((1,), -1, jnp.int32)])
    bucket_ids = jnp.arange(buckets, dtype=jnp.int32)
    hot_rev = (bucket_ids[:, None] == reversed_table[None, :]).astype(F32)
    rel_rev = jnp.dot(rel_bias.T, hot_rev, precision=HIGH)
    shifted = jnp.roll(reversed_table, 1 - TILE)
    hot_shifted = (shifted[:, None] == bucket_ids[None, :]).astype(F32)
    bias, normed, normt = prepare(rel_rev, tokens, gain_one)
    marks = jnp.arange(TILE, dtype=jnp.int32)[None, :]
    same = segments[0][:, None] == marks
    kseg = same.astype(BF16)
    qseg = jnp.where(same, 0.0, -1e9).astype(BF16)

    c_placed = place(target_row, cotangent, local, rows)
    c_here = []
    for part in c_placed:
        c_here.append(exchange_rows(after(part, c_here[-1]) if c_here else part))
    normed, *c_here = lax.optimization_barrier((normed, *c_here))
    *saved, ctxt = attend(normed, w_qkv, bias, kseg, qseg, heads, group)
    middle, *placed = middle_step(tokens, w_or, gain_two, target_row, ctxt, local, rows)
    arrived = [None] * local
    for l in reversed(range(local)):
        ready = after(placed[l], arrived[l + 1]) if l + 1 < local else placed[l]
        arrived[l] = exchange_rows(ready)
    x_all, c_all, backs, scaled, router_terms, numbers = ([None] * local for _ in range(6))
    for l in reversed(range(local)):
        numbers[l] = jnp.stack([dp_index, expert_index * local + l]).astype(jnp.int32)
        sources = (arrived[l], c_here[l])
        if l + 1 < local:
            *sources, _ = lax.optimization_barrier((*sources, scaled[l + 1]))
        x_all[l], c_all[l] = [lax.all_gather(a, "dp", axis=0, tiled=False) for a in sources]
        scaled[l], grad_x, router_terms[l] = expert_step(
            numbers[l], arrived[l], c_here[l], w_or, w_in, w_out, l, 1024, experts
        )
        backs[l] = exchange_rows(grad_x)

    def weight_terms(l, prior):
        return expert_grads(
            numbers[l], x_all[l], c_all[l], w_or, w_in, w_out, l, n_dp, experts, prior
        )

    expert_terms = weight_terms(local - 1, ())
    backs, expert_terms = lax.optimization_barrier((backs, expert_terms))
    scaled, _ = lax.optimization_barrier((scaled, backs))
    stacked = jnp.stack([part.reshape(peers, capacity, width) for part in scaled], axis=1)
    returned = exchange(stacked.reshape(peers, local * capacity, width)).reshape(-1, width)

    grad_middle, grad_ctx, keep_o, send_o, ggain_two = middle_back(
        number, cotangent, middle, gain_two, target_col, w_or, ctxt, backs, n_dp
    )
    keep, send, grads, diag = attend_back(number, normt, *saved, grad_ctx, group, n_dp)
    crossed_o = flip(send_o, "dp", 1)
    crossed_o, send, returned, x_all, c_all = lax.optimization_barrier(
        (crossed_o, send, returned, x_all, c_all)
    )
    crossed = flip(send, "dp", 1)
    part, sent = reduce_y([keep, crossed], dp_index)
    part_o, _ = reduce_y([keep_o, crossed_o], dp_index)
    if sent is not None:
        part_o = after(part_o, sent)
    shard_o = spread_expert(sum_expert(part_o), peers)
    grad_tokens, ggain_one = first_back(tokens, gain_one, grad_middle, grads, w_qkv, cols)
    part, grad_tokens, ggain_one, shard_o = lax.optimization_barrier(
        (part, grad_tokens, ggain_one, shard_o)
    )
    grad_rel = jnp.dot(diag.reshape(heads, 2 * seq), hot_shifted, precision=HIGH)
    rel_row = jnp.pad(grad_rel.reshape(1, heads * buckets), ((0, 0), (0, width - heads * buckets)))
    small = butterfly_sum(
        jnp.concatenate([sum(router_terms), ggain_two, ggain_one, rel_row], axis=0), ("dp",)
    )
    small_rows = small.shape[0]
    shard_rows = width // n_dp
    extra = -(-small.size // (shard_rows * TILE)) * TILE
    flat = jnp.pad(small.reshape(-1), (0, shard_rows * extra - small.size))
    summed = sum_expert(jnp.concatenate([part, flat.reshape(shard_rows, extra)], axis=1))
    for l in reversed(range(local - 1)):
        expert_terms = weight_terms(l, expert_terms)
    summed, expert_terms = lax.optimization_barrier((summed, expert_terms))
    shards = spread_expert(summed, peers)
    output = output_step(middle, by_peer[:, None], [returned])
    small = shards[:, 3 * width :].reshape(-1)[: small_rows * width].reshape(small_rows, width)
    grad_router = lax.dynamic_slice_in_dim(small[:experts], dp_index * shard_rows, shard_rows, 1).T
    total_rel = small[experts + 2, : heads * buckets].reshape(heads, buckets).T
    shard_q, shard_k, shard_v = [
        jnp.concatenate(
            [shards[:, g + i * cols : g + (i + 1) * cols] for g in range(0, 3 * width, 3 * cols)],
            axis=1,
        )
        for i in range(3)
    ]
    return (
        output,
        grad_tokens,
        small[experts + 1],
        shard_q,
        shard_k,
        shard_v,
        shard_o,
        total_rel,
        small[experts],
        grad_router,
        expert_terms[0],
        expert_terms[1],
    )


def solution(mesh):
    in_specs = (
        P(("dp", "expert"), None),
        P(("dp", "expert"), None),
        P(("dp", "expert")),
        P(("dp", "expert")),
        P(),
        P(),
        P("dp", None),
        P("dp", None),
        P("dp", None),
        P("dp", None),
        P(),
        P(),
        P("dp", None),
        P("expert", None, None),
        P("expert", None, None),
        P(("dp", "expert"), None),
    )
    out_specs = (
        P(("dp", "expert"), None),
        P(("dp", "expert"), None),
        P(),
        P("dp", None),
        P("dp", None),
        P("dp", None),
        P("dp", None),
        P(),
        P(),
        P("dp", None),
        P("expert", None, "dp"),
        P("expert", "dp", None),
    )
    return jax.shard_map(body, mesh=mesh, in_specs=in_specs, out_specs=out_specs, check_vma=False)
```

```python
import functools
import math

import jax
import jax.numpy as jnp
from jax import lax
from jax.experimental import pallas as pl
from jax.experimental.pallas import tpu as pltpu
from jax.sharding import PartitionSpec as P

EPS = 1e-06
HIGH = lax.Precision.HIGHEST
F32 = jnp.float32
BF16 = jnp.bfloat16
VMEM_LIMIT = 56 * 1024 * 1024
TILE = 128
STRIP = 256
SUB = 256
GELU_A = math.sqrt(2.0 / math.pi)
GELU_B = 0.044715


def dot(a, b):
    return jnp.dot(a, b, preferred_element_type=F32)


def dot_nt(a, b):
    return lax.dot_general(a, b, (((1,), (1,)), ((), ())), preferred_element_type=F32)


def params(**kw):
    return pltpu.CompilerParams(vmem_limit_bytes=VMEM_LIMIT, **kw)


def cost(flops, nbytes, trans=0):
    return pl.CostEstimate(flops=int(flops), bytes_accessed=int(nbytes), transcendentals=int(trans))


def rms_scale(stream):
    return lax.rsqrt(jnp.mean(stream * stream, axis=-1, keepdims=True) + EPS)


def norm_back(stream, gain, grad_out):
    scale = rms_scale(stream)
    grad_gain = jnp.sum(grad_out * (stream * scale), axis=0, keepdims=True)
    scaled = grad_out * gain
    inner = jnp.mean(scaled * stream, axis=-1, keepdims=True)
    grad_in = scale * scaled - stream * (scale * scale * scale * inner)
    return grad_in, grad_gain


def gelu_pair(v):
    sq = v * v
    power = jnp.minimum(v * (-2.0 * GELU_A - (2.0 * GELU_A * GELU_B) * sq), 80.0)
    total = 1.0 + jnp.exp(power)
    guess = pl.reciprocal(total, approx=True)
    half = guess * (2.0 - total * guess)
    value = v * half
    slope = half + value * (1.0 - half) * (2.0 * GELU_A + (6.0 * GELU_A * GELU_B) * sq)
    return value, slope


def slot_hot(target_row, start, rows):
    seq = target_row.shape[1]
    ids = lax.broadcasted_iota(jnp.int32, (rows, seq), 0) + start
    return (ids == target_row).astype(F32).astype(BF16)


def token_hot(target_col, start, rows):
    seq = target_col.shape[0]
    ids = lax.broadcasted_iota(jnp.int32, (seq, rows), 1) + start
    return (ids == target_col).astype(F32).astype(BF16)


def place_kernel(target_ref, rows_ref, out_ref):
    out_ref[...] = dot(slot_hot(target_ref[...], 0, out_ref.shape[0]), rows_ref[...]).astype(BF16)


def place(target_row, values, rows):
    seq, width = values.shape
    return pl.pallas_call(
        place_kernel,
        out_shape=jax.ShapeDtypeStruct((rows, width), BF16),
        compiler_params=params(),
        cost_estimate=cost(2 * rows * seq * width, 2 * (rows + seq) * width),
        name="place_cotangent",
    )(target_row, values)


def turn_kernel(w_ref, out_ref):
    out_ref[0] = w_ref[0].T


def turn(w, rows_block, cols_block):
    local, rows, cols = w.shape
    return pl.pallas_call(
        turn_kernel,
        grid=(local, rows // rows_block, cols // cols_block),
        in_specs=[pl.BlockSpec((1, rows_block, cols_block), lambda l, i, j: (l, i, j))],
        out_specs=pl.BlockSpec((1, cols_block, rows_block), lambda l, i, j: (l, j, i)),
        out_shape=jax.ShapeDtypeStruct((local, cols, rows), w.dtype),
        compiler_params=params(dimension_semantics=("arbitrary",) * 3),
        cost_estimate=cost(0, 4 * w.size),
        name="turn_weights",
    )(w)


def prepare_kernel(
    rel_ref, tok_ref, gain_ref, seg_ref, out_ref, normed_ref, normt_ref, kseg_ref, qseg_ref
):
    heads, width = rel_ref.shape
    wide = out_ref.shape[2]
    for h in range(heads):
        base = jnp.broadcast_to(rel_ref[h : h + 1, :], (TILE, width))
        turned = pltpu.roll(base, width - (TILE - 1), 1, stride=1, stride_axis=0)
        out_ref[h] = turned[:, :wide]
    stream = tok_ref[...].astype(F32)
    normed = stream * rms_scale(stream) * gain_ref[...]
    normed_ref[...] = normed.astype(BF16)
    normt_ref[...] = normed.T.astype(BF16)
    seq = tok_ref.shape[0]
    same = (lax.broadcasted_iota(jnp.int32, (TILE, seq), 0) == seg_ref[...]).astype(F32).T
    kseg_ref[...] = same.astype(BF16)
    qseg_ref[...] = ((same - 1.0) * 1e9).astype(BF16)


def prepare(rel_rev, tokens, gain, segments):
    heads, span = rel_rev.shape
    seq, width = tokens.shape
    wide = 2 * seq - TILE
    return pl.pallas_call(
        prepare_kernel,
        out_shape=[
            jax.ShapeDtypeStruct((heads, TILE, wide), F32),
            jax.ShapeDtypeStruct((seq, width), BF16),
            jax.ShapeDtypeStruct((width, seq), BF16),
            jax.ShapeDtypeStruct((seq, TILE), BF16),
            jax.ShapeDtypeStruct((seq, TILE), BF16),
        ],
        compiler_params=params(),
        cost_estimate=cost(heads * TILE * span, 4 * heads * TILE * wide + 6 * seq * width),
        name="bias_and_first_norm",
    )(rel_rev, tokens, gain, segments)


def attend_kernel(
    normed_ref, wq_ref, wk_ref, wv_ref, bias_ref, kseg_ref, qseg_ref,
    q_ref, k_ref, v_ref, kt_ref, e_ref, rinv_ref, ctxt_ref,
):
    seq, cols = q_ref.shape
    heads = e_ref.shape[0]
    hd = cols // heads
    per_tile = TILE // hd
    normed = normed_ref[...]
    q32 = dot(normed, wq_ref[...]).astype(BF16).astype(F32) * (1.0 / math.sqrt(hd))
    k32 = dot(normed, wk_ref[...])
    v32 = dot(normed, wv_ref[...])
    q_ref[...] = q32.astype(BF16)
    k_ref[...] = k32.astype(BF16)
    v_ref[...] = v32.astype(BF16)
    kt_ref[...] = k32.T.astype(BF16)
    vt = v32.T.astype(BF16)
    lane = lax.broadcasted_iota(jnp.int32, (STRIP, TILE), 1) // hd
    kseg = kseg_ref[...]

    def scores_of(h, start):
        sl = slice(h // per_tile * TILE, (h // per_tile + 1) * TILE)
        st = slice(start, start + STRIP)
        q_pair = q_ref[st, sl]
        q_own = jnp.where(lane == h % per_tile, q_pair, jnp.zeros_like(q_pair))
        k_all = jnp.concatenate([k_ref[:, sl], kseg], axis=1)
        return dot_nt(k_all, jnp.concatenate([q_own, qseg_ref[st]], axis=1))

    items = [(h, start) for h in range(heads) for start in range(0, seq, STRIP)]
    upcoming = scores_of(*items[0])
    for i, (h, start) in enumerate(items):
        scores = upcoming
        if i + 1 < len(items):
            upcoming = scores_of(*items[i + 1])
        parts = []
        for b in range(0, seq, TILE):
            off = seq - TILE - b + start
            parts.append(scores[b : b + TILE] + bias_ref[h, :, off : off + STRIP])
        scores = jnp.concatenate(parts, axis=0)
        e = jnp.exp(scores - jnp.max(scores, axis=0, keepdims=True))
        rinv = 1.0 / jnp.sum(e, axis=0, keepdims=True)
        eb = e.astype(BF16)
        e_ref[h, :, start : start + STRIP] = eb
        rinv_ref[h, :, start : start + STRIP] = rinv
        ctxt = dot(vt[h * hd : (h + 1) * hd], eb) * rinv
        ctxt_ref[h * hd : (h + 1) * hd, start : start + STRIP] = ctxt.astype(BF16)


def attend(normed, w_qkv, bias, kseg, qseg, heads, group):
    seq, width = normed.shape
    cols = width // heads * group
    steps = heads // group
    wide = bias.shape[2]
    whole = lambda a: pl.BlockSpec(a.shape, lambda g: (0,) * a.ndim)
    col = lambda base: pl.BlockSpec((width, cols), lambda g: (0, base * steps + g))
    nat = pl.BlockSpec((seq, cols), lambda g: (0, g))
    tr = pl.BlockSpec((cols, seq), lambda g: (g, 0))
    sds = jax.ShapeDtypeStruct
    return pl.pallas_call(
        attend_kernel,
        grid=(steps,),
        in_specs=[
            whole(normed), col(0), col(1), col(2),
            pl.BlockSpec((group, TILE, wide), lambda g: (g, 0, 0)), whole(kseg), whole(qseg),
        ],
        out_specs=[
            nat, nat, nat, tr,
            pl.BlockSpec((group, seq, seq), lambda g: (g, 0, 0)),
            pl.BlockSpec((group, 1, seq), lambda g: (g, 0, 0)),
            tr,
        ],
        out_shape=[
            sds((seq, width), BF16), sds((seq, width), BF16), sds((seq, width), BF16),
            sds((width, seq), BF16), sds((heads, seq, seq), BF16), sds((heads, 1, seq), F32),
            sds((width, seq), BF16),
        ],
        compiler_params=params(dimension_semantics=("arbitrary",)),
        cost_estimate=cost(
            6 * seq * width * width + 4 * seq * seq * width,
            2 * (3 * width * width + 9 * seq * width + heads * seq * seq) + 4 * bias.size,
            heads * seq * seq,
        ),
        name="attention_forward",
    )(normed, w_qkv, w_qkv, w_qkv, bias, kseg, qseg)


def middle_kernel(tok_ref, wo_ref, gain_ref, target_ref, ctx_ref, middle_ref, *placed_refs):
    width = tok_ref.shape[1]
    context = ctx_ref[...].astype(F32).T.astype(BF16)
    middle = tok_ref[...].astype(F32) + dot(context, wo_ref[:, :width])
    middle_ref[...] = middle
    normed = (middle * rms_scale(middle) * gain_ref[...]).astype(BF16)
    for l, placed_ref in enumerate(placed_refs):
        rows = placed_ref.shape[0]
        placed_ref[...] = dot(slot_hot(target_ref[...], l * rows, rows), normed).astype(BF16)


def middle_step(tokens, w_out, gain, target_row, ctxt, local, rows):
    seq, width = tokens.shape
    return pl.pallas_call(
        middle_kernel,
        out_shape=[jax.ShapeDtypeStruct((seq, width), F32)]
        + [jax.ShapeDtypeStruct((rows, width), BF16)] * local,
        compiler_params=params(),
        cost_estimate=cost(
            2 * seq * width * width + 2 * local * rows * seq * width,
            2 * width * width + 8 * seq * width + 2 * local * rows * width,
        ),
        name="output_projection_dispatch",
    )(tokens, w_out, gain, target_row, ctxt)


def gate_of(logits, expert):
    top = jnp.max(logits, axis=-1, keepdims=True)
    ex = jnp.exp(logits - top)
    prob = ex / jnp.sum(ex, axis=-1, keepdims=True)
    hot = lax.broadcasted_iota(jnp.int32, logits.shape, 1) == expert
    gate = jnp.sum(jnp.where(hot, prob, 0.0), axis=-1, keepdims=True)
    return prob, hot, gate


def expert_kernel(
    num_ref, x_ref, c_ref, wr_ref, win_ref, wout_ref, wint_ref, woutt_ref,
    scaled_ref, grad_ref, router_ref, gp_ref, acc_p, acc_g,
):
    step = pl.program_id(0)
    experts = router_ref.shape[0]

    @pl.when(step == 0)
    def _():
        _, _, gate = gate_of(dot(x_ref[...], wr_ref[...])[:, :experts], num_ref[1])
        gp_ref[...] = (gate * c_ref[...].astype(F32)).astype(BF16)
        acc_p[...] = jnp.zeros_like(acc_p)
        acc_g[...] = jnp.zeros_like(acc_g)

    def products(sub):
        pre = dot(x_ref[...], win_ref[0, :, sub : sub + SUB])
        return pre, dot(gp_ref[...], woutt_ref[0, :, sub : sub + SUB])

    hiddens, grads = [], []
    upcoming = products(0)
    for sub in range(SUB, win_ref.shape[2] + SUB, SUB):
        pre, grad_hidden = upcoming
        if sub < win_ref.shape[2]:
            upcoming = products(sub)
        hidden, slope = gelu_pair(pre)
        hiddens.append(hidden.astype(BF16))
        grads.append((grad_hidden * slope).astype(BF16))
    acc_p[...] += dot(jnp.concatenate(hiddens, axis=1), wout_ref[0])
    acc_g[...] += dot(jnp.concatenate(grads, axis=1), wint_ref[0])

    @pl.when(step == pl.num_programs(0) - 1)
    def _():
        x = x_ref[...]
        prob, hot, gate = gate_of(dot(x, wr_ref[...])[:, :experts], num_ref[1])
        produced = acc_p[...]
        scaled_ref[...] = (gate * produced).astype(BF16)
        grad_gate = jnp.sum(
            c_ref[...].astype(F32) * produced.astype(BF16).astype(F32), axis=-1, keepdims=True
        )
        grad_logits = prob * (jnp.where(hot, grad_gate, 0.0) - gate * grad_gate)
        logits_b = grad_logits.astype(BF16)
        grad_ref[...] = (acc_g[...] + dot_nt(logits_b, wr_ref[:, :experts])).astype(BF16)
        router_ref[...] = dot(grad_logits.T.astype(BF16), x)


def expert_step(number, x, c, w_or, w_in, w_out, w_in_t, w_out_t, local, block, experts):
    rows, width = x.shape
    ff = w_in.shape[2]
    router_cols = w_or.shape[1] - width
    whole = lambda a: pl.BlockSpec(a.shape, lambda f: (0,) * a.ndim)
    row_spec = pl.BlockSpec((rows, width), lambda f: (0, 0))
    return pl.pallas_call(
        expert_kernel,
        grid=(ff // block,),
        in_specs=[
            pl.BlockSpec(memory_space=pltpu.SMEM),
            whole(x),
            whole(c),
            pl.BlockSpec((width, router_cols), lambda f: (0, width // router_cols)),
            pl.BlockSpec((1, width, block), lambda f: (local, 0, f)),
            pl.BlockSpec((1, block, width), lambda f: (local, f, 0)),
            pl.BlockSpec((1, block, width), lambda f: (local, f, 0)),
            pl.BlockSpec((1, width, block), lambda f: (local, 0, f)),
        ],
        out_specs=[row_spec, row_spec, pl.BlockSpec((experts, width), lambda f: (0, 0))],
        out_shape=[
            jax.ShapeDtypeStruct((rows, width), BF16),
            jax.ShapeDtypeStruct((rows, width), BF16),
            jax.ShapeDtypeStruct((experts, width), F32),
        ],
        scratch_shapes=[
            pltpu.VMEM((rows, width), BF16),
            pltpu.VMEM((rows, width), F32),
            pltpu.VMEM((rows, width), F32),
        ],
        compiler_params=params(dimension_semantics=("arbitrary",)),
        cost_estimate=cost(
            8 * rows * width * ff, 4 * width * ff + 8 * rows * width, rows * ff
        ),
        name="expert_rows",
    )(number, x, c, w_or, w_in, w_out, w_in_t, w_out_t)


def expert_grad_kernel(experts, num_ref, x_ref, c_ref, wr_ref, wint_ref, wout_ref, *refs):
    gin_ref, gout_ref, gp_ref, xt_ref = refs[-4:]
    parts, rows, width = x_ref.shape
    x = x_ref[...].reshape(parts * rows, width)

    @pl.when(pl.program_id(0) == 0)
    def _():
        _, _, gate = gate_of(dot(x, wr_ref[...])[:, :experts], num_ref[1])
        c = c_ref[...].reshape(parts * rows, width)
        gp_ref[...] = (gate * c.astype(F32)).astype(BF16)
        xt_ref[...] = x.astype(F32).T.astype(BF16)

    gp = gp_ref[...]
    pre_t = dot(wint_ref[0], xt_ref[...])
    hidden_t, slope_t = gelu_pair(pre_t)
    grad_hidden_t = dot_nt(wout_ref[0], gp)
    gout_ref[0] = dot(hidden_t.astype(BF16), gp)
    gin_ref[0] = dot_nt(xt_ref[...], (grad_hidden_t * slope_t).astype(BF16))


def expert_grads(numbers, x_all, c_all, w_or, w_in_t, w_out, local, n_dp, experts, prior=()):
    parts, rows, width = x_all.shape
    ff = w_out.shape[1]
    router_cols = w_or.shape[1] - width
    part = ff // n_dp
    block = 256 if part % 256 == 0 else 128
    steps = part // block
    whole = lambda a: pl.BlockSpec(a.shape, lambda f, n: (0,) * a.ndim)
    return pl.pallas_call(
        functools.partial(expert_grad_kernel, experts),
        grid_spec=pltpu.PrefetchScalarGridSpec(
            num_scalar_prefetch=1,
            grid=(steps,),
            in_specs=[
                whole(x_all),
                whole(c_all),
                pl.BlockSpec((width, router_cols), lambda f, n: (0, width // router_cols)),
                pl.BlockSpec((1, block, width), lambda f, n: (local, n[0] * steps + f, 0)),
                pl.BlockSpec((1, block, width), lambda f, n: (local, n[0] * steps + f, 0)),
            ]
            + [pl.BlockSpec(memory_space=pl.ANY)] * len(prior),
            out_specs=[
                pl.BlockSpec((1, width, block), lambda f, n: (local, 0, f)),
                pl.BlockSpec((1, block, width), lambda f, n: (local, f, 0)),
            ],
            scratch_shapes=[
                pltpu.VMEM((parts * rows, width), BF16),
                pltpu.VMEM((width, parts * rows), BF16),
            ],
        ),
        out_shape=[
            jax.ShapeDtypeStruct((w_out.shape[0], width, part), F32),
            jax.ShapeDtypeStruct((w_out.shape[0], part, width), F32),
        ],
        compiler_params=params(dimension_semantics=("arbitrary",)),
        cost_estimate=cost(
            8 * parts * rows * width * part,
            4 * parts * rows * width + 12 * width * part,
            parts * rows * part,
        ),
        input_output_aliases={6 + i: i for i in range(len(prior))},
        name="expert_weight_grads",
    )(numbers, x_all, c_all, w_or, w_in_t, w_out, *prior)


def split_rows(num_ref, full_ref, keep_ref, send_ref):
    part = keep_ref.shape[1]
    core = num_ref[0] & 1
    for y in range(keep_ref.shape[0]):
        own = pl.multiple_of((2 * y + core) * part, 16)
        other = pl.multiple_of((2 * y + 1 - core) * part, 16)
        keep_ref[y] = full_ref[pl.ds(own, part), :]
        send_ref[y] = full_ref[pl.ds(other, part), :]


def middle_back_kernel(num_ref, cot_ref, middle_ref, gain_ref, target_ref, wo_ref, ctx_ref, *refs):
    back_refs, (gmid_ref, gctx_ref, keep_ref, send_ref, ggain_ref, gwo_ref) = refs[:-6], refs[-6:]
    seq, width = cot_ref.shape
    target = target_ref[...]
    grad = jnp.zeros((seq, width), F32)
    for l, back in enumerate(back_refs):
        rows = back.shape[0]
        grad = grad + dot(token_hot(target, l * rows, rows), back[...])
    grad_in, grad_gain = norm_back(middle_ref[...], gain_ref[...], grad)
    ggain_ref[...] = grad_gain
    grad_middle = cot_ref[...].astype(F32) + grad_in
    gmid_ref[...] = grad_middle
    grad_attn = grad_middle.astype(BF16)
    gctx_ref[...] = dot_nt(grad_attn, wo_ref[:, :width]).astype(BF16)
    gwo_ref[...] = dot(ctx_ref[...], grad_attn).astype(BF16)
    split_rows(num_ref, gwo_ref, keep_ref, send_ref)


def middle_back(number, cot, middle, gain, target_col, w_out, ctxt, backs, n_dp):
    seq, width = cot.shape
    sds = jax.ShapeDtypeStruct
    slots = sum(b.shape[0] for b in backs)
    half = sds((n_dp // 2, width // n_dp, width), BF16)
    vmem = pl.BlockSpec(memory_space=pltpu.VMEM)
    return pl.pallas_call(
        middle_back_kernel,
        in_specs=[pl.BlockSpec(memory_space=pltpu.SMEM)] + [vmem] * (6 + len(backs)),
        out_shape=[sds((seq, width), F32), sds((seq, width), BF16), half, half, sds((1, width), F32)],
        scratch_shapes=[pltpu.VMEM((width, width), BF16)],
        compiler_params=params(),
        cost_estimate=cost(
            4 * seq * width * width + 2 * slots * seq * width,
            4 * width * width + 14 * seq * width + 2 * slots * width,
        ),
        name="second_norm_backward",
    )(number, cot, middle, gain, target_col, w_out, ctxt, *backs)


def attend_back_kernel(
    num_ref, normt_ref, q_ref, k_ref, v_ref, kt_ref, e_ref, rinv_ref, do_ref,
    keep_ref, send_ref, grads_ref, diag_ref, acc_ref, gw_ref,
):
    seq, cols = q_ref.shape
    heads = e_ref.shape[0]
    hd = cols // heads
    per_tile = TILE // hd
    lane = lax.broadcasted_iota(jnp.int32, (STRIP, TILE), 1) // hd
    row_bit = lax.broadcasted_iota(jnp.int32, (8, 2 * seq), 0)
    zero = jnp.zeros((STRIP, TILE), BF16)

    def own(ref, h, start):
        sl = slice(h // per_tile * TILE, (h // per_tile + 1) * TILE)
        return jnp.where(lane == h % per_tile, ref[start : start + STRIP, sl], zero)

    def products(h, start):
        sl = slice(h // per_tile * TILE, (h // per_tile + 1) * TILE)
        do_own = own(do_ref, h, start)
        return do_own, dot_nt(v_ref[:, sl], do_own)

    dk_tiles, dv_tiles, dqt_rows = [], [], []
    items = [(h, start) for h in range(heads) for start in range(0, seq, STRIP)]
    upcoming = products(*items[0])
    for h in range(heads):
        acc_ref[...] = jnp.zeros_like(acc_ref)
        dk = jnp.zeros((seq, TILE), F32)
        dv = jnp.zeros((seq, TILE), F32)
        dqt_parts = []
        for start in range(0, seq, STRIP):
            st = slice(start, start + STRIP)
            do_own, grad_w = upcoming
            at = items.index((h, start)) + 1
            if at < len(items):
                upcoming = products(*items[at])
            p = e_ref[h, :, st].astype(F32) * rinv_ref[h, :, st]
            t = grad_w * p
            ds = t - p * jnp.sum(t, axis=0, keepdims=True)
            dsb = ds.astype(BF16)
            dv = dv + dot(p.astype(BF16), do_own)
            dk = dk + dot(dsb, own(q_ref, h, start))
            dqt_parts.append(dot(kt_ref[h * hd : (h + 1) * hd, :], dsb))
            for b in range(0, seq, TILE):
                off = seq - TILE - b + start
                acc_ref[:, off : off + STRIP] += ds[b : b + TILE]
        if h % per_tile == 0:
            dk_tiles.append(dk)
            dv_tiles.append(dv)
        else:
            dk_tiles[-1] = dk_tiles[-1] + dk
            dv_tiles[-1] = dv_tiles[-1] + dv
        dqt_rows.append(jnp.concatenate(dqt_parts, axis=1))
        folded = acc_ref[...]
        half = TILE // 2
        while half >= 8:
            folded = folded[:half] + pltpu.roll(folded[half:], 2 * seq - half, 1)
            half //= 2
        for bit in (4, 2, 1):
            turned = pltpu.roll(folded, 2 * seq - bit, 1)
            folded = jnp.where((row_bit & bit) != 0, turned, folded)
        diag_ref[h] = jnp.sum(folded, axis=0, keepdims=True)
    dqt = jnp.concatenate(dqt_rows, axis=0) * (1.0 / math.sqrt(hd))
    grads_ref[:, :cols] = dqt.T.astype(BF16)
    for base, tiles in ((1, dk_tiles), (2, dv_tiles)):
        grads_ref[:, base * cols : (base + 1) * cols] = jnp.concatenate(tiles, axis=1).astype(BF16)
    gw_ref[...] = dot(normt_ref[...], grads_ref[...]).astype(BF16)
    split_rows(num_ref, gw_ref, keep_ref, send_ref)


def attend_back(number, normt, q, k, v, kt, e, rinv, grad_ctx, group, n_dp):
    seq, width = q.shape
    heads = e.shape[0]
    cols = width // heads * group
    steps = heads // group
    whole = lambda a: pl.BlockSpec(a.shape, lambda g: (0,) * a.ndim)
    nat = pl.BlockSpec((seq, cols), lambda g: (0, g))
    sds = jax.ShapeDtypeStruct
    half = (n_dp // 2, width // n_dp, 3 * width)
    half_spec = pl.BlockSpec((n_dp // 2, width // n_dp, 3 * cols), lambda g: (0, 0, g))
    return pl.pallas_call(
        attend_back_kernel,
        grid=(steps,),
        in_specs=[
            pl.BlockSpec(memory_space=pltpu.SMEM), whole(normt), nat, nat, nat,
            pl.BlockSpec((cols, seq), lambda g: (g, 0)),
            pl.BlockSpec((group, seq, seq), lambda g: (g, 0, 0)),
            pl.BlockSpec((group, 1, seq), lambda g: (g, 0, 0)),
            nat,
        ],
        out_specs=[
            half_spec, half_spec, pl.BlockSpec((seq, 3 * cols), lambda g: (0, g)),
            pl.BlockSpec((group, 1, 2 * seq), lambda g: (g, 0, 0)),
        ],
        out_shape=[
            sds(half, BF16), sds(half, BF16), sds((seq, 3 * width), BF16),
            sds((heads, 1, 2 * seq), F32),
        ],
        scratch_shapes=[pltpu.VMEM((TILE, 2 * seq), F32), pltpu.VMEM((width, 3 * cols), BF16)],
        compiler_params=params(dimension_semantics=("arbitrary",)),
        cost_estimate=cost(
            6 * seq * width * width + 8 * seq * seq * width,
            2 * (6 * width * width + 8 * seq * width + heads * seq * seq),
        ),
        name="attention_backward",
    )(number, normt, q, k, v, kt, e, rinv, grad_ctx)


def first_back_kernel(cols, tok_ref, gain_ref, gmid_ref, grads_ref, w_ref, gtok_ref, ggain_ref):
    width = tok_ref.shape[1]
    grad = jnp.zeros(tok_ref.shape, F32)
    for i, start in enumerate(range(0, 3 * width, cols)):
        col = i % 3 * width + i // 3 * cols
        grad = grad + dot_nt(grads_ref[:, start : start + cols], w_ref[:, col : col + cols])
    grad_in, grad_gain = norm_back(tok_ref[...].astype(F32), gain_ref[...], grad)
    gtok_ref[...] = gmid_ref[...] + grad_in
    ggain_ref[...] = grad_gain


def first_back(tokens, gain, grad_middle, grads, w_qkv, cols):
    seq, width = tokens.shape
    return pl.pallas_call(
        functools.partial(first_back_kernel, cols),
        out_shape=[
            jax.ShapeDtypeStruct((seq, width), F32), jax.ShapeDtypeStruct((1, width), F32)
        ],
        compiler_params=params(),
        cost_estimate=cost(6 * seq * width * width, 6 * width * width + 16 * seq * width),
        name="first_norm_backward",
    )(tokens, gain, grad_middle, grads, w_qkv)


def output_kernel(middle_ref, target_ref, *refs):
    out_ref = refs[-1]
    total = middle_ref[...]
    for l, back in enumerate(refs[:-1]):
        rows = back.shape[0]
        total = total + dot(token_hot(target_ref[...], l * rows, rows), back[...])
    out_ref[...] = total.astype(BF16)


def output_step(middle, target_col, backs):
    seq, width = middle.shape
    slots = sum(b.shape[0] for b in backs)
    return pl.pallas_call(
        output_kernel,
        out_shape=jax.ShapeDtypeStruct((seq, width), BF16),
        compiler_params=params(),
        cost_estimate=cost(2 * slots * seq * width, 6 * seq * width + 2 * slots * width),
        name="layer_output",
    )(middle, target_col, *backs)


def flip(value, axis, bit):
    size = lax.axis_size(axis)
    return lax.ppermute(value, axis, [(i, i ^ bit) for i in range(size)])


def butterfly_sum(value, axes):
    for axis in axes:
        bit = 1
        while bit < lax.axis_size(axis):
            value = value + flip(value, axis, bit)
            bit *= 2
    return value


def after(value, *others):
    return lax.optimization_barrier((value, *others))[0]


def reduce_y(terms, dp_index):
    first = None
    bit = lax.axis_size("dp") // 2
    while bit > 1:
        mine = jnp.where((dp_index & bit) != 0, 1, 0)
        halves = [t.reshape(2, t.shape[0] // 2, *t.shape[1:]) for t in terms]
        pick = lambda i: [
            lax.dynamic_index_in_dim(t, i, 0, keepdims=False).astype(F32) for t in halves
        ]
        sent = sum(pick(1 - mine)).astype(BF16)
        first = sent if first is None else first
        terms = [sum(pick(mine)), flip(sent, "dp", bit)]
        bit //= 2
    return sum(t.astype(F32) for t in terms)[0], first


def sum_expert(total):
    peers = lax.axis_size("expert")
    rows, cols = total.shape
    parts = total.astype(BF16).reshape(peers, rows // peers, cols)
    arrived = lax.all_to_all(parts, "expert", split_axis=0, concat_axis=0, tiled=True)
    return jnp.sum(arrived.astype(F32), axis=0).astype(BF16)


def spread_expert(share, peers):
    rows, cols = share.shape
    spread = jnp.broadcast_to(share[None], (peers, rows, cols))
    shared = lax.all_to_all(spread, "expert", split_axis=0, concat_axis=0, tiled=True)
    return shared.reshape(peers * rows, cols).astype(F32)


def body(
    tokens, segments, routes, slots, bucket_table, gain_attn, w_query, w_key, w_value, w_output,
    rel_bias, gain_ffn, w_router, w_in, w_out, cotangent,
):
    seq, width = tokens.shape
    buckets, heads = rel_bias.shape
    experts = w_router.shape[1]
    n_dp = lax.axis_size("dp")
    peers = lax.axis_size("expert")
    local = w_in.shape[0]
    capacity = max(2, (5 * seq + 4 * experts - 1) // (4 * experts))
    rows = peers * capacity
    dp_index = lax.axis_index("dp")
    expert_index = lax.axis_index("expert")
    number = jnp.reshape(dp_index, (1,)).astype(jnp.int32)
    group = 4
    cols = width // heads * group

    w_qkv = lax.all_gather(
        jnp.concatenate([w_query, w_key, w_value], axis=1), "dp", axis=0, tiled=True
    )
    router_pad = jnp.pad(w_router, ((0, 0), (0, -experts % TILE)))
    w_or = lax.all_gather(
        jnp.concatenate([w_output, router_pad], axis=1), "dp", axis=0, tiled=True
    )

    order = (routes % local) * rows + (routes // local) * capacity + slots
    target = jnp.where(slots >= 0, order, -1)
    target_row = target[None, :]
    target_col = target[:, None]
    by_peer = jnp.where(slots >= 0, routes * capacity + slots, -1)
    gain_one = gain_attn[None, :]
    gain_two = gain_ffn[None, :]

    def exchange(values):
        return lax.all_to_all(values, "expert", split_axis=0, concat_axis=0, tiled=True)

    def exchange_rows(values):
        return exchange(values.reshape(peers, capacity, width)).reshape(rows, width)

    reversed_table = jnp.concatenate([bucket_table[::-1], jnp.full((1,), -1, jnp.int32)])
    bucket_ids = jnp.arange(buckets, dtype=jnp.int32)
    hot_rev = (bucket_ids[:, None] == reversed_table[None, :]).astype(F32)
    rel_rev = jnp.dot(rel_bias.T, hot_rev, precision=HIGH)
    shifted = jnp.roll(reversed_table, 1 - TILE)
    hot_shifted = (shifted[:, None] == bucket_ids[None, :]).astype(F32)
    bias, normed, normt, kseg, qseg = prepare(rel_rev, tokens, gain_one, segments)
    w_in_t = turn(w_in, width, 768)
    w_out_t = turn(w_out, 768, width)
    c_placed = place(by_peer[None, :], cotangent, local * rows)
    c_got = exchange(c_placed.reshape(peers, local * capacity, width))
    normed, bias, kseg, qseg, w_in_t, w_out_t, c_got = lax.optimization_barrier(
        (normed, bias, kseg, qseg, w_in_t, w_out_t, c_got)
    )
    c_split = c_got.reshape(peers, local, capacity, width)
    c_here = [c_split[:, l].reshape(rows, width) for l in range(local)]
    *saved, ctxt = attend(normed, w_qkv, bias, kseg, qseg, heads, group)
    middle, *placed = middle_step(tokens, w_or, gain_two, target_row, ctxt, local, rows)
    arrived = [None] * local
    for l in reversed(range(local)):
        ready = after(placed[l], arrived[l + 1]) if l + 1 < local else placed[l]
        arrived[l] = exchange_rows(ready)
    x_all, c_all, backs, scaled, router_terms, numbers = ([None] * local for _ in range(6))
    for l in reversed(range(local)):
        numbers[l] = jnp.stack([dp_index, expert_index * local + l]).astype(jnp.int32)
        sources = (arrived[l], c_here[l])
        if l + 1 < local:
            *sources, _ = lax.optimization_barrier((*sources, scaled[l + 1]))
        x_all[l], c_all[l] = [lax.all_gather(a, "dp", axis=0, tiled=False) for a in sources]
        scaled[l], grad_x, router_terms[l] = expert_step(
            numbers[l], arrived[l], c_here[l], w_or, w_in, w_out, w_in_t, w_out_t, l, 768, experts
        )
        backs[l] = exchange_rows(grad_x)

    def weight_terms(l, prior):
        return expert_grads(
            numbers[l], x_all[l], c_all[l], w_or, w_in_t, w_out, l, n_dp, experts, prior
        )

    expert_terms = weight_terms(local - 1, ())
    backs, expert_terms = lax.optimization_barrier((backs, expert_terms))
    scaled, _ = lax.optimization_barrier((scaled, backs))
    stacked = jnp.stack([part.reshape(peers, capacity, width) for part in scaled], axis=1)
    returned = exchange(stacked.reshape(peers, local * capacity, width)).reshape(-1, width)

    grad_middle, grad_ctx, keep_o, send_o, ggain_two = middle_back(
        number, cotangent, middle, gain_two, target_col, w_or, ctxt, backs, n_dp
    )
    keep, send, grads, diag = attend_back(number, normt, *saved, grad_ctx, group, n_dp)
    crossed_o = flip(send_o, "dp", 1)
    crossed_o, send, returned, x_all, c_all = lax.optimization_barrier(
        (crossed_o, send, returned, x_all, c_all)
    )
    crossed = flip(send, "dp", 1)
    part, sent = reduce_y([keep, crossed], dp_index)
    part_o, _ = reduce_y([keep_o, crossed_o], dp_index)
    grad_tokens, ggain_one = first_back(tokens, gain_one, grad_middle, grads, w_qkv, cols)
    part_o = after(part_o, grad_tokens, *([] if sent is None else [sent]))
    summed_o = sum_expert(part_o)
    part, grad_tokens, ggain_one, summed_o = lax.optimization_barrier(
        (part, grad_tokens, ggain_one, summed_o)
    )
    grad_rel = jnp.dot(diag.reshape(heads, 2 * seq), hot_shifted, precision=HIGH)
    rel_row = jnp.pad(grad_rel.reshape(1, heads * buckets), ((0, 0), (0, width - heads * buckets)))
    small = butterfly_sum(
        jnp.concatenate([sum(router_terms), ggain_two, ggain_one, rel_row], axis=0), ("dp",)
    )
    small_rows = small.shape[0]
    shard_rows = width // n_dp
    extra = -(-small.size // (shard_rows * TILE)) * TILE
    flat = jnp.pad(small.reshape(-1), (0, shard_rows * extra - small.size))
    summed = sum_expert(jnp.concatenate([part, flat.reshape(shard_rows, extra)], axis=1))
    for l in reversed(range(local - 1)):
        expert_terms = weight_terms(l, expert_terms)
    summed, expert_terms = lax.optimization_barrier((summed, expert_terms))
    shards = spread_expert(jnp.concatenate([summed, summed_o], axis=1), peers)
    shard_o = shards[:, 3 * width + extra :]
    output = output_step(middle, by_peer[:, None], [returned])
    small = shards[:, 3 * width : 3 * width + extra].reshape(-1)[: small_rows * width].reshape(small_rows, width)
    grad_router = lax.dynamic_slice_in_dim(small[:experts], dp_index * shard_rows, shard_rows, 1).T
    total_rel = small[experts + 2, : heads * buckets].reshape(heads, buckets).T
    shard_q, shard_k, shard_v = [
        jnp.concatenate(
            [shards[:, g + i * cols : g + (i + 1) * cols] for g in range(0, 3 * width, 3 * cols)],
            axis=1,
        )
        for i in range(3)
    ]
    return (
        output,
        grad_tokens,
        small[experts + 1],
        shard_q,
        shard_k,
        shard_v,
        shard_o,
        total_rel,
        small[experts],
        grad_router,
        expert_terms[0],
        expert_terms[1],
    )


def solution(mesh):
    in_specs = (
        P(("dp", "expert"), None),
        P(("dp", "expert"), None),
        P(("dp", "expert")),
        P(("dp", "expert")),
        P(),
        P(),
        P("dp", None),
        P("dp", None),
        P("dp", None),
        P("dp", None),
        P(),
        P(),
        P("dp", None),
        P("expert", None, None),
        P("expert", None, None),
        P(("dp", "expert"), None),
    )
    out_specs = (
        P(("dp", "expert"), None),
        P(("dp", "expert"), None),
        P(),
        P("dp", None),
        P("dp", None),
        P("dp", None),
        P("dp", None),
        P(),
        P(),
        P("dp", None),
        P("expert", None, "dp"),
        P("expert", "dp", None),
    )
    return jax.shard_map(body, mesh=mesh, in_specs=in_specs, out_specs=out_specs, check_vma=False)
```

```python
import functools
import math

import jax
import jax.numpy as jnp
from jax import lax
from jax.experimental import pallas as pl
from jax.experimental.pallas import tpu as pltpu
from jax.sharding import PartitionSpec as P

EPS = 1e-06
HIGH = lax.Precision.HIGHEST
F32 = jnp.float32
BF16 = jnp.bfloat16
VMEM_LIMIT = 56 * 1024 * 1024
TILE = 128
STRIP = 256
SUB = 256
GELU_A = math.sqrt(2.0 / math.pi)
GELU_B = 0.044715


def dot(a, b):
    return jnp.dot(a, b, preferred_element_type=F32)


def dot_nt(a, b):
    return lax.dot_general(a, b, (((1,), (1,)), ((), ())), preferred_element_type=F32)


def params(**kw):
    return pltpu.CompilerParams(vmem_limit_bytes=VMEM_LIMIT, **kw)


def cost(flops, nbytes, trans=0):
    return pl.CostEstimate(flops=int(flops), bytes_accessed=int(nbytes), transcendentals=int(trans))


def rms_scale(stream):
    return lax.rsqrt(jnp.mean(stream * stream, axis=-1, keepdims=True) + EPS)


def norm_back(stream, gain, grad_out):
    scale = rms_scale(stream)
    grad_gain = jnp.sum(grad_out * (stream * scale), axis=0, keepdims=True)
    scaled = grad_out * gain
    inner = jnp.mean(scaled * stream, axis=-1, keepdims=True)
    grad_in = scale * scaled - stream * (scale * scale * scale * inner)
    return grad_in, grad_gain


def gelu_pair(v):
    sq = v * v
    power = jnp.minimum(v * (-2.0 * GELU_A - (2.0 * GELU_A * GELU_B) * sq), 80.0)
    total = 1.0 + jnp.exp(power)
    guess = pl.reciprocal(total, approx=True)
    half = guess * (2.0 - total * guess)
    value = v * half
    slope = half + value * (1.0 - half) * (2.0 * GELU_A + (6.0 * GELU_A * GELU_B) * sq)
    return value, slope


def slot_hot(target_row, start, rows):
    seq = target_row.shape[1]
    ids = lax.broadcasted_iota(jnp.int32, (rows, seq), 0) + start
    return (ids == target_row).astype(F32).astype(BF16)


def token_hot(target_col, start, rows):
    seq = target_col.shape[0]
    ids = lax.broadcasted_iota(jnp.int32, (seq, rows), 1) + start
    return (ids == target_col).astype(F32).astype(BF16)


def place_kernel(target_ref, rows_ref, out_ref):
    out_ref[...] = dot(slot_hot(target_ref[...], 0, out_ref.shape[0]), rows_ref[...]).astype(BF16)


def place(target_row, values, rows):
    seq, width = values.shape
    return pl.pallas_call(
        place_kernel,
        out_shape=jax.ShapeDtypeStruct((rows, width), BF16),
        compiler_params=params(),
        cost_estimate=cost(2 * rows * seq * width, 2 * (rows + seq) * width),
        name="place_cotangent",
    )(target_row, values)


def prepare_kernel(
    rel_ref, tok_ref, gain_ref, seg_ref, out_ref, normed_ref, normt_ref, kseg_ref, qseg_ref
):
    heads, width = rel_ref.shape
    wide = out_ref.shape[2]
    for h in range(heads):
        base = jnp.broadcast_to(rel_ref[h : h + 1, :], (TILE, width))
        turned = pltpu.roll(base, width - (TILE - 1), 1, stride=1, stride_axis=0)
        out_ref[h] = turned[:, :wide]
    stream = tok_ref[...].astype(F32)
    normed = stream * rms_scale(stream) * gain_ref[...]
    normed_ref[...] = normed.astype(BF16)
    normt_ref[...] = normed.T.astype(BF16)
    seq = tok_ref.shape[0]
    same = (lax.broadcasted_iota(jnp.int32, (TILE, seq), 0) == seg_ref[...]).astype(F32).T
    kseg_ref[...] = same.astype(BF16)
    qseg_ref[...] = ((same - 1.0) * 1e9).astype(BF16)


def prepare(rel_rev, tokens, gain, segments):
    heads, span = rel_rev.shape
    seq, width = tokens.shape
    wide = 2 * seq - TILE
    return pl.pallas_call(
        prepare_kernel,
        out_shape=[
            jax.ShapeDtypeStruct((heads, TILE, wide), F32),
            jax.ShapeDtypeStruct((seq, width), BF16),
            jax.ShapeDtypeStruct((width, seq), BF16),
            jax.ShapeDtypeStruct((seq, TILE), BF16),
            jax.ShapeDtypeStruct((seq, TILE), BF16),
        ],
        compiler_params=params(),
        cost_estimate=cost(heads * TILE * span, 4 * heads * TILE * wide + 6 * seq * width),
        name="bias_and_first_norm",
    )(rel_rev, tokens, gain, segments)


def attend_kernel(
    normed_ref, wq_ref, wk_ref, wv_ref, bias_ref, kseg_ref, qseg_ref,
    q_ref, k_ref, v_ref, kt_ref, e_ref, rinv_ref, ctxt_ref,
):
    seq, cols = q_ref.shape
    heads = e_ref.shape[0]
    hd = cols // heads
    per_tile = TILE // hd
    normed = normed_ref[...]
    q32 = dot(normed, wq_ref[...]).astype(BF16).astype(F32) * (1.0 / math.sqrt(hd))
    k32 = dot(normed, wk_ref[...])
    v32 = dot(normed, wv_ref[...])
    q_ref[...] = q32.astype(BF16)
    k_ref[...] = k32.astype(BF16)
    v_ref[...] = v32.astype(BF16)
    kt_ref[...] = k32.T.astype(BF16)
    vt = v32.T.astype(BF16)
    lane = lax.broadcasted_iota(jnp.int32, (STRIP, TILE), 1) // hd
    kseg = kseg_ref[...]

    def scores_of(h, start):
        sl = slice(h // per_tile * TILE, (h // per_tile + 1) * TILE)
        st = slice(start, start + STRIP)
        q_pair = q_ref[st, sl]
        q_own = jnp.where(lane == h % per_tile, q_pair, jnp.zeros_like(q_pair))
        k_all = jnp.concatenate([k_ref[:, sl], kseg], axis=1)
        return dot_nt(k_all, jnp.concatenate([q_own, qseg_ref[st]], axis=1))

    items = [(h, start) for h in range(heads) for start in range(0, seq, STRIP)]
    upcoming = scores_of(*items[0])
    for i, (h, start) in enumerate(items):
        scores = upcoming
        if i + 1 < len(items):
            upcoming = scores_of(*items[i + 1])
        parts = []
        for b in range(0, seq, TILE):
            off = seq - TILE - b + start
            parts.append(scores[b : b + TILE] + bias_ref[h, :, off : off + STRIP])
        scores = jnp.concatenate(parts, axis=0)
        e = jnp.exp(scores - jnp.max(scores, axis=0, keepdims=True))
        rinv = 1.0 / jnp.sum(e, axis=0, keepdims=True)
        eb = e.astype(BF16)
        e_ref[h, :, start : start + STRIP] = eb
        rinv_ref[h, :, start : start + STRIP] = rinv
        ctxt = dot(vt[h * hd : (h + 1) * hd], eb) * rinv
        ctxt_ref[h * hd : (h + 1) * hd, start : start + STRIP] = ctxt.astype(BF16)


def attend(normed, w_qkv, bias, kseg, qseg, heads, group):
    seq, width = normed.shape
    cols = width // heads * group
    steps = heads // group
    wide = bias.shape[2]
    whole = lambda a: pl.BlockSpec(a.shape, lambda g: (0,) * a.ndim)
    col = lambda base: pl.BlockSpec((width, cols), lambda g: (0, base * steps + g))
    nat = pl.BlockSpec((seq, cols), lambda g: (0, g))
    tr = pl.BlockSpec((cols, seq), lambda g: (g, 0))
    sds = jax.ShapeDtypeStruct
    return pl.pallas_call(
        attend_kernel,
        grid=(steps,),
        in_specs=[
            whole(normed), col(0), col(1), col(2),
            pl.BlockSpec((group, TILE, wide), lambda g: (g, 0, 0)), whole(kseg), whole(qseg),
        ],
        out_specs=[
            nat, nat, nat, tr,
            pl.BlockSpec((group, seq, seq), lambda g: (g, 0, 0)),
            pl.BlockSpec((group, 1, seq), lambda g: (g, 0, 0)),
            tr,
        ],
        out_shape=[
            sds((seq, width), BF16), sds((seq, width), BF16), sds((seq, width), BF16),
            sds((width, seq), BF16), sds((heads, seq, seq), BF16), sds((heads, 1, seq), F32),
            sds((width, seq), BF16),
        ],
        compiler_params=params(dimension_semantics=("arbitrary",)),
        cost_estimate=cost(
            6 * seq * width * width + 4 * seq * seq * width,
            2 * (3 * width * width + 9 * seq * width + heads * seq * seq) + 4 * bias.size,
            heads * seq * seq,
        ),
        name="attention_forward",
    )(normed, w_qkv, w_qkv, w_qkv, bias, kseg, qseg)


def middle_kernel(tok_ref, wo_ref, gain_ref, target_ref, ctx_ref, middle_ref, *placed_refs):
    width = tok_ref.shape[1]
    context = ctx_ref[...].astype(F32).T.astype(BF16)
    middle = tok_ref[...].astype(F32) + dot(context, wo_ref[:, :width])
    middle_ref[...] = middle
    normed = (middle * rms_scale(middle) * gain_ref[...]).astype(BF16)
    for l, placed_ref in enumerate(placed_refs):
        rows = placed_ref.shape[0]
        placed_ref[...] = dot(slot_hot(target_ref[...], l * rows, rows), normed).astype(BF16)


def middle_step(tokens, w_out, gain, target_row, ctxt, local, rows):
    seq, width = tokens.shape
    return pl.pallas_call(
        middle_kernel,
        out_shape=[jax.ShapeDtypeStruct((seq, width), F32)]
        + [jax.ShapeDtypeStruct((rows, width), BF16)] * local,
        compiler_params=params(),
        cost_estimate=cost(
            2 * seq * width * width + 2 * local * rows * seq * width,
            2 * width * width + 8 * seq * width + 2 * local * rows * width,
        ),
        name="output_projection_dispatch",
    )(tokens, w_out, gain, target_row, ctxt)


def gate_of(logits, expert):
    top = jnp.max(logits, axis=-1, keepdims=True)
    ex = jnp.exp(logits - top)
    prob = ex / jnp.sum(ex, axis=-1, keepdims=True)
    hot = lax.broadcasted_iota(jnp.int32, logits.shape, 1) == expert
    gate = jnp.sum(jnp.where(hot, prob, 0.0), axis=-1, keepdims=True)
    return prob, hot, gate


def hidden_cot_kernel(*refs):
    c_refs, (wout_ref, out_ref) = refs[:-2], refs[-2:]
    for l, c_ref in enumerate(c_refs):

        @pl.when(pl.program_id(0) == l)
        def _():
            out_ref[0] = dot_nt(c_ref[...], wout_ref[0]).astype(BF16)


def hidden_cot(cs, w_out, block):
    rows, width = cs[0].shape
    local, ff = w_out.shape[:2]
    return pl.pallas_call(
        hidden_cot_kernel,
        grid=(local, ff // block),
        in_specs=[pl.BlockSpec((rows, width), lambda l, f: (0, 0)) for _ in cs]
        + [pl.BlockSpec((1, block, width), lambda l, f: (l, f, 0))],
        out_specs=pl.BlockSpec((1, rows, block), lambda l, f: (l, 0, f)),
        out_shape=jax.ShapeDtypeStruct((local, rows, ff), BF16),
        compiler_params=params(dimension_semantics=("arbitrary", "arbitrary")),
        cost_estimate=cost(2 * local * rows * width * ff, 2 * local * ff * (width + rows)),
        name="cotangent_hidden",
    )(*cs, w_out)


def expert_kernel(
    num_ref, x_ref, c_ref, ch_ref, wr_ref, win_ref, wout_ref,
    scaled_ref, grad_ref, router_ref, gate_ref, acc_p, acc_g,
):
    step = pl.program_id(0)
    experts = router_ref.shape[0]

    @pl.when(step == 0)
    def _():
        _, _, gate = gate_of(dot(x_ref[...], wr_ref[...])[:, :experts], num_ref[1])
        gate_ref[...] = gate
        acc_p[...] = jnp.zeros_like(acc_p)
        acc_g[...] = jnp.zeros_like(acc_g)

    gate = gate_ref[...]
    hiddens, grads = [], []
    upcoming = dot(x_ref[...], win_ref[0, :, :SUB])
    for sub in range(0, win_ref.shape[2], SUB):
        pre = upcoming
        if sub + SUB < win_ref.shape[2]:
            upcoming = dot(x_ref[...], win_ref[0, :, sub + SUB : sub + 2 * SUB])
        hidden, slope = gelu_pair(pre)
        hiddens.append(hidden.astype(BF16))
        grads.append((ch_ref[0, :, sub : sub + SUB].astype(F32) * gate * slope).astype(BF16))
    acc_p[...] += dot(jnp.concatenate(hiddens, axis=1), wout_ref[0])
    acc_g[...] += dot_nt(jnp.concatenate(grads, axis=1), win_ref[0])

    @pl.when(step == pl.num_programs(0) - 1)
    def _():
        x = x_ref[...]
        prob, hot, gate = gate_of(dot(x, wr_ref[...])[:, :experts], num_ref[1])
        produced = acc_p[...]
        scaled_ref[...] = (gate * produced).astype(BF16)
        grad_gate = jnp.sum(
            c_ref[...].astype(F32) * produced.astype(BF16).astype(F32), axis=-1, keepdims=True
        )
        grad_logits = prob * (jnp.where(hot, grad_gate, 0.0) - gate * grad_gate)
        logits_b = grad_logits.astype(BF16)
        grad_ref[...] = (acc_g[...] + dot_nt(logits_b, wr_ref[:, :experts])).astype(BF16)
        router_ref[...] = dot(grad_logits.T.astype(BF16), x)


def expert_step(number, x, c, ch, w_or, w_in, w_out, local, block, experts):
    rows, width = x.shape
    ff = w_in.shape[2]
    router_cols = w_or.shape[1] - width
    whole = lambda a: pl.BlockSpec(a.shape, lambda f: (0,) * a.ndim)
    row_spec = pl.BlockSpec((rows, width), lambda f: (0, 0))
    return pl.pallas_call(
        expert_kernel,
        grid=(ff // block,),
        in_specs=[
            pl.BlockSpec(memory_space=pltpu.SMEM),
            whole(x),
            whole(c),
            pl.BlockSpec((1, rows, block), lambda f: (local, 0, f)),
            pl.BlockSpec((width, router_cols), lambda f: (0, width // router_cols)),
            pl.BlockSpec((1, width, block), lambda f: (local, 0, f)),
            pl.BlockSpec((1, block, width), lambda f: (local, f, 0)),
        ],
        out_specs=[row_spec, row_spec, pl.BlockSpec((experts, width), lambda f: (0, 0))],
        out_shape=[
            jax.ShapeDtypeStruct((rows, width), BF16),
            jax.ShapeDtypeStruct((rows, width), BF16),
            jax.ShapeDtypeStruct((experts, width), F32),
        ],
        scratch_shapes=[
            pltpu.VMEM((rows, 1), F32),
            pltpu.VMEM((rows, width), F32),
            pltpu.VMEM((rows, width), F32),
        ],
        compiler_params=params(dimension_semantics=("arbitrary",)),
        cost_estimate=cost(
            6 * rows * width * ff, 4 * width * ff + 2 * rows * ff + 8 * rows * width, rows * ff
        ),
        name="expert_rows",
    )(number, x, c, ch, w_or, w_in, w_out)


def expert_grad_kernel(experts, num_ref, x_ref, c_ref, wr_ref, win_ref, wout_ref, *refs):
    gin_ref, gout_ref, gp_ref, xt_ref = refs[-4:]
    parts, rows, width = x_ref.shape
    x = x_ref[...].reshape(parts * rows, width)

    @pl.when(pl.program_id(0) == 0)
    def _():
        _, _, gate = gate_of(dot(x, wr_ref[...])[:, :experts], num_ref[1])
        c = c_ref[...].reshape(parts * rows, width)
        gp_ref[...] = (gate * c.astype(F32)).astype(BF16)
        xt_ref[...] = x.astype(F32).T.astype(BF16)

    gp = gp_ref[...]
    pre_t = dot(win_ref[0].T, xt_ref[...])
    hidden_t, slope_t = gelu_pair(pre_t)
    grad_hidden_t = dot_nt(wout_ref[0], gp)
    gout_ref[0] = dot(hidden_t.astype(BF16), gp)
    gin_ref[0] = dot_nt(xt_ref[...], (grad_hidden_t * slope_t).astype(BF16))


def expert_grads(numbers, x_all, c_all, w_or, w_in, w_out, local, n_dp, experts, prior=()):
    parts, rows, width = x_all.shape
    ff = w_out.shape[1]
    router_cols = w_or.shape[1] - width
    part = ff // n_dp
    block = 256 if part % 256 == 0 else 128
    steps = part // block
    whole = lambda a: pl.BlockSpec(a.shape, lambda f, n: (0,) * a.ndim)
    return pl.pallas_call(
        functools.partial(expert_grad_kernel, experts),
        grid_spec=pltpu.PrefetchScalarGridSpec(
            num_scalar_prefetch=1,
            grid=(steps,),
            in_specs=[
                whole(x_all),
                whole(c_all),
                pl.BlockSpec((width, router_cols), lambda f, n: (0, width // router_cols)),
                pl.BlockSpec((1, width, block), lambda f, n: (local, 0, n[0] * steps + f)),
                pl.BlockSpec((1, block, width), lambda f, n: (local, n[0] * steps + f, 0)),
            ]
            + [pl.BlockSpec(memory_space=pl.ANY)] * len(prior),
            out_specs=[
                pl.BlockSpec((1, width, block), lambda f, n: (local, 0, f)),
                pl.BlockSpec((1, block, width), lambda f, n: (local, f, 0)),
            ],
            scratch_shapes=[
                pltpu.VMEM((parts * rows, width), BF16),
                pltpu.VMEM((width, parts * rows), BF16),
            ],
        ),
        out_shape=[
            jax.ShapeDtypeStruct((w_out.shape[0], width, part), F32),
            jax.ShapeDtypeStruct((w_out.shape[0], part, width), F32),
        ],
        compiler_params=params(dimension_semantics=("arbitrary",)),
        cost_estimate=cost(
            8 * parts * rows * width * part,
            4 * parts * rows * width + 12 * width * part,
            parts * rows * part,
        ),
        input_output_aliases={6 + i: i for i in range(len(prior))},
        name="expert_weight_grads",
    )(numbers, x_all, c_all, w_or, w_in, w_out, *prior)


def split_rows(num_ref, full_ref, keep_ref, send_ref):
    part = keep_ref.shape[1]
    core = num_ref[0] & 1
    for y in range(keep_ref.shape[0]):
        own = pl.multiple_of((2 * y + core) * part, 16)
        other = pl.multiple_of((2 * y + 1 - core) * part, 16)
        keep_ref[y] = full_ref[pl.ds(own, part), :]
        send_ref[y] = full_ref[pl.ds(other, part), :]


def middle_back_kernel(num_ref, cot_ref, middle_ref, gain_ref, target_ref, wo_ref, ctx_ref, *refs):
    back_refs, (gmid_ref, gctx_ref, keep_ref, send_ref, ggain_ref, gwo_ref) = refs[:-6], refs[-6:]
    seq, width = cot_ref.shape
    target = target_ref[...]
    grad = jnp.zeros((seq, width), F32)
    for l, back in enumerate(back_refs):
        rows = back.shape[0]
        grad = grad + dot(token_hot(target, l * rows, rows), back[...])
    grad_in, grad_gain = norm_back(middle_ref[...], gain_ref[...], grad)
    ggain_ref[...] = grad_gain
    grad_middle = cot_ref[...].astype(F32) + grad_in
    gmid_ref[...] = grad_middle
    grad_attn = grad_middle.astype(BF16)
    gctx_ref[...] = dot_nt(grad_attn, wo_ref[:, :width]).astype(BF16)
    gwo_ref[...] = dot(ctx_ref[...], grad_attn).astype(BF16)
    split_rows(num_ref, gwo_ref, keep_ref, send_ref)


def middle_back(number, cot, middle, gain, target_col, w_out, ctxt, backs, n_dp):
    seq, width = cot.shape
    sds = jax.ShapeDtypeStruct
    slots = sum(b.shape[0] for b in backs)
    half = sds((n_dp // 2, width // n_dp, width), BF16)
    vmem = pl.BlockSpec(memory_space=pltpu.VMEM)
    return pl.pallas_call(
        middle_back_kernel,
        in_specs=[pl.BlockSpec(memory_space=pltpu.SMEM)] + [vmem] * (6 + len(backs)),
        out_shape=[sds((seq, width), F32), sds((seq, width), BF16), half, half, sds((1, width), F32)],
        scratch_shapes=[pltpu.VMEM((width, width), BF16)],
        compiler_params=params(),
        cost_estimate=cost(
            4 * seq * width * width + 2 * slots * seq * width,
            4 * width * width + 14 * seq * width + 2 * slots * width,
        ),
        name="second_norm_backward",
    )(number, cot, middle, gain, target_col, w_out, ctxt, *backs)


def attend_back_kernel(
    num_ref, normt_ref, q_ref, k_ref, v_ref, kt_ref, e_ref, rinv_ref, do_ref,
    keep_ref, send_ref, grads_ref, diag_ref, acc_ref, gw_ref,
):
    seq, cols = q_ref.shape
    heads = e_ref.shape[0]
    hd = cols // heads
    per_tile = TILE // hd
    lane = lax.broadcasted_iota(jnp.int32, (STRIP, TILE), 1) // hd
    row_bit = lax.broadcasted_iota(jnp.int32, (8, 2 * seq), 0)
    zero = jnp.zeros((STRIP, TILE), BF16)

    def own(ref, h, start):
        sl = slice(h // per_tile * TILE, (h // per_tile + 1) * TILE)
        return jnp.where(lane == h % per_tile, ref[start : start + STRIP, sl], zero)

    def products(h, start):
        sl = slice(h // per_tile * TILE, (h // per_tile + 1) * TILE)
        do_own = own(do_ref, h, start)
        return do_own, dot_nt(v_ref[:, sl], do_own)

    dk_tiles, dv_tiles, dqt_rows = [], [], []
    items = [(h, start) for h in range(heads) for start in range(0, seq, STRIP)]
    upcoming = products(*items[0])
    for h in range(heads):
        acc_ref[...] = jnp.zeros_like(acc_ref)
        dk = jnp.zeros((seq, TILE), F32)
        dv = jnp.zeros((seq, TILE), F32)
        dqt_parts = []
        for start in range(0, seq, STRIP):
            st = slice(start, start + STRIP)
            do_own, grad_w = upcoming
            at = items.index((h, start)) + 1
            if at < len(items):
                upcoming = products(*items[at])
            p = e_ref[h, :, st].astype(F32) * rinv_ref[h, :, st]
            t = grad_w * p
            ds = t - p * jnp.sum(t, axis=0, keepdims=True)
            dsb = ds.astype(BF16)
            dv = dv + dot(p.astype(BF16), do_own)
            dk = dk + dot(dsb, own(q_ref, h, start))
            dqt_parts.append(dot(kt_ref[h * hd : (h + 1) * hd, :], dsb))
            for b in range(0, seq, TILE):
                off = seq - TILE - b + start
                acc_ref[:, off : off + STRIP] += ds[b : b + TILE]
        if h % per_tile == 0:
            dk_tiles.append(dk)
            dv_tiles.append(dv)
        else:
            dk_tiles[-1] = dk_tiles[-1] + dk
            dv_tiles[-1] = dv_tiles[-1] + dv
        dqt_rows.append(jnp.concatenate(dqt_parts, axis=1))
        folded = acc_ref[...]
        half = TILE // 2
        while half >= 8:
            folded = folded[:half] + pltpu.roll(folded[half:], 2 * seq - half, 1)
            half //= 2
        for bit in (4, 2, 1):
            turned = pltpu.roll(folded, 2 * seq - bit, 1)
            folded = jnp.where((row_bit & bit) != 0, turned, folded)
        diag_ref[h] = jnp.sum(folded, axis=0, keepdims=True)
    dqt = jnp.concatenate(dqt_rows, axis=0) * (1.0 / math.sqrt(hd))
    grads_ref[:, :cols] = dqt.T.astype(BF16)
    for base, tiles in ((1, dk_tiles), (2, dv_tiles)):
        grads_ref[:, base * cols : (base + 1) * cols] = jnp.concatenate(tiles, axis=1).astype(BF16)
    gw_ref[...] = dot(normt_ref[...], grads_ref[...]).astype(BF16)
    split_rows(num_ref, gw_ref, keep_ref, send_ref)


def attend_back(number, normt, q, k, v, kt, e, rinv, grad_ctx, group, n_dp):
    seq, width = q.shape
    heads = e.shape[0]
    cols = width // heads * group
    steps = heads // group
    whole = lambda a: pl.BlockSpec(a.shape, lambda g: (0,) * a.ndim)
    nat = pl.BlockSpec((seq, cols), lambda g: (0, g))
    sds = jax.ShapeDtypeStruct
    half = (n_dp // 2, width // n_dp, 3 * width)
    half_spec = pl.BlockSpec((n_dp // 2, width // n_dp, 3 * cols), lambda g: (0, 0, g))
    return pl.pallas_call(
        attend_back_kernel,
        grid=(steps,),
        in_specs=[
            pl.BlockSpec(memory_space=pltpu.SMEM), whole(normt), nat, nat, nat,
            pl.BlockSpec((cols, seq), lambda g: (g, 0)),
            pl.BlockSpec((group, seq, seq), lambda g: (g, 0, 0)),
            pl.BlockSpec((group, 1, seq), lambda g: (g, 0, 0)),
            nat,
        ],
        out_specs=[
            half_spec, half_spec, pl.BlockSpec((seq, 3 * cols), lambda g: (0, g)),
            pl.BlockSpec((group, 1, 2 * seq), lambda g: (g, 0, 0)),
        ],
        out_shape=[
            sds(half, BF16), sds(half, BF16), sds((seq, 3 * width), BF16),
            sds((heads, 1, 2 * seq), F32),
        ],
        scratch_shapes=[pltpu.VMEM((TILE, 2 * seq), F32), pltpu.VMEM((width, 3 * cols), BF16)],
        compiler_params=params(dimension_semantics=("arbitrary",)),
        cost_estimate=cost(
            6 * seq * width * width + 8 * seq * seq * width,
            2 * (6 * width * width + 8 * seq * width + heads * seq * seq),
        ),
        name="attention_backward",
    )(number, normt, q, k, v, kt, e, rinv, grad_ctx)


def first_back_kernel(cols, tok_ref, gain_ref, gmid_ref, grads_ref, w_ref, gtok_ref, ggain_ref):
    width = tok_ref.shape[1]
    grad = jnp.zeros(tok_ref.shape, F32)
    for i, start in enumerate(range(0, 3 * width, cols)):
        col = i % 3 * width + i // 3 * cols
        grad = grad + dot_nt(grads_ref[:, start : start + cols], w_ref[:, col : col + cols])
    grad_in, grad_gain = norm_back(tok_ref[...].astype(F32), gain_ref[...], grad)
    gtok_ref[...] = gmid_ref[...] + grad_in
    ggain_ref[...] = grad_gain


def first_back(tokens, gain, grad_middle, grads, w_qkv, cols):
    seq, width = tokens.shape
    return pl.pallas_call(
        functools.partial(first_back_kernel, cols),
        out_shape=[
            jax.ShapeDtypeStruct((seq, width), F32), jax.ShapeDtypeStruct((1, width), F32)
        ],
        compiler_params=params(),
        cost_estimate=cost(6 * seq * width * width, 6 * width * width + 16 * seq * width),
        name="first_norm_backward",
    )(tokens, gain, grad_middle, grads, w_qkv)


def output_kernel(middle_ref, target_ref, *refs):
    out_ref = refs[-1]
    total = middle_ref[...]
    for l, back in enumerate(refs[:-1]):
        rows = back.shape[0]
        total = total + dot(token_hot(target_ref[...], l * rows, rows), back[...])
    out_ref[...] = total.astype(BF16)


def output_step(middle, target_col, backs):
    seq, width = middle.shape
    slots = sum(b.shape[0] for b in backs)
    return pl.pallas_call(
        output_kernel,
        out_shape=jax.ShapeDtypeStruct((seq, width), BF16),
        compiler_params=params(),
        cost_estimate=cost(2 * slots * seq * width, 6 * seq * width + 2 * slots * width),
        name="layer_output",
    )(middle, target_col, *backs)


def flip(value, axis, bit):
    size = lax.axis_size(axis)
    return lax.ppermute(value, axis, [(i, i ^ bit) for i in range(size)])


def butterfly_sum(value, axes):
    for axis in axes:
        bit = 1
        while bit < lax.axis_size(axis):
            value = value + flip(value, axis, bit)
            bit *= 2
    return value


def after(value, *others):
    return lax.optimization_barrier((value, *others))[0]


def reduce_y(terms, dp_index):
    first = None
    bit = lax.axis_size("dp") // 2
    while bit > 1:
        mine = jnp.where((dp_index & bit) != 0, 1, 0)
        halves = [t.reshape(2, t.shape[0] // 2, *t.shape[1:]) for t in terms]
        pick = lambda i: [
            lax.dynamic_index_in_dim(t, i, 0, keepdims=False).astype(F32) for t in halves
        ]
        sent = sum(pick(1 - mine)).astype(BF16)
        first = sent if first is None else first
        terms = [sum(pick(mine)), flip(sent, "dp", bit)]
        bit //= 2
    return sum(t.astype(F32) for t in terms)[0], first


def sum_expert(total):
    peers = lax.axis_size("expert")
    rows, cols = total.shape
    parts = total.astype(BF16).reshape(peers, rows // peers, cols)
    arrived = lax.all_to_all(parts, "expert", split_axis=0, concat_axis=0, tiled=True)
    return jnp.sum(arrived.astype(F32), axis=0).astype(BF16)


def spread_expert(share, peers):
    rows, cols = share.shape
    spread = jnp.broadcast_to(share[None], (peers, rows, cols))
    shared = lax.all_to_all(spread, "expert", split_axis=0, concat_axis=0, tiled=True)
    return shared.reshape(peers * rows, cols).astype(F32)


def body(
    tokens, segments, routes, slots, bucket_table, gain_attn, w_query, w_key, w_value, w_output,
    rel_bias, gain_ffn, w_router, w_in, w_out, cotangent,
):
    seq, width = tokens.shape
    buckets, heads = rel_bias.shape
    experts = w_router.shape[1]
    n_dp = lax.axis_size("dp")
    peers = lax.axis_size("expert")
    local = w_in.shape[0]
    capacity = max(2, (5 * seq + 4 * experts - 1) // (4 * experts))
    rows = peers * capacity
    dp_index = lax.axis_index("dp")
    expert_index = lax.axis_index("expert")
    number = jnp.reshape(dp_index, (1,)).astype(jnp.int32)
    group = 4
    cols = width // heads * group

    w_qkv = lax.all_gather(
        jnp.concatenate([w_query, w_key, w_value], axis=1), "dp", axis=0, tiled=True
    )
    router_pad = jnp.pad(w_router, ((0, 0), (0, -experts % TILE)))
    w_or = lax.all_gather(
        jnp.concatenate([w_output, router_pad], axis=1), "dp", axis=0, tiled=True
    )

    order = (routes % local) * rows + (routes // local) * capacity + slots
    target = jnp.where(slots >= 0, order, -1)
    target_row = target[None, :]
    target_col = target[:, None]
    by_peer = jnp.where(slots >= 0, routes * capacity + slots, -1)
    gain_one = gain_attn[None, :]
    gain_two = gain_ffn[None, :]

    def exchange(values):
        return lax.all_to_all(values, "expert", split_axis=0, concat_axis=0, tiled=True)

    def exchange_rows(values):
        return exchange(values.reshape(peers, capacity, width)).reshape(rows, width)

    reversed_table = jnp.concatenate([bucket_table[::-1], jnp.full((1,), -1, jnp.int32)])
    bucket_ids = jnp.arange(buckets, dtype=jnp.int32)
    hot_rev = (bucket_ids[:, None] == reversed_table[None, :]).astype(F32)
    rel_rev = jnp.dot(rel_bias.T, hot_rev, precision=HIGH)
    shifted = jnp.roll(reversed_table, 1 - TILE)
    hot_shifted = (shifted[:, None] == bucket_ids[None, :]).astype(F32)
    bias, normed, normt, kseg, qseg = prepare(rel_rev, tokens, gain_one, segments)
    c_placed = place(by_peer[None, :], cotangent, local * rows)
    c_got = exchange(c_placed.reshape(peers, local * capacity, width))
    normed, bias, kseg, qseg, c_got = lax.optimization_barrier((normed, bias, kseg, qseg, c_got))
    c_split = c_got.reshape(peers, local, capacity, width)
    c_here = [c_split[:, l].reshape(rows, width) for l in range(local)]
    *saved, ctxt = attend(normed, w_qkv, bias, kseg, qseg, heads, group)
    middle, *placed = middle_step(tokens, w_or, gain_two, target_row, ctxt, local, rows)
    arrived = [None] * local
    for l in reversed(range(local)):
        ready = after(placed[l], arrived[l + 1]) if l + 1 < local else placed[l]
        arrived[l] = exchange_rows(ready)
    c_late, _ = lax.optimization_barrier((c_here, placed))
    ch = hidden_cot(c_late, w_out, 1024)
    arrived[-1], ch = lax.optimization_barrier((arrived[-1], ch))
    x_all, c_all, backs, scaled, router_terms, numbers = ([None] * local for _ in range(6))
    for l in reversed(range(local)):
        numbers[l] = jnp.stack([dp_index, expert_index * local + l]).astype(jnp.int32)
        sources = (arrived[l], c_here[l])
        if l + 1 < local:
            *sources, _ = lax.optimization_barrier((*sources, scaled[l + 1]))
        x_all[l], c_all[l] = [lax.all_gather(a, "dp", axis=0, tiled=False) for a in sources]
        scaled[l], grad_x, router_terms[l] = expert_step(
            numbers[l], arrived[l], c_here[l], ch, w_or, w_in, w_out, l, 1024, experts
        )
        backs[l] = exchange_rows(grad_x)

    def weight_terms(l, prior):
        return expert_grads(
            numbers[l], x_all[l], c_all[l], w_or, w_in, w_out, l, n_dp, experts, prior
        )

    expert_terms = weight_terms(local - 1, ())
    backs, expert_terms = lax.optimization_barrier((backs, expert_terms))
    scaled, _ = lax.optimization_barrier((scaled, backs))
    stacked = jnp.stack([part.reshape(peers, capacity, width) for part in scaled], axis=1)
    returned = exchange(stacked.reshape(peers, local * capacity, width)).reshape(-1, width)

    grad_middle, grad_ctx, keep_o, send_o, ggain_two = middle_back(
        number, cotangent, middle, gain_two, target_col, w_or, ctxt, backs, n_dp
    )
    keep, send, grads, diag = attend_back(number, normt, *saved, grad_ctx, group, n_dp)
    crossed_o = flip(send_o, "dp", 1)
    crossed_o, send, returned, x_all, c_all = lax.optimization_barrier(
        (crossed_o, send, returned, x_all, c_all)
    )
    crossed = flip(send, "dp", 1)
    part, sent = reduce_y([keep, crossed], dp_index)
    part_o, _ = reduce_y([keep_o, crossed_o], dp_index)
    grad_tokens, ggain_one = first_back(tokens, gain_one, grad_middle, grads, w_qkv, cols)
    if sent is not None:
        part_o = after(part_o, sent)
    summed_o = sum_expert(part_o)
    part, grad_tokens, summed_o = lax.optimization_barrier((part, grad_tokens, summed_o))
    grad_rel = jnp.dot(diag.reshape(heads, 2 * seq), hot_shifted, precision=HIGH)
    rel_row = jnp.pad(grad_rel.reshape(1, heads * buckets), ((0, 0), (0, width - heads * buckets)))
    small = butterfly_sum(
        jnp.concatenate([sum(router_terms), ggain_two, rel_row], axis=0), ("dp",)
    )
    small_rows = small.shape[0]
    shard_rows = width // n_dp
    extra = -(-small.size // (shard_rows * TILE)) * TILE
    flat = jnp.pad(small.reshape(-1), (0, shard_rows * extra - small.size))
    summed = sum_expert(jnp.concatenate([part, flat.reshape(shard_rows, extra)], axis=1))
    for l in reversed(range(local - 1)):
        expert_terms = weight_terms(l, expert_terms)
    late = butterfly_sum(ggain_one, ("dp",))
    late = late + flip(late, "expert", 1)
    summed, expert_terms, late = lax.optimization_barrier((summed, expert_terms, late))
    bit = 2
    while bit < peers:
        late = late + flip(late, "expert", bit)
        bit *= 2
    ordered = [
        summed[:, g + i * cols : g + (i + 1) * cols]
        for i in range(3)
        for g in range(0, 3 * width, 3 * cols)
    ]
    shards = spread_expert(
        jnp.concatenate([*ordered, summed_o, summed[:, 3 * width :]], axis=1), peers
    )
    output = output_step(middle, by_peer[:, None], [returned])
    small = shards[:, 4 * width :].reshape(-1)[: small_rows * width].reshape(small_rows, width)
    grad_router = lax.dynamic_slice_in_dim(small[:experts], dp_index * shard_rows, shard_rows, 1).T
    total_rel = small[experts + 1, : heads * buckets].reshape(heads, buckets).T
    shard_q, shard_k, shard_v, shard_o = [
        shards[:, i * width : (i + 1) * width] for i in range(4)
    ]
    return (
        output,
        grad_tokens,
        late[0],
        shard_q,
        shard_k,
        shard_v,
        shard_o,
        total_rel,
        small[experts],
        grad_router,
        expert_terms[0],
        expert_terms[1],
    )


def solution(mesh):
    in_specs = (
        P(("dp", "expert"), None),
        P(("dp", "expert"), None),
        P(("dp", "expert")),
        P(("dp", "expert")),
        P(),
        P(),
        P("dp", None),
        P("dp", None),
        P("dp", None),
        P("dp", None),
        P(),
        P(),
        P("dp", None),
        P("expert", None, None),
        P("expert", None, None),
        P(("dp", "expert"), None),
    )
    out_specs = (
        P(("dp", "expert"), None),
        P(("dp", "expert"), None),
        P(),
        P("dp", None),
        P("dp", None),
        P("dp", None),
        P("dp", None),
        P(),
        P(),
        P("dp", None),
        P("expert", None, "dp"),
        P("expert", "dp", None),
    )
    return jax.shard_map(body, mesh=mesh, in_specs=in_specs, out_specs=out_specs, check_vma=False)
```

```python
import functools
import math

import jax
import jax.numpy as jnp
from jax import lax
from jax.experimental import pallas as pl
from jax.experimental.pallas import tpu as pltpu
from jax.sharding import PartitionSpec as P

EPS = 1e-06
HIGH = lax.Precision.HIGHEST
F32 = jnp.float32
BF16 = jnp.bfloat16
VMEM_LIMIT = 56 * 1024 * 1024
TILE = 128
STRIP = 256
SUB = 256
GELU_A = math.sqrt(2.0 / math.pi)
GELU_B = 0.044715


def dot(a, b):
    return jnp.dot(a, b, preferred_element_type=F32)


def dot_nt(a, b):
    return lax.dot_general(a, b, (((1,), (1,)), ((), ())), preferred_element_type=F32)


def params(**kw):
    return pltpu.CompilerParams(vmem_limit_bytes=VMEM_LIMIT, **kw)


def cost(flops, nbytes, trans=0):
    return pl.CostEstimate(flops=int(flops), bytes_accessed=int(nbytes), transcendentals=int(trans))


def rms_scale(stream):
    return lax.rsqrt(jnp.mean(stream * stream, axis=-1, keepdims=True) + EPS)


def norm_back(stream, gain, grad_out):
    scale = rms_scale(stream)
    grad_gain = jnp.sum(grad_out * (stream * scale), axis=0, keepdims=True)
    scaled = grad_out * gain
    inner = jnp.mean(scaled * stream, axis=-1, keepdims=True)
    grad_in = scale * scaled - stream * (scale * scale * scale * inner)
    return grad_in, grad_gain


def gelu_pair(v):
    sq = v * v
    power = jnp.minimum(v * (-2.0 * GELU_A - (2.0 * GELU_A * GELU_B) * sq), 80.0)
    total = 1.0 + jnp.exp(power)
    guess = pl.reciprocal(total, approx=True)
    half = guess * (2.0 - total * guess)
    value = v * half
    slope = half + value * (1.0 - half) * (2.0 * GELU_A + (6.0 * GELU_A * GELU_B) * sq)
    return value, slope


def slot_hot(target_row, start, rows):
    seq = target_row.shape[1]
    ids = lax.broadcasted_iota(jnp.int32, (rows, seq), 0) + start
    return (ids == target_row).astype(F32).astype(BF16)


def token_hot(target_col, start, rows):
    seq = target_col.shape[0]
    ids = lax.broadcasted_iota(jnp.int32, (seq, rows), 1) + start
    return (ids == target_col).astype(F32).astype(BF16)


def place_kernel(target_ref, rows_ref, out_ref):
    out_ref[...] = dot(slot_hot(target_ref[...], 0, out_ref.shape[0]), rows_ref[...]).astype(BF16)


def place(target_row, values, rows):
    seq, width = values.shape
    return pl.pallas_call(
        place_kernel,
        out_shape=jax.ShapeDtypeStruct((rows, width), BF16),
        compiler_params=params(),
        cost_estimate=cost(2 * rows * seq * width, 2 * (rows + seq) * width),
        name="place_cotangent",
    )(target_row, values)


def prepare_kernel(
    rel_ref, tok_ref, gain_ref, seg_ref, out_ref, normed_ref, normt_ref, kseg_ref, qseg_ref
):
    heads, width = rel_ref.shape
    wide = out_ref.shape[2]
    for h in range(heads):
        base = jnp.broadcast_to(rel_ref[h : h + 1, :], (TILE, width))
        turned = pltpu.roll(base, width - (TILE - 1), 1, stride=1, stride_axis=0)
        out_ref[h] = turned[:, :wide]
    stream = tok_ref[...].astype(F32)
    normed = stream * rms_scale(stream) * gain_ref[...]
    normed_ref[...] = normed.astype(BF16)
    normt_ref[...] = normed.T.astype(BF16)
    seq = tok_ref.shape[0]
    same = (lax.broadcasted_iota(jnp.int32, (TILE, seq), 0) == seg_ref[...]).astype(F32).T
    kseg_ref[...] = same.astype(BF16)
    qseg_ref[...] = ((same - 1.0) * 1e9).astype(BF16)


def prepare(rel_rev, tokens, gain, segments):
    heads, span = rel_rev.shape
    seq, width = tokens.shape
    wide = 2 * seq - TILE
    return pl.pallas_call(
        prepare_kernel,
        out_shape=[
            jax.ShapeDtypeStruct((heads, TILE, wide), F32),
            jax.ShapeDtypeStruct((seq, width), BF16),
            jax.ShapeDtypeStruct((width, seq), BF16),
            jax.ShapeDtypeStruct((seq, TILE), BF16),
            jax.ShapeDtypeStruct((seq, TILE), BF16),
        ],
        compiler_params=params(),
        cost_estimate=cost(heads * TILE * span, 4 * heads * TILE * wide + 6 * seq * width),
        name="bias_and_first_norm",
    )(rel_rev, tokens, gain, segments)


def attend_kernel(
    normed_ref, wq_ref, wk_ref, wv_ref, bias_ref, kseg_ref, qseg_ref,
    q_ref, k_ref, v_ref, kt_ref, e_ref, rinv_ref, ctxt_ref,
):
    seq, cols = q_ref.shape
    heads = e_ref.shape[0]
    hd = cols // heads
    per_tile = TILE // hd
    normed = normed_ref[...]
    q32 = dot(normed, wq_ref[...]).astype(BF16).astype(F32) * (1.0 / math.sqrt(hd))
    k32 = dot(normed, wk_ref[...])
    v32 = dot(normed, wv_ref[...])
    q_ref[...] = q32.astype(BF16)
    k_ref[...] = k32.astype(BF16)
    v_ref[...] = v32.astype(BF16)
    kt_ref[...] = k32.T.astype(BF16)
    vt = v32.T.astype(BF16)
    lane = lax.broadcasted_iota(jnp.int32, (STRIP, TILE), 1) // hd
    kseg = kseg_ref[...]

    def scores_of(h, start):
        sl = slice(h // per_tile * TILE, (h // per_tile + 1) * TILE)
        st = slice(start, start + STRIP)
        q_pair = q_ref[st, sl]
        q_own = jnp.where(lane == h % per_tile, q_pair, jnp.zeros_like(q_pair))
        k_all = jnp.concatenate([k_ref[:, sl], kseg], axis=1)
        return dot_nt(k_all, jnp.concatenate([q_own, qseg_ref[st]], axis=1))

    items = [(h, start) for h in range(heads) for start in range(0, seq, STRIP)]
    upcoming = scores_of(*items[0])
    for i, (h, start) in enumerate(items):
        scores = upcoming
        if i + 1 < len(items):
            upcoming = scores_of(*items[i + 1])
        parts = []
        for b in range(0, seq, TILE):
            off = seq - TILE - b + start
            parts.append(scores[b : b + TILE] + bias_ref[h, :, off : off + STRIP])
        scores = jnp.concatenate(parts, axis=0)
        e = jnp.exp(scores - jnp.max(scores, axis=0, keepdims=True))
        rinv = 1.0 / jnp.sum(e, axis=0, keepdims=True)
        eb = e.astype(BF16)
        e_ref[h, :, start : start + STRIP] = eb
        rinv_ref[h, :, start : start + STRIP] = rinv
        ctxt = dot(vt[h * hd : (h + 1) * hd], eb) * rinv
        ctxt_ref[h * hd : (h + 1) * hd, start : start + STRIP] = ctxt.astype(BF16)


def attend(normed, w_qkv, bias, kseg, qseg, heads, group):
    seq, width = normed.shape
    cols = width // heads * group
    steps = heads // group
    wide = bias.shape[2]
    whole = lambda a: pl.BlockSpec(a.shape, lambda g: (0,) * a.ndim)
    col = lambda base: pl.BlockSpec((width, cols), lambda g: (0, base * steps + g))
    nat = pl.BlockSpec((seq, cols), lambda g: (0, g))
    tr = pl.BlockSpec((cols, seq), lambda g: (g, 0))
    sds = jax.ShapeDtypeStruct
    return pl.pallas_call(
        attend_kernel,
        grid=(steps,),
        in_specs=[
            whole(normed), col(0), col(1), col(2),
            pl.BlockSpec((group, TILE, wide), lambda g: (g, 0, 0)), whole(kseg), whole(qseg),
        ],
        out_specs=[
            nat, nat, nat, tr,
            pl.BlockSpec((group, seq, seq), lambda g: (g, 0, 0)),
            pl.BlockSpec((group, 1, seq), lambda g: (g, 0, 0)),
            tr,
        ],
        out_shape=[
            sds((seq, width), BF16), sds((seq, width), BF16), sds((seq, width), BF16),
            sds((width, seq), BF16), sds((heads, seq, seq), BF16), sds((heads, 1, seq), F32),
            sds((width, seq), BF16),
        ],
        compiler_params=params(dimension_semantics=("arbitrary",)),
        cost_estimate=cost(
            6 * seq * width * width + 4 * seq * seq * width,
            2 * (3 * width * width + 9 * seq * width + heads * seq * seq) + 4 * bias.size,
            heads * seq * seq,
        ),
        name="attention_forward",
    )(normed, w_qkv, w_qkv, w_qkv, bias, kseg, qseg)


def middle_kernel(tok_ref, wo_ref, gain_ref, target_ref, ctx_ref, middle_ref, *placed_refs):
    width = tok_ref.shape[1]
    context = ctx_ref[...].astype(F32).T.astype(BF16)
    middle = tok_ref[...].astype(F32) + dot(context, wo_ref[:, :width])
    middle_ref[...] = middle
    normed = (middle * rms_scale(middle) * gain_ref[...]).astype(BF16)
    for l, placed_ref in enumerate(placed_refs):
        rows = placed_ref.shape[0]
        placed_ref[...] = dot(slot_hot(target_ref[...], l * rows, rows), normed).astype(BF16)


def middle_step(tokens, w_out, gain, target_row, ctxt, local, rows):
    seq, width = tokens.shape
    return pl.pallas_call(
        middle_kernel,
        out_shape=[jax.ShapeDtypeStruct((seq, width), F32)]
        + [jax.ShapeDtypeStruct((rows, width), BF16)] * local,
        compiler_params=params(),
        cost_estimate=cost(
            2 * seq * width * width + 2 * local * rows * seq * width,
            2 * width * width + 8 * seq * width + 2 * local * rows * width,
        ),
        name="output_projection_dispatch",
    )(tokens, w_out, gain, target_row, ctxt)


def gate_of(logits, expert):
    top = jnp.max(logits, axis=-1, keepdims=True)
    ex = jnp.exp(logits - top)
    prob = ex / jnp.sum(ex, axis=-1, keepdims=True)
    hot = lax.broadcasted_iota(jnp.int32, logits.shape, 1) == expert
    gate = jnp.sum(jnp.where(hot, prob, 0.0), axis=-1, keepdims=True)
    return prob, hot, gate


def expert_kernel(
    num_ref, x_ref, c_ref, wr_ref, win_ref, wout_ref,
    scaled_ref, grad_ref, router_ref, gp_ref, acc_p, acc_g,
):
    step = pl.program_id(0)
    experts = router_ref.shape[0]

    @pl.when(step == 0)
    def _():
        _, _, gate = gate_of(dot(x_ref[...], wr_ref[...])[:, :experts], num_ref[1])
        gp_ref[...] = (gate * c_ref[...].astype(F32)).astype(BF16)
        acc_p[...] = jnp.zeros_like(acc_p)
        acc_g[...] = jnp.zeros_like(acc_g)

    def products(sub):
        pre = dot(x_ref[...], win_ref[0, :, sub : sub + SUB])
        return pre, dot_nt(gp_ref[...], wout_ref[0, sub : sub + SUB, :])

    hiddens, grads = [], []
    upcoming = products(0)
    for sub in range(SUB, win_ref.shape[2] + SUB, SUB):
        pre, grad_hidden = upcoming
        if sub < win_ref.shape[2]:
            upcoming = products(sub)
        hidden, slope = gelu_pair(pre)
        hiddens.append(hidden.astype(BF16))
        grads.append((grad_hidden * slope).astype(BF16))
    acc_p[...] += dot(jnp.concatenate(hiddens, axis=1), wout_ref[0])
    acc_g[...] += dot_nt(jnp.concatenate(grads, axis=1), win_ref[0])

    @pl.when(step == pl.num_programs(0) - 1)
    def _():
        x = x_ref[...]
        prob, hot, gate = gate_of(dot(x, wr_ref[...])[:, :experts], num_ref[1])
        produced = acc_p[...]
        scaled_ref[...] = (gate * produced).astype(BF16)
        grad_gate = jnp.sum(
            c_ref[...].astype(F32) * produced.astype(BF16).astype(F32), axis=-1, keepdims=True
        )
        grad_logits = prob * (jnp.where(hot, grad_gate, 0.0) - gate * grad_gate)
        logits_b = grad_logits.astype(BF16)
        grad_ref[...] = (acc_g[...] + dot_nt(logits_b, wr_ref[:, :experts])).astype(BF16)
        router_ref[...] = dot(grad_logits.T.astype(BF16), x)


def expert_step(number, x, c, w_or, w_in, w_out, local, block, experts):
    rows, width = x.shape
    ff = w_in.shape[2]
    router_cols = w_or.shape[1] - width
    whole = lambda a: pl.BlockSpec(a.shape, lambda f: (0,) * a.ndim)
    row_spec = pl.BlockSpec((rows, width), lambda f: (0, 0))
    return pl.pallas_call(
        expert_kernel,
        grid=(ff // block,),
        in_specs=[
            pl.BlockSpec(memory_space=pltpu.SMEM),
            whole(x),
            whole(c),
            pl.BlockSpec((width, router_cols), lambda f: (0, width // router_cols)),
            pl.BlockSpec((1, width, block), lambda f: (local, 0, f)),
            pl.BlockSpec((1, block, width), lambda f: (local, f, 0)),
        ],
        out_specs=[row_spec, row_spec, pl.BlockSpec((experts, width), lambda f: (0, 0))],
        out_shape=[
            jax.ShapeDtypeStruct((rows, width), BF16),
            jax.ShapeDtypeStruct((rows, width), BF16),
            jax.ShapeDtypeStruct((experts, width), F32),
        ],
        scratch_shapes=[
            pltpu.VMEM((rows, width), BF16),
            pltpu.VMEM((rows, width), F32),
            pltpu.VMEM((rows, width), F32),
        ],
        compiler_params=params(dimension_semantics=("arbitrary",)),
        cost_estimate=cost(
            8 * rows * width * ff, 4 * width * ff + 8 * rows * width, rows * ff
        ),
        name="expert_rows",
    )(number, x, c, w_or, w_in, w_out)


def expert_grad_kernel(experts, num_ref, x_ref, c_ref, wr_ref, win_ref, wout_ref, *refs):
    gin_ref, gout_ref, gp_ref, xt_ref = refs[-4:]
    parts, rows, width = x_ref.shape
    x = x_ref[...].reshape(parts * rows, width)

    @pl.when(pl.program_id(0) == 0)
    def _():
        _, _, gate = gate_of(dot(x, wr_ref[...])[:, :experts], num_ref[1])
        c = c_ref[...].reshape(parts * rows, width)
        gp_ref[...] = (gate * c.astype(F32)).astype(BF16)
        xt_ref[...] = x.astype(F32).T.astype(BF16)

    gp = gp_ref[...]
    pre_t = dot(win_ref[0].T, xt_ref[...])
    hidden_t, slope_t = gelu_pair(pre_t)
    grad_hidden_t = dot_nt(wout_ref[0], gp)
    gout_ref[0] = dot(hidden_t.astype(BF16), gp)
    gin_ref[0] = dot_nt(xt_ref[...], (grad_hidden_t * slope_t).astype(BF16))


def expert_grads(numbers, x_all, c_all, w_or, w_in, w_out, local, n_dp, experts, prior=()):
    parts, rows, width = x_all.shape
    ff = w_out.shape[1]
    router_cols = w_or.shape[1] - width
    part = ff // n_dp
    block = part
    steps = part // block
    whole = lambda a: pl.BlockSpec(a.shape, lambda f, n: (0,) * a.ndim)
    return pl.pallas_call(
        functools.partial(expert_grad_kernel, experts),
        grid_spec=pltpu.PrefetchScalarGridSpec(
            num_scalar_prefetch=1,
            grid=(steps,),
            in_specs=[
                whole(x_all),
                whole(c_all),
                pl.BlockSpec((width, router_cols), lambda f, n: (0, width // router_cols)),
                pl.BlockSpec((1, width, block), lambda f, n: (local, 0, n[0] * steps + f)),
                pl.BlockSpec((1, block, width), lambda f, n: (local, n[0] * steps + f, 0)),
            ]
            + [pl.BlockSpec(memory_space=pl.ANY)] * len(prior),
            out_specs=[
                pl.BlockSpec((1, width, block), lambda f, n: (local, 0, f)),
                pl.BlockSpec((1, block, width), lambda f, n: (local, f, 0)),
            ],
            scratch_shapes=[
                pltpu.VMEM((parts * rows, width), BF16),
                pltpu.VMEM((width, parts * rows), BF16),
            ],
        ),
        out_shape=[
            jax.ShapeDtypeStruct((w_out.shape[0], width, part), F32),
            jax.ShapeDtypeStruct((w_out.shape[0], part, width), F32),
        ],
        compiler_params=params(dimension_semantics=("arbitrary",)),
        cost_estimate=cost(
            8 * parts * rows * width * part,
            4 * parts * rows * width + 12 * width * part,
            parts * rows * part,
        ),
        input_output_aliases={6 + i: i for i in range(len(prior))},
        name="expert_weight_grads",
    )(numbers, x_all, c_all, w_or, w_in, w_out, *prior)


def split_rows(num_ref, full_ref, keep_ref, send_ref):
    part = keep_ref.shape[1]
    core = num_ref[0] & 1
    for y in range(keep_ref.shape[0]):
        own = pl.multiple_of((2 * y + core) * part, 16)
        other = pl.multiple_of((2 * y + 1 - core) * part, 16)
        keep_ref[y] = full_ref[pl.ds(own, part), :]
        send_ref[y] = full_ref[pl.ds(other, part), :]


def middle_back_kernel(num_ref, cot_ref, middle_ref, gain_ref, target_ref, wo_ref, ctx_ref, *refs):
    refs, (gmid_ref, gctx_ref, keep_ref, send_ref, ggain_ref, gwo_ref) = refs[:-6], refs[-6:]
    local = len(refs) // 2
    back_refs, router_refs = refs[:local], refs[local:]
    seq, width = cot_ref.shape
    target = target_ref[...]
    grad = jnp.zeros((seq, width), F32)
    for l, back in enumerate(back_refs):
        rows = back.shape[0]
        grad = grad + dot(token_hot(target, l * rows, rows), back[...])
    grad_in, grad_gain = norm_back(middle_ref[...], gain_ref[...], grad)
    ggain_ref[...] = grad_gain
    grad_middle = cot_ref[...].astype(F32) + grad_in
    gmid_ref[...] = grad_middle
    grad_attn = grad_middle.astype(BF16)
    gctx_ref[...] = dot_nt(grad_attn, wo_ref[:, :width]).astype(BF16)
    gwo_ref[:, :width] = dot(ctx_ref[...], grad_attn).astype(BF16)
    router = sum(ref[...] for ref in router_refs)
    spare = jnp.zeros((gwo_ref.shape[1] - width - router.shape[0], width), F32)
    gwo_ref[:, width:] = jnp.concatenate([router, spare], axis=0).T.astype(BF16)
    split_rows(num_ref, gwo_ref, keep_ref, send_ref)


def middle_back(number, cot, middle, gain, target_col, w_or, ctxt, backs, routers, n_dp):
    seq, width = cot.shape
    sds = jax.ShapeDtypeStruct
    slots = sum(b.shape[0] for b in backs)
    half = sds((n_dp // 2, width // n_dp, w_or.shape[1]), BF16)
    vmem = pl.BlockSpec(memory_space=pltpu.VMEM)
    return pl.pallas_call(
        middle_back_kernel,
        in_specs=[pl.BlockSpec(memory_space=pltpu.SMEM)] + [vmem] * (6 + 2 * len(backs)),
        out_shape=[sds((seq, width), F32), sds((seq, width), BF16), half, half, sds((1, width), F32)],
        scratch_shapes=[pltpu.VMEM(w_or.shape, BF16)],
        compiler_params=params(),
        cost_estimate=cost(
            4 * seq * width * width + 2 * slots * seq * width,
            4 * width * width + 14 * seq * width + 2 * slots * width,
        ),
        name="second_norm_backward",
    )(number, cot, middle, gain, target_col, w_or, ctxt, *backs, *routers)


def attend_back_kernel(
    num_ref, normt_ref, q_ref, k_ref, v_ref, kt_ref, e_ref, rinv_ref, do_ref,
    keep_ref, send_ref, grads_ref, diag_ref, acc_ref, gw_ref,
):
    seq, cols = q_ref.shape
    heads = e_ref.shape[0]
    hd = cols // heads
    per_tile = TILE // hd
    lane = lax.broadcasted_iota(jnp.int32, (STRIP, TILE), 1) // hd
    row_bit = lax.broadcasted_iota(jnp.int32, (8, 2 * seq), 0)
    zero = jnp.zeros((STRIP, TILE), BF16)

    def own(ref, h, start):
        sl = slice(h // per_tile * TILE, (h // per_tile + 1) * TILE)
        return jnp.where(lane == h % per_tile, ref[start : start + STRIP, sl], zero)

    def products(h, start):
        sl = slice(h // per_tile * TILE, (h // per_tile + 1) * TILE)
        do_own = own(do_ref, h, start)
        return do_own, dot_nt(v_ref[:, sl], do_own)

    dk_tiles, dv_tiles, dqt_rows = [], [], []
    items = [(h, start) for h in range(heads) for start in range(0, seq, STRIP)]
    upcoming = products(*items[0])
    for h in range(heads):
        acc_ref[...] = jnp.zeros_like(acc_ref)
        dk = jnp.zeros((seq, TILE), F32)
        dv = jnp.zeros((seq, TILE), F32)
        dqt_parts = []
        for start in range(0, seq, STRIP):
            st = slice(start, start + STRIP)
            do_own, grad_w = upcoming
            at = items.index((h, start)) + 1
            if at < len(items):
                upcoming = products(*items[at])
            p = e_ref[h, :, st].astype(F32) * rinv_ref[h, :, st]
            t = grad_w * p
            ds = t - p * jnp.sum(t, axis=0, keepdims=True)
            dsb = ds.astype(BF16)
            dv = dv + dot(p.astype(BF16), do_own)
            dk = dk + dot(dsb, own(q_ref, h, start))
            dqt_parts.append(dot(kt_ref[h * hd : (h + 1) * hd, :], dsb))
            for b in range(0, seq, TILE):
                off = seq - TILE - b + start
                acc_ref[:, off : off + STRIP] += ds[b : b + TILE]
        if h % per_tile == 0:
            dk_tiles.append(dk)
            dv_tiles.append(dv)
        else:
            dk_tiles[-1] = dk_tiles[-1] + dk
            dv_tiles[-1] = dv_tiles[-1] + dv
        dqt_rows.append(jnp.concatenate(dqt_parts, axis=1))
        folded = acc_ref[...]
        half = TILE // 2
        while half >= 8:
            folded = folded[:half] + pltpu.roll(folded[half:], 2 * seq - half, 1)
            half //= 2
        for bit in (4, 2, 1):
            turned = pltpu.roll(folded, 2 * seq - bit, 1)
            folded = jnp.where((row_bit & bit) != 0, turned, folded)
        diag_ref[h] = jnp.sum(folded, axis=0, keepdims=True)
    dqt = jnp.concatenate(dqt_rows, axis=0) * (1.0 / math.sqrt(hd))
    grads_ref[:, :cols] = dqt.T.astype(BF16)
    for base, tiles in ((1, dk_tiles), (2, dv_tiles)):
        grads_ref[:, base * cols : (base + 1) * cols] = jnp.concatenate(tiles, axis=1).astype(BF16)
    gw_ref[...] = dot(normt_ref[...], grads_ref[...]).astype(BF16)
    split_rows(num_ref, gw_ref, keep_ref, send_ref)


def attend_back(number, normt, q, k, v, kt, e, rinv, grad_ctx, group, n_dp):
    seq, width = q.shape
    heads = e.shape[0]
    cols = width // heads * group
    steps = heads // group
    whole = lambda a: pl.BlockSpec(a.shape, lambda g: (0,) * a.ndim)
    nat = pl.BlockSpec((seq, cols), lambda g: (0, g))
    sds = jax.ShapeDtypeStruct
    half = (n_dp // 2, width // n_dp, 3 * width)
    half_spec = pl.BlockSpec((n_dp // 2, width // n_dp, 3 * cols), lambda g: (0, 0, g))
    return pl.pallas_call(
        attend_back_kernel,
        grid=(steps,),
        in_specs=[
            pl.BlockSpec(memory_space=pltpu.SMEM), whole(normt), nat, nat, nat,
            pl.BlockSpec((cols, seq), lambda g: (g, 0)),
            pl.BlockSpec((group, seq, seq), lambda g: (g, 0, 0)),
            pl.BlockSpec((group, 1, seq), lambda g: (g, 0, 0)),
            nat,
        ],
        out_specs=[
            half_spec, half_spec, pl.BlockSpec((seq, 3 * cols), lambda g: (0, g)),
            pl.BlockSpec((group, 1, 2 * seq), lambda g: (g, 0, 0)),
        ],
        out_shape=[
            sds(half, BF16), sds(half, BF16), sds((seq, 3 * width), BF16),
            sds((heads, 1, 2 * seq), F32),
        ],
        scratch_shapes=[pltpu.VMEM((TILE, 2 * seq), F32), pltpu.VMEM((width, 3 * cols), BF16)],
        compiler_params=params(dimension_semantics=("arbitrary",)),
        cost_estimate=cost(
            6 * seq * width * width + 8 * seq * seq * width,
            2 * (6 * width * width + 8 * seq * width + heads * seq * seq),
        ),
        name="attention_backward",
    )(number, normt, q, k, v, kt, e, rinv, grad_ctx)


def first_back_kernel(cols, tok_ref, gain_ref, gmid_ref, grads_ref, w_ref, gtok_ref, ggain_ref):
    width = tok_ref.shape[1]
    grad = jnp.zeros(tok_ref.shape, F32)
    for i, start in enumerate(range(0, 3 * width, cols)):
        col = i % 3 * width + i // 3 * cols
        grad = grad + dot_nt(grads_ref[:, start : start + cols], w_ref[:, col : col + cols])
    grad_in, grad_gain = norm_back(tok_ref[...].astype(F32), gain_ref[...], grad)
    gtok_ref[...] = gmid_ref[...] + grad_in
    ggain_ref[...] = grad_gain


def first_back(tokens, gain, grad_middle, grads, w_qkv, cols):
    seq, width = tokens.shape
    return pl.pallas_call(
        functools.partial(first_back_kernel, cols),
        out_shape=[
            jax.ShapeDtypeStruct((seq, width), F32), jax.ShapeDtypeStruct((1, width), F32)
        ],
        compiler_params=params(),
        cost_estimate=cost(6 * seq * width * width, 6 * width * width + 16 * seq * width),
        name="first_norm_backward",
    )(tokens, gain, grad_middle, grads, w_qkv)


def output_kernel(middle_ref, target_ref, *refs):
    out_ref = refs[-1]
    total = middle_ref[...]
    for l, back in enumerate(refs[:-1]):
        rows = back.shape[0]
        total = total + dot(token_hot(target_ref[...], l * rows, rows), back[...])
    out_ref[...] = total.astype(BF16)


def output_step(middle, target_col, backs):
    seq, width = middle.shape
    slots = sum(b.shape[0] for b in backs)
    return pl.pallas_call(
        output_kernel,
        out_shape=jax.ShapeDtypeStruct((seq, width), BF16),
        compiler_params=params(),
        cost_estimate=cost(2 * slots * seq * width, 6 * seq * width + 2 * slots * width),
        name="layer_output",
    )(middle, target_col, *backs)


def flip(value, axis, bit):
    size = lax.axis_size(axis)
    return lax.ppermute(value, axis, [(i, i ^ bit) for i in range(size)])


def butterfly_sum(value, axes):
    for axis in axes:
        bit = 1
        while bit < lax.axis_size(axis):
            value = value + flip(value, axis, bit)
            bit *= 2
    return value


def after(value, *others):
    return lax.optimization_barrier((value, *others))[0]


def gather_dp(piece, dp_index):
    size = lax.axis_size("dp")
    pieces = {0: piece}
    bits = []
    bit = 2
    while bit < size:
        bits.append(bit)
        bit *= 2
    for bit in bits + [1]:
        pieces.update({m | bit: flip(p, "dp", bit) for m, p in pieces.items()})
    rows, cols = piece.shape
    whole = jnp.zeros((size * rows, cols), piece.dtype)
    for mask, got in pieces.items():
        whole = lax.dynamic_update_slice(whole, got, ((dp_index ^ mask) * rows, 0))
    return whole


def reduce_y(terms, dp_index):
    first = None
    bit = lax.axis_size("dp") // 2
    while bit > 1:
        mine = jnp.where((dp_index & bit) != 0, 1, 0)
        halves = [t.reshape(2, t.shape[0] // 2, *t.shape[1:]) for t in terms]
        pick = lambda i: [
            lax.dynamic_index_in_dim(t, i, 0, keepdims=False).astype(F32) for t in halves
        ]
        sent = sum(pick(1 - mine)).astype(BF16)
        first = sent if first is None else first
        terms = [sum(pick(mine)), flip(sent, "dp", bit)]
        bit //= 2
    return sum(t.astype(F32) for t in terms)[0], first


def sum_expert(total):
    peers = lax.axis_size("expert")
    rows, cols = total.shape
    parts = total.astype(BF16).reshape(peers, rows // peers, cols)
    arrived = lax.all_to_all(parts, "expert", split_axis=0, concat_axis=0, tiled=True)
    return jnp.sum(arrived.astype(F32), axis=0).astype(BF16)


def spread_expert(share, peers):
    rows, cols = share.shape
    spread = jnp.broadcast_to(share[None], (peers, rows, cols))
    shared = lax.all_to_all(spread, "expert", split_axis=0, concat_axis=0, tiled=True)
    return shared.reshape(peers * rows, cols).astype(F32)


def body(
    tokens, segments, routes, slots, bucket_table, gain_attn, w_query, w_key, w_value, w_output,
    rel_bias, gain_ffn, w_router, w_in, w_out, cotangent,
):
    seq, width = tokens.shape
    buckets, heads = rel_bias.shape
    experts = w_router.shape[1]
    n_dp = lax.axis_size("dp")
    peers = lax.axis_size("expert")
    local = w_in.shape[0]
    capacity = max(2, (5 * seq + 4 * experts - 1) // (4 * experts))
    rows = peers * capacity
    dp_index = lax.axis_index("dp")
    expert_index = lax.axis_index("expert")
    number = jnp.reshape(dp_index, (1,)).astype(jnp.int32)
    group = 4
    cols = width // heads * group

    w_qkv = lax.all_gather(
        jnp.concatenate([w_query, w_key, w_value], axis=1), "dp", axis=0, tiled=True
    )
    router_pad = jnp.pad(w_router, ((0, 0), (0, -experts % TILE)))
    w_or = gather_dp(jnp.concatenate([w_output, router_pad], axis=1), dp_index)

    order = (routes % local) * rows + (routes // local) * capacity + slots
    target = jnp.where(slots >= 0, order, -1)
    target_row = target[None, :]
    target_col = target[:, None]
    by_peer = jnp.where(slots >= 0, routes * capacity + slots, -1)
    gain_one = gain_attn[None, :]
    gain_two = gain_ffn[None, :]

    def exchange(values):
        return lax.all_to_all(values, "expert", split_axis=0, concat_axis=0, tiled=True)

    def exchange_rows(values):
        return exchange(values.reshape(peers, capacity, width)).reshape(rows, width)

    reversed_table = jnp.concatenate([bucket_table[::-1], jnp.full((1,), -1, jnp.int32)])
    bucket_ids = jnp.arange(buckets, dtype=jnp.int32)
    hot_rev = (bucket_ids[:, None] == reversed_table[None, :]).astype(F32)
    rel_rev = jnp.dot(rel_bias.T, hot_rev, precision=HIGH)
    shifted = jnp.roll(reversed_table, 1 - TILE)
    hot_shifted = (shifted[:, None] == bucket_ids[None, :]).astype(F32)
    bias, normed, normt, kseg, qseg = prepare(rel_rev, tokens, gain_one, segments)
    c_placed = place(by_peer[None, :], cotangent, local * rows)
    c_got = exchange(c_placed.reshape(peers, local * capacity, width))
    normed, bias, kseg, qseg, c_got, w_or = lax.optimization_barrier(
        (normed, bias, kseg, qseg, c_got, w_or)
    )
    c_split = c_got.reshape(peers, local, capacity, width)
    c_here = [c_split[:, l].reshape(rows, width) for l in range(local)]
    *saved, ctxt = attend(normed, w_qkv, bias, kseg, qseg, heads, group)
    middle, *placed = middle_step(tokens, w_or, gain_two, target_row, ctxt, local, rows)
    arrived = [None] * local
    for l in reversed(range(local)):
        ready = after(placed[l], arrived[l + 1]) if l + 1 < local else placed[l]
        arrived[l] = exchange_rows(ready)
    x_all, c_all, backs, scaled, router_terms, numbers = ([None] * local for _ in range(6))
    for l in reversed(range(local)):
        numbers[l] = jnp.stack([dp_index, expert_index * local + l]).astype(jnp.int32)
        sources = (arrived[l], c_here[l])
        if l + 1 < local:
            *sources, _ = lax.optimization_barrier((*sources, scaled[l + 1]))
        x_all[l], c_all[l] = [lax.all_gather(a, "dp", axis=0, tiled=False) for a in sources]
        scaled[l], grad_x, router_terms[l] = expert_step(
            numbers[l], arrived[l], c_here[l], w_or, w_in, w_out, l, 1024, experts
        )
        backs[l] = exchange_rows(grad_x)

    def weight_terms(l, prior):
        return expert_grads(
            numbers[l], x_all[l], c_all[l], w_or, w_in, w_out, l, n_dp, experts, prior
        )

    expert_terms = weight_terms(local - 1, ())
    backs, expert_terms = lax.optimization_barrier((backs, expert_terms))
    scaled, _ = lax.optimization_barrier((scaled, backs))
    stacked = jnp.stack([part.reshape(peers, capacity, width) for part in scaled], axis=1)
    returned = exchange(stacked.reshape(peers, local * capacity, width)).reshape(-1, width)

    grad_middle, grad_ctx, keep_o, send_o, ggain_two = middle_back(
        number, cotangent, middle, gain_two, target_col, w_or, ctxt, backs, router_terms, n_dp
    )
    keep, send, grads, diag = attend_back(number, normt, *saved, grad_ctx, group, n_dp)
    crossed_o = flip(send_o, "dp", 1)
    crossed_o, send, returned, x_all, c_all = lax.optimization_barrier(
        (crossed_o, send, returned, x_all, c_all)
    )
    crossed = flip(send, "dp", 1)
    part, sent = reduce_y([keep, crossed], dp_index)
    part_o, _ = reduce_y([keep_o, crossed_o], dp_index)
    grad_tokens, ggain_one = first_back(tokens, gain_one, grad_middle, grads, w_qkv, cols)
    if sent is not None:
        part_o = after(part_o, sent)
    summed_o = sum_expert(part_o)
    part, grad_tokens, summed_o = lax.optimization_barrier((part, grad_tokens, summed_o))
    grad_rel = jnp.dot(diag.reshape(heads, 2 * seq), hot_shifted, precision=HIGH)
    rel_row = jnp.pad(grad_rel.reshape(1, heads * buckets), ((0, 0), (0, width - heads * buckets)))
    late = butterfly_sum(
        jnp.concatenate([ggain_two, ggain_one, rel_row], axis=0), ("dp", "expert")
    )
    summed = sum_expert(part)
    summed, late = lax.optimization_barrier((summed, late))
    ordered = [
        summed[:, g + i * cols : g + (i + 1) * cols]
        for i in range(3)
        for g in range(0, 3 * width, 3 * cols)
    ]
    shards = spread_expert(jnp.concatenate([*ordered, summed_o], axis=1), peers)
    for l in reversed(range(local - 1)):
        expert_terms = weight_terms(l, expert_terms)
    output = output_step(middle, by_peer[:, None], [returned])
    total_rel = late[2, : heads * buckets].reshape(heads, buckets).T
    shard_q, shard_k, shard_v, shard_o = [
        shards[:, i * width : (i + 1) * width] for i in range(4)
    ]
    return (
        output,
        grad_tokens,
        late[1],
        shard_q,
        shard_k,
        shard_v,
        shard_o,
        total_rel,
        late[0],
        shards[:, 4 * width : 4 * width + experts],
        expert_terms[0],
        expert_terms[1],
    )


def solution(mesh):
    in_specs = (
        P(("dp", "expert"), None),
        P(("dp", "expert"), None),
        P(("dp", "expert")),
        P(("dp", "expert")),
        P(),
        P(),
        P("dp", None),
        P("dp", None),
        P("dp", None),
        P("dp", None),
        P(),
        P(),
        P("dp", None),
        P("expert", None, None),
        P("expert", None, None),
        P(("dp", "expert"), None),
    )
    out_specs = (
        P(("dp", "expert"), None),
        P(("dp", "expert"), None),
        P(),
        P("dp", None),
        P("dp", None),
        P("dp", None),
        P("dp", None),
        P(),
        P(),
        P("dp", None),
        P("expert", None, "dp"),
        P("expert", "dp", None),
    )
    return jax.shard_map(body, mesh=mesh, in_specs=in_specs, out_specs=out_specs, check_vma=False)
```

```python
import functools
import math

import jax
import jax.numpy as jnp
from jax import lax
from jax.experimental import pallas as pl
from jax.experimental.pallas import tpu as pltpu
from jax.sharding import PartitionSpec as P

EPS = 1e-06
HIGH = lax.Precision.HIGHEST
F32 = jnp.float32
BF16 = jnp.bfloat16
VMEM_LIMIT = 30 * 1024 * 1024
VMEM_LARGE = 52 * 1024 * 1024
TILE = 128
STRIP = 256
SUB = 256
GELU_A = math.sqrt(2.0 / math.pi)
GELU_B = 0.044715


def dot(a, b):
    return jnp.dot(a, b, preferred_element_type=F32)


def dot_nt(a, b):
    return lax.dot_general(a, b, (((1,), (1,)), ((), ())), preferred_element_type=F32)


def params(limit=VMEM_LIMIT, **kw):
    return pltpu.CompilerParams(vmem_limit_bytes=limit, **kw)


def cost(flops, nbytes, trans=0):
    return pl.CostEstimate(flops=int(flops), bytes_accessed=int(nbytes), transcendentals=int(trans))


def rms_scale(stream):
    return lax.rsqrt(jnp.mean(stream * stream, axis=-1, keepdims=True) + EPS)


def norm_back(stream, gain, grad_out):
    scale = rms_scale(stream)
    grad_gain = jnp.sum(grad_out * (stream * scale), axis=0, keepdims=True)
    scaled = grad_out * gain
    inner = jnp.mean(scaled * stream, axis=-1, keepdims=True)
    grad_in = scale * scaled - stream * (scale * scale * scale * inner)
    return grad_in, grad_gain


def gelu_pair(v):
    sq = v * v
    power = jnp.minimum(v * (-2.0 * GELU_A - (2.0 * GELU_A * GELU_B) * sq), 80.0)
    total = 1.0 + jnp.exp(power)
    guess = pl.reciprocal(total, approx=True)
    half = guess * (2.0 - total * guess)
    value = v * half
    slope = half + value * (1.0 - half) * (2.0 * GELU_A + (6.0 * GELU_A * GELU_B) * sq)
    return value, slope


def slot_hot(target_row, start, rows):
    seq = target_row.shape[1]
    ids = lax.broadcasted_iota(jnp.int32, (rows, seq), 0) + start
    return (ids == target_row).astype(F32).astype(BF16)


def token_hot(target_col, start, rows):
    seq = target_col.shape[0]
    ids = lax.broadcasted_iota(jnp.int32, (seq, rows), 1) + start
    return (ids == target_col).astype(F32).astype(BF16)


def place_kernel(target_ref, rows_ref, *out_refs):
    for l, out_ref in enumerate(out_refs):
        rows = out_ref.shape[0]
        out_ref[...] = dot(slot_hot(target_ref[...], l * rows, rows), rows_ref[...]).astype(BF16)


def place(target_row, values, local, rows):
    seq, width = values.shape
    return pl.pallas_call(
        place_kernel,
        out_shape=[jax.ShapeDtypeStruct((rows, width), BF16)] * local,
        compiler_params=params(),
        cost_estimate=cost(2 * local * rows * seq * width, 2 * (local * rows + seq) * width),
        name="place_cotangent",
    )(target_row, values)


def prepare_kernel(
    rel_ref, tok_ref, gain_ref, seg_ref, out_ref, normed_ref, normt_ref, kseg_ref, qseg_ref
):
    heads, width = rel_ref.shape
    wide = out_ref.shape[2]
    for h in range(heads):
        base = jnp.broadcast_to(rel_ref[h : h + 1, :], (TILE, width))
        turned = pltpu.roll(base, width - (TILE - 1), 1, stride=1, stride_axis=0)
        out_ref[h] = turned[:, :wide]
    stream = tok_ref[...].astype(F32)
    normed = stream * rms_scale(stream) * gain_ref[...]
    normed_ref[...] = normed.astype(BF16)
    normt_ref[...] = normed.T.astype(BF16)
    seq = tok_ref.shape[0]
    same = (lax.broadcasted_iota(jnp.int32, (TILE, seq), 0) == seg_ref[...]).astype(F32).T
    kseg_ref[...] = same.astype(BF16)
    qseg_ref[...] = ((same - 1.0) * 1e9).astype(BF16)


def prepare(rel_rev, tokens, gain, segments):
    heads, span = rel_rev.shape
    seq, width = tokens.shape
    wide = 2 * seq - TILE
    return pl.pallas_call(
        prepare_kernel,
        out_shape=[
            jax.ShapeDtypeStruct((heads, TILE, wide), F32),
            jax.ShapeDtypeStruct((seq, width), BF16),
            jax.ShapeDtypeStruct((width, seq), BF16),
            jax.ShapeDtypeStruct((seq, TILE), BF16),
            jax.ShapeDtypeStruct((seq, TILE), BF16),
        ],
        compiler_params=params(),
        cost_estimate=cost(heads * TILE * span, 4 * heads * TILE * wide + 6 * seq * width),
        name="bias_and_first_norm",
    )(rel_rev, tokens, gain, segments)


def join_rows(num_ref, pieces, w_ref):
    part = pieces[0].shape[0]
    for mask, piece in enumerate(pieces):
        row = pl.multiple_of((num_ref[0] ^ mask) * part, 16)
        w_ref[pl.ds(row, part), :] = piece[...]


def attend_kernel(num_ref, normed_ref, bias_ref, kseg_ref, qseg_ref, *refs):
    pieces, refs = refs[:-8], refs[-8:]
    q_ref, k_ref, v_ref, kt_ref, e_ref, rinv_ref, ctxt_ref, w_ref = refs
    seq, cols = q_ref.shape
    width = normed_ref.shape[1]
    step = pl.program_id(0)

    @pl.when(step == 0)
    def _():
        join_rows(num_ref, pieces, w_ref)

    at = lambda base: pl.ds(pl.multiple_of(base * width + step * cols, TILE), cols)
    heads = e_ref.shape[0]
    hd = cols // heads
    per_tile = TILE // hd
    normed = normed_ref[...]
    q32 = dot(normed, w_ref[:, at(0)]).astype(BF16).astype(F32) * (1.0 / math.sqrt(hd))
    k32 = dot(normed, w_ref[:, at(1)])
    v32 = dot(normed, w_ref[:, at(2)])
    q_ref[...] = q32.astype(BF16)
    k_ref[...] = k32.astype(BF16)
    v_ref[...] = v32.astype(BF16)
    kt_ref[...] = k32.T.astype(BF16)
    vt = v32.T.astype(BF16)
    lane = lax.broadcasted_iota(jnp.int32, (STRIP, TILE), 1) // hd
    kseg = kseg_ref[...]

    def scores_of(h, start):
        sl = slice(h // per_tile * TILE, (h // per_tile + 1) * TILE)
        st = slice(start, start + STRIP)
        q_pair = q_ref[st, sl]
        q_own = jnp.where(lane == h % per_tile, q_pair, jnp.zeros_like(q_pair))
        k_all = jnp.concatenate([k_ref[:, sl], kseg], axis=1)
        return dot_nt(k_all, jnp.concatenate([q_own, qseg_ref[st]], axis=1))

    items = [(h, start) for h in range(heads) for start in range(0, seq, STRIP)]
    upcoming = scores_of(*items[0])
    for i, (h, start) in enumerate(items):
        scores = upcoming
        if i + 1 < len(items):
            upcoming = scores_of(*items[i + 1])
        parts = []
        for b in range(0, seq, TILE):
            off = seq - TILE - b + start
            parts.append(scores[b : b + TILE] + bias_ref[h, :, off : off + STRIP])
        scores = jnp.concatenate(parts, axis=0)
        e = jnp.exp(scores - jnp.max(scores, axis=0, keepdims=True))
        rinv = 1.0 / jnp.sum(e, axis=0, keepdims=True)
        eb = e.astype(BF16)
        e_ref[h, :, start : start + STRIP] = eb
        rinv_ref[h, :, start : start + STRIP] = rinv
        ctxt = dot(vt[h * hd : (h + 1) * hd], eb) * rinv
        ctxt_ref[h * hd : (h + 1) * hd, start : start + STRIP] = ctxt.astype(BF16)


def attend(number, normed, bias, kseg, qseg, pieces, heads, group):
    seq, width = normed.shape
    cols = width // heads * group
    steps = heads // group
    wide = bias.shape[2]
    whole = lambda a: pl.BlockSpec(a.shape, lambda g: (0,) * a.ndim)
    nat = pl.BlockSpec((seq, cols), lambda g: (0, g))
    tr = pl.BlockSpec((cols, seq), lambda g: (g, 0))
    sds = jax.ShapeDtypeStruct
    return pl.pallas_call(
        attend_kernel,
        grid=(steps,),
        in_specs=[
            pl.BlockSpec(memory_space=pltpu.SMEM), whole(normed),
            pl.BlockSpec((group, TILE, wide), lambda g: (g, 0, 0)), whole(kseg), whole(qseg),
        ]
        + [whole(p) for p in pieces],
        out_specs=[
            nat, nat, nat, tr,
            pl.BlockSpec((group, seq, seq), lambda g: (g, 0, 0)),
            pl.BlockSpec((group, 1, seq), lambda g: (g, 0, 0)),
            tr,
        ],
        out_shape=[
            sds((seq, width), BF16), sds((seq, width), BF16), sds((seq, width), BF16),
            sds((width, seq), BF16), sds((heads, seq, seq), BF16), sds((heads, 1, seq), F32),
            sds((width, seq), BF16),
        ],
        scratch_shapes=[pltpu.VMEM((width, 3 * width), BF16)],
        compiler_params=params(dimension_semantics=("arbitrary",)),
        cost_estimate=cost(
            6 * seq * width * width + 4 * seq * seq * width,
            2 * (3 * width * width + 9 * seq * width + heads * seq * seq) + 4 * bias.size,
            heads * seq * seq,
        ),
        name="attention_forward",
    )(number, normed, bias, kseg, qseg, *pieces)


def middle_kernel(tok_ref, wo_ref, gain_ref, target_ref, ctx_ref, middle_ref, *placed_refs):
    width = tok_ref.shape[1]
    context = ctx_ref[...].astype(F32).T.astype(BF16)
    middle = tok_ref[...].astype(F32) + dot(context, wo_ref[:, :width])
    middle_ref[...] = middle
    normed = (middle * rms_scale(middle) * gain_ref[...]).astype(BF16)
    for l, placed_ref in enumerate(placed_refs):
        rows = placed_ref.shape[0]
        placed_ref[...] = dot(slot_hot(target_ref[...], l * rows, rows), normed).astype(BF16)


def middle_step(tokens, w_out, gain, target_row, ctxt, local, rows):
    seq, width = tokens.shape
    return pl.pallas_call(
        middle_kernel,
        out_shape=[jax.ShapeDtypeStruct((seq, width), F32)]
        + [jax.ShapeDtypeStruct((rows, width), BF16)] * local,
        compiler_params=params(),
        cost_estimate=cost(
            2 * seq * width * width + 2 * local * rows * seq * width,
            2 * width * width + 8 * seq * width + 2 * local * rows * width,
        ),
        name="output_projection_dispatch",
    )(tokens, w_out, gain, target_row, ctxt)


def gate_of(logits, expert):
    top = jnp.max(logits, axis=-1, keepdims=True)
    ex = jnp.exp(logits - top)
    prob = ex / jnp.sum(ex, axis=-1, keepdims=True)
    hot = lax.broadcasted_iota(jnp.int32, logits.shape, 1) == expert
    gate = jnp.sum(jnp.where(hot, prob, 0.0), axis=-1, keepdims=True)
    return prob, hot, gate


def expert_kernel(
    num_ref, x_ref, c_ref, wr_ref, win_ref, wout_ref,
    scaled_ref, grad_ref, router_ref, gp_ref, acc_p, acc_g,
):
    step = pl.program_id(0)
    experts = router_ref.shape[0]

    @pl.when(step == 0)
    def _():
        _, _, gate = gate_of(dot(x_ref[...], wr_ref[...])[:, :experts], num_ref[1])
        gp_ref[...] = (gate * c_ref[...].astype(F32)).astype(BF16)
        acc_p[...] = jnp.zeros_like(acc_p)
        acc_g[...] = jnp.zeros_like(acc_g)

    def products(sub):
        pre = dot(x_ref[...], win_ref[0, :, sub : sub + SUB])
        return pre, dot_nt(gp_ref[...], wout_ref[0, sub : sub + SUB, :])

    hiddens, grads = [], []
    upcoming = products(0)
    for sub in range(SUB, win_ref.shape[2] + SUB, SUB):
        pre, grad_hidden = upcoming
        if sub < win_ref.shape[2]:
            upcoming = products(sub)
        hidden, slope = gelu_pair(pre)
        hiddens.append(hidden.astype(BF16))
        grads.append((grad_hidden * slope).astype(BF16))
    acc_p[...] += dot(jnp.concatenate(hiddens, axis=1), wout_ref[0])
    acc_g[...] += dot_nt(jnp.concatenate(grads, axis=1), win_ref[0])

    @pl.when(step == pl.num_programs(0) - 1)
    def _():
        x = x_ref[...]
        prob, hot, gate = gate_of(dot(x, wr_ref[...])[:, :experts], num_ref[1])
        produced = acc_p[...]
        scaled_ref[...] = (gate * produced).astype(BF16)
        grad_gate = jnp.sum(
            c_ref[...].astype(F32) * produced.astype(BF16).astype(F32), axis=-1, keepdims=True
        )
        grad_logits = prob * (jnp.where(hot, grad_gate, 0.0) - gate * grad_gate)
        logits_b = grad_logits.astype(BF16)
        grad_ref[...] = (acc_g[...] + dot_nt(logits_b, wr_ref[:, :experts])).astype(BF16)
        router_ref[...] = dot(grad_logits.T.astype(BF16), x)


def expert_step(number, x, c, w_or, w_in, w_out, local, block, experts):
    rows, width = x.shape
    ff = w_in.shape[2]
    router_cols = w_or.shape[1] - width
    whole = lambda a: pl.BlockSpec(a.shape, lambda f: (0,) * a.ndim)
    row_spec = pl.BlockSpec((rows, width), lambda f: (0, 0))
    return pl.pallas_call(
        expert_kernel,
        grid=(ff // block,),
        in_specs=[
            pl.BlockSpec(memory_space=pltpu.SMEM),
            whole(x),
            whole(c),
            pl.BlockSpec((width, router_cols), lambda f: (0, width // router_cols)),
            pl.BlockSpec((1, width, block), lambda f: (local, 0, f)),
            pl.BlockSpec((1, block, width), lambda f: (local, f, 0)),
        ],
        out_specs=[row_spec, row_spec, pl.BlockSpec((experts, width), lambda f: (0, 0))],
        out_shape=[
            jax.ShapeDtypeStruct((rows, width), BF16),
            jax.ShapeDtypeStruct((rows, width), BF16),
            jax.ShapeDtypeStruct((experts, width), F32),
        ],
        scratch_shapes=[
            pltpu.VMEM((rows, width), BF16),
            pltpu.VMEM((rows, width), F32),
            pltpu.VMEM((rows, width), F32),
        ],
        compiler_params=params(dimension_semantics=("arbitrary",)),
        cost_estimate=cost(
            8 * rows * width * ff, 4 * width * ff + 8 * rows * width, rows * ff
        ),
        name="expert_rows",
    )(number, x, c, w_or, w_in, w_out)


def expert_grad_kernel(experts, num_ref, x_ref, c_ref, wr_ref, win_ref, wout_ref, *refs):
    gin_ref, gout_ref, gp_ref, xt_ref = refs[-4:]
    parts, rows, width = x_ref.shape
    x = x_ref[...].reshape(parts * rows, width)

    @pl.when(pl.program_id(0) == 0)
    def _():
        _, _, gate = gate_of(dot(x, wr_ref[...])[:, :experts], num_ref[1])
        c = c_ref[...].reshape(parts * rows, width)
        gp_ref[...] = (gate * c.astype(F32)).astype(BF16)
        xt_ref[...] = x.astype(F32).T.astype(BF16)

    gp = gp_ref[...]
    pre_t = dot(win_ref[0].T, xt_ref[...])
    hidden_t, slope_t = gelu_pair(pre_t)
    grad_hidden_t = dot_nt(wout_ref[0], gp)
    gout_ref[0] = dot(hidden_t.astype(BF16), gp)
    gin_ref[0] = dot_nt(xt_ref[...], (grad_hidden_t * slope_t).astype(BF16))


def expert_grads(numbers, x_all, c_all, w_or, w_in, w_out, local, n_dp, experts, prior=()):
    parts, rows, width = x_all.shape
    ff = w_out.shape[1]
    router_cols = w_or.shape[1] - width
    part = ff // n_dp
    block = part
    steps = part // block
    whole = lambda a: pl.BlockSpec(a.shape, lambda f, n: (0,) * a.ndim)
    return pl.pallas_call(
        functools.partial(expert_grad_kernel, experts),
        grid_spec=pltpu.PrefetchScalarGridSpec(
            num_scalar_prefetch=1,
            grid=(steps,),
            in_specs=[
                whole(x_all),
                whole(c_all),
                pl.BlockSpec((width, router_cols), lambda f, n: (0, width // router_cols)),
                pl.BlockSpec((1, width, block), lambda f, n: (local, 0, n[0] * steps + f)),
                pl.BlockSpec((1, block, width), lambda f, n: (local, n[0] * steps + f, 0)),
            ]
            + [pl.BlockSpec(memory_space=pl.ANY)] * len(prior),
            out_specs=[
                pl.BlockSpec((1, width, block), lambda f, n: (local, 0, f)),
                pl.BlockSpec((1, block, width), lambda f, n: (local, f, 0)),
            ],
            scratch_shapes=[
                pltpu.VMEM((parts * rows, width), BF16),
                pltpu.VMEM((width, parts * rows), BF16),
            ],
        ),
        out_shape=[
            jax.ShapeDtypeStruct((w_out.shape[0], width, part), F32),
            jax.ShapeDtypeStruct((w_out.shape[0], part, width), F32),
        ],
        compiler_params=params(VMEM_LARGE, dimension_semantics=("arbitrary",)),
        cost_estimate=cost(
            8 * parts * rows * width * part,
            4 * parts * rows * width + 12 * width * part,
            parts * rows * part,
        ),
        input_output_aliases={6 + i: i for i in range(len(prior))},
        name="expert_weight_grads",
    )(numbers, x_all, c_all, w_or, w_in, w_out, *prior)


def split_rows(num_ref, full_ref, keep_ref, send_ref):
    part = keep_ref.shape[1]
    core = num_ref[0] & 1
    for y in range(keep_ref.shape[0]):
        own = pl.multiple_of((2 * y + core) * part, 16)
        other = pl.multiple_of((2 * y + 1 - core) * part, 16)
        keep_ref[y] = full_ref[pl.ds(own, part), :]
        send_ref[y] = full_ref[pl.ds(other, part), :]


def middle_back_kernel(num_ref, cot_ref, middle_ref, gain_ref, target_ref, wo_ref, ctx_ref, *refs):
    refs, (gmid_ref, gctx_ref, keep_ref, send_ref, ggain_ref, gwo_ref) = refs[:-6], refs[-6:]
    local = len(refs) // 2
    back_refs, router_refs = refs[:local], refs[local:]
    seq, width = cot_ref.shape
    target = target_ref[...]
    grad = jnp.zeros((seq, width), F32)
    for l, back in enumerate(back_refs):
        rows = back.shape[0]
        grad = grad + dot(token_hot(target, l * rows, rows), back[...])
    grad_in, grad_gain = norm_back(middle_ref[...], gain_ref[...], grad)
    ggain_ref[...] = grad_gain
    grad_middle = cot_ref[...].astype(F32) + grad_in
    gmid_ref[...] = grad_middle
    grad_attn = grad_middle.astype(BF16)
    gctx_ref[...] = dot_nt(grad_attn, wo_ref[:, :width]).astype(BF16)
    gwo_ref[:, :width] = dot(ctx_ref[...], grad_attn).astype(BF16)
    router = sum(ref[...] for ref in router_refs)
    spare = jnp.zeros((gwo_ref.shape[1] - width - router.shape[0], width), F32)
    gwo_ref[:, width:] = jnp.concatenate([router, spare], axis=0).T.astype(BF16)
    split_rows(num_ref, gwo_ref, keep_ref, send_ref)


def middle_back(number, cot, middle, gain, target_col, w_or, ctxt, backs, routers, n_dp):
    seq, width = cot.shape
    sds = jax.ShapeDtypeStruct
    slots = sum(b.shape[0] for b in backs)
    half = sds((n_dp // 2, width // n_dp, w_or.shape[1]), BF16)
    vmem = pl.BlockSpec(memory_space=pltpu.VMEM)
    return pl.pallas_call(
        middle_back_kernel,
        in_specs=[pl.BlockSpec(memory_space=pltpu.SMEM)] + [vmem] * (6 + 2 * len(backs)),
        out_shape=[sds((seq, width), F32), sds((seq, width), BF16), half, half, sds((1, width), F32)],
        scratch_shapes=[pltpu.VMEM(w_or.shape, BF16)],
        compiler_params=params(),
        cost_estimate=cost(
            4 * seq * width * width + 2 * slots * seq * width,
            4 * width * width + 14 * seq * width + 2 * slots * width,
        ),
        name="second_norm_backward",
    )(number, cot, middle, gain, target_col, w_or, ctxt, *backs, *routers)


def attend_back_kernel(
    num_ref, normt_ref, q_ref, k_ref, v_ref, kt_ref, e_ref, rinv_ref, do_ref,
    keep_ref, send_ref, grads_ref, diag_ref, acc_ref, gw_ref,
):
    seq, cols = q_ref.shape
    heads = e_ref.shape[0]
    hd = cols // heads
    per_tile = TILE // hd
    lane = lax.broadcasted_iota(jnp.int32, (STRIP, TILE), 1) // hd
    row_bit = lax.broadcasted_iota(jnp.int32, (8, 2 * seq), 0)
    zero = jnp.zeros((STRIP, TILE), BF16)

    def own(ref, h, start):
        sl = slice(h // per_tile * TILE, (h // per_tile + 1) * TILE)
        return jnp.where(lane == h % per_tile, ref[start : start + STRIP, sl], zero)

    def products(h, start):
        sl = slice(h // per_tile * TILE, (h // per_tile + 1) * TILE)
        do_own = own(do_ref, h, start)
        return do_own, dot_nt(v_ref[:, sl], do_own)

    dk_tiles, dv_tiles, dqt_rows = [], [], []
    items = [(h, start) for h in range(heads) for start in range(0, seq, STRIP)]
    upcoming = products(*items[0])
    for h in range(heads):
        acc_ref[...] = jnp.zeros_like(acc_ref)
        dk = jnp.zeros((seq, TILE), F32)
        dv = jnp.zeros((seq, TILE), F32)
        dqt_parts = []
        for start in range(0, seq, STRIP):
            st = slice(start, start + STRIP)
            do_own, grad_w = upcoming
            at = items.index((h, start)) + 1
            if at < len(items):
                upcoming = products(*items[at])
            p = e_ref[h, :, st].astype(F32) * rinv_ref[h, :, st]
            t = grad_w * p
            ds = t - p * jnp.sum(t, axis=0, keepdims=True)
            dsb = ds.astype(BF16)
            dv = dv + dot(p.astype(BF16), do_own)
            dk = dk + dot(dsb, own(q_ref, h, start))
            dqt_parts.append(dot(kt_ref[h * hd : (h + 1) * hd, :], dsb))
            for b in range(0, seq, TILE):
                off = seq - TILE - b + start
                acc_ref[:, off : off + STRIP] += ds[b : b + TILE]
        if h % per_tile == 0:
            dk_tiles.append(dk)
            dv_tiles.append(dv)
        else:
            dk_tiles[-1] = dk_tiles[-1] + dk
            dv_tiles[-1] = dv_tiles[-1] + dv
        dqt_rows.append(jnp.concatenate(dqt_parts, axis=1))
        folded = acc_ref[...]
        half = TILE // 2
        while half >= 8:
            folded = folded[:half] + pltpu.roll(folded[half:], 2 * seq - half, 1)
            half //= 2
        for bit in (4, 2, 1):
            turned = pltpu.roll(folded, 2 * seq - bit, 1)
            folded = jnp.where((row_bit & bit) != 0, turned, folded)
        diag_ref[h] = jnp.sum(folded, axis=0, keepdims=True)
    dqt = jnp.concatenate(dqt_rows, axis=0) * (1.0 / math.sqrt(hd))
    grads_ref[:, :cols] = dqt.T.astype(BF16)
    for base, tiles in ((1, dk_tiles), (2, dv_tiles)):
        grads_ref[:, base * cols : (base + 1) * cols] = jnp.concatenate(tiles, axis=1).astype(BF16)
    gw_ref[...] = dot(normt_ref[...], grads_ref[...]).astype(BF16)
    split_rows(num_ref, gw_ref, keep_ref, send_ref)


def attend_back(number, normt, q, k, v, kt, e, rinv, grad_ctx, group, n_dp):
    seq, width = q.shape
    heads = e.shape[0]
    cols = width // heads * group
    steps = heads // group
    whole = lambda a: pl.BlockSpec(a.shape, lambda g: (0,) * a.ndim)
    nat = pl.BlockSpec((seq, cols), lambda g: (0, g))
    sds = jax.ShapeDtypeStruct
    half = (n_dp // 2, width // n_dp, 3 * width)
    half_spec = pl.BlockSpec((n_dp // 2, width // n_dp, 3 * cols), lambda g: (0, 0, g))
    return pl.pallas_call(
        attend_back_kernel,
        grid=(steps,),
        in_specs=[
            pl.BlockSpec(memory_space=pltpu.SMEM), whole(normt), nat, nat, nat,
            pl.BlockSpec((cols, seq), lambda g: (g, 0)),
            pl.BlockSpec((group, seq, seq), lambda g: (g, 0, 0)),
            pl.BlockSpec((group, 1, seq), lambda g: (g, 0, 0)),
            nat,
        ],
        out_specs=[
            half_spec, half_spec, pl.BlockSpec((seq, 3 * cols), lambda g: (0, g)),
            pl.BlockSpec((group, 1, 2 * seq), lambda g: (g, 0, 0)),
        ],
        out_shape=[
            sds(half, BF16), sds(half, BF16), sds((seq, 3 * width), BF16),
            sds((heads, 1, 2 * seq), F32),
        ],
        scratch_shapes=[pltpu.VMEM((TILE, 2 * seq), F32), pltpu.VMEM((width, 3 * cols), BF16)],
        compiler_params=params(dimension_semantics=("arbitrary",)),
        cost_estimate=cost(
            6 * seq * width * width + 8 * seq * seq * width,
            2 * (6 * width * width + 8 * seq * width + heads * seq * seq),
        ),
        name="attention_backward",
    )(number, normt, q, k, v, kt, e, rinv, grad_ctx)


def first_back_kernel(cols, num_ref, tok_ref, gain_ref, gmid_ref, grads_ref, *refs):
    pieces, (gtok_ref, ggain_ref, w_ref) = refs[:-3], refs[-3:]
    width = tok_ref.shape[1]
    join_rows(num_ref, pieces, w_ref)
    grad = jnp.zeros(tok_ref.shape, F32)
    for i, start in enumerate(range(0, 3 * width, cols)):
        col = i % 3 * width + i // 3 * cols
        grad = grad + dot_nt(grads_ref[:, start : start + cols], w_ref[:, col : col + cols])
    grad_in, grad_gain = norm_back(tok_ref[...].astype(F32), gain_ref[...], grad)
    gtok_ref[...] = gmid_ref[...] + grad_in
    ggain_ref[...] = grad_gain


def first_back(number, tokens, gain, grad_middle, grads, pieces, cols):
    seq, width = tokens.shape
    vmem = pl.BlockSpec(memory_space=pltpu.VMEM)
    return pl.pallas_call(
        functools.partial(first_back_kernel, cols),
        in_specs=[pl.BlockSpec(memory_space=pltpu.SMEM)] + [vmem] * (4 + len(pieces)),
        out_shape=[
            jax.ShapeDtypeStruct((seq, width), F32), jax.ShapeDtypeStruct((1, width), F32)
        ],
        scratch_shapes=[pltpu.VMEM((width, 3 * width), BF16)],
        compiler_params=params(),
        cost_estimate=cost(6 * seq * width * width, 6 * width * width + 16 * seq * width),
        name="first_norm_backward",
    )(number, tokens, gain, grad_middle, grads, *pieces)


def output_kernel(middle_ref, target_ref, *refs):
    out_ref = refs[-1]
    total = middle_ref[...]
    for l, back in enumerate(refs[:-1]):
        rows = back.shape[0]
        total = total + dot(token_hot(target_ref[...], l * rows, rows), back[...])
    out_ref[...] = total.astype(BF16)


def output_step(middle, target_col, backs):
    seq, width = middle.shape
    slots = sum(b.shape[0] for b in backs)
    return pl.pallas_call(
        output_kernel,
        out_shape=jax.ShapeDtypeStruct((seq, width), BF16),
        compiler_params=params(),
        cost_estimate=cost(2 * slots * seq * width, 6 * seq * width + 2 * slots * width),
        name="layer_output",
    )(middle, target_col, *backs)


def flip(value, axis, bit):
    size = lax.axis_size(axis)
    return lax.ppermute(value, axis, [(i, i ^ bit) for i in range(size)])


def butterfly_sum(value, axes):
    for axis in axes:
        bit = 1
        while bit < lax.axis_size(axis):
            value = value + flip(value, axis, bit)
            bit *= 2
    return value


def after(value, *others):
    return lax.optimization_barrier((value, *others))[0]


def gather_y(piece):
    pieces = {0: piece}
    bit = 2
    while bit < lax.axis_size("dp"):
        pieces.update({m | bit: flip(p, "dp", bit) for m, p in pieces.items()})
        bit *= 2
    return pieces


def gather_cores(pieces):
    pieces = {**pieces, **{m | 1: flip(p, "dp", 1) for m, p in pieces.items()}}
    return [pieces[m] for m in sorted(pieces)]


def reduce_y(terms, dp_index):
    first = None
    bit = lax.axis_size("dp") // 2
    while bit > 1:
        mine = jnp.where((dp_index & bit) != 0, 1, 0)
        halves = [t.reshape(2, t.shape[0] // 2, *t.shape[1:]) for t in terms]
        pick = lambda i: [
            lax.dynamic_index_in_dim(t, i, 0, keepdims=False).astype(F32) for t in halves
        ]
        sent = sum(pick(1 - mine)).astype(BF16)
        first = sent if first is None else first
        terms = [sum(pick(mine)), flip(sent, "dp", bit)]
        bit //= 2
    return sum(t.astype(F32) for t in terms)[0], first


def sum_expert(total):
    peers = lax.axis_size("expert")
    rows, cols = total.shape
    parts = total.astype(BF16).reshape(peers, rows // peers, cols)
    arrived = lax.all_to_all(parts, "expert", split_axis=0, concat_axis=0, tiled=True)
    return jnp.sum(arrived.astype(F32), axis=0).astype(BF16)


def spread_expert(share, peers):
    rows, cols = share.shape
    spread = jnp.broadcast_to(share[None], (peers, rows, cols))
    shared = lax.all_to_all(spread, "expert", split_axis=0, concat_axis=0, tiled=True)
    return shared.reshape(peers * rows, cols).astype(F32)


def body(
    tokens, segments, routes, slots, bucket_table, gain_attn, w_query, w_key, w_value, w_output,
    rel_bias, gain_ffn, w_router, w_in, w_out, cotangent,
):
    seq, width = tokens.shape
    buckets, heads = rel_bias.shape
    experts = w_router.shape[1]
    n_dp = lax.axis_size("dp")
    peers = lax.axis_size("expert")
    local = w_in.shape[0]
    capacity = max(2, (5 * seq + 4 * experts - 1) // (4 * experts))
    rows = peers * capacity
    dp_index = lax.axis_index("dp")
    expert_index = lax.axis_index("expert")
    number = jnp.reshape(dp_index, (1,)).astype(jnp.int32)
    group = 4
    cols = width // heads * group

    along_y = gather_y(jnp.concatenate([w_query, w_key, w_value], axis=1))
    router_pad = jnp.pad(w_router, ((0, 0), (0, -experts % TILE)))
    w_or = lax.all_gather(
        jnp.concatenate([w_output, router_pad], axis=1), "dp", axis=0, tiled=True
    )

    order = (routes % local) * rows + (routes // local) * capacity + slots
    target = jnp.where(slots >= 0, order, -1)
    target_row = target[None, :]
    target_col = target[:, None]
    by_peer = jnp.where(slots >= 0, routes * capacity + slots, -1)
    gain_one = gain_attn[None, :]
    gain_two = gain_ffn[None, :]

    def exchange(values):
        return lax.all_to_all(values, "expert", split_axis=0, concat_axis=0, tiled=True)

    def exchange_rows(values):
        return exchange(values.reshape(peers, capacity, width)).reshape(rows, width)

    reversed_table = jnp.concatenate([bucket_table[::-1], jnp.full((1,), -1, jnp.int32)])
    bucket_ids = jnp.arange(buckets, dtype=jnp.int32)
    hot_rev = (bucket_ids[:, None] == reversed_table[None, :]).astype(F32)
    rel_rev = jnp.dot(rel_bias.T, hot_rev, precision=HIGH)
    shifted = jnp.roll(reversed_table, 1 - TILE)
    hot_shifted = (shifted[:, None] == bucket_ids[None, :]).astype(F32)
    bias, normed, normt, kseg, qseg = prepare(rel_rev, tokens, gain_one, segments)
    c_placed = place(target_row, cotangent, local, rows)
    c_here = [exchange_rows(c_placed[0])]
    along_y, bias, normed, normt, kseg, qseg, c_here[0] = lax.optimization_barrier(
        (along_y, bias, normed, normt, kseg, qseg, c_here[0])
    )
    pieces = gather_cores(along_y)
    *saved, ctxt = attend(number, normed, bias, kseg, qseg, pieces, heads, group)
    for part in c_placed[1:]:
        c_here.append(exchange_rows(after(part, *pieces)))
    middle, *placed = middle_step(tokens, w_or, gain_two, target_row, ctxt, local, rows)
    placed, *c_here = lax.optimization_barrier((placed, *c_here))
    arrived = [None] * local
    for l in reversed(range(local)):
        ready = after(placed[l], arrived[l + 1]) if l + 1 < local else placed[l]
        arrived[l] = exchange_rows(ready)
    x_all, c_all, backs, scaled, router_terms, numbers = ([None] * local for _ in range(6))
    for l in reversed(range(local)):
        numbers[l] = jnp.stack([dp_index, expert_index * local + l]).astype(jnp.int32)
        sources = (arrived[l], c_here[l])
        if l + 1 < local:
            *sources, _ = lax.optimization_barrier((*sources, scaled[l + 1]))
        x_all[l], c_all[l] = [lax.all_gather(a, "dp", axis=0, tiled=False) for a in sources]
        scaled[l], grad_x, router_terms[l] = expert_step(
            numbers[l], arrived[l], c_here[l], w_or, w_in, w_out, l, 1024, experts
        )
        backs[l] = exchange_rows(grad_x)

    def weight_terms(l, prior):
        return expert_grads(
            numbers[l], x_all[l], c_all[l], w_or, w_in, w_out, l, n_dp, experts, prior
        )

    expert_terms = weight_terms(local - 1, ())
    backs, expert_terms = lax.optimization_barrier((backs, expert_terms))
    scaled, _ = lax.optimization_barrier((scaled, backs))
    stacked = jnp.stack([part.reshape(peers, capacity, width) for part in scaled], axis=1)
    returned = exchange(stacked.reshape(peers, local * capacity, width)).reshape(-1, width)

    grad_middle, grad_ctx, keep_o, send_o, ggain_two = middle_back(
        number, cotangent, middle, gain_two, target_col, w_or, ctxt, backs, router_terms, n_dp
    )
    keep, send, grads, diag = attend_back(number, normt, *saved, grad_ctx, group, n_dp)
    crossed_o = flip(send_o, "dp", 1)
    crossed_o, send, returned, x_all, c_all = lax.optimization_barrier(
        (crossed_o, send, returned, x_all, c_all)
    )
    crossed = flip(send, "dp", 1)
    part, sent = reduce_y([keep, crossed], dp_index)
    part_o, _ = reduce_y([keep_o, crossed_o], dp_index)
    grad_tokens, ggain_one = first_back(
        number, tokens, gain_one, grad_middle, grads, pieces, cols
    )
    if sent is not None:
        part_o = after(part_o, sent)
    summed_o = sum_expert(part_o)
    part, grad_tokens, summed_o = lax.optimization_barrier((part, grad_tokens, summed_o))
    grad_rel = jnp.dot(diag.reshape(heads, 2 * seq), hot_shifted, precision=HIGH)
    rel_row = jnp.pad(grad_rel.reshape(1, heads * buckets), ((0, 0), (0, width - heads * buckets)))
    late = butterfly_sum(
        jnp.concatenate([ggain_two, ggain_one, rel_row], axis=0), ("dp", "expert")
    )
    summed = sum_expert(part)
    summed, late = lax.optimization_barrier((summed, late))
    ordered = [
        summed[:, g + i * cols : g + (i + 1) * cols]
        for i in range(3)
        for g in range(0, 3 * width, 3 * cols)
    ]
    shards = spread_expert(jnp.concatenate([*ordered, summed_o], axis=1), peers)
    for l in reversed(range(local - 1)):
        expert_terms = weight_terms(l, expert_terms)
    output = output_step(middle, by_peer[:, None], [returned])
    total_rel = late[2, : heads * buckets].reshape(heads, buckets).T
    shard_q, shard_k, shard_v, shard_o = [
        shards[:, i * width : (i + 1) * width] for i in range(4)
    ]
    return (
        output,
        grad_tokens,
        late[1],
        shard_q,
        shard_k,
        shard_v,
        shard_o,
        total_rel,
        late[0],
        shards[:, 4 * width : 4 * width + experts],
        expert_terms[0],
        expert_terms[1],
    )


def solution(mesh):
    in_specs = (
        P(("dp", "expert"), None),
        P(("dp", "expert"), None),
        P(("dp", "expert")),
        P(("dp", "expert")),
        P(),
        P(),
        P("dp", None),
        P("dp", None),
        P("dp", None),
        P("dp", None),
        P(),
        P(),
        P("dp", None),
        P("expert", None, None),
        P("expert", None, None),
        P(("dp", "expert"), None),
    )
    out_specs = (
        P(("dp", "expert"), None),
        P(("dp", "expert"), None),
        P(),
        P("dp", None),
        P("dp", None),
        P("dp", None),
        P("dp", None),
        P(),
        P(),
        P("dp", None),
        P("expert", None, "dp"),
        P("expert", "dp", None),
    )
    return jax.shard_map(body, mesh=mesh, in_specs=in_specs, out_specs=out_specs, check_vma=False)
```

```python
import functools
import math

import jax
import jax.numpy as jnp
from jax import lax
from jax.experimental import pallas as pl
from jax.experimental.pallas import tpu as pltpu
from jax.sharding import PartitionSpec as P

EPS = 1e-06
HIGH = lax.Precision.HIGHEST
F32 = jnp.float32
BF16 = jnp.bfloat16
VMEM_LIMIT = 56 * 1024 * 1024
TILE = 128
STRIP = 256
SUB = 256
GELU_A = math.sqrt(2.0 / math.pi)
GELU_B = 0.044715


def dot(a, b):
    return jnp.dot(a, b, preferred_element_type=F32)


def dot_nt(a, b):
    return lax.dot_general(a, b, (((1,), (1,)), ((), ())), preferred_element_type=F32)


def params(**kw):
    return pltpu.CompilerParams(vmem_limit_bytes=VMEM_LIMIT, **kw)


def cost(flops, nbytes, trans=0):
    return pl.CostEstimate(flops=int(flops), bytes_accessed=int(nbytes), transcendentals=int(trans))


def rms_scale(stream):
    return lax.rsqrt(jnp.mean(stream * stream, axis=-1, keepdims=True) + EPS)


def norm_back(stream, gain, grad_out):
    scale = rms_scale(stream)
    grad_gain = jnp.sum(grad_out * (stream * scale), axis=0, keepdims=True)
    scaled = grad_out * gain
    inner = jnp.mean(scaled * stream, axis=-1, keepdims=True)
    grad_in = scale * scaled - stream * (scale * scale * scale * inner)
    return grad_in, grad_gain


def gelu_pair(v):
    sq = v * v
    power = jnp.minimum(v * (-2.0 * GELU_A - (2.0 * GELU_A * GELU_B) * sq), 80.0)
    total = 1.0 + jnp.exp(power)
    guess = pl.reciprocal(total, approx=True)
    half = guess * (2.0 - total * guess)
    value = v * half
    slope = half + value * (1.0 - half) * (2.0 * GELU_A + (6.0 * GELU_A * GELU_B) * sq)
    return value, slope


def slot_hot(target_row, start, rows):
    seq = target_row.shape[1]
    ids = lax.broadcasted_iota(jnp.int32, (rows, seq), 0) + start
    return (ids == target_row).astype(F32).astype(BF16)


def token_hot(target_col, start, rows):
    seq = target_col.shape[0]
    ids = lax.broadcasted_iota(jnp.int32, (seq, rows), 1) + start
    return (ids == target_col).astype(F32).astype(BF16)


def place_kernel(target_ref, rows_ref, *out_refs):
    for l, out_ref in enumerate(out_refs):
        rows = out_ref.shape[0]
        out_ref[...] = dot(slot_hot(target_ref[...], l * rows, rows), rows_ref[...]).astype(BF16)


def place(target_row, values, local, rows):
    seq, width = values.shape
    return pl.pallas_call(
        place_kernel,
        out_shape=[jax.ShapeDtypeStruct((rows, width), BF16)] * local,
        compiler_params=params(),
        cost_estimate=cost(2 * local * rows * seq * width, 2 * (local * rows + seq) * width),
        name="place_cotangent",
    )(target_row, values)


def prepare_kernel(
    rel_ref, tok_ref, gain_ref, seg_ref, out_ref, normed_ref, normt_ref, kseg_ref, qseg_ref
):
    heads, width = rel_ref.shape
    wide = out_ref.shape[2]
    for h in range(heads):
        base = jnp.broadcast_to(rel_ref[h : h + 1, :], (TILE, width))
        turned = pltpu.roll(base, width - (TILE - 1), 1, stride=1, stride_axis=0)
        out_ref[h] = turned[:, :wide]
    stream = tok_ref[...].astype(F32)
    normed = stream * rms_scale(stream) * gain_ref[...]
    normed_ref[...] = normed.astype(BF16)
    normt_ref[...] = normed.T.astype(BF16)
    seq = tok_ref.shape[0]
    same = (lax.broadcasted_iota(jnp.int32, (TILE, seq), 0) == seg_ref[...]).astype(F32).T
    kseg_ref[...] = same.astype(BF16)
    qseg_ref[...] = ((same - 1.0) * 1e9).astype(BF16)


def prepare(rel_rev, tokens, gain, segments):
    heads, span = rel_rev.shape
    seq, width = tokens.shape
    wide = 2 * seq - TILE
    return pl.pallas_call(
        prepare_kernel,
        out_shape=[
            jax.ShapeDtypeStruct((heads, TILE, wide), F32),
            jax.ShapeDtypeStruct((seq, width), BF16),
            jax.ShapeDtypeStruct((width, seq), BF16),
            jax.ShapeDtypeStruct((seq, TILE), BF16),
            jax.ShapeDtypeStruct((seq, TILE), BF16),
        ],
        compiler_params=params(),
        cost_estimate=cost(heads * TILE * span, 4 * heads * TILE * wide + 6 * seq * width),
        name="bias_and_first_norm",
    )(rel_rev, tokens, gain, segments)


def join_rows(num_ref, pieces, w_ref):
    part = pieces[0].shape[0]
    for mask, piece in enumerate(pieces):
        row = pl.multiple_of((num_ref[0] ^ mask) * part, 16)
        w_ref[pl.ds(row, part), :] = piece[...]


def attend_kernel(num_ref, normed_ref, bias_ref, kseg_ref, qseg_ref, *refs):
    pieces, refs = refs[:-8], refs[-8:]
    q_ref, k_ref, v_ref, kt_ref, e_ref, rinv_ref, ctxt_ref, w_ref = refs
    seq, cols = q_ref.shape
    width = normed_ref.shape[1]
    step = pl.program_id(0)

    @pl.when(step == 0)
    def _():
        join_rows(num_ref, pieces, w_ref)

    at = lambda base: pl.ds(pl.multiple_of(base * width + step * cols, TILE), cols)
    heads = e_ref.shape[0]
    hd = cols // heads
    per_tile = TILE // hd
    normed = normed_ref[...]
    q32 = dot(normed, w_ref[:, at(0)]).astype(BF16).astype(F32) * (1.0 / math.sqrt(hd))
    k32 = dot(normed, w_ref[:, at(1)])
    v32 = dot(normed, w_ref[:, at(2)])
    q_ref[...] = q32.astype(BF16)
    k_ref[...] = k32.astype(BF16)
    v_ref[...] = v32.astype(BF16)
    kt_ref[...] = k32.T.astype(BF16)
    vt = v32.T.astype(BF16)
    lane = lax.broadcasted_iota(jnp.int32, (STRIP, TILE), 1) // hd
    kseg = kseg_ref[...]

    def scores_of(h, start):
        sl = slice(h // per_tile * TILE, (h // per_tile + 1) * TILE)
        st = slice(start, start + STRIP)
        q_pair = q_ref[st, sl]
        q_own = jnp.where(lane == h % per_tile, q_pair, jnp.zeros_like(q_pair))
        k_all = jnp.concatenate([k_ref[:, sl], kseg], axis=1)
        return dot_nt(k_all, jnp.concatenate([q_own, qseg_ref[st]], axis=1))

    items = [(h, start) for h in range(heads) for start in range(0, seq, STRIP)]
    upcoming = scores_of(*items[0])
    for i, (h, start) in enumerate(items):
        scores = upcoming
        if i + 1 < len(items):
            upcoming = scores_of(*items[i + 1])
        parts = []
        for b in range(0, seq, TILE):
            off = seq - TILE - b + start
            parts.append(scores[b : b + TILE] + bias_ref[h, :, off : off + STRIP])
        scores = jnp.concatenate(parts, axis=0)
        e = jnp.exp(scores - jnp.max(scores, axis=0, keepdims=True))
        rinv = 1.0 / jnp.sum(e, axis=0, keepdims=True)
        eb = e.astype(BF16)
        e_ref[h, :, start : start + STRIP] = eb
        rinv_ref[h, :, start : start + STRIP] = rinv
        ctxt = dot(vt[h * hd : (h + 1) * hd], eb) * rinv
        ctxt_ref[h * hd : (h + 1) * hd, start : start + STRIP] = ctxt.astype(BF16)


def attend(number, normed, bias, kseg, qseg, pieces, heads, group):
    seq, width = normed.shape
    cols = width // heads * group
    steps = heads // group
    wide = bias.shape[2]
    whole = lambda a: pl.BlockSpec(a.shape, lambda g: (0,) * a.ndim)
    nat = pl.BlockSpec((seq, cols), lambda g: (0, g))
    tr = pl.BlockSpec((cols, seq), lambda g: (g, 0))
    sds = jax.ShapeDtypeStruct
    return pl.pallas_call(
        attend_kernel,
        grid=(steps,),
        in_specs=[
            pl.BlockSpec(memory_space=pltpu.SMEM), whole(normed),
            pl.BlockSpec((group, TILE, wide), lambda g: (g, 0, 0)), whole(kseg), whole(qseg),
        ]
        + [whole(p) for p in pieces],
        out_specs=[
            nat, nat, nat, tr,
            pl.BlockSpec((group, seq, seq), lambda g: (g, 0, 0)),
            pl.BlockSpec((group, 1, seq), lambda g: (g, 0, 0)),
            tr,
        ],
        out_shape=[
            sds((seq, width), BF16), sds((seq, width), BF16), sds((seq, width), BF16),
            sds((width, seq), BF16), sds((heads, seq, seq), BF16), sds((heads, 1, seq), F32),
            sds((width, seq), BF16),
        ],
        scratch_shapes=[pltpu.VMEM((width, 3 * width), BF16)],
        compiler_params=params(dimension_semantics=("arbitrary",)),
        cost_estimate=cost(
            6 * seq * width * width + 4 * seq * seq * width,
            2 * (3 * width * width + 9 * seq * width + heads * seq * seq) + 4 * bias.size,
            heads * seq * seq,
        ),
        name="attention_forward",
    )(number, normed, bias, kseg, qseg, *pieces)


def middle_kernel(tok_ref, wo_ref, gain_ref, target_ref, ctx_ref, middle_ref, *placed_refs):
    width = tok_ref.shape[1]
    context = ctx_ref[...].astype(F32).T.astype(BF16)
    middle = tok_ref[...].astype(F32) + dot(context, wo_ref[:, :width])
    middle_ref[...] = middle
    normed = (middle * rms_scale(middle) * gain_ref[...]).astype(BF16)
    for l, placed_ref in enumerate(placed_refs):
        rows = placed_ref.shape[0]
        placed_ref[...] = dot(slot_hot(target_ref[...], l * rows, rows), normed).astype(BF16)


def middle_step(tokens, w_out, gain, target_row, ctxt, local, rows):
    seq, width = tokens.shape
    return pl.pallas_call(
        middle_kernel,
        out_shape=[jax.ShapeDtypeStruct((seq, width), F32)]
        + [jax.ShapeDtypeStruct((rows, width), BF16)] * local,
        compiler_params=params(),
        cost_estimate=cost(
            2 * seq * width * width + 2 * local * rows * seq * width,
            2 * width * width + 8 * seq * width + 2 * local * rows * width,
        ),
        name="output_projection_dispatch",
    )(tokens, w_out, gain, target_row, ctxt)


def gate_of(logits, expert):
    top = jnp.max(logits, axis=-1, keepdims=True)
    ex = jnp.exp(logits - top)
    prob = ex / jnp.sum(ex, axis=-1, keepdims=True)
    hot = lax.broadcasted_iota(jnp.int32, logits.shape, 1) == expert
    gate = jnp.sum(jnp.where(hot, prob, 0.0), axis=-1, keepdims=True)
    return prob, hot, gate


def expert_kernel(
    num_ref, x_ref, c_ref, wr_ref, win_ref, wout_ref,
    scaled_ref, grad_ref, router_ref, gp_ref, acc_p, acc_g,
):
    step = pl.program_id(0)
    experts = router_ref.shape[0]

    @pl.when(step == 0)
    def _():
        _, _, gate = gate_of(dot(x_ref[...], wr_ref[...])[:, :experts], num_ref[1])
        gp_ref[...] = (gate * c_ref[...].astype(F32)).astype(BF16)
        acc_p[...] = jnp.zeros_like(acc_p)
        acc_g[...] = jnp.zeros_like(acc_g)

    def products(sub):
        pre = dot(x_ref[...], win_ref[0, :, sub : sub + SUB])
        return pre, dot_nt(gp_ref[...], wout_ref[0, sub : sub + SUB, :])

    hiddens, grads = [], []
    upcoming = products(0)
    for sub in range(SUB, win_ref.shape[2] + SUB, SUB):
        pre, grad_hidden = upcoming
        if sub < win_ref.shape[2]:
            upcoming = products(sub)
        hidden, slope = gelu_pair(pre)
        hiddens.append(hidden.astype(BF16))
        grads.append((grad_hidden * slope).astype(BF16))
    acc_p[...] += dot(jnp.concatenate(hiddens, axis=1), wout_ref[0])
    acc_g[...] += dot_nt(jnp.concatenate(grads, axis=1), win_ref[0])

    @pl.when(step == pl.num_programs(0) - 1)
    def _():
        x = x_ref[...]
        prob, hot, gate = gate_of(dot(x, wr_ref[...])[:, :experts], num_ref[1])
        produced = acc_p[...]
        scaled_ref[...] = (gate * produced).astype(BF16)
        grad_gate = jnp.sum(
            c_ref[...].astype(F32) * produced.astype(BF16).astype(F32), axis=-1, keepdims=True
        )
        grad_logits = prob * (jnp.where(hot, grad_gate, 0.0) - gate * grad_gate)
        logits_b = grad_logits.astype(BF16)
        grad_ref[...] = (acc_g[...] + dot_nt(logits_b, wr_ref[:, :experts])).astype(BF16)
        router_ref[...] = dot(grad_logits.T.astype(BF16), x)


def expert_step(number, x, c, w_or, w_in, w_out, local, block, experts):
    rows, width = x.shape
    ff = w_in.shape[2]
    router_cols = w_or.shape[1] - width
    whole = lambda a: pl.BlockSpec(a.shape, lambda f: (0,) * a.ndim)
    row_spec = pl.BlockSpec((rows, width), lambda f: (0, 0))
    return pl.pallas_call(
        expert_kernel,
        grid=(ff // block,),
        in_specs=[
            pl.BlockSpec(memory_space=pltpu.SMEM),
            whole(x),
            whole(c),
            pl.BlockSpec((width, router_cols), lambda f: (0, width // router_cols)),
            pl.BlockSpec((1, width, block), lambda f: (local, 0, f)),
            pl.BlockSpec((1, block, width), lambda f: (local, f, 0)),
        ],
        out_specs=[row_spec, row_spec, pl.BlockSpec((experts, width), lambda f: (0, 0))],
        out_shape=[
            jax.ShapeDtypeStruct((rows, width), BF16),
            jax.ShapeDtypeStruct((rows, width), BF16),
            jax.ShapeDtypeStruct((experts, width), F32),
        ],
        scratch_shapes=[
            pltpu.VMEM((rows, width), BF16),
            pltpu.VMEM((rows, width), F32),
            pltpu.VMEM((rows, width), F32),
        ],
        compiler_params=params(dimension_semantics=("arbitrary",)),
        cost_estimate=cost(
            8 * rows * width * ff, 4 * width * ff + 8 * rows * width, rows * ff
        ),
        name="expert_rows",
    )(number, x, c, w_or, w_in, w_out)


def expert_grad_kernel(experts, num_ref, x_ref, c_ref, wr_ref, win_ref, wout_ref, *refs):
    gin_ref, gout_ref, gp_ref, xt_ref = refs[-4:]
    parts, rows, width = x_ref.shape
    x = x_ref[...].reshape(parts * rows, width)

    @pl.when(pl.program_id(0) == 0)
    def _():
        _, _, gate = gate_of(dot(x, wr_ref[...])[:, :experts], num_ref[1])
        c = c_ref[...].reshape(parts * rows, width)
        gp_ref[...] = (gate * c.astype(F32)).astype(BF16)
        xt_ref[...] = x.astype(F32).T.astype(BF16)

    gp = gp_ref[...]
    pre_t = dot(win_ref[0].T, xt_ref[...])
    hidden_t, slope_t = gelu_pair(pre_t)
    grad_hidden_t = dot_nt(wout_ref[0], gp)
    gout_ref[0] = dot(hidden_t.astype(BF16), gp)
    gin_ref[0] = dot_nt(xt_ref[...], (grad_hidden_t * slope_t).astype(BF16))


def expert_grads(numbers, x_all, c_all, w_or, w_in, w_out, local, n_dp, experts, prior=()):
    parts, rows, width = x_all.shape
    ff = w_out.shape[1]
    router_cols = w_or.shape[1] - width
    part = ff // n_dp
    block = part
    steps = part // block
    whole = lambda a: pl.BlockSpec(a.shape, lambda f, n: (0,) * a.ndim)
    return pl.pallas_call(
        functools.partial(expert_grad_kernel, experts),
        grid_spec=pltpu.PrefetchScalarGridSpec(
            num_scalar_prefetch=1,
            grid=(steps,),
            in_specs=[
                whole(x_all),
                whole(c_all),
                pl.BlockSpec((width, router_cols), lambda f, n: (0, width // router_cols)),
                pl.BlockSpec((1, width, block), lambda f, n: (local, 0, n[0] * steps + f)),
                pl.BlockSpec((1, block, width), lambda f, n: (local, n[0] * steps + f, 0)),
            ]
            + [pl.BlockSpec(memory_space=pl.ANY)] * len(prior),
            out_specs=[
                pl.BlockSpec((1, width, block), lambda f, n: (local, 0, f)),
                pl.BlockSpec((1, block, width), lambda f, n: (local, f, 0)),
            ],
            scratch_shapes=[
                pltpu.VMEM((parts * rows, width), BF16),
                pltpu.VMEM((width, parts * rows), BF16),
            ],
        ),
        out_shape=[
            jax.ShapeDtypeStruct((w_out.shape[0], width, part), F32),
            jax.ShapeDtypeStruct((w_out.shape[0], part, width), F32),
        ],
        compiler_params=params(dimension_semantics=("arbitrary",)),
        cost_estimate=cost(
            8 * parts * rows * width * part,
            4 * parts * rows * width + 12 * width * part,
            parts * rows * part,
        ),
        input_output_aliases={6 + i: i for i in range(len(prior))},
        name="expert_weight_grads",
    )(numbers, x_all, c_all, w_or, w_in, w_out, *prior)


def split_rows(num_ref, full_ref, keep_ref, send_ref):
    part = keep_ref.shape[1]
    core = num_ref[0] & 1
    for y in range(keep_ref.shape[0]):
        own = pl.multiple_of((2 * y + core) * part, 16)
        other = pl.multiple_of((2 * y + 1 - core) * part, 16)
        keep_ref[y] = full_ref[pl.ds(own, part), :]
        send_ref[y] = full_ref[pl.ds(other, part), :]


def middle_back_kernel(num_ref, cot_ref, middle_ref, gain_ref, target_ref, wo_ref, ctx_ref, *refs):
    refs, (gmid_ref, gctx_ref, keep_ref, send_ref, ggain_ref, gwo_ref) = refs[:-6], refs[-6:]
    local = len(refs) // 2
    back_refs, router_refs = refs[:local], refs[local:]
    seq, width = cot_ref.shape
    target = target_ref[...]
    grad = jnp.zeros((seq, width), F32)
    for l, back in enumerate(back_refs):
        rows = back.shape[0]
        grad = grad + dot(token_hot(target, l * rows, rows), back[...])
    grad_in, grad_gain = norm_back(middle_ref[...], gain_ref[...], grad)
    ggain_ref[...] = grad_gain
    grad_middle = cot_ref[...].astype(F32) + grad_in
    gmid_ref[...] = grad_middle
    grad_attn = grad_middle.astype(BF16)
    gctx_ref[...] = dot_nt(grad_attn, wo_ref[:, :width]).astype(BF16)
    gwo_ref[:, :width] = dot(ctx_ref[...], grad_attn).astype(BF16)
    router = sum(ref[...] for ref in router_refs)
    spare = jnp.zeros((gwo_ref.shape[1] - width - router.shape[0], width), F32)
    gwo_ref[:, width:] = jnp.concatenate([router, spare], axis=0).T.astype(BF16)
    half = keep_ref.shape[0]
    top = num_ref[0] // num_ref[1]
    keep_ref[...] = gwo_ref[pl.ds(pl.multiple_of(top * half, 16), half), :]
    send_ref[...] = gwo_ref[pl.ds(pl.multiple_of((1 - top) * half, 16), half), :]


def middle_back(number, cot, middle, gain, target_col, w_or, ctxt, backs, routers, n_dp):
    seq, width = cot.shape
    sds = jax.ShapeDtypeStruct
    slots = sum(b.shape[0] for b in backs)
    half = sds((width // 2, w_or.shape[1]), BF16)
    vmem = pl.BlockSpec(memory_space=pltpu.VMEM)
    return pl.pallas_call(
        middle_back_kernel,
        in_specs=[pl.BlockSpec(memory_space=pltpu.SMEM)] + [vmem] * (6 + 2 * len(backs)),
        out_shape=[sds((seq, width), F32), sds((seq, width), BF16), half, half, sds((1, width), F32)],
        scratch_shapes=[pltpu.VMEM(w_or.shape, BF16)],
        compiler_params=params(),
        cost_estimate=cost(
            4 * seq * width * width + 2 * slots * seq * width,
            4 * width * width + 14 * seq * width + 2 * slots * width,
        ),
        name="second_norm_backward",
    )(number, cot, middle, gain, target_col, w_or, ctxt, *backs, *routers)


def attend_back_kernel(
    num_ref, normt_ref, q_ref, k_ref, v_ref, kt_ref, e_ref, rinv_ref, do_ref,
    keep_ref, send_ref, grads_ref, diag_ref, acc_ref, gw_ref,
):
    seq, cols = q_ref.shape
    heads = e_ref.shape[0]
    hd = cols // heads
    per_tile = TILE // hd
    lane = lax.broadcasted_iota(jnp.int32, (STRIP, TILE), 1) // hd
    row_bit = lax.broadcasted_iota(jnp.int32, (8, 2 * seq), 0)
    zero = jnp.zeros((STRIP, TILE), BF16)

    def own(ref, h, start):
        sl = slice(h // per_tile * TILE, (h // per_tile + 1) * TILE)
        return jnp.where(lane == h % per_tile, ref[start : start + STRIP, sl], zero)

    def products(h, start):
        sl = slice(h // per_tile * TILE, (h // per_tile + 1) * TILE)
        do_own = own(do_ref, h, start)
        return do_own, dot_nt(v_ref[:, sl], do_own)

    dk_tiles, dv_tiles, dqt_rows = [], [], []
    items = [(h, start) for h in range(heads) for start in range(0, seq, STRIP)]
    upcoming = products(*items[0])
    for h in range(heads):
        acc_ref[...] = jnp.zeros_like(acc_ref)
        dk = jnp.zeros((seq, TILE), F32)
        dv = jnp.zeros((seq, TILE), F32)
        dqt_parts = []
        for start in range(0, seq, STRIP):
            st = slice(start, start + STRIP)
            do_own, grad_w = upcoming
            at = items.index((h, start)) + 1
            if at < len(items):
                upcoming = products(*items[at])
            p = e_ref[h, :, st].astype(F32) * rinv_ref[h, :, st]
            t = grad_w * p
            ds = t - p * jnp.sum(t, axis=0, keepdims=True)
            dsb = ds.astype(BF16)
            dv = dv + dot(p.astype(BF16), do_own)
            dk = dk + dot(dsb, own(q_ref, h, start))
            dqt_parts.append(dot(kt_ref[h * hd : (h + 1) * hd, :], dsb))
            for b in range(0, seq, TILE):
                off = seq - TILE - b + start
                acc_ref[:, off : off + STRIP] += ds[b : b + TILE]
        if h % per_tile == 0:
            dk_tiles.append(dk)
            dv_tiles.append(dv)
        else:
            dk_tiles[-1] = dk_tiles[-1] + dk
            dv_tiles[-1] = dv_tiles[-1] + dv
        dqt_rows.append(jnp.concatenate(dqt_parts, axis=1))
        folded = acc_ref[...]
        half = TILE // 2
        while half >= 8:
            folded = folded[:half] + pltpu.roll(folded[half:], 2 * seq - half, 1)
            half //= 2
        for bit in (4, 2, 1):
            turned = pltpu.roll(folded, 2 * seq - bit, 1)
            folded = jnp.where((row_bit & bit) != 0, turned, folded)
        diag_ref[h] = jnp.sum(folded, axis=0, keepdims=True)
    dqt = jnp.concatenate(dqt_rows, axis=0) * (1.0 / math.sqrt(hd))
    grads_ref[:, :cols] = dqt.T.astype(BF16)
    for base, tiles in ((1, dk_tiles), (2, dv_tiles)):
        grads_ref[:, base * cols : (base + 1) * cols] = jnp.concatenate(tiles, axis=1).astype(BF16)
    gw_ref[...] = dot(normt_ref[...], grads_ref[...]).astype(BF16)
    split_rows(num_ref, gw_ref, keep_ref, send_ref)


def attend_back(number, normt, q, k, v, kt, e, rinv, grad_ctx, group, n_dp):
    seq, width = q.shape
    heads = e.shape[0]
    cols = width // heads * group
    steps = heads // group
    whole = lambda a: pl.BlockSpec(a.shape, lambda g: (0,) * a.ndim)
    nat = pl.BlockSpec((seq, cols), lambda g: (0, g))
    sds = jax.ShapeDtypeStruct
    half = (n_dp // 2, width // n_dp, 3 * width)
    half_spec = pl.BlockSpec((n_dp // 2, width // n_dp, 3 * cols), lambda g: (0, 0, g))
    return pl.pallas_call(
        attend_back_kernel,
        grid=(steps,),
        in_specs=[
            pl.BlockSpec(memory_space=pltpu.SMEM), whole(normt), nat, nat, nat,
            pl.BlockSpec((cols, seq), lambda g: (g, 0)),
            pl.BlockSpec((group, seq, seq), lambda g: (g, 0, 0)),
            pl.BlockSpec((group, 1, seq), lambda g: (g, 0, 0)),
            nat,
        ],
        out_specs=[
            half_spec, half_spec, pl.BlockSpec((seq, 3 * cols), lambda g: (0, g)),
            pl.BlockSpec((group, 1, 2 * seq), lambda g: (g, 0, 0)),
        ],
        out_shape=[
            sds(half, BF16), sds(half, BF16), sds((seq, 3 * width), BF16),
            sds((heads, 1, 2 * seq), F32),
        ],
        scratch_shapes=[pltpu.VMEM((TILE, 2 * seq), F32), pltpu.VMEM((width, 3 * cols), BF16)],
        compiler_params=params(dimension_semantics=("arbitrary",)),
        cost_estimate=cost(
            6 * seq * width * width + 8 * seq * seq * width,
            2 * (6 * width * width + 8 * seq * width + heads * seq * seq),
        ),
        name="attention_backward",
    )(number, normt, q, k, v, kt, e, rinv, grad_ctx)


def first_back_kernel(cols, num_ref, tok_ref, gain_ref, gmid_ref, grads_ref, *refs):
    pieces, (gtok_ref, ggain_ref, w_ref) = refs[:-3], refs[-3:]
    width = tok_ref.shape[1]
    join_rows(num_ref, pieces, w_ref)
    grad = jnp.zeros(tok_ref.shape, F32)
    for i, start in enumerate(range(0, 3 * width, cols)):
        col = i % 3 * width + i // 3 * cols
        grad = grad + dot_nt(grads_ref[:, start : start + cols], w_ref[:, col : col + cols])
    grad_in, grad_gain = norm_back(tok_ref[...].astype(F32), gain_ref[...], grad)
    gtok_ref[...] = gmid_ref[...] + grad_in
    ggain_ref[...] = grad_gain


def first_back(number, tokens, gain, grad_middle, grads, pieces, cols):
    seq, width = tokens.shape
    vmem = pl.BlockSpec(memory_space=pltpu.VMEM)
    return pl.pallas_call(
        functools.partial(first_back_kernel, cols),
        in_specs=[pl.BlockSpec(memory_space=pltpu.SMEM)] + [vmem] * (4 + len(pieces)),
        out_shape=[
            jax.ShapeDtypeStruct((seq, width), F32), jax.ShapeDtypeStruct((1, width), F32)
        ],
        scratch_shapes=[pltpu.VMEM((width, 3 * width), BF16)],
        compiler_params=params(),
        cost_estimate=cost(6 * seq * width * width, 6 * width * width + 16 * seq * width),
        name="first_norm_backward",
    )(number, tokens, gain, grad_middle, grads, *pieces)


def output_kernel(middle_ref, target_ref, *refs):
    out_ref = refs[-1]
    total = middle_ref[...]
    for l, back in enumerate(refs[:-1]):
        rows = back.shape[0]
        total = total + dot(token_hot(target_ref[...], l * rows, rows), back[...])
    out_ref[...] = total.astype(BF16)


def output_step(middle, target_col, backs):
    seq, width = middle.shape
    slots = sum(b.shape[0] for b in backs)
    return pl.pallas_call(
        output_kernel,
        out_shape=jax.ShapeDtypeStruct((seq, width), BF16),
        compiler_params=params(),
        cost_estimate=cost(2 * slots * seq * width, 6 * seq * width + 2 * slots * width),
        name="layer_output",
    )(middle, target_col, *backs)


def flip(value, axis, bit):
    size = lax.axis_size(axis)
    return lax.ppermute(value, axis, [(i, i ^ bit) for i in range(size)])


def butterfly_sum(value, axes):
    for axis in axes:
        bit = 1
        while bit < lax.axis_size(axis):
            value = value + flip(value, axis, bit)
            bit *= 2
    return value


def after(value, *others):
    return lax.optimization_barrier((value, *others))[0]


def gather_y(piece):
    pieces = {0: piece}
    bit = 2
    while bit < lax.axis_size("dp"):
        pieces.update({m | bit: flip(p, "dp", bit) for m, p in pieces.items()})
        bit *= 2
    return pieces


def gather_cores(pieces):
    pieces = {**pieces, **{m | 1: flip(p, "dp", 1) for m, p in pieces.items()}}
    return [pieces[m] for m in sorted(pieces)]


def reduce_bits(terms, bits, dp_index):
    first = None
    for bit in bits:
        mine = jnp.where((dp_index & bit) != 0, 1, 0)
        halves = [t.reshape(2, t.shape[0] // 2, *t.shape[1:]) for t in terms]
        pick = lambda i: [
            lax.dynamic_index_in_dim(t, i, 0, keepdims=False).astype(F32) for t in halves
        ]
        sent = sum(pick(1 - mine)).astype(BF16)
        first = sent if first is None else first
        terms = [sum(pick(mine)), flip(sent, "dp", bit)]
    return sum(t.astype(F32) for t in terms)[0], first


def sum_expert(total):
    peers = lax.axis_size("expert")
    rows, cols = total.shape
    parts = total.astype(BF16).reshape(peers, rows // peers, cols)
    arrived = lax.all_to_all(parts, "expert", split_axis=0, concat_axis=0, tiled=True)
    return jnp.sum(arrived.astype(F32), axis=0).astype(BF16)


def spread_expert(share, peers):
    rows, cols = share.shape
    spread = jnp.broadcast_to(share[None], (peers, rows, cols))
    shared = lax.all_to_all(spread, "expert", split_axis=0, concat_axis=0, tiled=True)
    return shared.reshape(peers * rows, cols).astype(F32)


def body(
    tokens, segments, routes, slots, bucket_table, gain_attn, w_query, w_key, w_value, w_output,
    rel_bias, gain_ffn, w_router, w_in, w_out, cotangent,
):
    seq, width = tokens.shape
    buckets, heads = rel_bias.shape
    experts = w_router.shape[1]
    n_dp = lax.axis_size("dp")
    peers = lax.axis_size("expert")
    local = w_in.shape[0]
    capacity = max(2, (5 * seq + 4 * experts - 1) // (4 * experts))
    rows = peers * capacity
    dp_index = lax.axis_index("dp")
    expert_index = lax.axis_index("expert")
    number = jnp.reshape(dp_index, (1,)).astype(jnp.int32)
    dp_bits = [1 << b for b in reversed(range(n_dp.bit_length() - 1))]
    group = 4
    cols = width // heads * group

    along_y = gather_y(jnp.concatenate([w_query, w_key, w_value], axis=1))
    router_pad = jnp.pad(w_router, ((0, 0), (0, -experts % TILE)))
    w_or = lax.all_gather(
        jnp.concatenate([w_output, router_pad], axis=1), "dp", axis=0, tiled=True
    )

    order = (routes % local) * rows + (routes // local) * capacity + slots
    target = jnp.where(slots >= 0, order, -1)
    target_row = target[None, :]
    target_col = target[:, None]
    by_peer = jnp.where(slots >= 0, routes * capacity + slots, -1)
    gain_one = gain_attn[None, :]
    gain_two = gain_ffn[None, :]

    def exchange(values):
        return lax.all_to_all(values, "expert", split_axis=0, concat_axis=0, tiled=True)

    def exchange_rows(values):
        return exchange(values.reshape(peers, capacity, width)).reshape(rows, width)

    reversed_table = jnp.concatenate([bucket_table[::-1], jnp.full((1,), -1, jnp.int32)])
    bucket_ids = jnp.arange(buckets, dtype=jnp.int32)
    hot_rev = (bucket_ids[:, None] == reversed_table[None, :]).astype(F32)
    rel_rev = jnp.dot(rel_bias.T, hot_rev, precision=HIGH)
    shifted = jnp.roll(reversed_table, 1 - TILE)
    hot_shifted = (shifted[:, None] == bucket_ids[None, :]).astype(F32)
    bias, normed, normt, kseg, qseg = prepare(rel_rev, tokens, gain_one, segments)
    c_placed = place(target_row, cotangent, local, rows)
    c_here = [exchange_rows(c_placed[0])]
    by_col = by_peer[:, None]
    along_y, bias, normed, normt, kseg, qseg, target_col, by_col, c_here[0] = (
        lax.optimization_barrier(
            (along_y, bias, normed, normt, kseg, qseg, target_col, by_col, c_here[0])
        )
    )
    pieces = gather_cores(along_y)
    *saved, ctxt = attend(number, normed, bias, kseg, qseg, pieces, heads, group)
    for part in c_placed[1:]:
        c_here.append(exchange_rows(after(part, *pieces)))
    middle, *placed = middle_step(tokens, w_or, gain_two, target_row, ctxt, local, rows)
    placed, *c_here = lax.optimization_barrier((placed, *c_here))
    arrived = [None] * local
    for l in reversed(range(local)):
        ready = after(placed[l], arrived[l + 1]) if l + 1 < local else placed[l]
        arrived[l] = exchange_rows(ready)
    x_all, c_all, backs, scaled, router_terms, numbers = ([None] * local for _ in range(6))
    for l in reversed(range(local)):
        numbers[l] = jnp.stack([dp_index, expert_index * local + l]).astype(jnp.int32)
        sources = (arrived[l], c_here[l])
        if l + 1 < local:
            *sources, _ = lax.optimization_barrier((*sources, scaled[l + 1]))
        x_all[l], c_all[l] = [lax.all_gather(a, "dp", axis=0, tiled=False) for a in sources]
        scaled[l], grad_x, router_terms[l] = expert_step(
            numbers[l], arrived[l], c_here[l], w_or, w_in, w_out, l, 1024, experts
        )
        backs[l] = exchange_rows(grad_x)

    def weight_terms(l, prior):
        return expert_grads(
            numbers[l], x_all[l], c_all[l], w_or, w_in, w_out, l, n_dp, experts, prior
        )

    expert_terms = weight_terms(local - 1, ())
    backs, expert_terms = lax.optimization_barrier((backs, expert_terms))
    scaled, _ = lax.optimization_barrier((scaled, backs))
    stacked = jnp.stack([part.reshape(peers, capacity, width) for part in scaled], axis=1)
    returned = exchange(stacked.reshape(peers, local * capacity, width)).reshape(-1, width)

    grad_middle, grad_ctx, keep_o, send_o, ggain_two = middle_back(
        jnp.stack([dp_index, jnp.int32(n_dp // 2)]), cotangent, middle, gain_two, target_col, w_or, ctxt, backs, router_terms, n_dp
    )
    keep, send, grads, diag = attend_back(number, normt, *saved, grad_ctx, group, n_dp)
    crossed_o = flip(send_o, "dp", dp_bits[0])
    crossed_o, send, returned, x_all, c_all = lax.optimization_barrier(
        (crossed_o, send, returned, x_all, c_all)
    )
    crossed = flip(send, "dp", 1)
    part, sent = reduce_bits([keep, crossed], dp_bits[:-1], dp_index)
    by_index = (n_dp // 2, width // n_dp, w_or.shape[1])
    terms_o = [t.reshape(by_index) for t in (keep_o, crossed_o)]
    part_o, _ = reduce_bits(terms_o, dp_bits[1:], dp_index)
    grad_tokens, ggain_one = first_back(
        number, tokens, gain_one, grad_middle, grads, pieces, cols
    )
    if sent is not None:
        part_o = after(part_o, sent)
    summed_o = sum_expert(part_o)
    grad_rel = jnp.dot(diag.reshape(heads, 2 * seq), hot_shifted, precision=HIGH)
    rel_row = jnp.pad(grad_rel.reshape(1, heads * buckets), ((0, 0), (0, width - heads * buckets)))
    late = jnp.concatenate([ggain_two, ggain_one, rel_row], axis=0)
    late = late + flip(late, "dp", 1)
    part, grad_tokens, summed_o, late = lax.optimization_barrier(
        (part, grad_tokens, summed_o, late)
    )
    for bit in dp_bits[:-1]:
        late = late + flip(late, "dp", bit)
    late = butterfly_sum(late, ("expert",))
    summed = sum_expert(part)
    summed, late = lax.optimization_barrier((summed, late))
    ordered = [
        summed[:, g + i * cols : g + (i + 1) * cols]
        for i in range(3)
        for g in range(0, 3 * width, 3 * cols)
    ]
    shards = spread_expert(jnp.concatenate([*ordered, summed_o], axis=1), peers)
    for l in reversed(range(local - 1)):
        expert_terms = weight_terms(l, expert_terms)
    output = output_step(middle, by_col, [returned])
    total_rel = late[2, : heads * buckets].reshape(heads, buckets).T
    shard_q, shard_k, shard_v, shard_o = [
        shards[:, i * width : (i + 1) * width] for i in range(4)
    ]
    return (
        output,
        grad_tokens,
        late[1],
        shard_q,
        shard_k,
        shard_v,
        shard_o,
        total_rel,
        late[0],
        shards[:, 4 * width : 4 * width + experts],
        expert_terms[0],
        expert_terms[1],
    )


def solution(mesh):
    in_specs = (
        P(("dp", "expert"), None),
        P(("dp", "expert"), None),
        P(("dp", "expert")),
        P(("dp", "expert")),
        P(),
        P(),
        P("dp", None),
        P("dp", None),
        P("dp", None),
        P("dp", None),
        P(),
        P(),
        P("dp", None),
        P("expert", None, None),
        P("expert", None, None),
        P(("dp", "expert"), None),
    )
    out_specs = (
        P(("dp", "expert"), None),
        P(("dp", "expert"), None),
        P(),
        P("dp", None),
        P("dp", None),
        P("dp", None),
        P("dp", None),
        P(),
        P(),
        P("dp", None),
        P("expert", None, "dp"),
        P("expert", "dp", None),
    )
    return jax.shard_map(body, mesh=mesh, in_specs=in_specs, out_specs=out_specs, check_vma=False)
```

```python
import functools
import math

import jax
import jax.numpy as jnp
from jax import lax
from jax.experimental import pallas as pl
from jax.experimental.pallas import tpu as pltpu
from jax.sharding import PartitionSpec as P

EPS = 1e-06
HIGH = lax.Precision.HIGHEST
F32 = jnp.float32
BF16 = jnp.bfloat16
VMEM_LIMIT = 56 * 1024 * 1024
TILE = 128
STRIP = 256
SUB = 256
GELU_A = math.sqrt(2.0 / math.pi)
GELU_B = 0.044715


def dot(a, b):
    return jnp.dot(a, b, preferred_element_type=F32)


def dot_nt(a, b):
    return lax.dot_general(a, b, (((1,), (1,)), ((), ())), preferred_element_type=F32)


def params(**kw):
    return pltpu.CompilerParams(vmem_limit_bytes=VMEM_LIMIT, **kw)


def cost(flops, nbytes, trans=0):
    return pl.CostEstimate(flops=int(flops), bytes_accessed=int(nbytes), transcendentals=int(trans))


def rms_scale(stream):
    return lax.rsqrt(jnp.mean(stream * stream, axis=-1, keepdims=True) + EPS)


def norm_back(stream, gain, grad_out):
    scale = rms_scale(stream)
    grad_gain = jnp.sum(grad_out * (stream * scale), axis=0, keepdims=True)
    scaled = grad_out * gain
    inner = jnp.mean(scaled * stream, axis=-1, keepdims=True)
    grad_in = scale * scaled - stream * (scale * scale * scale * inner)
    return grad_in, grad_gain


def gelu_pair(v):
    sq = v * v
    power = jnp.minimum(v * (-2.0 * GELU_A - (2.0 * GELU_A * GELU_B) * sq), 80.0)
    total = 1.0 + jnp.exp(power)
    guess = pl.reciprocal(total, approx=True)
    half = guess * (2.0 - total * guess)
    value = v * half
    slope = half + value * (1.0 - half) * (2.0 * GELU_A + (6.0 * GELU_A * GELU_B) * sq)
    return value, slope


def slot_hot(target_row, start, rows):
    seq = target_row.shape[1]
    ids = lax.broadcasted_iota(jnp.int32, (rows, seq), 0) + start
    return (ids == target_row).astype(F32).astype(BF16)


def token_hot(target_col, start, rows):
    seq = target_col.shape[0]
    ids = lax.broadcasted_iota(jnp.int32, (seq, rows), 1) + start
    return (ids == target_col).astype(F32).astype(BF16)


def beside_kernel(*refs):
    width = refs[0].shape[1]
    for i, ref in enumerate(refs[:-1]):
        refs[-1][:, i * width : (i + 1) * width] = ref[...]


def beside(*arrays):
    rows, width = arrays[0].shape
    return pl.pallas_call(
        beside_kernel,
        out_shape=jax.ShapeDtypeStruct((rows, width * len(arrays)), arrays[0].dtype),
        compiler_params=params(),
        cost_estimate=cost(0, 4 * rows * width * len(arrays)),
        name="weights_side_by_side",
    )(*arrays)


def place_kernel(target_ref, rows_ref, *out_refs):
    for l, out_ref in enumerate(out_refs):
        rows = out_ref.shape[0]
        out_ref[...] = dot(slot_hot(target_ref[...], l * rows, rows), rows_ref[...]).astype(BF16)


def place(target_row, values, local, rows):
    seq, width = values.shape
    return pl.pallas_call(
        place_kernel,
        out_shape=[jax.ShapeDtypeStruct((rows, width), BF16)] * local,
        compiler_params=params(),
        cost_estimate=cost(2 * local * rows * seq * width, 2 * (local * rows + seq) * width),
        name="place_cotangent",
    )(target_row, values)


def prepare_kernel(
    rel_ref, tok_ref, gain_ref, seg_ref, rows_ref,
    out_ref, normed_ref, normt_ref, kseg_ref, qseg_ref, *col_refs,
):
    heads, width = rel_ref.shape
    wide = out_ref.shape[2]
    for h in range(heads):
        base = jnp.broadcast_to(rel_ref[h : h + 1, :], (TILE, width))
        turned = pltpu.roll(base, width - (TILE - 1), 1, stride=1, stride_axis=0)
        out_ref[h] = turned[:, :wide]
    stream = tok_ref[...].astype(F32)
    normed = stream * rms_scale(stream) * gain_ref[...]
    normed_ref[...] = normed.astype(BF16)
    normt_ref[...] = normed.T.astype(BF16)
    seq = tok_ref.shape[0]
    same = (lax.broadcasted_iota(jnp.int32, (TILE, seq), 0) == seg_ref[...]).astype(F32).T
    kseg_ref[...] = same.astype(BF16)
    qseg_ref[...] = ((same - 1.0) * 1e9).astype(BF16)
    for i, col_ref in enumerate(col_refs):
        row = jnp.broadcast_to(rows_ref[i : i + 1, :].astype(F32), (TILE, seq))
        col_ref[...] = row.T[:, :1].astype(jnp.int32)


def prepare(rel_rev, tokens, gain, segments, slot_rows):
    heads, span = rel_rev.shape
    seq, width = tokens.shape
    wide = 2 * seq - TILE
    return pl.pallas_call(
        prepare_kernel,
        out_shape=[
            jax.ShapeDtypeStruct((heads, TILE, wide), F32),
            jax.ShapeDtypeStruct((seq, width), BF16),
            jax.ShapeDtypeStruct((width, seq), BF16),
            jax.ShapeDtypeStruct((seq, TILE), BF16),
            jax.ShapeDtypeStruct((seq, TILE), BF16),
        ]
        + [jax.ShapeDtypeStruct((seq, 1), jnp.int32)] * slot_rows.shape[0],
        compiler_params=params(),
        cost_estimate=cost(heads * TILE * span, 4 * heads * TILE * wide + 6 * seq * width),
        name="bias_and_first_norm",
    )(rel_rev, tokens, gain, segments, slot_rows)


def join_rows(num_ref, pieces, w_ref):
    part = pieces[0].shape[0]
    for mask, piece in enumerate(pieces):
        row = pl.multiple_of((num_ref[0] ^ mask) * part, 16)
        w_ref[pl.ds(row, part), :] = piece[...]


def attend_kernel(num_ref, normed_ref, bias_ref, kseg_ref, qseg_ref, *refs):
    pieces, refs = refs[:-8], refs[-8:]
    q_ref, k_ref, v_ref, kt_ref, e_ref, rinv_ref, ctxt_ref, w_ref = refs
    seq, cols = q_ref.shape
    width = normed_ref.shape[1]
    step = pl.program_id(0)

    @pl.when(step == 0)
    def _():
        join_rows(num_ref, pieces, w_ref)

    at = lambda base: pl.ds(pl.multiple_of(base * width + step * cols, TILE), cols)
    heads = e_ref.shape[0]
    hd = cols // heads
    per_tile = TILE // hd
    normed = normed_ref[...]
    q32 = dot(normed, w_ref[:, at(0)]).astype(BF16).astype(F32) * (1.0 / math.sqrt(hd))
    k32 = dot(normed, w_ref[:, at(1)])
    v32 = dot(normed, w_ref[:, at(2)])
    q_ref[...] = q32.astype(BF16)
    k_ref[...] = k32.astype(BF16)
    v_ref[...] = v32.astype(BF16)
    kt_ref[...] = k32.T.astype(BF16)
    vt = v32.T.astype(BF16)
    lane = lax.broadcasted_iota(jnp.int32, (STRIP, TILE), 1) // hd
    kseg = kseg_ref[...]

    def scores_of(h, start):
        sl = slice(h // per_tile * TILE, (h // per_tile + 1) * TILE)
        st = slice(start, start + STRIP)
        q_pair = q_ref[st, sl]
        q_own = jnp.where(lane == h % per_tile, q_pair, jnp.zeros_like(q_pair))
        k_all = jnp.concatenate([k_ref[:, sl], kseg], axis=1)
        return dot_nt(k_all, jnp.concatenate([q_own, qseg_ref[st]], axis=1))

    items = [(h, start) for h in range(heads) for start in range(0, seq, STRIP)]
    upcoming = scores_of(*items[0])
    for i, (h, start) in enumerate(items):
        scores = upcoming
        if i + 1 < len(items):
            upcoming = scores_of(*items[i + 1])
        parts = []
        for b in range(0, seq, TILE):
            off = seq - TILE - b + start
            parts.append(scores[b : b + TILE] + bias_ref[h, :, off : off + STRIP])
        scores = jnp.concatenate(parts, axis=0)
        e = jnp.exp(scores - jnp.max(scores, axis=0, keepdims=True))
        rinv = 1.0 / jnp.sum(e, axis=0, keepdims=True)
        eb = e.astype(BF16)
        e_ref[h, :, start : start + STRIP] = eb
        rinv_ref[h, :, start : start + STRIP] = rinv
        ctxt = dot(vt[h * hd : (h + 1) * hd], eb) * rinv
        ctxt_ref[h * hd : (h + 1) * hd, start : start + STRIP] = ctxt.astype(BF16)


def attend(number, normed, bias, kseg, qseg, pieces, heads, group):
    seq, width = normed.shape
    cols = width // heads * group
    steps = heads // group
    wide = bias.shape[2]
    whole = lambda a: pl.BlockSpec(a.shape, lambda g: (0,) * a.ndim)
    nat = pl.BlockSpec((seq, cols), lambda g: (0, g))
    tr = pl.BlockSpec((cols, seq), lambda g: (g, 0))
    sds = jax.ShapeDtypeStruct
    return pl.pallas_call(
        attend_kernel,
        grid=(steps,),
        in_specs=[
            pl.BlockSpec(memory_space=pltpu.SMEM), whole(normed),
            pl.BlockSpec((group, TILE, wide), lambda g: (g, 0, 0)), whole(kseg), whole(qseg),
        ]
        + [whole(p) for p in pieces],
        out_specs=[
            nat, nat, nat, tr,
            pl.BlockSpec((group, seq, seq), lambda g: (g, 0, 0)),
            pl.BlockSpec((group, 1, seq), lambda g: (g, 0, 0)),
            tr,
        ],
        out_shape=[
            sds((seq, width), BF16), sds((seq, width), BF16), sds((seq, width), BF16),
            sds((width, seq), BF16), sds((heads, seq, seq), BF16), sds((heads, 1, seq), F32),
            sds((width, seq), BF16),
        ],
        scratch_shapes=[pltpu.VMEM((width, 3 * width), BF16)],
        compiler_params=params(dimension_semantics=("arbitrary",)),
        cost_estimate=cost(
            6 * seq * width * width + 4 * seq * seq * width,
            2 * (3 * width * width + 9 * seq * width + heads * seq * seq) + 4 * bias.size,
            heads * seq * seq,
        ),
        name="attention_forward",
    )(number, normed, bias, kseg, qseg, *pieces)


def middle_kernel(tok_ref, wo_ref, gain_ref, target_ref, ctx_ref, middle_ref, *placed_refs):
    width = tok_ref.shape[1]
    context = ctx_ref[...].astype(F32).T.astype(BF16)
    middle = tok_ref[...].astype(F32) + dot(context, wo_ref[:, :width])
    middle_ref[...] = middle
    normed = (middle * rms_scale(middle) * gain_ref[...]).astype(BF16)
    for l, placed_ref in enumerate(placed_refs):
        rows = placed_ref.shape[0]
        placed_ref[...] = dot(slot_hot(target_ref[...], l * rows, rows), normed).astype(BF16)


def middle_step(tokens, w_out, gain, target_row, ctxt, local, rows):
    seq, width = tokens.shape
    return pl.pallas_call(
        middle_kernel,
        out_shape=[jax.ShapeDtypeStruct((seq, width), F32)]
        + [jax.ShapeDtypeStruct((rows, width), BF16)] * local,
        compiler_params=params(),
        cost_estimate=cost(
            2 * seq * width * width + 2 * local * rows * seq * width,
            2 * width * width + 8 * seq * width + 2 * local * rows * width,
        ),
        name="output_projection_dispatch",
    )(tokens, w_out, gain, target_row, ctxt)


def gate_of(logits, expert):
    top = jnp.max(logits, axis=-1, keepdims=True)
    ex = jnp.exp(logits - top)
    prob = ex / jnp.sum(ex, axis=-1, keepdims=True)
    hot = lax.broadcasted_iota(jnp.int32, logits.shape, 1) == expert
    gate = jnp.sum(jnp.where(hot, prob, 0.0), axis=-1, keepdims=True)
    return prob, hot, gate


def expert_kernel(
    num_ref, x_ref, c_ref, wr_ref, win_ref, wout_ref,
    scaled_ref, grad_ref, router_ref, gp_ref, acc_p, acc_g,
):
    step = pl.program_id(0)
    experts = router_ref.shape[0]

    @pl.when(step == 0)
    def _():
        _, _, gate = gate_of(dot(x_ref[...], wr_ref[...])[:, :experts], num_ref[1])
        gp_ref[...] = (gate * c_ref[...].astype(F32)).astype(BF16)
        acc_p[...] = jnp.zeros_like(acc_p)
        acc_g[...] = jnp.zeros_like(acc_g)

    def products(sub):
        pre = dot(x_ref[...], win_ref[0, :, sub : sub + SUB])
        return pre, dot_nt(gp_ref[...], wout_ref[0, sub : sub + SUB, :])

    hiddens, grads = [], []
    upcoming = products(0)
    for sub in range(SUB, win_ref.shape[2] + SUB, SUB):
        pre, grad_hidden = upcoming
        if sub < win_ref.shape[2]:
            upcoming = products(sub)
        hidden, slope = gelu_pair(pre)
        hiddens.append(hidden.astype(BF16))
        grads.append((grad_hidden * slope).astype(BF16))
    acc_p[...] += dot(jnp.concatenate(hiddens, axis=1), wout_ref[0])
    acc_g[...] += dot_nt(jnp.concatenate(grads, axis=1), win_ref[0])

    @pl.when(step == pl.num_programs(0) - 1)
    def _():
        x = x_ref[...]
        prob, hot, gate = gate_of(dot(x, wr_ref[...])[:, :experts], num_ref[1])
        produced = acc_p[...]
        scaled_ref[...] = (gate * produced).astype(BF16)
        grad_gate = jnp.sum(
            c_ref[...].astype(F32) * produced.astype(BF16).astype(F32), axis=-1, keepdims=True
        )
        grad_logits = prob * (jnp.where(hot, grad_gate, 0.0) - gate * grad_gate)
        logits_b = grad_logits.astype(BF16)
        grad_ref[...] = (acc_g[...] + dot_nt(logits_b, wr_ref[:, :experts])).astype(BF16)
        router_ref[...] = dot(grad_logits.T.astype(BF16), x)


def expert_step(number, x, c, w_or, w_in, w_out, local, block, experts):
    rows, width = x.shape
    ff = w_in.shape[2]
    router_cols = w_or.shape[1] - width
    whole = lambda a: pl.BlockSpec(a.shape, lambda f: (0,) * a.ndim)
    row_spec = pl.BlockSpec((rows, width), lambda f: (0, 0))
    return pl.pallas_call(
        expert_kernel,
        grid=(ff // block,),
        in_specs=[
            pl.BlockSpec(memory_space=pltpu.SMEM),
            whole(x),
            whole(c),
            pl.BlockSpec((width, router_cols), lambda f: (0, width // router_cols)),
            pl.BlockSpec((1, width, block), lambda f: (local, 0, f)),
            pl.BlockSpec((1, block, width), lambda f: (local, f, 0)),
        ],
        out_specs=[row_spec, row_spec, pl.BlockSpec((experts, width), lambda f: (0, 0))],
        out_shape=[
            jax.ShapeDtypeStruct((rows, width), BF16),
            jax.ShapeDtypeStruct((rows, width), BF16),
            jax.ShapeDtypeStruct((experts, width), F32),
        ],
        scratch_shapes=[
            pltpu.VMEM((rows, width), BF16),
            pltpu.VMEM((rows, width), F32),
            pltpu.VMEM((rows, width), F32),
        ],
        compiler_params=params(dimension_semantics=("arbitrary",)),
        cost_estimate=cost(
            8 * rows * width * ff, 4 * width * ff + 8 * rows * width, rows * ff
        ),
        name="expert_rows",
    )(number, x, c, w_or, w_in, w_out)


def expert_grad_kernel(experts, num_ref, x_ref, c_ref, wr_ref, win_ref, wout_ref, *refs):
    gin_ref, gout_ref, gp_ref, xt_ref = refs[-4:]
    parts, rows, width = x_ref.shape
    x = x_ref[...].reshape(parts * rows, width)

    @pl.when(pl.program_id(0) == 0)
    def _():
        _, _, gate = gate_of(dot(x, wr_ref[...])[:, :experts], num_ref[1])
        c = c_ref[...].reshape(parts * rows, width)
        gp_ref[...] = (gate * c.astype(F32)).astype(BF16)
        xt_ref[...] = x.astype(F32).T.astype(BF16)

    gp = gp_ref[...]
    pre_t = dot(win_ref[0].T, xt_ref[...])
    hidden_t, slope_t = gelu_pair(pre_t)
    grad_hidden_t = dot_nt(wout_ref[0], gp)
    gout_ref[0] = dot(hidden_t.astype(BF16), gp)
    gin_ref[0] = dot_nt(xt_ref[...], (grad_hidden_t * slope_t).astype(BF16))


def expert_grads(numbers, x_all, c_all, w_or, w_in, w_out, local, n_dp, experts, prior=()):
    parts, rows, width = x_all.shape
    ff = w_out.shape[1]
    router_cols = w_or.shape[1] - width
    part = ff // n_dp
    block = part
    steps = part // block
    whole = lambda a: pl.BlockSpec(a.shape, lambda f, n: (0,) * a.ndim)
    return pl.pallas_call(
        functools.partial(expert_grad_kernel, experts),
        grid_spec=pltpu.PrefetchScalarGridSpec(
            num_scalar_prefetch=1,
            grid=(steps,),
            in_specs=[
                whole(x_all),
                whole(c_all),
                pl.BlockSpec((width, router_cols), lambda f, n: (0, width // router_cols)),
                pl.BlockSpec((1, width, block), lambda f, n: (local, 0, n[0] * steps + f)),
                pl.BlockSpec((1, block, width), lambda f, n: (local, n[0] * steps + f, 0)),
            ]
            + [pl.BlockSpec(memory_space=pl.ANY)] * len(prior),
            out_specs=[
                pl.BlockSpec((1, width, block), lambda f, n: (local, 0, f)),
                pl.BlockSpec((1, block, width), lambda f, n: (local, f, 0)),
            ],
            scratch_shapes=[
                pltpu.VMEM((parts * rows, width), BF16),
                pltpu.VMEM((width, parts * rows), BF16),
            ],
        ),
        out_shape=[
            jax.ShapeDtypeStruct((w_out.shape[0], width, part), F32),
            jax.ShapeDtypeStruct((w_out.shape[0], part, width), F32),
        ],
        compiler_params=params(dimension_semantics=("arbitrary",)),
        cost_estimate=cost(
            8 * parts * rows * width * part,
            4 * parts * rows * width + 12 * width * part,
            parts * rows * part,
        ),
        input_output_aliases={6 + i: i for i in range(len(prior))},
        name="expert_weight_grads",
    )(numbers, x_all, c_all, w_or, w_in, w_out, *prior)


def split_rows(num_ref, full_ref, keep_ref, send_ref):
    part = keep_ref.shape[1]
    core = num_ref[0] & 1
    for y in range(keep_ref.shape[0]):
        own = pl.multiple_of((2 * y + core) * part, 16)
        other = pl.multiple_of((2 * y + 1 - core) * part, 16)
        keep_ref[y] = full_ref[pl.ds(own, part), :]
        send_ref[y] = full_ref[pl.ds(other, part), :]


def middle_back_kernel(top_size, num_ref, cot_ref, middle_ref, gain_ref, target_ref, wo_ref, ctx_ref, *refs):
    refs, (gmid_ref, gctx_ref, keep_ref, send_ref, ggain_ref, gwo_ref) = refs[:-6], refs[-6:]
    local = len(refs) // 2
    back_refs, router_refs = refs[:local], refs[local:]
    seq, width = cot_ref.shape
    target = target_ref[...]
    grad = jnp.zeros((seq, width), F32)
    for l, back in enumerate(back_refs):
        rows = back.shape[0]
        grad = grad + dot(token_hot(target, l * rows, rows), back[...])
    grad_in, grad_gain = norm_back(middle_ref[...], gain_ref[...], grad)
    ggain_ref[...] = grad_gain
    grad_middle = cot_ref[...].astype(F32) + grad_in
    gmid_ref[...] = grad_middle
    grad_attn = grad_middle.astype(BF16)
    gctx_ref[...] = dot_nt(grad_attn, wo_ref[:, :width]).astype(BF16)
    gwo_ref[:, :width] = dot(ctx_ref[...], grad_attn).astype(BF16)
    router = sum(ref[...] for ref in router_refs)
    spare = jnp.zeros((gwo_ref.shape[1] - width - router.shape[0], width), F32)
    gwo_ref[:, width:] = jnp.concatenate([router, spare], axis=0).T.astype(BF16)
    half = keep_ref.shape[0]
    top = num_ref[0] // top_size
    keep_ref[...] = gwo_ref[pl.ds(pl.multiple_of(top * half, 16), half), :]
    send_ref[...] = gwo_ref[pl.ds(pl.multiple_of((1 - top) * half, 16), half), :]


def middle_back(number, cot, middle, gain, target_col, w_or, ctxt, backs, routers, n_dp):
    seq, width = cot.shape
    sds = jax.ShapeDtypeStruct
    slots = sum(b.shape[0] for b in backs)
    half = sds((width // 2, w_or.shape[1]), BF16)
    vmem = pl.BlockSpec(memory_space=pltpu.VMEM)
    return pl.pallas_call(
        functools.partial(middle_back_kernel, n_dp // 2),
        in_specs=[pl.BlockSpec(memory_space=pltpu.SMEM)] + [vmem] * (6 + 2 * len(backs)),
        out_shape=[sds((seq, width), F32), sds((seq, width), BF16), half, half, sds((1, width), F32)],
        scratch_shapes=[pltpu.VMEM(w_or.shape, BF16)],
        compiler_params=params(),
        cost_estimate=cost(
            4 * seq * width * width + 2 * slots * seq * width,
            4 * width * width + 14 * seq * width + 2 * slots * width,
        ),
        name="second_norm_backward",
    )(number, cot, middle, gain, target_col, w_or, ctxt, *backs, *routers)


def attend_back_kernel(
    num_ref, normt_ref, q_ref, k_ref, v_ref, kt_ref, e_ref, rinv_ref, do_ref,
    keep_ref, send_ref, grads_ref, diag_ref, acc_ref, gw_ref,
):
    seq, cols = q_ref.shape
    heads = e_ref.shape[0]
    hd = cols // heads
    per_tile = TILE // hd
    lane = lax.broadcasted_iota(jnp.int32, (STRIP, TILE), 1) // hd
    row_bit = lax.broadcasted_iota(jnp.int32, (8, 2 * seq), 0)
    zero = jnp.zeros((STRIP, TILE), BF16)

    def own(ref, h, start):
        sl = slice(h // per_tile * TILE, (h // per_tile + 1) * TILE)
        return jnp.where(lane == h % per_tile, ref[start : start + STRIP, sl], zero)

    def products(h, start):
        sl = slice(h // per_tile * TILE, (h // per_tile + 1) * TILE)
        do_own = own(do_ref, h, start)
        return do_own, dot_nt(v_ref[:, sl], do_own)

    dk_tiles, dv_tiles, dqt_rows = [], [], []
    items = [(h, start) for h in range(heads) for start in range(0, seq, STRIP)]
    upcoming = products(*items[0])
    for h in range(heads):
        acc_ref[...] = jnp.zeros_like(acc_ref)
        dk = jnp.zeros((seq, TILE), F32)
        dv = jnp.zeros((seq, TILE), F32)
        dqt_parts = []
        for start in range(0, seq, STRIP):
            st = slice(start, start + STRIP)
            do_own, grad_w = upcoming
            at = items.index((h, start)) + 1
            if at < len(items):
                upcoming = products(*items[at])
            p = e_ref[h, :, st].astype(F32) * rinv_ref[h, :, st]
            t = grad_w * p
            ds = t - p * jnp.sum(t, axis=0, keepdims=True)
            dsb = ds.astype(BF16)
            dv = dv + dot(p.astype(BF16), do_own)
            dk = dk + dot(dsb, own(q_ref, h, start))
            dqt_parts.append(dot(kt_ref[h * hd : (h + 1) * hd, :], dsb))
            for b in range(0, seq, TILE):
                off = seq - TILE - b + start
                acc_ref[:, off : off + STRIP] += ds[b : b + TILE]
        if h % per_tile == 0:
            dk_tiles.append(dk)
            dv_tiles.append(dv)
        else:
            dk_tiles[-1] = dk_tiles[-1] + dk
            dv_tiles[-1] = dv_tiles[-1] + dv
        dqt_rows.append(jnp.concatenate(dqt_parts, axis=1))
        folded = acc_ref[...]
        half = TILE // 2
        while half >= 8:
            folded = folded[:half] + pltpu.roll(folded[half:], 2 * seq - half, 1)
            half //= 2
        for bit in (4, 2, 1):
            turned = pltpu.roll(folded, 2 * seq - bit, 1)
            folded = jnp.where((row_bit & bit) != 0, turned, folded)
        diag_ref[h] = jnp.sum(folded, axis=0, keepdims=True)
    dqt = jnp.concatenate(dqt_rows, axis=0) * (1.0 / math.sqrt(hd))
    grads_ref[:, :cols] = dqt.T.astype(BF16)
    for base, tiles in ((1, dk_tiles), (2, dv_tiles)):
        grads_ref[:, base * cols : (base + 1) * cols] = jnp.concatenate(tiles, axis=1).astype(BF16)
    gw_ref[...] = dot(normt_ref[...], grads_ref[...]).astype(BF16)
    split_rows(num_ref, gw_ref, keep_ref, send_ref)


def attend_back(number, normt, q, k, v, kt, e, rinv, grad_ctx, group, n_dp):
    seq, width = q.shape
    heads = e.shape[0]
    cols = width // heads * group
    steps = heads // group
    whole = lambda a: pl.BlockSpec(a.shape, lambda g: (0,) * a.ndim)
    nat = pl.BlockSpec((seq, cols), lambda g: (0, g))
    sds = jax.ShapeDtypeStruct
    half = (n_dp // 2, width // n_dp, 3 * width)
    half_spec = pl.BlockSpec((n_dp // 2, width // n_dp, 3 * cols), lambda g: (0, 0, g))
    return pl.pallas_call(
        attend_back_kernel,
        grid=(steps,),
        in_specs=[
            pl.BlockSpec(memory_space=pltpu.SMEM), whole(normt), nat, nat, nat,
            pl.BlockSpec((cols, seq), lambda g: (g, 0)),
            pl.BlockSpec((group, seq, seq), lambda g: (g, 0, 0)),
            pl.BlockSpec((group, 1, seq), lambda g: (g, 0, 0)),
            nat,
        ],
        out_specs=[
            half_spec, half_spec, pl.BlockSpec((seq, 3 * cols), lambda g: (0, g)),
            pl.BlockSpec((group, 1, 2 * seq), lambda g: (g, 0, 0)),
        ],
        out_shape=[
            sds(half, BF16), sds(half, BF16), sds((seq, 3 * width), BF16),
            sds((heads, 1, 2 * seq), F32),
        ],
        scratch_shapes=[pltpu.VMEM((TILE, 2 * seq), F32), pltpu.VMEM((width, 3 * cols), BF16)],
        compiler_params=params(dimension_semantics=("arbitrary",)),
        cost_estimate=cost(
            6 * seq * width * width + 8 * seq * seq * width,
            2 * (6 * width * width + 8 * seq * width + heads * seq * seq),
        ),
        name="attention_backward",
    )(number, normt, q, k, v, kt, e, rinv, grad_ctx)


def first_back_kernel(cols, num_ref, tok_ref, gain_ref, gmid_ref, grads_ref, *refs):
    pieces, (gtok_ref, ggain_ref, w_ref) = refs[:-3], refs[-3:]
    width = tok_ref.shape[1]
    join_rows(num_ref, pieces, w_ref)
    grad = jnp.zeros(tok_ref.shape, F32)
    for i, start in enumerate(range(0, 3 * width, cols)):
        col = i % 3 * width + i // 3 * cols
        grad = grad + dot_nt(grads_ref[:, start : start + cols], w_ref[:, col : col + cols])
    grad_in, grad_gain = norm_back(tok_ref[...].astype(F32), gain_ref[...], grad)
    gtok_ref[...] = gmid_ref[...] + grad_in
    ggain_ref[...] = grad_gain


def first_back(number, tokens, gain, grad_middle, grads, pieces, cols):
    seq, width = tokens.shape
    vmem = pl.BlockSpec(memory_space=pltpu.VMEM)
    return pl.pallas_call(
        functools.partial(first_back_kernel, cols),
        in_specs=[pl.BlockSpec(memory_space=pltpu.SMEM)] + [vmem] * (4 + len(pieces)),
        out_shape=[
            jax.ShapeDtypeStruct((seq, width), F32), jax.ShapeDtypeStruct((1, width), F32)
        ],
        scratch_shapes=[pltpu.VMEM((width, 3 * width), BF16)],
        compiler_params=params(),
        cost_estimate=cost(6 * seq * width * width, 6 * width * width + 16 * seq * width),
        name="first_norm_backward",
    )(number, tokens, gain, grad_middle, grads, *pieces)


def output_kernel(middle_ref, target_ref, *refs):
    out_ref = refs[-1]
    total = middle_ref[...]
    for l, back in enumerate(refs[:-1]):
        rows = back.shape[0]
        total = total + dot(token_hot(target_ref[...], l * rows, rows), back[...])
    out_ref[...] = total.astype(BF16)


def output_step(middle, target_col, backs):
    seq, width = middle.shape
    slots = sum(b.shape[0] for b in backs)
    return pl.pallas_call(
        output_kernel,
        out_shape=jax.ShapeDtypeStruct((seq, width), BF16),
        compiler_params=params(),
        cost_estimate=cost(2 * slots * seq * width, 6 * seq * width + 2 * slots * width),
        name="layer_output",
    )(middle, target_col, *backs)


def flip(value, axis, bit):
    size = lax.axis_size(axis)
    return lax.ppermute(value, axis, [(i, i ^ bit) for i in range(size)])


def butterfly_sum(value, axes):
    for axis in axes:
        bit = 1
        while bit < lax.axis_size(axis):
            value = value + flip(value, axis, bit)
            bit *= 2
    return value


def after(value, *others):
    return lax.optimization_barrier((value, *others))[0]


def gather_y(piece):
    pieces = {0: piece}
    bit = 2
    while bit < lax.axis_size("dp"):
        pieces.update({m | bit: flip(p, "dp", bit) for m, p in pieces.items()})
        bit *= 2
    return pieces


def gather_cores(pieces):
    pieces = {**pieces, **{m | 1: flip(p, "dp", 1) for m, p in pieces.items()}}
    return [pieces[m] for m in sorted(pieces)]


def reduce_bits(terms, bits, dp_index):
    first = None
    for bit in bits:
        mine = jnp.where((dp_index & bit) != 0, 1, 0)
        halves = [t.reshape(2, t.shape[0] // 2, *t.shape[1:]) for t in terms]
        pick = lambda i: [
            lax.dynamic_index_in_dim(t, i, 0, keepdims=False).astype(F32) for t in halves
        ]
        sent = sum(pick(1 - mine)).astype(BF16)
        first = sent if first is None else first
        terms = [sum(pick(mine)), flip(sent, "dp", bit)]
    return sum(t.astype(F32) for t in terms)[0], first


def sum_expert(total):
    peers = lax.axis_size("expert")
    rows, cols = total.shape
    parts = total.astype(BF16).reshape(peers, rows // peers, cols)
    arrived = lax.all_to_all(parts, "expert", split_axis=0, concat_axis=0, tiled=True)
    return jnp.sum(arrived.astype(F32), axis=0).astype(BF16)


def spread_expert(share, peers):
    rows, cols = share.shape
    spread = jnp.broadcast_to(share[None], (peers, rows, cols))
    shared = lax.all_to_all(spread, "expert", split_axis=0, concat_axis=0, tiled=True)
    return shared.reshape(peers * rows, cols).astype(F32)


def body(
    tokens, segments, routes, slots, bucket_table, gain_attn, w_query, w_key, w_value, w_output,
    rel_bias, gain_ffn, w_router, w_in, w_out, cotangent,
):
    seq, width = tokens.shape
    buckets, heads = rel_bias.shape
    experts = w_router.shape[1]
    n_dp = lax.axis_size("dp")
    peers = lax.axis_size("expert")
    local = w_in.shape[0]
    capacity = max(2, (5 * seq + 4 * experts - 1) // (4 * experts))
    rows = peers * capacity
    dp_index = lax.axis_index("dp")
    expert_index = lax.axis_index("expert")
    number = jnp.reshape(dp_index, (1,)).astype(jnp.int32)
    dp_bits = [1 << b for b in reversed(range(n_dp.bit_length() - 1))]
    group = 4
    cols = width // heads * group

    along_y = gather_y(beside(w_query, w_key, w_value))
    router_pad = jnp.pad(w_router, ((0, 0), (0, -experts % TILE)))
    w_or = lax.all_gather(
        jnp.concatenate([w_output, router_pad], axis=1), "dp", axis=0, tiled=True
    )

    order = (routes % local) * rows + (routes // local) * capacity + slots
    target = jnp.where(slots >= 0, order, -1)
    target_row = target[None, :]
    by_peer = jnp.where(slots >= 0, routes * capacity + slots, -1)
    gain_one = gain_attn[None, :]
    gain_two = gain_ffn[None, :]

    def exchange(values):
        return lax.all_to_all(values, "expert", split_axis=0, concat_axis=0, tiled=True)

    def exchange_rows(values):
        return exchange(values.reshape(peers, capacity, width)).reshape(rows, width)

    reversed_table = jnp.concatenate([bucket_table[::-1], jnp.full((1,), -1, jnp.int32)])
    bucket_ids = jnp.arange(buckets, dtype=jnp.int32)
    hot_rev = (bucket_ids[:, None] == reversed_table[None, :]).astype(F32)
    rel_rev = jnp.dot(rel_bias.T, hot_rev, precision=HIGH)
    shifted = jnp.roll(reversed_table, 1 - TILE)
    hot_shifted = (shifted[:, None] == bucket_ids[None, :]).astype(F32)
    bias, normed, normt, kseg, qseg, target_col, by_col = prepare(
        rel_rev, tokens, gain_one, segments, jnp.stack([target, by_peer])
    )
    c_placed = list(place(target_row, cotangent, local, rows))
    c_here = [exchange_rows(c_placed[0])]
    along_y, bias, normed, normt, kseg, qseg, c_here[0], c_placed[1:] = (
        lax.optimization_barrier(
            (along_y, bias, normed, normt, kseg, qseg, c_here[0], c_placed[1:])
        )
    )
    pieces = gather_cores(along_y)
    *saved, ctxt = attend(number, normed, bias, kseg, qseg, pieces, heads, group)
    for part in c_placed[1:]:
        c_here.append(exchange_rows(part))
    middle, *placed = middle_step(tokens, w_or, gain_two, target_row, ctxt, local, rows)
    placed, *c_here = lax.optimization_barrier((placed, *c_here))
    arrived = [None] * local
    for l in reversed(range(local)):
        ready = after(placed[l], arrived[l + 1]) if l + 1 < local else placed[l]
        arrived[l] = exchange_rows(ready)
    x_all, c_all, backs, scaled, router_terms, numbers = ([None] * local for _ in range(6))
    for l in reversed(range(local)):
        numbers[l] = jnp.stack([dp_index, expert_index * local + l]).astype(jnp.int32)
        sources = (arrived[l], c_here[l])
        if l + 1 < local:
            *sources, _ = lax.optimization_barrier((*sources, scaled[l + 1]))
        x_all[l], c_all[l] = [lax.all_gather(a, "dp", axis=0, tiled=False) for a in sources]
        scaled[l], grad_x, router_terms[l] = expert_step(
            numbers[l], arrived[l], c_here[l], w_or, w_in, w_out, l, 1024, experts
        )
        backs[l] = exchange_rows(grad_x)

    def weight_terms(l, prior):
        return expert_grads(
            numbers[l], x_all[l], c_all[l], w_or, w_in, w_out, l, n_dp, experts, prior
        )

    expert_terms = weight_terms(local - 1, ())
    backs, expert_terms = lax.optimization_barrier((backs, expert_terms))
    scaled, _ = lax.optimization_barrier((scaled, backs))
    stacked = jnp.stack([part.reshape(peers, capacity, width) for part in scaled], axis=1)
    returned = exchange(stacked.reshape(peers, local * capacity, width)).reshape(-1, width)

    grad_middle, grad_ctx, keep_o, send_o, ggain_two = middle_back(
        number, cotangent, middle, gain_two, target_col, w_or, ctxt, backs, router_terms, n_dp
    )
    keep, send, grads, diag = attend_back(number, normt, *saved, grad_ctx, group, n_dp)
    crossed_o = flip(send_o, "dp", dp_bits[0])
    crossed_o, send, returned, x_all, c_all = lax.optimization_barrier(
        (crossed_o, send, returned, x_all, c_all)
    )
    crossed = flip(send, "dp", 1)
    part, sent = reduce_bits([keep, crossed], dp_bits[:-1], dp_index)
    by_index = (n_dp // 2, width // n_dp, w_or.shape[1])
    terms_o = [t.reshape(by_index) for t in (keep_o, crossed_o)]
    part_o, _ = reduce_bits(terms_o, dp_bits[1:], dp_index)
    grad_tokens, ggain_one = first_back(
        number, tokens, gain_one, grad_middle, grads, pieces, cols
    )
    if sent is not None:
        part_o = after(part_o, sent)
    summed_o = sum_expert(part_o)
    grad_rel = jnp.dot(diag.reshape(heads, 2 * seq), hot_shifted, precision=HIGH)
    rel_row = jnp.pad(grad_rel.reshape(1, heads * buckets), ((0, 0), (0, width - heads * buckets)))
    late = jnp.concatenate([ggain_two, ggain_one, rel_row], axis=0)
    late = butterfly_sum(late, ("dp",))
    part, grad_tokens, summed_o, late = lax.optimization_barrier(
        (part, grad_tokens, summed_o, late)
    )
    late = butterfly_sum(late, ("expert",))
    summed = sum_expert(part)
    summed, late = lax.optimization_barrier((summed, late))
    ordered = [
        summed[:, g + i * cols : g + (i + 1) * cols]
        for i in range(3)
        for g in range(0, 3 * width, 3 * cols)
    ]
    shards = spread_expert(jnp.concatenate([*ordered, summed_o], axis=1), peers)
    for l in reversed(range(local - 1)):
        expert_terms = weight_terms(l, expert_terms)
    output = output_step(middle, by_col, [returned])
    total_rel = late[2, : heads * buckets].reshape(heads, buckets).T
    shard_q, shard_k, shard_v, shard_o = [
        shards[:, i * width : (i + 1) * width] for i in range(4)
    ]
    return (
        output,
        grad_tokens,
        late[1],
        shard_q,
        shard_k,
        shard_v,
        shard_o,
        total_rel,
        late[0],
        shards[:, 4 * width : 4 * width + experts],
        expert_terms[0],
        expert_terms[1],
    )


def solution(mesh):
    in_specs = (
        P(("dp", "expert"), None),
        P(("dp", "expert"), None),
        P(("dp", "expert")),
        P(("dp", "expert")),
        P(),
        P(),
        P("dp", None),
        P("dp", None),
        P("dp", None),
        P("dp", None),
        P(),
        P(),
        P("dp", None),
        P("expert", None, None),
        P("expert", None, None),
        P(("dp", "expert"), None),
    )
    out_specs = (
        P(("dp", "expert"), None),
        P(("dp", "expert"), None),
        P(),
        P("dp", None),
        P("dp", None),
        P("dp", None),
        P("dp", None),
        P(),
        P(),
        P("dp", None),
        P("expert", None, "dp"),
        P("expert", "dp", None),
    )
    return jax.shard_map(body, mesh=mesh, in_specs=in_specs, out_specs=out_specs, check_vma=False)
```

```python
import functools
import math

import jax
import jax.numpy as jnp
from jax import lax
from jax.experimental import pallas as pl
from jax.experimental.pallas import tpu as pltpu
from jax.sharding import PartitionSpec as P

EPS = 1e-06
HIGH = lax.Precision.HIGHEST
F32 = jnp.float32
BF16 = jnp.bfloat16
VMEM_LIMIT = 56 * 1024 * 1024
TILE = 128
STRIP = 256
SUB = 256
GELU_A = math.sqrt(2.0 / math.pi)
GELU_B = 0.044715


def dot(a, b):
    return jnp.dot(a, b, preferred_element_type=F32)


def dot_nt(a, b):
    return lax.dot_general(a, b, (((1,), (1,)), ((), ())), preferred_element_type=F32)


def params(**kw):
    return pltpu.CompilerParams(vmem_limit_bytes=VMEM_LIMIT, **kw)


def cost(flops, nbytes, trans=0):
    return pl.CostEstimate(flops=int(flops), bytes_accessed=int(nbytes), transcendentals=int(trans))


def rms_scale(stream):
    return lax.rsqrt(jnp.mean(stream * stream, axis=-1, keepdims=True) + EPS)


def norm_back(stream, gain, grad_out):
    scale = rms_scale(stream)
    grad_gain = jnp.sum(grad_out * (stream * scale), axis=0, keepdims=True)
    scaled = grad_out * gain
    inner = jnp.mean(scaled * stream, axis=-1, keepdims=True)
    grad_in = scale * scaled - stream * (scale * scale * scale * inner)
    return grad_in, grad_gain


def gelu_pair(v):
    sq = v * v
    power = jnp.minimum(v * (-2.0 * GELU_A - (2.0 * GELU_A * GELU_B) * sq), 80.0)
    total = 1.0 + jnp.exp(power)
    guess = pl.reciprocal(total, approx=True)
    half = guess * (2.0 - total * guess)
    value = v * half
    slope = half + value * (1.0 - half) * (2.0 * GELU_A + (6.0 * GELU_A * GELU_B) * sq)
    return value, slope


def slot_hot(target_row, start, rows):
    seq = target_row.shape[1]
    ids = lax.broadcasted_iota(jnp.int32, (rows, seq), 0) + start
    return (ids == target_row).astype(F32).astype(BF16)


def token_hot(target_col, start, rows):
    seq = target_col.shape[0]
    ids = lax.broadcasted_iota(jnp.int32, (seq, rows), 1) + start
    return (ids == target_col).astype(F32).astype(BF16)


def beside_kernel(*refs):
    width = refs[0].shape[1]
    for i, ref in enumerate(refs[:-1]):
        refs[-1][:, i * width : (i + 1) * width] = ref[...]


def beside(*arrays):
    rows, width = arrays[0].shape
    return pl.pallas_call(
        beside_kernel,
        out_shape=jax.ShapeDtypeStruct((rows, width * len(arrays)), arrays[0].dtype),
        compiler_params=params(),
        cost_estimate=cost(0, 4 * rows * width * len(arrays)),
        name="weights_side_by_side",
    )(*arrays)


def place_kernel(target_ref, rows_ref, *out_refs):
    for l, out_ref in enumerate(out_refs):
        rows = out_ref.shape[0]
        out_ref[...] = dot(slot_hot(target_ref[...], l * rows, rows), rows_ref[...]).astype(BF16)


def place(target_row, values, local, rows):
    seq, width = values.shape
    return pl.pallas_call(
        place_kernel,
        out_shape=[jax.ShapeDtypeStruct((rows, width), BF16)] * local,
        compiler_params=params(),
        cost_estimate=cost(2 * local * rows * seq * width, 2 * (local * rows + seq) * width),
        name="place_cotangent",
    )(target_row, values)


def prepare_kernel(
    rel_ref, tok_ref, gain_ref, seg_ref, rows_ref,
    out_ref, normed_ref, normt_ref, kseg_ref, qseg_ref, *col_refs,
):
    heads, width = rel_ref.shape
    wide = out_ref.shape[2]
    for h in range(heads):
        base = jnp.broadcast_to(rel_ref[h : h + 1, :], (TILE, width))
        turned = pltpu.roll(base, width - (TILE - 1), 1, stride=1, stride_axis=0)
        out_ref[h] = turned[:, :wide]
    stream = tok_ref[...].astype(F32)
    normed = stream * rms_scale(stream) * gain_ref[...]
    normed_ref[...] = normed.astype(BF16)
    normt_ref[...] = normed.T.astype(BF16)
    seq = tok_ref.shape[0]
    same = (lax.broadcasted_iota(jnp.int32, (TILE, seq), 0) == seg_ref[...]).astype(F32).T
    kseg_ref[...] = same.astype(BF16)
    qseg_ref[...] = ((same - 1.0) * 1e9).astype(BF16)
    for i, col_ref in enumerate(col_refs):
        row = jnp.broadcast_to(rows_ref[i : i + 1, :].astype(F32), (TILE, seq))
        col_ref[...] = row.T[:, :1].astype(jnp.int32)


def prepare(rel_rev, tokens, gain, segments, slot_rows):
    heads, span = rel_rev.shape
    seq, width = tokens.shape
    wide = 2 * seq - TILE
    return pl.pallas_call(
        prepare_kernel,
        out_shape=[
            jax.ShapeDtypeStruct((heads, TILE, wide), F32),
            jax.ShapeDtypeStruct((seq, width), BF16),
            jax.ShapeDtypeStruct((width, seq), BF16),
            jax.ShapeDtypeStruct((seq, TILE), BF16),
            jax.ShapeDtypeStruct((seq, TILE), BF16),
        ]
        + [jax.ShapeDtypeStruct((seq, 1), jnp.int32)] * slot_rows.shape[0],
        compiler_params=params(),
        cost_estimate=cost(heads * TILE * span, 4 * heads * TILE * wide + 6 * seq * width),
        name="bias_and_first_norm",
    )(rel_rev, tokens, gain, segments, slot_rows)


def join_rows(num_ref, pieces, w_ref):
    part = pieces[0].shape[0]
    for mask, piece in enumerate(pieces):
        row = pl.multiple_of((num_ref[0] ^ mask) * part, 16)
        w_ref[pl.ds(row, part), :] = piece[...]


def attend_kernel(num_ref, normed_ref, bias_ref, kseg_ref, qseg_ref, *refs):
    pieces, refs = refs[:-8], refs[-8:]
    q_ref, k_ref, v_ref, kt_ref, e_ref, rinv_ref, ctxt_ref, w_ref = refs
    seq, cols = q_ref.shape
    width = normed_ref.shape[1]
    step = pl.program_id(0)

    @pl.when(step == 0)
    def _():
        join_rows(num_ref, pieces, w_ref)

    at = lambda base: pl.ds(pl.multiple_of(base * width + step * cols, TILE), cols)
    heads = e_ref.shape[0]
    hd = cols // heads
    per_tile = TILE // hd
    normed = normed_ref[...]
    q32 = dot(normed, w_ref[:, at(0)]).astype(BF16).astype(F32) * (1.0 / math.sqrt(hd))
    k32 = dot(normed, w_ref[:, at(1)])
    v32 = dot(normed, w_ref[:, at(2)])
    q_ref[...] = q32.astype(BF16)
    k_ref[...] = k32.astype(BF16)
    v_ref[...] = v32.astype(BF16)
    kt_ref[...] = k32.T.astype(BF16)
    vt = v32.T.astype(BF16)
    lane = lax.broadcasted_iota(jnp.int32, (STRIP, TILE), 1) // hd
    kseg = kseg_ref[...]

    def scores_of(h, start):
        sl = slice(h // per_tile * TILE, (h // per_tile + 1) * TILE)
        st = slice(start, start + STRIP)
        q_pair = q_ref[st, sl]
        q_own = jnp.where(lane == h % per_tile, q_pair, jnp.zeros_like(q_pair))
        k_all = jnp.concatenate([k_ref[:, sl], kseg], axis=1)
        return dot_nt(k_all, jnp.concatenate([q_own, qseg_ref[st]], axis=1))

    items = [(h, start) for h in range(heads) for start in range(0, seq, STRIP)]
    upcoming = scores_of(*items[0])
    for i, (h, start) in enumerate(items):
        scores = upcoming
        if i + 1 < len(items):
            upcoming = scores_of(*items[i + 1])
        parts = []
        for b in range(0, seq, TILE):
            off = seq - TILE - b + start
            parts.append(scores[b : b + TILE] + bias_ref[h, :, off : off + STRIP])
        scores = jnp.concatenate(parts, axis=0)
        e = jnp.exp(scores - jnp.max(scores, axis=0, keepdims=True))
        rinv = 1.0 / jnp.sum(e, axis=0, keepdims=True)
        eb = e.astype(BF16)
        e_ref[h, :, start : start + STRIP] = eb
        rinv_ref[h, :, start : start + STRIP] = rinv
        ctxt = dot(vt[h * hd : (h + 1) * hd], eb) * rinv
        ctxt_ref[h * hd : (h + 1) * hd, start : start + STRIP] = ctxt.astype(BF16)


def attend(number, normed, bias, kseg, qseg, pieces, heads, group):
    seq, width = normed.shape
    cols = width // heads * group
    steps = heads // group
    wide = bias.shape[2]
    whole = lambda a: pl.BlockSpec(a.shape, lambda g: (0,) * a.ndim)
    nat = pl.BlockSpec((seq, cols), lambda g: (0, g))
    tr = pl.BlockSpec((cols, seq), lambda g: (g, 0))
    sds = jax.ShapeDtypeStruct
    return pl.pallas_call(
        attend_kernel,
        grid=(steps,),
        in_specs=[
            pl.BlockSpec(memory_space=pltpu.SMEM), whole(normed),
            pl.BlockSpec((group, TILE, wide), lambda g: (g, 0, 0)), whole(kseg), whole(qseg),
        ]
        + [whole(p) for p in pieces],
        out_specs=[
            nat, nat, nat, tr,
            pl.BlockSpec((group, seq, seq), lambda g: (g, 0, 0)),
            pl.BlockSpec((group, 1, seq), lambda g: (g, 0, 0)),
            tr,
        ],
        out_shape=[
            sds((seq, width), BF16), sds((seq, width), BF16), sds((seq, width), BF16),
            sds((width, seq), BF16), sds((heads, seq, seq), BF16), sds((heads, 1, seq), F32),
            sds((width, seq), BF16),
        ],
        scratch_shapes=[pltpu.VMEM((width, 3 * width), BF16)],
        compiler_params=params(dimension_semantics=("arbitrary",)),
        cost_estimate=cost(
            6 * seq * width * width + 4 * seq * seq * width,
            2 * (3 * width * width + 9 * seq * width + heads * seq * seq) + 4 * bias.size,
            heads * seq * seq,
        ),
        name="attention_forward",
    )(number, normed, bias, kseg, qseg, *pieces)


def middle_kernel(tok_ref, wo_ref, gain_ref, target_ref, ctx_ref, middle_ref, *placed_refs):
    width = tok_ref.shape[1]
    context = ctx_ref[...].astype(F32).T.astype(BF16)
    middle = tok_ref[...].astype(F32) + dot(context, wo_ref[:, :width])
    middle_ref[...] = middle
    normed = (middle * rms_scale(middle) * gain_ref[...]).astype(BF16)
    for l, placed_ref in enumerate(placed_refs):
        rows = placed_ref.shape[0]
        placed_ref[...] = dot(slot_hot(target_ref[...], l * rows, rows), normed).astype(BF16)


def middle_step(tokens, w_out, gain, target_row, ctxt, local, rows):
    seq, width = tokens.shape
    return pl.pallas_call(
        middle_kernel,
        out_shape=[jax.ShapeDtypeStruct((seq, width), F32)]
        + [jax.ShapeDtypeStruct((rows, width), BF16)] * local,
        compiler_params=params(),
        cost_estimate=cost(
            2 * seq * width * width + 2 * local * rows * seq * width,
            2 * width * width + 8 * seq * width + 2 * local * rows * width,
        ),
        name="output_projection_dispatch",
    )(tokens, w_out, gain, target_row, ctxt)


def gate_of(logits, expert):
    top = jnp.max(logits, axis=-1, keepdims=True)
    ex = jnp.exp(logits - top)
    prob = ex / jnp.sum(ex, axis=-1, keepdims=True)
    hot = lax.broadcasted_iota(jnp.int32, logits.shape, 1) == expert
    gate = jnp.sum(jnp.where(hot, prob, 0.0), axis=-1, keepdims=True)
    return prob, hot, gate


def expert_kernel(
    num_ref, x_ref, c_ref, wr_ref, win_ref, wout_ref,
    scaled_ref, grad_ref, router_ref, gp_ref, acc_p, acc_g,
):
    step = pl.program_id(0)
    experts = router_ref.shape[0]

    @pl.when(step == 0)
    def _():
        _, _, gate = gate_of(dot(x_ref[...], wr_ref[...])[:, :experts], num_ref[1])
        gp_ref[...] = (gate * c_ref[...].astype(F32)).astype(BF16)
        acc_p[...] = jnp.zeros_like(acc_p)
        acc_g[...] = jnp.zeros_like(acc_g)

    def products(sub):
        pre = dot(x_ref[...], win_ref[0, :, sub : sub + SUB])
        return pre, dot_nt(gp_ref[...], wout_ref[0, sub : sub + SUB, :])

    hiddens, grads = [], []
    upcoming = products(0)
    for sub in range(SUB, win_ref.shape[2] + SUB, SUB):
        pre, grad_hidden = upcoming
        if sub < win_ref.shape[2]:
            upcoming = products(sub)
        hidden, slope = gelu_pair(pre)
        hiddens.append(hidden.astype(BF16))
        grads.append((grad_hidden * slope).astype(BF16))
    acc_p[...] += dot(jnp.concatenate(hiddens, axis=1), wout_ref[0])
    acc_g[...] += dot_nt(jnp.concatenate(grads, axis=1), win_ref[0])

    @pl.when(step == pl.num_programs(0) - 1)
    def _():
        x = x_ref[...]
        prob, hot, gate = gate_of(dot(x, wr_ref[...])[:, :experts], num_ref[1])
        produced = acc_p[...]
        scaled_ref[...] = (gate * produced).astype(BF16)
        grad_gate = jnp.sum(
            c_ref[...].astype(F32) * produced.astype(BF16).astype(F32), axis=-1, keepdims=True
        )
        grad_logits = prob * (jnp.where(hot, grad_gate, 0.0) - gate * grad_gate)
        logits_b = grad_logits.astype(BF16)
        grad_ref[...] = (acc_g[...] + dot_nt(logits_b, wr_ref[:, :experts])).astype(BF16)
        router_ref[...] = dot(grad_logits.T.astype(BF16), x)


def expert_step(number, x, c, w_or, w_in, w_out, local, block, experts):
    rows, width = x.shape
    ff = w_in.shape[2]
    router_cols = w_or.shape[1] - width
    whole = lambda a: pl.BlockSpec(a.shape, lambda f: (0,) * a.ndim)
    row_spec = pl.BlockSpec((rows, width), lambda f: (0, 0))
    return pl.pallas_call(
        expert_kernel,
        grid=(ff // block,),
        in_specs=[
            pl.BlockSpec(memory_space=pltpu.SMEM),
            whole(x),
            whole(c),
            pl.BlockSpec((width, router_cols), lambda f: (0, width // router_cols)),
            pl.BlockSpec((1, width, block), lambda f: (local, 0, f)),
            pl.BlockSpec((1, block, width), lambda f: (local, f, 0)),
        ],
        out_specs=[row_spec, row_spec, pl.BlockSpec((experts, width), lambda f: (0, 0))],
        out_shape=[
            jax.ShapeDtypeStruct((rows, width), BF16),
            jax.ShapeDtypeStruct((rows, width), BF16),
            jax.ShapeDtypeStruct((experts, width), F32),
        ],
        scratch_shapes=[
            pltpu.VMEM((rows, width), BF16),
            pltpu.VMEM((rows, width), F32),
            pltpu.VMEM((rows, width), F32),
        ],
        compiler_params=params(dimension_semantics=("arbitrary",)),
        cost_estimate=cost(
            8 * rows * width * ff, 4 * width * ff + 8 * rows * width, rows * ff
        ),
        name="expert_rows",
    )(number, x, c, w_or, w_in, w_out)


def expert_grad_kernel(experts, num_ref, x_ref, c_ref, wr_ref, win_ref, wout_ref, *refs):
    gin_ref, gout_ref, gp_ref, xt_ref = refs[-4:]
    parts, rows, width = x_ref.shape
    x = x_ref[...].reshape(parts * rows, width)

    @pl.when(pl.program_id(0) == 0)
    def _():
        _, _, gate = gate_of(dot(x, wr_ref[...])[:, :experts], num_ref[1])
        c = c_ref[...].reshape(parts * rows, width)
        gp_ref[...] = (gate * c.astype(F32)).astype(BF16)
        xt_ref[...] = x.astype(F32).T.astype(BF16)

    gp = gp_ref[...]
    pre_t = dot(win_ref[0].T, xt_ref[...])
    hidden_t, slope_t = gelu_pair(pre_t)
    grad_hidden_t = dot_nt(wout_ref[0], gp)
    gout_ref[0] = dot(hidden_t.astype(BF16), gp)
    gin_ref[0] = dot_nt(xt_ref[...], (grad_hidden_t * slope_t).astype(BF16))


def expert_grads(numbers, x_all, c_all, w_or, w_in, w_out, local, n_dp, experts, prior=()):
    parts, rows, width = x_all.shape
    ff = w_out.shape[1]
    router_cols = w_or.shape[1] - width
    part = ff // n_dp
    block = part
    steps = part // block
    whole = lambda a: pl.BlockSpec(a.shape, lambda f, n: (0,) * a.ndim)
    return pl.pallas_call(
        functools.partial(expert_grad_kernel, experts),
        grid_spec=pltpu.PrefetchScalarGridSpec(
            num_scalar_prefetch=1,
            grid=(steps,),
            in_specs=[
                whole(x_all),
                whole(c_all),
                pl.BlockSpec((width, router_cols), lambda f, n: (0, width // router_cols)),
                pl.BlockSpec((1, width, block), lambda f, n: (local, 0, n[0] * steps + f)),
                pl.BlockSpec((1, block, width), lambda f, n: (local, n[0] * steps + f, 0)),
            ]
            + [pl.BlockSpec(memory_space=pl.ANY)] * len(prior),
            out_specs=[
                pl.BlockSpec((1, width, block), lambda f, n: (local, 0, f)),
                pl.BlockSpec((1, block, width), lambda f, n: (local, f, 0)),
            ],
            scratch_shapes=[
                pltpu.VMEM((parts * rows, width), BF16),
                pltpu.VMEM((width, parts * rows), BF16),
            ],
        ),
        out_shape=[
            jax.ShapeDtypeStruct((w_out.shape[0], width, part), F32),
            jax.ShapeDtypeStruct((w_out.shape[0], part, width), F32),
        ],
        compiler_params=params(dimension_semantics=("arbitrary",)),
        cost_estimate=cost(
            8 * parts * rows * width * part,
            4 * parts * rows * width + 12 * width * part,
            parts * rows * part,
        ),
        input_output_aliases={6 + i: i for i in range(len(prior))},
        name="expert_weight_grads",
    )(numbers, x_all, c_all, w_or, w_in, w_out, *prior)


def split_rows(num_ref, full_ref, keep_ref, send_ref):
    part = keep_ref.shape[1]
    core = num_ref[0] & 1
    for y in range(keep_ref.shape[0]):
        own = pl.multiple_of((2 * y + core) * part, 16)
        other = pl.multiple_of((2 * y + 1 - core) * part, 16)
        keep_ref[y] = full_ref[pl.ds(own, part), :]
        send_ref[y] = full_ref[pl.ds(other, part), :]


def middle_back_kernel(top_size, num_ref, cot_ref, middle_ref, gain_ref, target_ref, wo_ref, ctx_ref, *refs):
    refs, (gmid_ref, gctx_ref, keep_ref, send_ref, ggain_ref, gwo_ref) = refs[:-6], refs[-6:]
    local = len(refs) // 2
    back_refs, router_refs = refs[:local], refs[local:]
    seq, width = cot_ref.shape
    target = target_ref[...]
    grad = jnp.zeros((seq, width), F32)
    for l, back in enumerate(back_refs):
        rows = back.shape[0]
        grad = grad + dot(token_hot(target, l * rows, rows), back[...])
    grad_in, grad_gain = norm_back(middle_ref[...], gain_ref[...], grad)
    ggain_ref[...] = grad_gain
    grad_middle = cot_ref[...].astype(F32) + grad_in
    gmid_ref[...] = grad_middle
    grad_attn = grad_middle.astype(BF16)
    gctx_ref[...] = dot_nt(grad_attn, wo_ref[:, :width]).astype(BF16)
    gwo_ref[:, :width] = dot(ctx_ref[...], grad_attn).astype(BF16)
    router = sum(ref[...] for ref in router_refs)
    spare = jnp.zeros((gwo_ref.shape[1] - width - router.shape[0], width), F32)
    gwo_ref[:, width:] = jnp.concatenate([router, spare], axis=0).T.astype(BF16)
    half = keep_ref.shape[0]
    top = num_ref[0] // top_size
    keep_ref[...] = gwo_ref[pl.ds(pl.multiple_of(top * half, 16), half), :]
    send_ref[...] = gwo_ref[pl.ds(pl.multiple_of((1 - top) * half, 16), half), :]


def middle_back(number, cot, middle, gain, target_col, w_or, ctxt, backs, routers, n_dp):
    seq, width = cot.shape
    sds = jax.ShapeDtypeStruct
    slots = sum(b.shape[0] for b in backs)
    half = sds((width // 2, w_or.shape[1]), BF16)
    vmem = pl.BlockSpec(memory_space=pltpu.VMEM)
    return pl.pallas_call(
        functools.partial(middle_back_kernel, n_dp // 2),
        in_specs=[pl.BlockSpec(memory_space=pltpu.SMEM)] + [vmem] * (6 + 2 * len(backs)),
        out_shape=[sds((seq, width), F32), sds((seq, width), BF16), half, half, sds((1, width), F32)],
        scratch_shapes=[pltpu.VMEM(w_or.shape, BF16)],
        compiler_params=params(),
        cost_estimate=cost(
            4 * seq * width * width + 2 * slots * seq * width,
            4 * width * width + 14 * seq * width + 2 * slots * width,
        ),
        name="second_norm_backward",
    )(number, cot, middle, gain, target_col, w_or, ctxt, *backs, *routers)


def attend_back_kernel(
    num_ref, normt_ref, q_ref, k_ref, v_ref, kt_ref, e_ref, rinv_ref, do_ref,
    keep_ref, send_ref, grads_ref, diag_ref, acc_ref, gw_ref,
):
    seq, cols = q_ref.shape
    heads = e_ref.shape[0]
    hd = cols // heads
    per_tile = TILE // hd
    lane = lax.broadcasted_iota(jnp.int32, (STRIP, TILE), 1) // hd
    row_bit = lax.broadcasted_iota(jnp.int32, (8, 2 * seq), 0)
    zero = jnp.zeros((STRIP, TILE), BF16)

    def own(ref, h, start):
        sl = slice(h // per_tile * TILE, (h // per_tile + 1) * TILE)
        return jnp.where(lane == h % per_tile, ref[start : start + STRIP, sl], zero)

    def products(h, start):
        sl = slice(h // per_tile * TILE, (h // per_tile + 1) * TILE)
        do_own = own(do_ref, h, start)
        return do_own, dot_nt(v_ref[:, sl], do_own)

    dk_tiles, dv_tiles, dqt_rows = [], [], []
    items = [(h, start) for h in range(heads) for start in range(0, seq, STRIP)]
    upcoming = products(*items[0])
    for h in range(heads):
        acc_ref[...] = jnp.zeros_like(acc_ref)
        dk = jnp.zeros((seq, TILE), F32)
        dv = jnp.zeros((seq, TILE), F32)
        dqt_parts = []
        for start in range(0, seq, STRIP):
            st = slice(start, start + STRIP)
            do_own, grad_w = upcoming
            at = items.index((h, start)) + 1
            if at < len(items):
                upcoming = products(*items[at])
            p = e_ref[h, :, st].astype(F32) * rinv_ref[h, :, st]
            t = grad_w * p
            ds = t - p * jnp.sum(t, axis=0, keepdims=True)
            dsb = ds.astype(BF16)
            dv = dv + dot(p.astype(BF16), do_own)
            dk = dk + dot(dsb, own(q_ref, h, start))
            dqt_parts.append(dot(kt_ref[h * hd : (h + 1) * hd, :], dsb))
            for b in range(0, seq, TILE):
                off = seq - TILE - b + start
                acc_ref[:, off : off + STRIP] += ds[b : b + TILE]
        if h % per_tile == 0:
            dk_tiles.append(dk)
            dv_tiles.append(dv)
        else:
            dk_tiles[-1] = dk_tiles[-1] + dk
            dv_tiles[-1] = dv_tiles[-1] + dv
        dqt_rows.append(jnp.concatenate(dqt_parts, axis=1))
        folded = acc_ref[...]
        half = TILE // 2
        while half >= 8:
            folded = folded[:half] + pltpu.roll(folded[half:], 2 * seq - half, 1)
            half //= 2
        for bit in (4, 2, 1):
            turned = pltpu.roll(folded, 2 * seq - bit, 1)
            folded = jnp.where((row_bit & bit) != 0, turned, folded)
        diag_ref[h] = jnp.sum(folded, axis=0, keepdims=True)
    dqt = jnp.concatenate(dqt_rows, axis=0) * (1.0 / math.sqrt(hd))
    grads_ref[:, :cols] = dqt.T.astype(BF16)
    for base, tiles in ((1, dk_tiles), (2, dv_tiles)):
        grads_ref[:, base * cols : (base + 1) * cols] = jnp.concatenate(tiles, axis=1).astype(BF16)
    gw_ref[...] = dot(normt_ref[...], grads_ref[...]).astype(BF16)
    split_rows(num_ref, gw_ref, keep_ref, send_ref)


def attend_back(number, normt, q, k, v, kt, e, rinv, grad_ctx, group, n_dp):
    seq, width = q.shape
    heads = e.shape[0]
    cols = width // heads * group
    steps = heads // group
    whole = lambda a: pl.BlockSpec(a.shape, lambda g: (0,) * a.ndim)
    nat = pl.BlockSpec((seq, cols), lambda g: (0, g))
    sds = jax.ShapeDtypeStruct
    half = (n_dp // 2, width // n_dp, 3 * width)
    half_spec = pl.BlockSpec((n_dp // 2, width // n_dp, 3 * cols), lambda g: (0, 0, g))
    return pl.pallas_call(
        attend_back_kernel,
        grid=(steps,),
        in_specs=[
            pl.BlockSpec(memory_space=pltpu.SMEM), whole(normt), nat, nat, nat,
            pl.BlockSpec((cols, seq), lambda g: (g, 0)),
            pl.BlockSpec((group, seq, seq), lambda g: (g, 0, 0)),
            pl.BlockSpec((group, 1, seq), lambda g: (g, 0, 0)),
            nat,
        ],
        out_specs=[
            half_spec, half_spec, pl.BlockSpec((seq, 3 * cols), lambda g: (0, g)),
            pl.BlockSpec((group, 1, 2 * seq), lambda g: (g, 0, 0)),
        ],
        out_shape=[
            sds(half, BF16), sds(half, BF16), sds((seq, 3 * width), BF16),
            sds((heads, 1, 2 * seq), F32),
        ],
        scratch_shapes=[pltpu.VMEM((TILE, 2 * seq), F32), pltpu.VMEM((width, 3 * cols), BF16)],
        compiler_params=params(dimension_semantics=("arbitrary",)),
        cost_estimate=cost(
            6 * seq * width * width + 8 * seq * seq * width,
            2 * (6 * width * width + 8 * seq * width + heads * seq * seq),
        ),
        name="attention_backward",
    )(number, normt, q, k, v, kt, e, rinv, grad_ctx)


def first_back_kernel(cols, num_ref, tok_ref, gain_ref, gmid_ref, grads_ref, *refs):
    pieces, (gtok_ref, ggain_ref, w_ref) = refs[:-3], refs[-3:]
    width = tok_ref.shape[1]
    join_rows(num_ref, pieces, w_ref)
    grad = jnp.zeros(tok_ref.shape, F32)
    for i, start in enumerate(range(0, 3 * width, cols)):
        col = i % 3 * width + i // 3 * cols
        grad = grad + dot_nt(grads_ref[:, start : start + cols], w_ref[:, col : col + cols])
    grad_in, grad_gain = norm_back(tok_ref[...].astype(F32), gain_ref[...], grad)
    gtok_ref[...] = gmid_ref[...] + grad_in
    ggain_ref[...] = grad_gain


def first_back(number, tokens, gain, grad_middle, grads, pieces, cols):
    seq, width = tokens.shape
    vmem = pl.BlockSpec(memory_space=pltpu.VMEM)
    return pl.pallas_call(
        functools.partial(first_back_kernel, cols),
        in_specs=[pl.BlockSpec(memory_space=pltpu.SMEM)] + [vmem] * (4 + len(pieces)),
        out_shape=[
            jax.ShapeDtypeStruct((seq, width), F32), jax.ShapeDtypeStruct((1, width), F32)
        ],
        scratch_shapes=[pltpu.VMEM((width, 3 * width), BF16)],
        compiler_params=params(),
        cost_estimate=cost(6 * seq * width * width, 6 * width * width + 16 * seq * width),
        name="first_norm_backward",
    )(number, tokens, gain, grad_middle, grads, *pieces)


def output_kernel(middle_ref, target_ref, *refs):
    out_ref = refs[-1]
    total = middle_ref[...]
    for l, back in enumerate(refs[:-1]):
        rows = back.shape[0]
        total = total + dot(token_hot(target_ref[...], l * rows, rows), back[...])
    out_ref[...] = total.astype(BF16)


def output_step(middle, target_col, backs):
    seq, width = middle.shape
    slots = sum(b.shape[0] for b in backs)
    return pl.pallas_call(
        output_kernel,
        out_shape=jax.ShapeDtypeStruct((seq, width), BF16),
        compiler_params=params(),
        cost_estimate=cost(2 * slots * seq * width, 6 * seq * width + 2 * slots * width),
        name="layer_output",
    )(middle, target_col, *backs)


def flip(value, axis, bit):
    size = lax.axis_size(axis)
    return lax.ppermute(value, axis, [(i, i ^ bit) for i in range(size)])


def butterfly_sum(value, axes):
    for axis in axes:
        bit = 1
        while bit < lax.axis_size(axis):
            value = value + flip(value, axis, bit)
            bit *= 2
    return value


def after(value, *others):
    return lax.optimization_barrier((value, *others))[0]


def gather_y(piece):
    pieces = {0: piece}
    bit = 2
    while bit < lax.axis_size("dp"):
        pieces.update({m | bit: flip(p, "dp", bit) for m, p in pieces.items()})
        bit *= 2
    return pieces


def gather_cores(pieces):
    pieces = {**pieces, **{m | 1: flip(p, "dp", 1) for m, p in pieces.items()}}
    return [pieces[m] for m in sorted(pieces)]


def reduce_bits(terms, bits, dp_index):
    first = None
    for bit in bits:
        mine = jnp.where((dp_index & bit) != 0, 1, 0)
        halves = [t.reshape(2, t.shape[0] // 2, *t.shape[1:]) for t in terms]
        pick = lambda i: [
            lax.dynamic_index_in_dim(t, i, 0, keepdims=False).astype(F32) for t in halves
        ]
        sent = sum(pick(1 - mine)).astype(BF16)
        first = sent if first is None else first
        terms = [sum(pick(mine)), flip(sent, "dp", bit)]
    return sum(t.astype(F32) for t in terms)[0], first


def sum_expert(total):
    peers = lax.axis_size("expert")
    rows, cols = total.shape
    parts = total.astype(BF16).reshape(peers, rows // peers, cols)
    arrived = lax.all_to_all(parts, "expert", split_axis=0, concat_axis=0, tiled=True)
    return jnp.sum(arrived.astype(F32), axis=0).astype(BF16)


def spread_expert(share, peers):
    rows, cols = share.shape
    spread = jnp.broadcast_to(share[None], (peers, rows, cols))
    shared = lax.all_to_all(spread, "expert", split_axis=0, concat_axis=0, tiled=True)
    return shared.reshape(peers * rows, cols).astype(F32)


def body(
    tokens, segments, routes, slots, bucket_table, gain_attn, w_query, w_key, w_value, w_output,
    rel_bias, gain_ffn, w_router, w_in, w_out, cotangent,
):
    seq, width = tokens.shape
    buckets, heads = rel_bias.shape
    experts = w_router.shape[1]
    n_dp = lax.axis_size("dp")
    peers = lax.axis_size("expert")
    local = w_in.shape[0]
    capacity = max(2, (5 * seq + 4 * experts - 1) // (4 * experts))
    rows = peers * capacity
    dp_index = lax.axis_index("dp")
    expert_index = lax.axis_index("expert")
    number = jnp.reshape(dp_index, (1,)).astype(jnp.int32)
    dp_bits = [1 << b for b in reversed(range(n_dp.bit_length() - 1))]
    group = 4
    cols = width // heads * group

    along_y = gather_y(beside(w_query, w_key, w_value))
    order = (routes % local) * rows + (routes // local) * capacity + slots
    target = jnp.where(slots >= 0, order, -1)
    target_row = target[None, :]
    by_peer = jnp.where(slots >= 0, routes * capacity + slots, -1)
    gain_one = gain_attn[None, :]
    gain_two = gain_ffn[None, :]

    def exchange(values):
        return lax.all_to_all(values, "expert", split_axis=0, concat_axis=0, tiled=True)

    def exchange_rows(values):
        return exchange(values.reshape(peers, capacity, width)).reshape(rows, width)

    reversed_table = jnp.concatenate([bucket_table[::-1], jnp.full((1,), -1, jnp.int32)])
    bucket_ids = jnp.arange(buckets, dtype=jnp.int32)
    hot_rev = (bucket_ids[:, None] == reversed_table[None, :]).astype(F32)
    rel_rev = jnp.dot(rel_bias.T, hot_rev, precision=HIGH)
    shifted = jnp.roll(reversed_table, 1 - TILE)
    hot_shifted = (shifted[:, None] == bucket_ids[None, :]).astype(F32)
    bias, normed, normt, kseg, qseg, target_col, by_col = prepare(
        rel_rev, tokens, gain_one, segments, jnp.stack([target, by_peer])
    )
    c_placed = list(place(target_row, cotangent, local, rows))
    c_here = [exchange_rows(c_placed[0])]
    numbers = [
        jnp.stack([dp_index, expert_index * local + l]).astype(jnp.int32) for l in range(local)
    ]
    along_y, bias, normed, normt, kseg, qseg, c_here[0], c_placed[1:], w_output, numbers = (
        lax.optimization_barrier(
            (along_y, bias, normed, normt, kseg, qseg, c_here[0], c_placed[1:], w_output, numbers)
        )
    )
    router_pad = jnp.pad(w_router, ((0, 0), (0, -experts % TILE)))
    w_or = lax.all_gather(
        jnp.concatenate([w_output, router_pad], axis=1), "dp", axis=0, tiled=True
    )
    pieces = gather_cores(along_y)
    *saved, ctxt = attend(number, normed, bias, kseg, qseg, pieces, heads, group)
    for part in c_placed[1:]:
        c_here.append(exchange_rows(part))
    middle, *placed = middle_step(tokens, w_or, gain_two, target_row, ctxt, local, rows)
    placed, *c_here = lax.optimization_barrier((placed, *c_here))
    arrived = [None] * local
    for l in reversed(range(local)):
        ready = after(placed[l], arrived[l + 1]) if l + 1 < local else placed[l]
        arrived[l] = exchange_rows(ready)
    x_all, c_all, backs, scaled, router_terms = ([None] * local for _ in range(5))
    for l in reversed(range(local)):
        sources = (arrived[l], c_here[l])
        if l + 1 < local:
            *sources, _ = lax.optimization_barrier((*sources, scaled[l + 1]))
        x_all[l], c_all[l] = [lax.all_gather(a, "dp", axis=0, tiled=False) for a in sources]
        scaled[l], grad_x, router_terms[l] = expert_step(
            numbers[l], arrived[l], c_here[l], w_or, w_in, w_out, l, 1024, experts
        )
        backs[l] = exchange_rows(grad_x)

    def weight_terms(l, prior):
        return expert_grads(
            numbers[l], x_all[l], c_all[l], w_or, w_in, w_out, l, n_dp, experts, prior
        )

    expert_terms = weight_terms(local - 1, ())
    backs, expert_terms = lax.optimization_barrier((backs, expert_terms))
    scaled, _ = lax.optimization_barrier((scaled, backs))
    stacked = jnp.stack([part.reshape(peers, capacity, width) for part in scaled], axis=1)
    returned = exchange(stacked.reshape(peers, local * capacity, width)).reshape(-1, width)

    grad_middle, grad_ctx, keep_o, send_o, ggain_two = middle_back(
        number, cotangent, middle, gain_two, target_col, w_or, ctxt, backs, router_terms, n_dp
    )
    keep, send, grads, diag = attend_back(number, normt, *saved, grad_ctx, group, n_dp)
    crossed_o = flip(send_o, "dp", dp_bits[0])
    crossed_o, send, returned, x_all, c_all = lax.optimization_barrier(
        (crossed_o, send, returned, x_all, c_all)
    )
    crossed = flip(send, "dp", 1)
    part, sent = reduce_bits([keep, crossed], dp_bits[:-1], dp_index)
    by_index = (n_dp // 2, width // n_dp, w_or.shape[1])
    terms_o = [t.reshape(by_index) for t in (keep_o, crossed_o)]
    part_o, _ = reduce_bits(terms_o, dp_bits[1:], dp_index)
    grad_tokens, ggain_one = first_back(
        number, tokens, gain_one, grad_middle, grads, pieces, cols
    )
    if sent is not None:
        part_o = after(part_o, sent)
    summed_o = sum_expert(part_o)
    grad_rel = jnp.dot(diag.reshape(heads, 2 * seq), hot_shifted, precision=HIGH)
    rel_row = jnp.pad(grad_rel.reshape(1, heads * buckets), ((0, 0), (0, width - heads * buckets)))
    late = jnp.concatenate([ggain_two, ggain_one, rel_row], axis=0)
    late = butterfly_sum(late, ("dp",))
    part, grad_tokens, summed_o, late = lax.optimization_barrier(
        (part, grad_tokens, summed_o, late)
    )
    late = butterfly_sum(late, ("expert",))
    summed = sum_expert(part)
    summed, late = lax.optimization_barrier((summed, late))
    ordered = [
        summed[:, g + i * cols : g + (i + 1) * cols]
        for i in range(3)
        for g in range(0, 3 * width, 3 * cols)
    ]
    shards = spread_expert(jnp.concatenate([*ordered, summed_o], axis=1), peers)
    for l in reversed(range(local - 1)):
        expert_terms = weight_terms(l, expert_terms)
    output = output_step(middle, by_col, [returned])
    total_rel = late[2, : heads * buckets].reshape(heads, buckets).T
    shard_q, shard_k, shard_v, shard_o = [
        shards[:, i * width : (i + 1) * width] for i in range(4)
    ]
    return (
        output,
        grad_tokens,
        late[1],
        shard_q,
        shard_k,
        shard_v,
        shard_o,
        total_rel,
        late[0],
        shards[:, 4 * width : 4 * width + experts],
        expert_terms[0],
        expert_terms[1],
    )


def solution(mesh):
    in_specs = (
        P(("dp", "expert"), None),
        P(("dp", "expert"), None),
        P(("dp", "expert")),
        P(("dp", "expert")),
        P(),
        P(),
        P("dp", None),
        P("dp", None),
        P("dp", None),
        P("dp", None),
        P(),
        P(),
        P("dp", None),
        P("expert", None, None),
        P("expert", None, None),
        P(("dp", "expert"), None),
    )
    out_specs = (
        P(("dp", "expert"), None),
        P(("dp", "expert"), None),
        P(),
        P("dp", None),
        P("dp", None),
        P("dp", None),
        P("dp", None),
        P(),
        P(),
        P("dp", None),
        P("expert", None, "dp"),
        P("expert", "dp", None),
    )
    return jax.shard_map(body, mesh=mesh, in_specs=in_specs, out_specs=out_specs, check_vma=False)
```

```python
import functools
import math

import jax
import jax.numpy as jnp
from jax import lax
from jax.experimental import pallas as pl
from jax.experimental.pallas import tpu as pltpu
from jax.sharding import PartitionSpec as P

EPS = 1e-06
HIGH = lax.Precision.HIGHEST
F32 = jnp.float32
BF16 = jnp.bfloat16
VMEM_LIMIT = 56 * 1024 * 1024
TILE = 128
STRIP = 256
SUB = 256
GELU_A = math.sqrt(2.0 / math.pi)
GELU_B = 0.044715


def dot(a, b):
    return jnp.dot(a, b, preferred_element_type=F32)


def dot_nt(a, b):
    return lax.dot_general(a, b, (((1,), (1,)), ((), ())), preferred_element_type=F32)


def params(**kw):
    return pltpu.CompilerParams(vmem_limit_bytes=VMEM_LIMIT, **kw)


def cost(flops, nbytes, trans=0):
    return pl.CostEstimate(flops=int(flops), bytes_accessed=int(nbytes), transcendentals=int(trans))


def rms_scale(stream):
    return lax.rsqrt(jnp.mean(stream * stream, axis=-1, keepdims=True) + EPS)


def norm_back(stream, gain, grad_out):
    scale = rms_scale(stream)
    grad_gain = jnp.sum(grad_out * (stream * scale), axis=0, keepdims=True)
    scaled = grad_out * gain
    inner = jnp.mean(scaled * stream, axis=-1, keepdims=True)
    grad_in = scale * scaled - stream * (scale * scale * scale * inner)
    return grad_in, grad_gain


def gelu_pair(v):
    sq = v * v
    power = jnp.minimum(v * (-2.0 * GELU_A - (2.0 * GELU_A * GELU_B) * sq), 80.0)
    total = 1.0 + jnp.exp(power)
    guess = pl.reciprocal(total, approx=True)
    half = guess * (2.0 - total * guess)
    value = v * half
    slope = half + value * (1.0 - half) * (2.0 * GELU_A + (6.0 * GELU_A * GELU_B) * sq)
    return value, slope


def slot_hot(target_row, start, rows):
    seq = target_row.shape[1]
    ids = lax.broadcasted_iota(jnp.int32, (rows, seq), 0) + start
    return (ids == target_row).astype(F32).astype(BF16)


def token_hot(target_col, start, rows):
    seq = target_col.shape[0]
    ids = lax.broadcasted_iota(jnp.int32, (seq, rows), 1) + start
    return (ids == target_col).astype(F32).astype(BF16)


def beside_kernel(*refs):
    width = refs[0].shape[1]
    for i, ref in enumerate(refs[:-1]):
        refs[-1][:, i * width : (i + 1) * width] = ref[...]


def beside(*arrays):
    rows, width = arrays[0].shape
    return pl.pallas_call(
        beside_kernel,
        out_shape=jax.ShapeDtypeStruct((rows, width * len(arrays)), arrays[0].dtype),
        compiler_params=params(),
        cost_estimate=cost(0, 4 * rows * width * len(arrays)),
        name="weights_side_by_side",
    )(*arrays)


def place_kernel(target_ref, rows_ref, *out_refs):
    for l, out_ref in enumerate(out_refs):
        rows = out_ref.shape[0]
        out_ref[...] = dot(slot_hot(target_ref[...], l * rows, rows), rows_ref[...]).astype(BF16)


def place(target_row, values, local, rows):
    seq, width = values.shape
    return pl.pallas_call(
        place_kernel,
        out_shape=[jax.ShapeDtypeStruct((rows, width), BF16)] * local,
        compiler_params=params(),
        cost_estimate=cost(2 * local * rows * seq * width, 2 * (local * rows + seq) * width),
        name="place_cotangent",
    )(target_row, values)


def prepare_kernel(
    rel_ref, tok_ref, gain_ref, seg_ref, rows_ref,
    out_ref, normed_ref, normt_ref, kseg_ref, qseg_ref, *col_refs,
):
    heads, width = rel_ref.shape
    wide = out_ref.shape[2]
    for h in range(heads):
        base = jnp.broadcast_to(rel_ref[h : h + 1, :], (TILE, width))
        turned = pltpu.roll(base, width - (TILE - 1), 1, stride=1, stride_axis=0)
        out_ref[h] = turned[:, :wide]
    stream = tok_ref[...].astype(F32)
    normed = stream * rms_scale(stream) * gain_ref[...]
    normed_ref[...] = normed.astype(BF16)
    normt_ref[...] = normed.T.astype(BF16)
    seq = tok_ref.shape[0]
    same = (lax.broadcasted_iota(jnp.int32, (TILE, seq), 0) == seg_ref[...]).astype(F32).T
    kseg_ref[...] = same.astype(BF16)
    qseg_ref[...] = ((same - 1.0) * 1e9).astype(BF16)
    for i, col_ref in enumerate(col_refs):
        row = jnp.broadcast_to(rows_ref[i : i + 1, :].astype(F32), (TILE, seq))
        col_ref[...] = row.T[:, :1].astype(jnp.int32)


def prepare(rel_rev, tokens, gain, segments, slot_rows):
    heads, span = rel_rev.shape
    seq, width = tokens.shape
    wide = 2 * seq - TILE
    return pl.pallas_call(
        prepare_kernel,
        out_shape=[
            jax.ShapeDtypeStruct((heads, TILE, wide), F32),
            jax.ShapeDtypeStruct((seq, width), BF16),
            jax.ShapeDtypeStruct((width, seq), BF16),
            jax.ShapeDtypeStruct((seq, TILE), BF16),
            jax.ShapeDtypeStruct((seq, TILE), BF16),
        ]
        + [jax.ShapeDtypeStruct((seq, 1), jnp.int32)] * slot_rows.shape[0],
        compiler_params=params(),
        cost_estimate=cost(heads * TILE * span, 4 * heads * TILE * wide + 6 * seq * width),
        name="bias_and_first_norm",
    )(rel_rev, tokens, gain, segments, slot_rows)


def join_rows(num_ref, pieces, w_ref):
    part = pieces[0].shape[0]
    for mask, piece in enumerate(pieces):
        row = pl.multiple_of((num_ref[0] ^ mask) * part, 16)
        w_ref[pl.ds(row, part), :] = piece[...]


def attend_kernel(num_ref, normed_ref, bias_ref, kseg_ref, qseg_ref, *refs):
    pieces, refs = refs[:-8], refs[-8:]
    q_ref, k_ref, v_ref, kt_ref, e_ref, rinv_ref, ctxt_ref, w_ref = refs
    seq, cols = q_ref.shape
    width = normed_ref.shape[1]
    step = pl.program_id(0)

    @pl.when(step == 0)
    def _():
        join_rows(num_ref, pieces, w_ref)

    at = lambda base: pl.ds(pl.multiple_of(base * width + step * cols, TILE), cols)
    heads = e_ref.shape[0]
    hd = cols // heads
    per_tile = TILE // hd
    normed = normed_ref[...]
    q32 = dot(normed, w_ref[:, at(0)]).astype(BF16).astype(F32) * (1.0 / math.sqrt(hd))
    k32 = dot(normed, w_ref[:, at(1)])
    v32 = dot(normed, w_ref[:, at(2)])
    q_ref[...] = q32.astype(BF16)
    k_ref[...] = k32.astype(BF16)
    v_ref[...] = v32.astype(BF16)
    kt_ref[...] = k32.T.astype(BF16)
    vt = v32.T.astype(BF16)
    lane = lax.broadcasted_iota(jnp.int32, (STRIP, TILE), 1) // hd
    kseg = kseg_ref[...]

    def scores_of(h, start):
        sl = slice(h // per_tile * TILE, (h // per_tile + 1) * TILE)
        st = slice(start, start + STRIP)
        q_pair = q_ref[st, sl]
        q_own = jnp.where(lane == h % per_tile, q_pair, jnp.zeros_like(q_pair))
        k_all = jnp.concatenate([k_ref[:, sl], kseg], axis=1)
        return dot_nt(k_all, jnp.concatenate([q_own, qseg_ref[st]], axis=1))

    items = [(h, start) for h in range(heads) for start in range(0, seq, STRIP)]
    upcoming = scores_of(*items[0])
    for i, (h, start) in enumerate(items):
        scores = upcoming
        if i + 1 < len(items):
            upcoming = scores_of(*items[i + 1])
        parts = []
        for b in range(0, seq, TILE):
            off = seq - TILE - b + start
            parts.append(scores[b : b + TILE] + bias_ref[h, :, off : off + STRIP])
        scores = jnp.concatenate(parts, axis=0)
        e = jnp.exp(scores - jnp.max(scores, axis=0, keepdims=True))
        rinv = 1.0 / jnp.sum(e, axis=0, keepdims=True)
        eb = e.astype(BF16)
        e_ref[h, :, start : start + STRIP] = eb
        rinv_ref[h, :, start : start + STRIP] = rinv
        ctxt = dot(vt[h * hd : (h + 1) * hd], eb) * rinv
        ctxt_ref[h * hd : (h + 1) * hd, start : start + STRIP] = ctxt.astype(BF16)


def attend(number, normed, bias, kseg, qseg, pieces, heads, group):
    seq, width = normed.shape
    cols = width // heads * group
    steps = heads // group
    wide = bias.shape[2]
    whole = lambda a: pl.BlockSpec(a.shape, lambda g: (0,) * a.ndim)
    nat = pl.BlockSpec((seq, cols), lambda g: (0, g))
    tr = pl.BlockSpec((cols, seq), lambda g: (g, 0))
    sds = jax.ShapeDtypeStruct
    return pl.pallas_call(
        attend_kernel,
        grid=(steps,),
        in_specs=[
            pl.BlockSpec(memory_space=pltpu.SMEM), whole(normed),
            pl.BlockSpec((group, TILE, wide), lambda g: (g, 0, 0)), whole(kseg), whole(qseg),
        ]
        + [whole(p) for p in pieces],
        out_specs=[
            nat, nat, nat, tr,
            pl.BlockSpec((group, seq, seq), lambda g: (g, 0, 0)),
            pl.BlockSpec((group, 1, seq), lambda g: (g, 0, 0)),
            tr,
        ],
        out_shape=[
            sds((seq, width), BF16), sds((seq, width), BF16), sds((seq, width), BF16),
            sds((width, seq), BF16), sds((heads, seq, seq), BF16), sds((heads, 1, seq), F32),
            sds((width, seq), BF16),
        ],
        scratch_shapes=[pltpu.VMEM((width, 3 * width), BF16)],
        compiler_params=params(dimension_semantics=("arbitrary",)),
        cost_estimate=cost(
            6 * seq * width * width + 4 * seq * seq * width,
            2 * (3 * width * width + 9 * seq * width + heads * seq * seq) + 4 * bias.size,
            heads * seq * seq,
        ),
        name="attention_forward",
    )(number, normed, bias, kseg, qseg, *pieces)


def middle_kernel(tok_ref, wo_ref, gain_ref, target_ref, ctx_ref, middle_ref, *placed_refs):
    width = tok_ref.shape[1]
    context = ctx_ref[...].astype(F32).T.astype(BF16)
    middle = tok_ref[...].astype(F32) + dot(context, wo_ref[:, :width])
    middle_ref[...] = middle
    normed = (middle * rms_scale(middle) * gain_ref[...]).astype(BF16)
    for l, placed_ref in enumerate(placed_refs):
        rows = placed_ref.shape[0]
        placed_ref[...] = dot(slot_hot(target_ref[...], l * rows, rows), normed).astype(BF16)


def middle_step(tokens, w_out, gain, target_row, ctxt, local, rows):
    seq, width = tokens.shape
    return pl.pallas_call(
        middle_kernel,
        out_shape=[jax.ShapeDtypeStruct((seq, width), F32)]
        + [jax.ShapeDtypeStruct((rows, width), BF16)] * local,
        compiler_params=params(),
        cost_estimate=cost(
            2 * seq * width * width + 2 * local * rows * seq * width,
            2 * width * width + 8 * seq * width + 2 * local * rows * width,
        ),
        name="output_projection_dispatch",
    )(tokens, w_out, gain, target_row, ctxt)


def gate_of(logits, expert):
    top = jnp.max(logits, axis=-1, keepdims=True)
    ex = jnp.exp(logits - top)
    prob = ex / jnp.sum(ex, axis=-1, keepdims=True)
    hot = lax.broadcasted_iota(jnp.int32, logits.shape, 1) == expert
    gate = jnp.sum(jnp.where(hot, prob, 0.0), axis=-1, keepdims=True)
    return prob, hot, gate


def expert_kernel(
    num_ref, x_ref, c_ref, wr_ref, win_ref, wout_ref,
    scaled_ref, grad_ref, router_ref, gp_ref, acc_p, acc_g,
):
    step = pl.program_id(0)
    experts = router_ref.shape[0]

    @pl.when(step == 0)
    def _():
        _, _, gate = gate_of(dot(x_ref[...], wr_ref[...])[:, :experts], num_ref[1])
        gp_ref[...] = (gate * c_ref[...].astype(F32)).astype(BF16)
        acc_p[...] = jnp.zeros_like(acc_p)
        acc_g[...] = jnp.zeros_like(acc_g)

    def products(sub):
        pre = dot(x_ref[...], win_ref[0, :, sub : sub + SUB])
        return pre, dot_nt(gp_ref[...], wout_ref[0, sub : sub + SUB, :])

    hiddens, grads = [], []
    upcoming = products(0)
    for sub in range(SUB, win_ref.shape[2] + SUB, SUB):
        pre, grad_hidden = upcoming
        if sub < win_ref.shape[2]:
            upcoming = products(sub)
        hidden, slope = gelu_pair(pre)
        hiddens.append(hidden.astype(BF16))
        grads.append((grad_hidden * slope).astype(BF16))
    acc_p[...] += dot(jnp.concatenate(hiddens, axis=1), wout_ref[0])
    acc_g[...] += dot_nt(jnp.concatenate(grads, axis=1), win_ref[0])

    @pl.when(step == pl.num_programs(0) - 1)
    def _():
        x = x_ref[...]
        prob, hot, gate = gate_of(dot(x, wr_ref[...])[:, :experts], num_ref[1])
        produced = acc_p[...]
        scaled_ref[...] = (gate * produced).astype(BF16)
        grad_gate = jnp.sum(
            c_ref[...].astype(F32) * produced.astype(BF16).astype(F32), axis=-1, keepdims=True
        )
        grad_logits = prob * (jnp.where(hot, grad_gate, 0.0) - gate * grad_gate)
        logits_b = grad_logits.astype(BF16)
        grad_ref[...] = (acc_g[...] + dot_nt(logits_b, wr_ref[:, :experts])).astype(BF16)
        router_ref[...] = dot(grad_logits.T.astype(BF16), x)


def expert_step(number, x, c, w_or, w_in, w_out, local, block, experts):
    rows, width = x.shape
    ff = w_in.shape[2]
    router_cols = w_or.shape[1] - width
    whole = lambda a: pl.BlockSpec(a.shape, lambda f: (0,) * a.ndim)
    row_spec = pl.BlockSpec((rows, width), lambda f: (0, 0))
    return pl.pallas_call(
        expert_kernel,
        grid=(ff // block,),
        in_specs=[
            pl.BlockSpec(memory_space=pltpu.SMEM),
            whole(x),
            whole(c),
            pl.BlockSpec((width, router_cols), lambda f: (0, width // router_cols)),
            pl.BlockSpec((1, width, block), lambda f: (local, 0, f)),
            pl.BlockSpec((1, block, width), lambda f: (local, f, 0)),
        ],
        out_specs=[row_spec, row_spec, pl.BlockSpec((experts, width), lambda f: (0, 0))],
        out_shape=[
            jax.ShapeDtypeStruct((rows, width), BF16),
            jax.ShapeDtypeStruct((rows, width), BF16),
            jax.ShapeDtypeStruct((experts, width), F32),
        ],
        scratch_shapes=[
            pltpu.VMEM((rows, width), BF16),
            pltpu.VMEM((rows, width), F32),
            pltpu.VMEM((rows, width), F32),
        ],
        compiler_params=params(dimension_semantics=("arbitrary",)),
        cost_estimate=cost(
            8 * rows * width * ff, 4 * width * ff + 8 * rows * width, rows * ff
        ),
        name="expert_rows",
    )(number, x, c, w_or, w_in, w_out)


def expert_grad_kernel(experts, num_ref, x_ref, c_ref, wr_ref, win_ref, wout_ref, *refs):
    gin_ref, gout_ref, gp_ref, xt_ref = refs[-4:]
    parts, rows, width = x_ref.shape
    x = x_ref[...].reshape(parts * rows, width)

    @pl.when(pl.program_id(0) == 0)
    def _():
        _, _, gate = gate_of(dot(x, wr_ref[...])[:, :experts], num_ref[1])
        c = c_ref[...].reshape(parts * rows, width)
        gp_ref[...] = (gate * c.astype(F32)).astype(BF16)
        xt_ref[...] = x.astype(F32).T.astype(BF16)

    gp = gp_ref[...]
    pre_t = dot(win_ref[0].T, xt_ref[...])
    hidden_t, slope_t = gelu_pair(pre_t)
    grad_hidden_t = dot_nt(wout_ref[0], gp)
    gout_ref[0] = dot(hidden_t.astype(BF16), gp)
    gin_ref[0] = dot_nt(xt_ref[...], (grad_hidden_t * slope_t).astype(BF16))


def expert_grads(numbers, x_all, c_all, w_or, w_in, w_out, local, n_dp, experts, prior=()):
    parts, rows, width = x_all.shape
    ff = w_out.shape[1]
    router_cols = w_or.shape[1] - width
    part = ff // n_dp
    block = part
    steps = part // block
    whole = lambda a: pl.BlockSpec(a.shape, lambda f, n: (0,) * a.ndim)
    return pl.pallas_call(
        functools.partial(expert_grad_kernel, experts),
        grid_spec=pltpu.PrefetchScalarGridSpec(
            num_scalar_prefetch=1,
            grid=(steps,),
            in_specs=[
                whole(x_all),
                whole(c_all),
                pl.BlockSpec((width, router_cols), lambda f, n: (0, width // router_cols)),
                pl.BlockSpec((1, width, block), lambda f, n: (local, 0, n[0] * steps + f)),
                pl.BlockSpec((1, block, width), lambda f, n: (local, n[0] * steps + f, 0)),
            ]
            + [pl.BlockSpec(memory_space=pl.ANY)] * len(prior),
            out_specs=[
                pl.BlockSpec((1, width, block), lambda f, n: (local, 0, f)),
                pl.BlockSpec((1, block, width), lambda f, n: (local, f, 0)),
            ],
            scratch_shapes=[
                pltpu.VMEM((parts * rows, width), BF16),
                pltpu.VMEM((width, parts * rows), BF16),
            ],
        ),
        out_shape=[
            jax.ShapeDtypeStruct((w_out.shape[0], width, part), F32),
            jax.ShapeDtypeStruct((w_out.shape[0], part, width), F32),
        ],
        compiler_params=params(dimension_semantics=("arbitrary",)),
        cost_estimate=cost(
            8 * parts * rows * width * part,
            4 * parts * rows * width + 12 * width * part,
            parts * rows * part,
        ),
        input_output_aliases={6 + i: i for i in range(len(prior))},
        name="expert_weight_grads",
    )(numbers, x_all, c_all, w_or, w_in, w_out, *prior)


def split_rows(num_ref, full_ref, keep_ref, send_ref):
    part = keep_ref.shape[1]
    core = num_ref[0] & 1
    for y in range(keep_ref.shape[0]):
        own = pl.multiple_of((2 * y + core) * part, 16)
        other = pl.multiple_of((2 * y + 1 - core) * part, 16)
        keep_ref[y] = full_ref[pl.ds(own, part), :]
        send_ref[y] = full_ref[pl.ds(other, part), :]


def middle_back_kernel(top_size, num_ref, cot_ref, middle_ref, gain_ref, target_ref, wo_ref, ctx_ref, *refs):
    refs, (gmid_ref, gctx_ref, keep_ref, send_ref, ggain_ref, gwo_ref) = refs[:-6], refs[-6:]
    local = len(refs) // 2
    back_refs, router_refs = refs[:local], refs[local:]
    seq, width = cot_ref.shape
    target = target_ref[...]
    grad = jnp.zeros((seq, width), F32)
    for l, back in enumerate(back_refs):
        rows = back.shape[0]
        grad = grad + dot(token_hot(target, l * rows, rows), back[...])
    grad_in, grad_gain = norm_back(middle_ref[...], gain_ref[...], grad)
    ggain_ref[...] = grad_gain
    grad_middle = cot_ref[...].astype(F32) + grad_in
    gmid_ref[...] = grad_middle
    grad_attn = grad_middle.astype(BF16)
    gctx_ref[...] = dot_nt(grad_attn, wo_ref[:, :width]).astype(BF16)
    gwo_ref[:, :width] = dot(ctx_ref[...], grad_attn).astype(BF16)
    router = sum(ref[...] for ref in router_refs)
    spare = jnp.zeros((gwo_ref.shape[1] - width - router.shape[0], width), F32)
    gwo_ref[:, width:] = jnp.concatenate([router, spare], axis=0).T.astype(BF16)
    half = keep_ref.shape[0]
    top = num_ref[0] // top_size
    keep_ref[...] = gwo_ref[pl.ds(pl.multiple_of(top * half, 16), half), :]
    send_ref[...] = gwo_ref[pl.ds(pl.multiple_of((1 - top) * half, 16), half), :]


def middle_back(number, cot, middle, gain, target_col, w_or, ctxt, backs, routers, n_dp):
    seq, width = cot.shape
    sds = jax.ShapeDtypeStruct
    slots = sum(b.shape[0] for b in backs)
    half = sds((width // 2, w_or.shape[1]), BF16)
    vmem = pl.BlockSpec(memory_space=pltpu.VMEM)
    return pl.pallas_call(
        functools.partial(middle_back_kernel, n_dp // 2),
        in_specs=[pl.BlockSpec(memory_space=pltpu.SMEM)] + [vmem] * (6 + 2 * len(backs)),
        out_shape=[sds((seq, width), F32), sds((seq, width), BF16), half, half, sds((1, width), F32)],
        scratch_shapes=[pltpu.VMEM(w_or.shape, BF16)],
        compiler_params=params(),
        cost_estimate=cost(
            4 * seq * width * width + 2 * slots * seq * width,
            4 * width * width + 14 * seq * width + 2 * slots * width,
        ),
        name="second_norm_backward",
    )(number, cot, middle, gain, target_col, w_or, ctxt, *backs, *routers)


def attend_back_kernel(
    num_ref, normt_ref, q_ref, k_ref, v_ref, kt_ref, e_ref, rinv_ref, do_ref,
    keep_ref, send_ref, grads_ref, diag_ref, acc_ref, gw_ref,
):
    seq, cols = q_ref.shape
    heads = e_ref.shape[0]
    hd = cols // heads
    per_tile = TILE // hd
    lane = lax.broadcasted_iota(jnp.int32, (STRIP, TILE), 1) // hd
    row_bit = lax.broadcasted_iota(jnp.int32, (8, 2 * seq), 0)
    zero = jnp.zeros((STRIP, TILE), BF16)

    def own(ref, h, start):
        sl = slice(h // per_tile * TILE, (h // per_tile + 1) * TILE)
        return jnp.where(lane == h % per_tile, ref[start : start + STRIP, sl], zero)

    def products(h, start):
        sl = slice(h // per_tile * TILE, (h // per_tile + 1) * TILE)
        do_own = own(do_ref, h, start)
        return do_own, dot_nt(v_ref[:, sl], do_own)

    dk_tiles, dv_tiles, dqt_rows = [], [], []
    items = [(h, start) for h in range(heads) for start in range(0, seq, STRIP)]
    upcoming = products(*items[0])
    for h in range(heads):
        acc_ref[...] = jnp.zeros_like(acc_ref)
        dk = jnp.zeros((seq, TILE), F32)
        dv = jnp.zeros((seq, TILE), F32)
        dqt_parts = []
        for start in range(0, seq, STRIP):
            st = slice(start, start + STRIP)
            do_own, grad_w = upcoming
            at = items.index((h, start)) + 1
            if at < len(items):
                upcoming = products(*items[at])
            p = e_ref[h, :, st].astype(F32) * rinv_ref[h, :, st]
            t = grad_w * p
            ds = t - p * jnp.sum(t, axis=0, keepdims=True)
            dsb = ds.astype(BF16)
            dv = dv + dot(p.astype(BF16), do_own)
            dk = dk + dot(dsb, own(q_ref, h, start))
            dqt_parts.append(dot(kt_ref[h * hd : (h + 1) * hd, :], dsb))
            for b in range(0, seq, TILE):
                off = seq - TILE - b + start
                acc_ref[:, off : off + STRIP] += ds[b : b + TILE]
        if h % per_tile == 0:
            dk_tiles.append(dk)
            dv_tiles.append(dv)
        else:
            dk_tiles[-1] = dk_tiles[-1] + dk
            dv_tiles[-1] = dv_tiles[-1] + dv
        dqt_rows.append(jnp.concatenate(dqt_parts, axis=1))
        folded = acc_ref[...]
        half = TILE // 2
        while half >= 8:
            folded = folded[:half] + pltpu.roll(folded[half:], 2 * seq - half, 1)
            half //= 2
        for bit in (4, 2, 1):
            turned = pltpu.roll(folded, 2 * seq - bit, 1)
            folded = jnp.where((row_bit & bit) != 0, turned, folded)
        diag_ref[h] = jnp.sum(folded, axis=0, keepdims=True)
    dqt = jnp.concatenate(dqt_rows, axis=0) * (1.0 / math.sqrt(hd))
    grads_ref[:, :cols] = dqt.T.astype(BF16)
    for base, tiles in ((1, dk_tiles), (2, dv_tiles)):
        grads_ref[:, base * cols : (base + 1) * cols] = jnp.concatenate(tiles, axis=1).astype(BF16)
    gw_ref[...] = dot(normt_ref[...], grads_ref[...]).astype(BF16)
    split_rows(num_ref, gw_ref, keep_ref, send_ref)


def attend_back(number, normt, q, k, v, kt, e, rinv, grad_ctx, group, n_dp):
    seq, width = q.shape
    heads = e.shape[0]
    cols = width // heads * group
    steps = heads // group
    whole = lambda a: pl.BlockSpec(a.shape, lambda g: (0,) * a.ndim)
    nat = pl.BlockSpec((seq, cols), lambda g: (0, g))
    sds = jax.ShapeDtypeStruct
    half = (n_dp // 2, width // n_dp, 3 * width)
    half_spec = pl.BlockSpec((n_dp // 2, width // n_dp, 3 * cols), lambda g: (0, 0, g))
    return pl.pallas_call(
        attend_back_kernel,
        grid=(steps,),
        in_specs=[
            pl.BlockSpec(memory_space=pltpu.SMEM), whole(normt), nat, nat, nat,
            pl.BlockSpec((cols, seq), lambda g: (g, 0)),
            pl.BlockSpec((group, seq, seq), lambda g: (g, 0, 0)),
            pl.BlockSpec((group, 1, seq), lambda g: (g, 0, 0)),
            nat,
        ],
        out_specs=[
            half_spec, half_spec, pl.BlockSpec((seq, 3 * cols), lambda g: (0, g)),
            pl.BlockSpec((group, 1, 2 * seq), lambda g: (g, 0, 0)),
        ],
        out_shape=[
            sds(half, BF16), sds(half, BF16), sds((seq, 3 * width), BF16),
            sds((heads, 1, 2 * seq), F32),
        ],
        scratch_shapes=[pltpu.VMEM((TILE, 2 * seq), F32), pltpu.VMEM((width, 3 * cols), BF16)],
        compiler_params=params(dimension_semantics=("arbitrary",)),
        cost_estimate=cost(
            6 * seq * width * width + 8 * seq * seq * width,
            2 * (6 * width * width + 8 * seq * width + heads * seq * seq),
        ),
        name="attention_backward",
    )(number, normt, q, k, v, kt, e, rinv, grad_ctx)


def first_back_kernel(cols, num_ref, tok_ref, gain_ref, gmid_ref, grads_ref, *refs):
    pieces, (gtok_ref, ggain_ref, w_ref) = refs[:-3], refs[-3:]
    width = tok_ref.shape[1]
    join_rows(num_ref, pieces, w_ref)
    grad = jnp.zeros(tok_ref.shape, F32)
    for i, start in enumerate(range(0, 3 * width, cols)):
        col = i % 3 * width + i // 3 * cols
        grad = grad + dot_nt(grads_ref[:, start : start + cols], w_ref[:, col : col + cols])
    grad_in, grad_gain = norm_back(tok_ref[...].astype(F32), gain_ref[...], grad)
    gtok_ref[...] = gmid_ref[...] + grad_in
    ggain_ref[...] = grad_gain


def first_back(number, tokens, gain, grad_middle, grads, pieces, cols):
    seq, width = tokens.shape
    vmem = pl.BlockSpec(memory_space=pltpu.VMEM)
    return pl.pallas_call(
        functools.partial(first_back_kernel, cols),
        in_specs=[pl.BlockSpec(memory_space=pltpu.SMEM)] + [vmem] * (4 + len(pieces)),
        out_shape=[
            jax.ShapeDtypeStruct((seq, width), F32), jax.ShapeDtypeStruct((1, width), F32)
        ],
        scratch_shapes=[pltpu.VMEM((width, 3 * width), BF16)],
        compiler_params=params(),
        cost_estimate=cost(6 * seq * width * width, 6 * width * width + 16 * seq * width),
        name="first_norm_backward",
    )(number, tokens, gain, grad_middle, grads, *pieces)


def output_kernel(middle_ref, target_ref, *refs):
    out_ref = refs[-1]
    total = middle_ref[...]
    for l, back in enumerate(refs[:-1]):
        rows = back.shape[0]
        total = total + dot(token_hot(target_ref[...], l * rows, rows), back[...])
    out_ref[...] = total.astype(BF16)


def output_step(middle, target_col, backs):
    seq, width = middle.shape
    slots = sum(b.shape[0] for b in backs)
    return pl.pallas_call(
        output_kernel,
        out_shape=jax.ShapeDtypeStruct((seq, width), BF16),
        compiler_params=params(),
        cost_estimate=cost(2 * slots * seq * width, 6 * seq * width + 2 * slots * width),
        name="layer_output",
    )(middle, target_col, *backs)


def flip(value, axis, bit):
    size = lax.axis_size(axis)
    return lax.ppermute(value, axis, [(i, i ^ bit) for i in range(size)])


def butterfly_sum(value, axes):
    for axis in axes:
        bit = 1
        while bit < lax.axis_size(axis):
            value = value + flip(value, axis, bit)
            bit *= 2
    return value


def after(value, *others):
    return lax.optimization_barrier((value, *others))[0]


def gather_y(piece):
    pieces = {0: piece}
    bit = 2
    while bit < lax.axis_size("dp"):
        pieces.update({m | bit: flip(p, "dp", bit) for m, p in pieces.items()})
        bit *= 2
    return pieces


def gather_cores(pieces):
    pieces = {**pieces, **{m | 1: flip(p, "dp", 1) for m, p in pieces.items()}}
    return [pieces[m] for m in sorted(pieces)]


def reduce_bits(terms, bits, dp_index):
    first = None
    for bit in bits:
        mine = jnp.where((dp_index & bit) != 0, 1, 0)
        halves = [t.reshape(2, t.shape[0] // 2, *t.shape[1:]) for t in terms]
        pick = lambda i: [
            lax.dynamic_index_in_dim(t, i, 0, keepdims=False).astype(F32) for t in halves
        ]
        sent = sum(pick(1 - mine)).astype(BF16)
        first = sent if first is None else first
        terms = [sum(pick(mine)), flip(sent, "dp", bit)]
    return sum(t.astype(F32) for t in terms)[0], first


def sum_expert(total):
    peers = lax.axis_size("expert")
    rows, cols = total.shape
    parts = total.astype(BF16).reshape(peers, rows // peers, cols)
    arrived = lax.all_to_all(parts, "expert", split_axis=0, concat_axis=0, tiled=True)
    return jnp.sum(arrived.astype(F32), axis=0).astype(BF16)


def spread_expert(share, peers):
    rows, cols = share.shape
    spread = jnp.broadcast_to(share[None], (peers, rows, cols))
    shared = lax.all_to_all(spread, "expert", split_axis=0, concat_axis=0, tiled=True)
    return shared.reshape(peers * rows, cols).astype(F32)


def body(
    tokens, segments, routes, slots, bucket_table, gain_attn, w_query, w_key, w_value, w_output,
    rel_bias, gain_ffn, w_router, w_in, w_out, cotangent,
):
    seq, width = tokens.shape
    buckets, heads = rel_bias.shape
    experts = w_router.shape[1]
    n_dp = lax.axis_size("dp")
    peers = lax.axis_size("expert")
    local = w_in.shape[0]
    capacity = max(2, (5 * seq + 4 * experts - 1) // (4 * experts))
    rows = peers * capacity
    dp_index = lax.axis_index("dp")
    expert_index = lax.axis_index("expert")
    number = jnp.reshape(dp_index, (1,)).astype(jnp.int32)
    dp_bits = [1 << b for b in reversed(range(n_dp.bit_length() - 1))]
    group = 4
    cols = width // heads * group

    along_y = gather_y(beside(w_query, w_key, w_value))
    order = (routes % local) * rows + (routes // local) * capacity + slots
    target = jnp.where(slots >= 0, order, -1)
    target_row = target[None, :]
    by_peer = jnp.where(slots >= 0, routes * capacity + slots, -1)
    gain_one = gain_attn[None, :]
    gain_two = gain_ffn[None, :]

    def exchange(values):
        return lax.all_to_all(values, "expert", split_axis=0, concat_axis=0, tiled=True)

    def exchange_rows(values):
        return exchange(values.reshape(peers, capacity, width)).reshape(rows, width)

    reversed_table = jnp.concatenate([bucket_table[::-1], jnp.full((1,), -1, jnp.int32)])
    bucket_ids = jnp.arange(buckets, dtype=jnp.int32)
    hot_rev = (bucket_ids[:, None] == reversed_table[None, :]).astype(F32)
    rel_rev = jnp.dot(rel_bias.T, hot_rev, precision=HIGH)
    shifted = jnp.roll(reversed_table, 1 - TILE)
    hot_shifted = (shifted[:, None] == bucket_ids[None, :]).astype(F32)
    bias, normed, normt, kseg, qseg, target_col, by_col = prepare(
        rel_rev, tokens, gain_one, segments, jnp.stack([target, by_peer])
    )
    c_placed = list(place(target_row, cotangent, local, rows))
    c_here = [exchange_rows(c_placed[0])]
    numbers = [
        jnp.stack([dp_index, expert_index * local + l]).astype(jnp.int32) for l in range(local)
    ]
    along_y, bias, normed, normt, kseg, qseg, c_here[0], c_placed[1:], w_output, numbers = (
        lax.optimization_barrier(
            (along_y, bias, normed, normt, kseg, qseg, c_here[0], c_placed[1:], w_output, numbers)
        )
    )
    router_pad = jnp.pad(w_router, ((0, 0), (0, -experts % TILE)))
    w_or = lax.all_gather(
        jnp.concatenate([w_output, router_pad], axis=1), "dp", axis=0, tiled=True
    )
    pieces = gather_cores(along_y)
    *saved, ctxt = attend(number, normed, bias, kseg, qseg, pieces, heads, group)
    for part in c_placed[1:]:
        c_here.append(exchange_rows(part))
    middle, *placed = middle_step(tokens, w_or, gain_two, target_row, ctxt, local, rows)
    placed, *c_here = lax.optimization_barrier((placed, *c_here))
    arrived = [None] * local
    for l in reversed(range(local)):
        ready = after(placed[l], arrived[l + 1]) if l + 1 < local else placed[l]
        arrived[l] = exchange_rows(ready)
    x_all, c_all, backs, scaled, router_terms = ([None] * local for _ in range(5))
    for l in reversed(range(local)):
        sources = (arrived[l], c_here[l])
        if l + 1 < local:
            *sources, _ = lax.optimization_barrier((*sources, scaled[l + 1]))
        x_all[l], c_all[l] = [lax.all_gather(a, "dp", axis=0, tiled=False) for a in sources]
        scaled[l], grad_x, router_terms[l] = expert_step(
            numbers[l], arrived[l], c_here[l], w_or, w_in, w_out, l, 1024, experts
        )
        backs[l] = exchange_rows(grad_x)

    def weight_terms(l, prior):
        return expert_grads(
            numbers[l], x_all[l], c_all[l], w_or, w_in, w_out, l, n_dp, experts, prior
        )

    expert_terms = weight_terms(local - 1, ())
    backs, expert_terms = lax.optimization_barrier((backs, expert_terms))
    scaled, _ = lax.optimization_barrier((scaled, backs))
    stacked = jnp.stack([part.reshape(peers, capacity, width) for part in scaled], axis=1)
    returned = exchange(stacked.reshape(peers, local * capacity, width)).reshape(-1, width)

    grad_middle, grad_ctx, keep_o, send_o, ggain_two = middle_back(
        number, cotangent, middle, gain_two, target_col, w_or, ctxt, backs, router_terms, n_dp
    )
    keep, send, grads, diag = attend_back(number, normt, *saved, grad_ctx, group, n_dp)
    crossed_o = flip(send_o, "dp", dp_bits[0])
    crossed_o, send, returned, x_all, c_all = lax.optimization_barrier(
        (crossed_o, send, returned, x_all, c_all)
    )
    crossed = flip(send, "dp", 1)
    part, sent = reduce_bits([keep, crossed], dp_bits[:-1], dp_index)
    by_index = (n_dp // 2, width // n_dp, w_or.shape[1])
    terms_o = [t.reshape(by_index) for t in (keep_o, crossed_o)]
    part_o, _ = reduce_bits(terms_o, dp_bits[1:], dp_index)
    grad_tokens, ggain_one = first_back(
        number, tokens, gain_one, grad_middle, grads, pieces, cols
    )
    if sent is not None:
        part_o = after(part_o, sent)
    summed_o = sum_expert(part_o)
    grad_rel = jnp.dot(diag.reshape(heads, 2 * seq), hot_shifted, precision=HIGH)
    rel_row = jnp.pad(grad_rel.reshape(1, heads * buckets), ((0, 0), (0, width - heads * buckets)))
    late = jnp.concatenate([ggain_two, ggain_one, rel_row], axis=0)
    late = butterfly_sum(late, ("dp",))
    part, grad_tokens, summed_o, late = lax.optimization_barrier(
        (part, grad_tokens, summed_o, late)
    )
    bit = 1
    while 2 * bit < peers:
        late = late + flip(late, "expert", bit)
        bit *= 2
    summed = sum_expert(part)
    summed, late = lax.optimization_barrier((summed, late))
    if bit < peers:
        late = late + flip(late, "expert", bit)
    ordered = [
        summed[:, g + i * cols : g + (i + 1) * cols]
        for i in range(3)
        for g in range(0, 3 * width, 3 * cols)
    ]
    shards = spread_expert(jnp.concatenate([*ordered, summed_o], axis=1), peers)
    for l in reversed(range(local - 1)):
        expert_terms = weight_terms(l, expert_terms)
    output = output_step(middle, by_col, [returned])
    total_rel = late[2, : heads * buckets].reshape(heads, buckets).T
    shard_q, shard_k, shard_v, shard_o = [
        shards[:, i * width : (i + 1) * width] for i in range(4)
    ]
    return (
        output,
        grad_tokens,
        late[1],
        shard_q,
        shard_k,
        shard_v,
        shard_o,
        total_rel,
        late[0],
        shards[:, 4 * width : 4 * width + experts],
        expert_terms[0],
        expert_terms[1],
    )


def solution(mesh):
    in_specs = (
        P(("dp", "expert"), None),
        P(("dp", "expert"), None),
        P(("dp", "expert")),
        P(("dp", "expert")),
        P(),
        P(),
        P("dp", None),
        P("dp", None),
        P("dp", None),
        P("dp", None),
        P(),
        P(),
        P("dp", None),
        P("expert", None, None),
        P("expert", None, None),
        P(("dp", "expert"), None),
    )
    out_specs = (
        P(("dp", "expert"), None),
        P(("dp", "expert"), None),
        P(),
        P("dp", None),
        P("dp", None),
        P("dp", None),
        P("dp", None),
        P(),
        P(),
        P("dp", None),
        P("expert", None, "dp"),
        P("expert", "dp", None),
    )
    return jax.shard_map(body, mesh=mesh, in_specs=in_specs, out_specs=out_specs, check_vma=False)
```
